32 devices in a mesh: layer: 4 (over y, x), latent: 4 (over z), dp: 2 (over core).
Axes of the slice: x: 2, y: 2, z: 4, core: 2. Of those that a mesh axis runs over, the one named last changes fastest.
Arguments:
- pre_codes: bfloat16 [4, 1024, 2, 128], P('layer', ('latent', 'dp')), may hold values from -6 to 6
- block_ids: int32 [4, 1024, 2], P('layer', ('latent', 'dp')), may hold values from 0 to 63, as said below
- activations: bfloat16 [4, 1024, 4096], P('layer', ('latent', 'dp')), may hold values from -6 to 6
- target: bfloat16 [1024, 4096], P(('latent', 'dp')), may hold values from -6 to 6
- decoder: bfloat16 [4, 8192, 4096], P('layer', 'latent'), may hold values from -0.25 to 0.25
Outputs:
- decoder_grad: bfloat16 [4, 8192, 4096], P('layer', 'latent', 'dp')
- encoder_grad: bfloat16 [4, 8192, 4096], P('layer', 'latent', 'dp')
The draws below stay inside these ranges and needn't reach their ends.
Inputs may be any that keep to these rules, and one draw needn't show every extreme that they name: `block_ids`: the 2 block numbers of a token in one layer are distinct. Among the tokens of one device in one layer (aligned blocks of 128 tokens), each block number is named at most 8 times, and in every layer some block number is named exactly 8 times by the tokens of every device.
All inputs are finite; a program needn't handle non-finite values.
Results may differ from the reference program's by a relative error of at most 0.0053.
Values may be sent and summed in bfloat16 or wider, within the bound.
No kernel may reach another device: no remote copies, remote signals or barrier semaphores. Data moves between devices by JAX's collectives and lax.ppermute only.
A program may use at most 192 MiB of HBM per device.

```python
import jax
import jax.numpy as jnp
from jax import lax

D = 4096
BLOCK = 128
BLOCKS = 64
ACTIVE = 2
TOK_DEV = 128
SOURCES = 4
TOKENS = 1024
LATENTS = 8192
CAP = 8


def draw_block_ids(key, part):
    groups = TOKENS // TOK_DEV
    pair_count = TOK_DEV * ACTIVE
    key_hot = jax.random.fold_in(key, 11)
    key_len = jax.random.fold_in(key, 12)
    key_perm = jax.random.fold_in(key, 13)
    hot_block = jax.random.randint(key_hot, (SOURCES, 1, 1), 0, BLOCKS, dtype=jnp.int32)
    lengths = jax.random.randint(key_len, (SOURCES, groups, BLOCKS), CAP // 2, CAP + 1, dtype=jnp.int32)
    first_run = (jnp.arange(BLOCKS, dtype=jnp.int32) == 0)[None, None, :]
    lengths = jnp.where(first_run, jnp.int32(CAP), lengths).astype(jnp.int32)
    run_ends = jnp.cumsum(lengths, axis=2, dtype=jnp.int32)
    position = jnp.arange(pair_count, dtype=jnp.int32)
    run_index = jnp.sum((position[None, None, :, None] >= run_ends[:, :, None, :]).astype(jnp.int32), axis=3, dtype=jnp.int32)
    raw_scores = jax.random.randint(key_perm, (SOURCES, groups, BLOCKS - 1), 0, 1 << 20, dtype=jnp.int32)
    scores = raw_scores * BLOCKS + jnp.arange(BLOCKS - 1, dtype=jnp.int32)[None, None, :]
    offsets = jnp.argsort(scores, axis=2).astype(jnp.int32) + 1
    run_table = jnp.concatenate([jnp.zeros((SOURCES, groups, 1), jnp.int32), offsets], axis=2)
    run_offset = jnp.take_along_axis(run_table, run_index, axis=2)
    chosen = (hot_block + run_offset) % BLOCKS
    chosen = chosen.reshape(SOURCES, groups, ACTIVE, TOK_DEV)
    chosen = jnp.transpose(chosen, (0, 1, 3, 2)).reshape(SOURCES, TOKENS, ACTIVE)
    return chosen.astype(jnp.int32)


def block_scale(rng, extent, shards, least, high):
    def one(dim, parts):
        steps = jax.random.uniform(jax.random.fold_in(jax.random.fold_in(rng, 6), dim), (parts,), jnp.float32, least / len(shards), high / len(shards))
        return jnp.repeat(jnp.exp(steps), extent[dim] // parts).reshape((-1,) + (1,) * (len(extent) - dim - 1))

    gain = one(*shards[0])
    for cut in shards[1:]:
        gain = gain * one(*cut)
    return gain


def bell_draw(stream_key, dims, spread, most, split=(), kind=jnp.bfloat16):
    result = spread * jax.random.normal(stream_key, dims, jnp.float32)
    if split:
        result = result * block_scale(stream_key, dims, split, -0.22, 0.18)
    return jnp.clip(result, -most, most).astype(kind)


def setup_inputs(seed: int = 0) -> dict:
    key_list = jax.random.split(jax.random.key(seed), 6)
    return {
        "pre_codes": bell_draw(key_list[0], (SOURCES, TOKENS, ACTIVE, BLOCK), 1.0, 6.0, ((0, 4), (1, 8))),
        "block_ids": draw_block_ids(jax.random.fold_in(key_list[5], 71), 0),
        "activations": bell_draw(key_list[2], (SOURCES, TOKENS, D), 1.0, 6.0, ((0, 4), (1, 8))),
        "target": bell_draw(key_list[3], (TOKENS, D), 1.0, 6.0, ((0, 8),)),
        "decoder": bell_draw(key_list[4], (SOURCES, LATENTS, D), (SOURCES * ACTIVE * BLOCK // 2) ** -0.5, 0.25, ((0, 4), (1, 4))),
    }


def reference(pre_codes, block_ids, activations, target, decoder):
    pair_count = TOKENS * ACTIVE
    rows_max = (TOKENS // TOK_DEV) * CAP
    code_vals = jnp.maximum(pre_codes, jnp.zeros((), pre_codes.dtype))
    flat_ids = block_ids.reshape(SOURCES, pair_count).astype(jnp.int32)
    sorted_pairs = jnp.argsort(flat_ids, axis=1, stable=True).astype(jnp.int32)
    sorted_pairs = jnp.concatenate([sorted_pairs, jnp.zeros((SOURCES, rows_max), jnp.int32)], axis=1)
    block_range = jnp.arange(BLOCKS, dtype=jnp.int32)
    counts = jnp.sum((flat_ids[:, :, None] == block_range[None, None, :]).astype(jnp.int32), axis=1).astype(jnp.int32)
    starts = (jnp.cumsum(counts, axis=1) - counts).astype(jnp.int32)
    code_pairs = code_vals.reshape(SOURCES, pair_count, BLOCK)
    pre_pairs = pre_codes.reshape(SOURCES, pair_count, BLOCK)
    weights = decoder.reshape(SOURCES, BLOCKS, BLOCK, D)
    layer_index = jnp.repeat(jnp.arange(SOURCES, dtype=jnp.int32), BLOCKS)
    block_index = jnp.tile(block_range, SOURCES)
    row_index = jnp.arange(rows_max, dtype=jnp.int32)

    def select_rows(layer_now, block_now):
        picked = lax.dynamic_slice(sorted_pairs[layer_now], (starts[layer_now, block_now],), (rows_max,))
        in_block = row_index < counts[layer_now, block_now]
        token_index = (picked // ACTIVE).astype(jnp.int32)
        return picked, in_block, token_index

    def forward(rebuilt, step_pair):
        layer_now, block_now = step_pair
        picked, in_block, token_index = select_rows(layer_now, block_now)
        bf_zero = jnp.zeros((), code_pairs.dtype)
        row_codes = jnp.where(in_block[:, None], code_pairs[layer_now][picked], bf_zero)
        contrib = jnp.dot(row_codes, weights[layer_now, block_now], preferred_element_type=jnp.float32)
        contrib = lax.optimization_barrier(contrib.astype(jnp.bfloat16)).astype(jnp.float32)
        return rebuilt.at[token_index].add(contrib), None

    rebuilt, _ = lax.scan(forward, jnp.zeros((TOKENS, D), jnp.float32), (layer_index, block_index))
    errors = ((rebuilt - target.astype(jnp.float32)) / TOK_DEV).astype(jnp.bfloat16)

    def backward(unused_carry, step_pair):
        layer_now, block_now = step_pair
        picked, in_block, token_index = select_rows(layer_now, block_now)
        bf_zero = jnp.zeros((), code_pairs.dtype)
        row_codes = jnp.where(in_block[:, None], code_pairs[layer_now][picked], bf_zero)
        row_pre = pre_pairs[layer_now][picked]
        row_errors = jnp.where(in_block[:, None], errors[token_index], jnp.zeros((), errors.dtype))
        row_inputs = activations[layer_now][token_index]
        block_rows = weights[layer_now, block_now]
        code_grad = jnp.dot(row_errors, block_rows.T, preferred_element_type=jnp.float32)
        pre_grad = jnp.where(row_pre > 0, code_grad, jnp.zeros((), jnp.float32)).astype(jnp.bfloat16)
        dec_part = jnp.dot(row_codes.T, row_errors, preferred_element_type=jnp.float32)
        enc_part = jnp.dot(pre_grad.T, row_inputs, preferred_element_type=jnp.float32)
        return unused_carry, (dec_part.astype(jnp.bfloat16), enc_part.astype(jnp.bfloat16))

    _, (dec_rows, enc_rows) = lax.scan(backward, jnp.zeros((), jnp.float32), (layer_index, block_index))
    decoder_grad = dec_rows.reshape(SOURCES, LATENTS, D)
    encoder_grad = enc_rows.reshape(SOURCES, LATENTS, D)
    return decoder_grad, encoder_grad
```

```python
import jax
import jax.numpy as jnp
from jax import lax
from jax.sharding import PartitionSpec as P

CHUNKS = 2


def local_contrib(received_pre, weights, lat_count, local_blocks):
    code_vals = jnp.maximum(received_pre, jnp.zeros((), received_pre.dtype))
    slot_span = received_pre.shape[1]
    block_size = received_pre.shape[2]
    grouped = code_vals.reshape(lat_count, local_blocks, slot_span, block_size)
    contrib = jnp.einsum("sbcl,bld->sbcd", grouped, weights, preferred_element_type=jnp.float32)
    contrib = contrib.astype(jnp.bfloat16).reshape(
        lat_count * local_blocks, slot_span, weights.shape[2]
    )
    return lax.all_to_all(contrib, "latent", split_axis=0, concat_axis=0, tiled=True)


def slot_plan(pre_codes, block_ids, activations, target, decoder):
    lat_count = lax.axis_size("latent")
    tok_count = activations.shape[1]
    model_width = activations.shape[2]
    active_count = block_ids.shape[2]
    block_size = pre_codes.shape[3]
    lat_rows = decoder.shape[1]
    local_blocks = lat_rows // block_size
    all_blocks = local_blocks * lat_count
    capacity = 2 * tok_count * active_count // all_blocks
    slot_count = all_blocks * capacity
    pair_count = tok_count * active_count
    pair_block = block_ids[0].T.reshape(pair_count)
    member = (pair_block[:, None] == jnp.arange(all_blocks, dtype=jnp.int32)[None, :]).astype(
        jnp.int32
    )
    before = jnp.cumsum(member, axis=0) - member
    pair_rank = jnp.sum(before * member, axis=1)
    target_slot = pair_block * capacity + pair_rank
    slot_pair = (jnp.arange(slot_count, dtype=jnp.int32)[:, None] == target_slot[None, :]).astype(
        jnp.bfloat16
    )
    slot_token = jnp.sum(slot_pair.reshape(slot_count, active_count, tok_count), axis=1)
    pre_pairs = jnp.transpose(pre_codes[0], (1, 0, 2)).reshape(pair_count, block_size)
    pre_slots = jnp.dot(slot_pair, pre_pairs, preferred_element_type=jnp.float32).astype(
        jnp.bfloat16
    )
    pre_slots = pre_slots.reshape(all_blocks, capacity, block_size)
    inputs = activations[0]
    weights = decoder[0].reshape(local_blocks, block_size, model_width)
    input_slots = jnp.dot(slot_token, inputs, preferred_element_type=jnp.float32).astype(
        jnp.bfloat16
    )
    input_slots = input_slots.reshape(all_blocks, capacity, model_width)
    pieces = (
        lax.all_to_all(pre_slots, "latent", split_axis=0, concat_axis=0, tiled=True),
        lax.all_to_all(input_slots, "latent", split_axis=0, concat_axis=0, tiled=True),
    )
    returned = local_contrib(pieces[0], weights, lat_count, local_blocks)
    returned, received_pre, received_inputs = (returned, pieces[0], pieces[1])
    part_sum = jnp.einsum(
        "st,sd->td",
        slot_token,
        returned.reshape(slot_count, model_width),
        preferred_element_type=jnp.float32,
    )
    rebuilt = lax.psum(part_sum, "layer")
    errors = ((rebuilt - target.astype(jnp.float32)) / tok_count).astype(jnp.bfloat16)
    error_slots = jnp.dot(slot_token, errors, preferred_element_type=jnp.float32).astype(
        jnp.bfloat16
    )
    error_slots = error_slots.reshape(all_blocks, capacity, model_width)
    received_errors = lax.all_to_all(error_slots, "latent", split_axis=0, concat_axis=0, tiled=True)
    pre_blocks = received_pre.reshape(lat_count, local_blocks, capacity, block_size)
    code_blocks = jnp.maximum(pre_blocks, jnp.zeros((), pre_blocks.dtype))
    error_blocks = received_errors.reshape(lat_count, local_blocks, capacity, model_width)
    input_blocks = received_inputs.reshape(lat_count, local_blocks, capacity, model_width)
    code_grad = jnp.einsum(
        "sbcd,bld->sbcl", error_blocks, weights, preferred_element_type=jnp.float32
    )
    pre_grad = jnp.where(pre_blocks > 0, code_grad, jnp.zeros((), jnp.float32)).astype(jnp.bfloat16)
    dec_term = jnp.einsum(
        "sbcl,sbcd->bld", code_blocks, error_blocks, preferred_element_type=jnp.float32
    )
    enc_term = jnp.einsum(
        "sbcl,sbcd->bld", pre_grad, input_blocks, preferred_element_type=jnp.float32
    )
    dec_term = dec_term.reshape(lat_rows, model_width)
    enc_term = enc_term.reshape(lat_rows, model_width)
    dec_half, enc_half = (
        lax.psum_scatter(dec_term, "dp", scatter_dimension=1, tiled=True),
        lax.psum_scatter(enc_term, "dp", scatter_dimension=1, tiled=True),
    )
    return (dec_half.astype(jnp.bfloat16)[None], enc_half.astype(jnp.bfloat16)[None])


def shift(value, axis, step):
    count = lax.axis_size(axis)
    return lax.ppermute(value, axis, [(i, (i + step) % count) for i in range(count)])


def flip(value, axis, bit):
    count = lax.axis_size(axis)
    return lax.ppermute(value, axis, [(i, i ^ bit) for i in range(count)])


def hop(value, axis, step, least):
    count = lax.axis_size(axis)
    if step > 0:
        pairs = [(i, i + 1) for i in range(least, count - 1)]
    else:
        pairs = [(i, i - 1) for i in range(1, count - least)]
    return lax.ppermute(value, axis, pairs)


def gather_line(own, axis):
    count = lax.axis_size(axis)
    up, down = [own], [own]
    for step in range(1, count):
        up.append(hop(up[-1], axis, 1, step - 1))
        down.append(hop(down[-1], axis, -1, step - 1))
    return [own] + [down[k] + up[count - k] for k in range(1, count)]


def dense_plan(pre_codes, block_ids, activations, target, decoder):
    lay_count = lax.axis_size("layer")
    lat_count = lax.axis_size("latent")
    dp_count = lax.axis_size("dp")
    lay_here = lax.axis_index("layer")
    lat_here = lax.axis_index("latent")
    dp_here = lax.axis_index("dp")
    tok_count = activations.shape[1]
    model_width = activations.shape[2]
    active_count = block_ids.shape[2]
    block_size = pre_codes.shape[3]
    lat_rows = decoder.shape[1]
    local_blocks = lat_rows // block_size
    half = model_width // dp_count
    part = tok_count // lay_count
    piece = dp_count * part
    f32, bf16 = jnp.float32, jnp.bfloat16

    def arrange(rows):
        cut = rows.reshape((lay_count, part) + rows.shape[1:])
        return jnp.concatenate(
            [lax.dynamic_index_in_dim(cut, lay_here ^ r, 0, False) for r in range(lay_count)], axis=0
        )

    def columns(rows, which):
        return lax.dynamic_slice_in_dim(rows, which * half, half, axis=1)

    pre_rows = arrange(pre_codes[0]).reshape(tok_count * active_count, block_size)
    id_rows = arrange(block_ids[0]).T.reshape(-1, block_size).astype(bf16)
    message = jnp.concatenate([pre_rows, id_rows], axis=0)
    message = jnp.stack([message] + [shift(message, "latent", -k) for k in range(1, lat_count)])
    message = jnp.stack([message, flip(message, "dp", 1)], axis=1)
    pair_rows = tok_count * active_count
    pre_all = message[:, :, :pair_rows].reshape(
        lat_count, dp_count, lay_count, part, active_count, block_size
    )
    id_all = message[:, :, pair_rows:].reshape(lat_count, dp_count, active_count, lay_count, part)
    pre_all = jnp.transpose(pre_all, (2, 0, 1, 3, 4, 5))
    id_all = jnp.transpose(id_all, (3, 0, 1, 4, 2))
    all_tok = lay_count * lat_count * piece
    pre_all = pre_all.reshape(all_tok, active_count, block_size)
    id_all = id_all.reshape(all_tok, active_count).astype(jnp.int32) - lat_here * local_blocks
    here = id_all[:, :, None] == jnp.arange(local_blocks, dtype=jnp.int32)

    def spread(pairs, mask):
        out = jnp.zeros((), pairs.dtype)
        for j in range(active_count):
            out = jnp.where(mask[:, j, :, None], pairs[:, j, None, :], out)
        return out.reshape(all_tok, lat_rows)

    codes = spread(jnp.maximum(pre_all, jnp.zeros((), bf16)), here)

    acts = arrange(activations[0])
    acts = jnp.stack([columns(acts, dp_here), flip(columns(acts, 1 - dp_here), "dp", 1)])
    acts = jnp.stack(gather_line(acts, "latent"))

    weights = columns(decoder[0], dp_here)
    goal = arrange(target)[:part]
    goal = jnp.concatenate([columns(goal, dp_here), flip(columns(goal, 1 - dp_here), "dp", 1)])

    code_rows = codes.reshape(lay_count, lat_count * piece, lat_rows)
    chunks = CHUNKS
    width = half // chunks
    bits = [1 << i for i in range(lay_count.bit_length() - 1)]

    def rows_of(order, fixed):
        out = [fixed]
        for bit in order:
            out = out + [r | bit for r in out]
        return out

    def reduce_layer(chunk):
        order = bits if chunk % 2 == 0 else bits[::-1]
        w = weights[:, chunk * width:(chunk + 1) * width]

        def partial(names):
            rows = jnp.concatenate([code_rows[r] for r in names], axis=0)
            return jnp.dot(rows, w, preferred_element_type=f32).astype(bf16)

        sent = partial(rows_of(order[1:], order[0]))
        got = flip(sent, "layer", order[0])
        total = got.astype(f32) + partial(rows_of(order[1:], 0)).astype(f32)
        for bit in order[1:]:
            size = total.shape[0] // 2
            got = flip(total[size:].astype(bf16), "layer", bit)
            total = total[:size] + got.astype(f32)
        return total

    def reduce_latent(total, chunk):
        cut = total.reshape(lat_count, piece, width)
        out = cut[0]
        for k in range(1, lat_count):
            out = out + shift(cut[k].astype(bf16), "latent", k).astype(f32)
        want = goal[:, chunk * width:(chunk + 1) * width].astype(f32)
        return ((out - want) / tok_count).astype(bf16)

    def gather_errors(own, chunk):
        rows = jnp.concatenate([own] + [shift(own, "latent", -k) for k in range(1, lat_count)], axis=0)
        order = bits if chunk % 2 == 0 else bits[::-1]
        for bit in order[::-1]:
            rows = jnp.concatenate([rows, flip(rows, "layer", bit)], axis=0)
        names = rows_of(order[::-1], 0)
        rows = rows.reshape(lay_count, lat_count * piece, width)
        return jnp.concatenate([rows[names.index(r)] for r in range(lay_count)], axis=0)

    errors = []
    for chunk in range(chunks):
        errors.append(gather_errors(reduce_latent(reduce_layer(chunk), chunk), chunk))

    grad_pairs = jnp.zeros((all_tok, active_count, block_size), f32)
    dec_parts = []
    for chunk in range(chunks):
        w = weights[:, chunk * width:(chunk + 1) * width]
        dec_parts.append(lax.dot_general(codes, errors[chunk], (((0,), (0,)), ((), ())), preferred_element_type=f32).astype(bf16))
        grad = lax.dot_general(errors[chunk], w, (((1,), (1,)), ((), ())), preferred_element_type=f32)
        grad = grad.reshape(all_tok, 1, local_blocks, block_size)
        grad_pairs = grad_pairs + jnp.sum(jnp.where(here[:, :, :, None], grad, 0.0), axis=2)
    theirs = flip(grad_pairs, "dp", 1).reshape(lay_count * lat_count, dp_count, part, active_count, block_size)
    grad_pairs = grad_pairs + theirs[:, ::-1].reshape(grad_pairs.shape)
    pre_grad = jnp.where(pre_all > 0, grad_pairs, 0.0).astype(bf16)

    def by_latent(rows):
        cut = rows.reshape((lay_count, lat_count * dp_count, part) + rows.shape[1:])
        return jnp.swapaxes(cut, 0, 1).reshape(rows.shape)

    pre_grad = spread(by_latent(pre_grad), by_latent(here))
    enc = lax.dot_general(
        pre_grad, acts.reshape(all_tok, half), (((0,), (0,)), ((), ())), preferred_element_type=f32
    )
    return jnp.concatenate(dec_parts, axis=1)[None], enc.astype(bf16)[None]


def per_device(pre_codes, block_ids, activations, target, decoder):
    lat_count = lax.axis_size("latent")
    lay_count = lax.axis_size("layer")
    dp_count = lax.axis_size("dp")
    tok_count = activations.shape[1]
    active_count = block_ids.shape[2]
    block_size = pre_codes.shape[3]
    all_blocks = decoder.shape[1] // block_size * lat_count
    slots = 2 * tok_count * active_count // lat_count
    dense = (
        slots >= tok_count
        and dp_count == 2
        and lay_count & (lay_count - 1) == 0
        and tok_count % lay_count == 0
        and tok_count * active_count % block_size == 0
        and all_blocks <= 256
    )
    plan = dense_plan if dense else slot_plan
    return plan(pre_codes, block_ids, activations, target, decoder)


def solution(mesh):
    placed = (
        P("layer", ("latent", "dp"), None, None),
        P("layer", ("latent", "dp"), None),
        P("layer", ("latent", "dp"), None),
        P(("latent", "dp"), None),
        P("layer", "latent", None),
    )
    return jax.shard_map(
        per_device,
        mesh=mesh,
        in_specs=placed,
        out_specs=(P("layer", "latent", "dp"), P("layer", "latent", "dp")),
        check_vma=False,
    )
```

```python
import functools

import jax
import jax.numpy as jnp
from jax import lax
from jax.experimental import pallas as pl
from jax.experimental.pallas import tpu as pltpu
from jax.sharding import PartitionSpec as P

PAIRS = 1
VMEM_BYTES = 48 * 1024 * 1024


def local_contrib(received_pre, weights, lat_count, local_blocks):
    code_vals = jnp.maximum(received_pre, jnp.zeros((), received_pre.dtype))
    slot_span = received_pre.shape[1]
    block_size = received_pre.shape[2]
    grouped = code_vals.reshape(lat_count, local_blocks, slot_span, block_size)
    contrib = jnp.einsum("sbcl,bld->sbcd", grouped, weights, preferred_element_type=jnp.float32)
    contrib = contrib.astype(jnp.bfloat16).reshape(
        lat_count * local_blocks, slot_span, weights.shape[2]
    )
    return lax.all_to_all(contrib, "latent", split_axis=0, concat_axis=0, tiled=True)


def slot_plan(pre_codes, block_ids, activations, target, decoder):
    lat_count = lax.axis_size("latent")
    tok_count = activations.shape[1]
    model_width = activations.shape[2]
    active_count = block_ids.shape[2]
    block_size = pre_codes.shape[3]
    lat_rows = decoder.shape[1]
    local_blocks = lat_rows // block_size
    all_blocks = local_blocks * lat_count
    capacity = 2 * tok_count * active_count // all_blocks
    slot_count = all_blocks * capacity
    pair_count = tok_count * active_count
    pair_block = block_ids[0].T.reshape(pair_count)
    member = (pair_block[:, None] == jnp.arange(all_blocks, dtype=jnp.int32)[None, :]).astype(
        jnp.int32
    )
    before = jnp.cumsum(member, axis=0) - member
    pair_rank = jnp.sum(before * member, axis=1)
    target_slot = pair_block * capacity + pair_rank
    slot_pair = (jnp.arange(slot_count, dtype=jnp.int32)[:, None] == target_slot[None, :]).astype(
        jnp.bfloat16
    )
    slot_token = jnp.sum(slot_pair.reshape(slot_count, active_count, tok_count), axis=1)
    pre_pairs = jnp.transpose(pre_codes[0], (1, 0, 2)).reshape(pair_count, block_size)
    pre_slots = jnp.dot(slot_pair, pre_pairs, preferred_element_type=jnp.float32).astype(
        jnp.bfloat16
    )
    pre_slots = pre_slots.reshape(all_blocks, capacity, block_size)
    inputs = activations[0]
    weights = decoder[0].reshape(local_blocks, block_size, model_width)
    input_slots = jnp.dot(slot_token, inputs, preferred_element_type=jnp.float32).astype(
        jnp.bfloat16
    )
    input_slots = input_slots.reshape(all_blocks, capacity, model_width)
    pieces = (
        lax.all_to_all(pre_slots, "latent", split_axis=0, concat_axis=0, tiled=True),
        lax.all_to_all(input_slots, "latent", split_axis=0, concat_axis=0, tiled=True),
    )
    returned = local_contrib(pieces[0], weights, lat_count, local_blocks)
    returned, received_pre, received_inputs = (returned, pieces[0], pieces[1])
    part_sum = jnp.einsum(
        "st,sd->td",
        slot_token,
        returned.reshape(slot_count, model_width),
        preferred_element_type=jnp.float32,
    )
    rebuilt = lax.psum(part_sum, "layer")
    errors = ((rebuilt - target.astype(jnp.float32)) / tok_count).astype(jnp.bfloat16)
    error_slots = jnp.dot(slot_token, errors, preferred_element_type=jnp.float32).astype(
        jnp.bfloat16
    )
    error_slots = error_slots.reshape(all_blocks, capacity, model_width)
    received_errors = lax.all_to_all(error_slots, "latent", split_axis=0, concat_axis=0, tiled=True)
    pre_blocks = received_pre.reshape(lat_count, local_blocks, capacity, block_size)
    code_blocks = jnp.maximum(pre_blocks, jnp.zeros((), pre_blocks.dtype))
    error_blocks = received_errors.reshape(lat_count, local_blocks, capacity, model_width)
    input_blocks = received_inputs.reshape(lat_count, local_blocks, capacity, model_width)
    code_grad = jnp.einsum(
        "sbcd,bld->sbcl", error_blocks, weights, preferred_element_type=jnp.float32
    )
    pre_grad = jnp.where(pre_blocks > 0, code_grad, jnp.zeros((), jnp.float32)).astype(jnp.bfloat16)
    dec_term = jnp.einsum(
        "sbcl,sbcd->bld", code_blocks, error_blocks, preferred_element_type=jnp.float32
    )
    enc_term = jnp.einsum(
        "sbcl,sbcd->bld", pre_grad, input_blocks, preferred_element_type=jnp.float32
    )
    dec_term = dec_term.reshape(lat_rows, model_width)
    enc_term = enc_term.reshape(lat_rows, model_width)
    dec_half, enc_half = (
        lax.psum_scatter(dec_term, "dp", scatter_dimension=1, tiled=True),
        lax.psum_scatter(enc_term, "dp", scatter_dimension=1, tiled=True),
    )
    return (dec_half.astype(jnp.bfloat16)[None], enc_half.astype(jnp.bfloat16)[None])


def shift(value, axis, step):
    count = lax.axis_size(axis)
    return lax.ppermute(value, axis, [(i, (i + step) % count) for i in range(count)])


def flip(value, axis, bit):
    count = lax.axis_size(axis)
    return lax.ppermute(value, axis, [(i, i ^ bit) for i in range(count)])


def hop(value, axis, step, least):
    count = lax.axis_size(axis)
    if step > 0:
        pairs = [(i, i + 1) for i in range(least, count - 1)]
    else:
        pairs = [(i, i - 1) for i in range(1, count - least)]
    return lax.ppermute(value, axis, pairs)


def gather_line(own, axis):
    count = lax.axis_size(axis)
    up, down = [own], [own]
    for step in range(1, count):
        up.append(hop(up[-1], axis, 1, step - 1))
        down.append(hop(down[-1], axis, -1, step - 1))
    return [own] + [down[k] + up[count - k] for k in range(1, count)]


def spread_rows(ids, rows, first, count):
    out = []
    for i in range(count):
        block = (first + i).astype(jnp.float32)
        value = jnp.where(ids[1:2] == block, rows[1], 0.0)
        out.append(jnp.where(ids[0:1] == block, rows[0], value).astype(jnp.bfloat16))
    return jnp.concatenate(out, axis=0)


def forward_kernel(groups, blocks, place_ref, message_ref, weight_ref, out_ref, codes, id_map):
    tok = message_ref.shape[2]
    pad = message_ref.shape[1] - 2 * tok

    @pl.when(pl.program_id(0) == 0)
    def _():
        first = place_ref[0].astype(jnp.float32)
        rows = [message_ref[g, 2 * tok:2 * tok + pad, :].astype(jnp.float32) for g in range(groups)]
        fill = tok - groups * pad
        if fill:
            rows.append(jnp.zeros((fill, tok), jnp.float32))
        table = jnp.concatenate(rows, axis=0).T - first
        for g in range(groups):
            for j in range(2):
                at = g * pad + j
                id_map[g, j] = jnp.broadcast_to(table[:, at:at + 1], (tok, tok))

        def block_step(b, carry):
            block = b.astype(jnp.float32)
            at = pl.multiple_of(b * tok, tok)
            for g in range(groups):
                pre0 = jnp.maximum(message_ref[g, 0:tok, :].astype(jnp.float32), 0.0)
                pre1 = jnp.maximum(message_ref[g, tok:2 * tok, :].astype(jnp.float32), 0.0)
                value = jnp.where(id_map[g, 1] == block, pre1, 0.0)
                value = jnp.where(id_map[g, 0] == block, pre0, value)
                codes[g * tok:(g + 1) * tok, pl.ds(at, tok)] = value.astype(jnp.bfloat16)
            return carry

        lax.fori_loop(0, blocks, block_step, 0)

    step_rows = 2 * tok

    def row_step(i, carry):
        at = pl.multiple_of(i * step_rows, step_rows)
        out_ref[0, pl.ds(at, step_rows), :] = jnp.dot(
            codes[pl.ds(at, step_rows), :], weight_ref[0], preferred_element_type=jnp.float32
        ).astype(jnp.bfloat16)
        return carry

    lax.fori_loop(0, codes.shape[0] // step_rows, row_step, 0)


def forward(message, decoder, place, columns, width):
    groups, _, tok = message.shape
    lat_rows = decoder.shape[1]
    steps = columns.shape[0]
    scalars = jnp.concatenate([place[None], columns]).astype(jnp.int32)
    return pl.pallas_call(
        functools.partial(forward_kernel, groups, lat_rows // tok),
        out_shape=jax.ShapeDtypeStruct((steps, groups * tok, width), jnp.bfloat16),
        grid_spec=pltpu.PrefetchScalarGridSpec(
            num_scalar_prefetch=1,
            grid=(steps,),
            in_specs=[
                pl.BlockSpec(message.shape, lambda i, s: (0, 0, 0)),
                pl.BlockSpec((1, lat_rows, width), lambda i, s: (0, 0, s[i + 1])),
            ],
            out_specs=pl.BlockSpec((1, groups * tok, width), lambda i, s: (i, 0, 0)),
            scratch_shapes=[
                pltpu.VMEM((groups * tok, lat_rows), jnp.bfloat16),
                pltpu.VMEM((groups, 2, tok, tok), jnp.float32),
            ],
        ),
        compiler_params=pltpu.CompilerParams(vmem_limit_bytes=VMEM_BYTES),
        cost_estimate=pl.CostEstimate(
            flops=2 * steps * groups * tok * lat_rows * width,
            bytes_accessed=2 * steps * (groups * tok + lat_rows) * width,
            transcendentals=0,
        ),
        name="forward",
    )(scalars, message, decoder)


def spread_into(target, ids, rows, first, size):
    def build(b, carry):
        at = pl.multiple_of(b * size, size)
        target[pl.ds(at, size), :] = spread_rows(ids, rows, first + b, 1)
        return carry

    lax.fori_loop(0, target.shape[0] // size, build, 0)


def take_piece(pieces, now):
    for i, piece in enumerate(pieces):

        @pl.when(pl.program_id(0) == i)
        def _(piece=piece):
            now[...] = piece[...]


def code_grad_kernel(size, place_ref, ids_ref, weight_ref, *refs):
    pieces, (grad_ref, now) = refs[:-2], refs[-2:]
    take_piece(pieces, now)
    several = 4 * size if weight_ref.shape[1] % (4 * size) == 0 else size

    @pl.when(pl.program_id(0) == 0)
    def _():
        grad_ref[...] = jnp.zeros_like(grad_ref)

    def step(i, carry):
        at = pl.multiple_of(i * several, several)
        grad = lax.dot_general(
            weight_ref[0, pl.ds(at, several), :],
            now[...],
            (((1,), (1,)), ((), ())),
            preferred_element_type=jnp.float32,
        )
        add0, add1 = 0.0, 0.0
        for n in range(several // size):
            block = (place_ref[0] + i * (several // size) + n).astype(jnp.float32)
            part = grad[n * size:(n + 1) * size]
            add0 = jnp.where(ids_ref[0:1] == block, part, add0)
            add1 = jnp.where(ids_ref[1:2] == block, part, add1)
        grad_ref[0] += add0
        grad_ref[1] += add1
        return carry

    lax.fori_loop(0, weight_ref.shape[1] // several, step, 0)


def code_grad(pieces, ids, decoder, first, columns, size):
    lat_rows = decoder.shape[1]
    tokens, width = pieces[0].shape
    scalars = jnp.concatenate([first[None], columns]).astype(jnp.int32)
    whole = pl.BlockSpec((tokens, width), lambda i, s: (0, 0))
    return pl.pallas_call(
        functools.partial(code_grad_kernel, size),
        out_shape=jax.ShapeDtypeStruct((2, size, tokens), jnp.float32),
        grid_spec=pltpu.PrefetchScalarGridSpec(
            num_scalar_prefetch=1,
            grid=(len(pieces),),
            in_specs=[
                pl.BlockSpec(ids.shape, lambda i, s: (0, 0)),
                pl.BlockSpec((1, lat_rows, width), lambda i, s: (0, 0, s[i + 1])),
            ]
            + [whole] * len(pieces),
            out_specs=pl.BlockSpec((2, size, tokens), lambda i, s: (0, 0, 0)),
            scratch_shapes=[pltpu.VMEM((tokens, width), jnp.bfloat16)],
        ),
        compiler_params=pltpu.CompilerParams(vmem_limit_bytes=VMEM_BYTES),
        cost_estimate=pl.CostEstimate(
            flops=2 * len(pieces) * tokens * lat_rows * width,
            bytes_accessed=2 * len(pieces) * (tokens + lat_rows) * width,
            transcendentals=0,
        ),
        name="code_grad",
    )(scalars, ids, decoder, *pieces)


def decoder_kernel(size, place_ref, ids_ref, pre_ref, *refs):
    pieces, (out_ref, now, codes) = refs[:-3], refs[-3:]
    take_piece(pieces, now)

    @pl.when(pl.program_id(0) == 0)
    def _():
        rows = [jnp.maximum(pre_ref[j].astype(jnp.float32), 0.0) for j in range(2)]
        spread_into(codes, ids_ref[...], rows, place_ref[0], size)

    several = 2 * size if codes.shape[0] % (2 * size) == 0 else size

    def step(i, carry):
        at = pl.multiple_of(i * several, several)
        out_ref[pl.ds(at, several), :] = jnp.dot(
            codes[pl.ds(at, several), :], now[...], preferred_element_type=jnp.float32
        ).astype(jnp.bfloat16)
        return carry

    lax.fori_loop(0, codes.shape[0] // several, step, 0)


def decoder_kernel_onto(size, place_ref, ids_ref, pre_ref, held_ref, *refs):
    decoder_kernel(size, place_ref, ids_ref, pre_ref, *refs)


def decoder_part(pieces, ids, pre_lanes, first, columns, lat_rows, half, held):
    _, size, tokens = pre_lanes.shape
    width = pieces[0].shape[1]
    scalars = jnp.concatenate([first[None], columns]).astype(jnp.int32)
    whole = pl.BlockSpec((tokens, width), lambda i, s: (0, 0))
    return pl.pallas_call(
        functools.partial(decoder_kernel if held is None else decoder_kernel_onto, size),
        out_shape=jax.ShapeDtypeStruct((lat_rows, half), jnp.bfloat16),
        grid_spec=pltpu.PrefetchScalarGridSpec(
            num_scalar_prefetch=1,
            grid=(len(pieces),),
            in_specs=[
                pl.BlockSpec(ids.shape, lambda i, s: (0, 0)),
                pl.BlockSpec(pre_lanes.shape, lambda i, s: (0, 0, 0)),
            ]
            + ([] if held is None else [pl.BlockSpec(memory_space=pl.ANY)])
            + [whole] * len(pieces),
            out_specs=pl.BlockSpec((lat_rows, width), lambda i, s: (0, s[i + 1])),
            scratch_shapes=[
                pltpu.VMEM((tokens, width), jnp.bfloat16),
                pltpu.VMEM((lat_rows, tokens), jnp.bfloat16),
            ],
        ),
        compiler_params=pltpu.CompilerParams(vmem_limit_bytes=VMEM_BYTES),
        input_output_aliases={} if held is None else {3: 0},
        cost_estimate=pl.CostEstimate(
            flops=2 * len(pieces) * tokens * lat_rows * width,
            bytes_accessed=2 * len(pieces) * (tokens + lat_rows) * width,
            transcendentals=0,
        ),
        name="decoder_part",
    )(scalars, ids, pre_lanes, *([] if held is None else [held]), *pieces)


def encoder_kernel(size, place_ref, ids_ref, pre_ref, *refs):
    out_ref, grads = refs[-2:]
    parts = [r for r in refs[:-2] if r.dtype == jnp.float32]
    acts = [r for r in refs[:-2] if r.dtype == jnp.bfloat16]

    @pl.when(pl.program_id(0) == 0)
    def _():
        rows = []
        for j in range(2):
            total = parts[0][j]
            for part in parts[1:]:
                total = total + part[j]
            rows.append(jnp.where(pre_ref[j].astype(jnp.float32) > 0, total, 0.0))
        spread_into(grads, ids_ref[...], rows, place_ref[0], size)

    several = 2 * size if grads.shape[0] % (2 * size) == 0 else size

    def step(i, carry):
        at = pl.multiple_of(i * several, several)
        total = 0.0
        for k, act in enumerate(acts):
            span = act.shape[0]
            total = total + jnp.dot(
                grads[pl.ds(at, several), k * span:(k + 1) * span], act[...], preferred_element_type=jnp.float32
            )
        out_ref[pl.ds(at, several), :] = total.astype(jnp.bfloat16)
        return carry

    lax.fori_loop(0, grads.shape[0] // several, step, 0)


def encoder_part(parts, acts, ids, pre_lanes, first, lat_rows, half):
    _, size, tokens = pre_lanes.shape
    tile = 256 if half % 256 == 0 else half
    scalars = first[None].astype(jnp.int32)
    whole = pl.BlockSpec(pre_lanes.shape, lambda i, s: (0, 0, 0))
    return pl.pallas_call(
        functools.partial(encoder_kernel, size),
        out_shape=jax.ShapeDtypeStruct((lat_rows, half), jnp.bfloat16),
        grid_spec=pltpu.PrefetchScalarGridSpec(
            num_scalar_prefetch=1,
            grid=(half // tile,),
            in_specs=[pl.BlockSpec(ids.shape, lambda i, s: (0, 0)), whole]
            + [whole] * len(parts)
            + [pl.BlockSpec((act.shape[0], tile), lambda i, s: (0, i)) for act in acts],
            out_specs=pl.BlockSpec((lat_rows, tile), lambda i, s: (0, i)),
            scratch_shapes=[pltpu.VMEM((lat_rows, tokens), jnp.bfloat16)],
        ),
        compiler_params=pltpu.CompilerParams(vmem_limit_bytes=VMEM_BYTES),
        cost_estimate=pl.CostEstimate(
            flops=2 * tokens * lat_rows * half,
            bytes_accessed=2 * (tokens + lat_rows) * half,
            transcendentals=0,
        ),
        name="encoder_part",
    )(scalars, ids, pre_lanes, *parts, *acts)


def dense_plan(pre_codes, block_ids, activations, target, decoder):
    lay_count = lax.axis_size("layer")
    lat_count = lax.axis_size("latent")
    dp_count = lax.axis_size("dp")
    lay_here = lax.axis_index("layer")
    lat_here = lax.axis_index("latent")
    dp_here = lax.axis_index("dp")
    tok_count = activations.shape[1]
    model_width = activations.shape[2]
    active_count = block_ids.shape[2]
    block_size = pre_codes.shape[3]
    lat_rows = decoder.shape[1]
    local_blocks = lat_rows // block_size
    half = model_width // dp_count
    group = dp_count * tok_count
    tokens = lat_count * group
    bits = [1 << i for i in range(lay_count.bit_length() - 1)]
    chunks = 2 * PAIRS
    width = half // (chunks * lay_count)
    f32, bf16 = jnp.float32, jnp.bfloat16
    first = lat_here * local_blocks

    def columns(rows, which):
        return lax.dynamic_slice_in_dim(rows, which * half, half, axis=1)

    pre_rows = jnp.swapaxes(pre_codes[0], 0, 1).reshape(active_count * tok_count, block_size)
    id_rows = jnp.pad(block_ids[0].T, ((0, 16 - active_count), (0, 0))).astype(bf16)
    own = jnp.concatenate([pre_rows, id_rows], axis=0)
    message = jnp.stack([own] + [shift(own, "latent", -k) for k in range(1, lat_count)])
    message = jnp.stack([message, flip(message, "dp", 1)], axis=1)
    message = message.reshape(lat_count * dp_count, own.shape[0], block_size)

    acts = jnp.concatenate(
        [columns(activations[0], dp_here), flip(columns(activations[0], 1 - dp_here), "dp", 1)]
    )
    acts = gather_line(acts, "latent")

    goal = target.reshape(tok_count, dp_count, chunks, lay_count, width)

    def goal_of(which):
        cut = lax.dynamic_index_in_dim(goal, which, 1, False)
        return lax.dynamic_index_in_dim(cut, lay_here, 2, False)

    goals = jnp.concatenate([goal_of(dp_here), flip(goal_of(1 - dp_here), "dp", 1)])

    def order_of(chunk):
        return bits if chunk % 2 == 0 else bits[::-1]

    def rows_of(order, fixed):
        out = [fixed]
        for bit in order:
            out = out + [r | bit for r in out]
        return out

    def places(names, offset):
        return jnp.stack([offset + chunk * lay_count + (lay_here ^ r) for chunk, r in names])

    def weight_places(names):
        return places(names, dp_here * (half // width))

    every = range(chunks)
    sent_names = [(c, r) for c in every for r in rows_of(order_of(c)[1:], order_of(c)[0])]
    kept_names = [(c, r) for c in every for r in rows_of(order_of(c)[1:], 0)]
    per = lay_count // 2
    sent = forward(message, decoder, first, weight_places(sent_names), width)
    kept = forward(message, decoder, first, weight_places(kept_names), width)

    def reduce_layer(chunk):
        order = order_of(chunk)
        got = flip(sent[chunk * per:(chunk + 1) * per], "layer", order[0])
        terms = [got, kept[chunk * per:(chunk + 1) * per]]
        for bit in order[1:]:
            size = terms[0].shape[0] // 2
            far = sum(term[size:].astype(f32) for term in terms).astype(bf16)
            terms = [term[:size] for term in terms] + [flip(far, "layer", bit)]
        return sum(term[0].astype(f32) for term in terms)

    def reduce_latent(total, chunk):
        cut = total.reshape(lat_count, group, width)
        out = cut[0]
        for k in range(1, lat_count):
            out = out + shift(cut[k].astype(bf16), "latent", k).astype(f32)
        want = goals[:, chunk].astype(f32)
        return ((out - want) / tok_count).astype(bf16)

    pieces = {}
    for chunk in every:
        own_errors = reduce_latent(reduce_layer(chunk), chunk)
        rows = jnp.concatenate([own_errors] + [shift(own_errors, "latent", -k) for k in range(1, lat_count)], axis=0)
        pieces[chunk, 0] = rows
        done = [0]
        for bit in order_of(chunk)[::-1]:
            for r in done:
                pieces[chunk, r | bit] = flip(pieces[chunk, r], "layer", bit)
            done = done + [r | bit for r in done]

    cut = message.reshape(tokens // tok_count, own.shape[0], block_size)
    pre_lanes = cut[:, :active_count * tok_count].reshape(-1, active_count, tok_count, block_size)
    pre_lanes = jnp.transpose(pre_lanes, (1, 3, 0, 2)).reshape(active_count, block_size, tokens)
    ids = cut[:, active_count * tok_count:active_count * tok_count + active_count]
    ids = jnp.swapaxes(ids, 0, 1).reshape(active_count, tokens).astype(f32)

    grads = []
    dec = None
    for r in range(lay_count):
        names = [(c, r ^ 0) for c in every]
        here = [pieces[name] for name in names]
        grads.append(code_grad(here, ids, decoder, first, weight_places(names), block_size))
        dec = decoder_part(here, ids, pre_lanes, first, places(names, 0), lat_rows, half, dec)
    grad = sum(grads)
    enc = encoder_part([grad, swap_cores(flip(grad, "dp", 1), tok_count)], acts, ids, pre_lanes, first, lat_rows, half)
    return dec[None], enc[None]


def swap_cores(value, tok_count):
    cut = value.reshape(value.shape[:-1] + (-1, 2, tok_count))
    return cut[..., ::-1, :].reshape(value.shape)


def per_device(pre_codes, block_ids, activations, target, decoder):
    lat_count = lax.axis_size("latent")
    lay_count = lax.axis_size("layer")
    dp_count = lax.axis_size("dp")
    tok_count = activations.shape[1]
    model_width = activations.shape[2]
    active_count = block_ids.shape[2]
    block_size = pre_codes.shape[3]
    all_blocks = decoder.shape[1] // block_size * lat_count
    slots = 2 * tok_count * active_count // lat_count
    dense = (
        slots >= tok_count
        and dp_count == 2
        and active_count == 2
        and lay_count > 1
        and lay_count & (lay_count - 1) == 0
        and tok_count == block_size
        and lat_count * dp_count * 16 <= tok_count
        and model_width % (dp_count * 2 * PAIRS * lay_count * 128) == 0
        and all_blocks <= 256
    )
    plan = dense_plan if dense else slot_plan
    return plan(pre_codes, block_ids, activations, target, decoder)


def solution(mesh):
    placed = (
        P("layer", ("latent", "dp"), None, None),
        P("layer", ("latent", "dp"), None),
        P("layer", ("latent", "dp"), None),
        P(("latent", "dp"), None),
        P("layer", "latent", None),
    )
    return jax.shard_map(
        per_device,
        mesh=mesh,
        in_specs=placed,
        out_specs=(P("layer", "latent", "dp"), P("layer", "latent", "dp")),
        check_vma=False,
    )
```

```python
import functools

import jax
import jax.numpy as jnp
from jax import lax
from jax.experimental import pallas as pl
from jax.experimental.pallas import tpu as pltpu
from jax.sharding import PartitionSpec as P

PAIRS = 2
VMEM_BYTES = 40 * 1024 * 1024


def local_contrib(received_pre, weights, lat_count, local_blocks):
    code_vals = jnp.maximum(received_pre, jnp.zeros((), received_pre.dtype))
    slot_span = received_pre.shape[1]
    block_size = received_pre.shape[2]
    grouped = code_vals.reshape(lat_count, local_blocks, slot_span, block_size)
    contrib = jnp.einsum("sbcl,bld->sbcd", grouped, weights, preferred_element_type=jnp.float32)
    contrib = contrib.astype(jnp.bfloat16).reshape(
        lat_count * local_blocks, slot_span, weights.shape[2]
    )
    return lax.all_to_all(contrib, "latent", split_axis=0, concat_axis=0, tiled=True)


def slot_plan(pre_codes, block_ids, activations, target, decoder):
    lat_count = lax.axis_size("latent")
    tok_count = activations.shape[1]
    model_width = activations.shape[2]
    active_count = block_ids.shape[2]
    block_size = pre_codes.shape[3]
    lat_rows = decoder.shape[1]
    local_blocks = lat_rows // block_size
    all_blocks = local_blocks * lat_count
    capacity = 2 * tok_count * active_count // all_blocks
    slot_count = all_blocks * capacity
    pair_count = tok_count * active_count
    pair_block = block_ids[0].T.reshape(pair_count)
    member = (pair_block[:, None] == jnp.arange(all_blocks, dtype=jnp.int32)[None, :]).astype(
        jnp.int32
    )
    before = jnp.cumsum(member, axis=0) - member
    pair_rank = jnp.sum(before * member, axis=1)
    target_slot = pair_block * capacity + pair_rank
    slot_pair = (jnp.arange(slot_count, dtype=jnp.int32)[:, None] == target_slot[None, :]).astype(
        jnp.bfloat16
    )
    slot_token = jnp.sum(slot_pair.reshape(slot_count, active_count, tok_count), axis=1)
    pre_pairs = jnp.transpose(pre_codes[0], (1, 0, 2)).reshape(pair_count, block_size)
    pre_slots = jnp.dot(slot_pair, pre_pairs, preferred_element_type=jnp.float32).astype(
        jnp.bfloat16
    )
    pre_slots = pre_slots.reshape(all_blocks, capacity, block_size)
    inputs = activations[0]
    weights = decoder[0].reshape(local_blocks, block_size, model_width)
    input_slots = jnp.dot(slot_token, inputs, preferred_element_type=jnp.float32).astype(
        jnp.bfloat16
    )
    input_slots = input_slots.reshape(all_blocks, capacity, model_width)
    pieces = (
        lax.all_to_all(pre_slots, "latent", split_axis=0, concat_axis=0, tiled=True),
        lax.all_to_all(input_slots, "latent", split_axis=0, concat_axis=0, tiled=True),
    )
    returned = local_contrib(pieces[0], weights, lat_count, local_blocks)
    returned, received_pre, received_inputs = (returned, pieces[0], pieces[1])
    part_sum = jnp.einsum(
        "st,sd->td",
        slot_token,
        returned.reshape(slot_count, model_width),
        preferred_element_type=jnp.float32,
    )
    rebuilt = lax.psum(part_sum, "layer")
    errors = ((rebuilt - target.astype(jnp.float32)) / tok_count).astype(jnp.bfloat16)
    error_slots = jnp.dot(slot_token, errors, preferred_element_type=jnp.float32).astype(
        jnp.bfloat16
    )
    error_slots = error_slots.reshape(all_blocks, capacity, model_width)
    received_errors = lax.all_to_all(error_slots, "latent", split_axis=0, concat_axis=0, tiled=True)
    pre_blocks = received_pre.reshape(lat_count, local_blocks, capacity, block_size)
    code_blocks = jnp.maximum(pre_blocks, jnp.zeros((), pre_blocks.dtype))
    error_blocks = received_errors.reshape(lat_count, local_blocks, capacity, model_width)
    input_blocks = received_inputs.reshape(lat_count, local_blocks, capacity, model_width)
    code_grad = jnp.einsum(
        "sbcd,bld->sbcl", error_blocks, weights, preferred_element_type=jnp.float32
    )
    pre_grad = jnp.where(pre_blocks > 0, code_grad, jnp.zeros((), jnp.float32)).astype(jnp.bfloat16)
    dec_term = jnp.einsum(
        "sbcl,sbcd->bld", code_blocks, error_blocks, preferred_element_type=jnp.float32
    )
    enc_term = jnp.einsum(
        "sbcl,sbcd->bld", pre_grad, input_blocks, preferred_element_type=jnp.float32
    )
    dec_term = dec_term.reshape(lat_rows, model_width)
    enc_term = enc_term.reshape(lat_rows, model_width)
    dec_half, enc_half = (
        lax.psum_scatter(dec_term, "dp", scatter_dimension=1, tiled=True),
        lax.psum_scatter(enc_term, "dp", scatter_dimension=1, tiled=True),
    )
    return (dec_half.astype(jnp.bfloat16)[None], enc_half.astype(jnp.bfloat16)[None])


def flip(value, axis, bit):
    count = lax.axis_size(axis)
    return lax.ppermute(value, axis, [(i, i ^ bit) for i in range(count)])


def hop(value, axis, step, least):
    count = lax.axis_size(axis)
    if step > 0:
        pairs = [(i, i + 1) for i in range(least, count - 1)]
    else:
        pairs = [(i, i - 1) for i in range(1, count - least)]
    return lax.ppermute(value, axis, pairs)


def after(value, *others):
    return lax.optimization_barrier((value,) + others)[0]


def params():
    return pltpu.CompilerParams(vmem_limit_bytes=VMEM_BYTES)


def cost(rows, depth, columns):
    return pl.CostEstimate(
        flops=2 * rows * depth * columns,
        bytes_accessed=2 * (rows * depth + depth * columns + rows * columns),
        transcendentals=0,
    )


def resident(shape):
    return pl.BlockSpec(shape, lambda i, s: (0,) * len(shape))


def forward_kernel(groups, blocks, scalar_ref, message_ref, weight_ref, *refs):
    outs, (codes, id_map, pre) = refs[:4], refs[4:]
    tok = message_ref.shape[2]
    pad = message_ref.shape[1] - 2 * tok
    half = outs[0].shape[2]
    step = pl.program_id(0)

    @pl.when(step == 0)
    def _():
        first = scalar_ref[0].astype(jnp.float32)
        rows = [message_ref[g, 2 * tok:2 * tok + pad, :].astype(jnp.float32) for g in range(groups)]
        fill = tok - groups * pad
        if fill:
            rows.append(jnp.zeros((fill, tok), jnp.float32))
        table = jnp.concatenate(rows, axis=0).T - first
        for g in range(groups):
            pre[g] = jnp.maximum(message_ref[g, 0:2 * tok, :], jnp.zeros((), jnp.bfloat16))
            for j in range(2):
                at = g * pad + j
                wide = jnp.broadcast_to(table[:, at:at + 1], (tok, tok))
                id_map[g, j * tok:(j + 1) * tok, :] = wide.astype(jnp.bfloat16)

        def block_step(b, carry):
            block = b.astype(jnp.float32).astype(jnp.bfloat16)
            at = pl.multiple_of(b * tok, tok)
            for g in range(groups):
                value = jnp.where(id_map[g, tok:2 * tok, :] == block, pre[g, tok:2 * tok, :], jnp.zeros((), jnp.bfloat16))
                value = jnp.where(id_map[g, 0:tok, :] == block, pre[g, 0:tok, :], value)
                codes[g * tok:(g + 1) * tok, pl.ds(at, tok)] = value
            return carry

        lax.fori_loop(0, blocks, block_step, 0)

    step_rows = 4 * tok if codes.shape[0] % (4 * tok) == 0 else tok
    stores = {0: (0, 2), 1: (0, 3), 2: (1, 2), 3: (1, 3)}

    def row_step(i, carry):
        at = pl.multiple_of(i * step_rows, step_rows)
        rows = pl.ds(at, step_rows)
        value = jnp.dot(codes[rows, :], weight_ref[0], preferred_element_type=jnp.float32).astype(jnp.bfloat16)
        for n, (to_a, to_b) in {0: (0, 2), 1: (0, 3), 2: (1, 2), 3: (1, 3)}.items():

            @pl.when(step == n)
            def _(to_a=to_a, to_b=to_b):
                outs[to_a][0, rows, :] = value[:, :half]
                outs[to_b][0, rows, :] = value[:, half:]

        return carry

    lax.fori_loop(0, codes.shape[0] // step_rows, row_step, 0)


def forward(message, decoder, first, columns, width):
    groups, _, tok = message.shape
    lat_rows = decoder.shape[1]
    rows = groups * tok
    scalars = jnp.concatenate([first[None], columns]).astype(jnp.int32)
    part = jax.ShapeDtypeStruct((2, rows, width // 2), jnp.bfloat16)
    block = (1, rows, width // 2)
    return pl.pallas_call(
        functools.partial(forward_kernel, groups, lat_rows // tok),
        out_shape=[part] * 4,
        grid_spec=pltpu.PrefetchScalarGridSpec(
            num_scalar_prefetch=1,
            grid=(4,),
            in_specs=[
                resident(message.shape),
                pl.BlockSpec((1, lat_rows, width), lambda i, s: (0, 0, s[i + 1])),
            ],
            out_specs=[
                pl.BlockSpec(block, lambda i, s: (jnp.where(i < 1, 1, 0), 0, 0)),
                pl.BlockSpec(block, lambda i, s: (jnp.where(i < 3, 1, 0), 0, 0)),
                pl.BlockSpec(block, lambda i, s: (jnp.where(i < 2, 1, 0), 0, 0)),
                pl.BlockSpec(block, lambda i, s: (jnp.where(i < 3, 1, 0), 0, 0)),
            ],
            scratch_shapes=[
                pltpu.VMEM((rows, lat_rows), jnp.bfloat16),
                pltpu.VMEM((groups, 2 * tok, tok), jnp.bfloat16),
                pltpu.VMEM((groups, 2 * tok, tok), jnp.bfloat16),
            ],
        ),
        compiler_params=params(),
        cost_estimate=cost(rows, lat_rows, 4 * width),
        name="forward",
    )(scalars, message, decoder)


def layer_sum_kernel(got_a, kept_a, far_a, got_b, kept_b, far_b, sent_ref, held_ref):
    half = got_a.shape[2]
    rows = sent_ref.shape[1]
    for side, (got, kept, far) in enumerate(((got_a, kept_a, far_a), (got_b, kept_b, far_b))):
        lanes = slice(side * half, (side + 1) * half)
        for n in range(2 * sent_ref.shape[0]):
            at = slice(n * rows, (n + 1) * rows)
            total = got[0, at, :].astype(jnp.float32) + kept[0, at, :].astype(jnp.float32)
            total = total + far[0, at, :].astype(jnp.float32)
            if n % 2:
                sent_ref[n // 2, :, lanes] = total.astype(jnp.bfloat16)
            else:
                held_ref[n // 2, :, lanes] = total


def layer_sum(terms_a, terms_b, blocks):
    _, rows, half = terms_a[0].shape
    cut = (blocks // 2, rows // blocks, 2 * half)
    return pl.pallas_call(
        layer_sum_kernel,
        out_shape=[jax.ShapeDtypeStruct(cut, jnp.bfloat16), jax.ShapeDtypeStruct(cut, jnp.float32)],
        grid=(1,),
        in_specs=[
            pl.BlockSpec((1, rows, half), lambda i: (0, 0, 0)) for _ in range(6)
        ],
        out_specs=[pl.BlockSpec(cut, lambda i: (0, 0, 0))] * 2,
        compiler_params=params(),
        cost_estimate=cost(rows, 4, half),
        name="layer_sum",
    )(*terms_a, *terms_b)


def spread_into(target, ids_ref, rows_refs, first, size):
    low = ids_ref.shape[1]

    def build(b, carry):
        at = pl.multiple_of(b * size, size)
        block = (first + b).astype(jnp.float32).astype(jnp.bfloat16)
        here = [ids_ref[j] == block for j in range(2)]
        for n in range(size // low):
            rows = slice(n * low, (n + 1) * low)
            value = jnp.where(here[1], rows_refs[1][rows, :], jnp.zeros((), jnp.bfloat16))
            target[pl.ds(at + n * low, low), :] = jnp.where(here[0], rows_refs[0][rows, :], value)
        return carry

    lax.fori_loop(0, target.shape[0] // size, build, 0)


def lanes_of(refs):
    return refs[0][...] if len(refs) == 1 else jnp.concatenate([r[...] for r in refs], axis=1)


def code_grad_kernel(size, shape, scalar_ref, ids_ref, *refs):
    grad_ref = refs[-1]
    weights, pieces = refs[:len(shape)], refs[len(shape):-1]

    @pl.when(pl.program_id(0) == 0)
    def _():
        grad_ref[...] = jnp.zeros_like(grad_ref)

    weight = jnp.concatenate([w[0] for w in weights], axis=1)
    grad = lax.dot_general(
        weight, lanes_of(pieces), (((1,), (1,)), ((), ())), preferred_element_type=jnp.float32
    )
    several = weight.shape[0] // size
    add0, add1 = 0.0, 0.0
    for n in range(several):
        block = (scalar_ref[0] + pl.program_id(0) * several + n).astype(jnp.float32)
        part = grad[n * size:(n + 1) * size]
        add0 = jnp.where(ids_ref[0:1] == block, part, add0)
        add1 = jnp.where(ids_ref[1:2] == block, part, add1)
    grad_ref[0] += add0
    grad_ref[1] += add1


def code_grad(pieces, ids, decoder, first, columns, size):
    lat_rows = decoder.shape[1]
    tokens = pieces[0][0].shape[0]
    width = sum(p.shape[1] for p in pieces[0])
    scalars = jnp.concatenate([first[None], columns]).astype(jnp.int32)
    flat = [p for piece in pieces for p in piece]
    several = 4 * size if lat_rows % (4 * size) == 0 else size
    return pl.pallas_call(
        functools.partial(code_grad_kernel, size, [len(p) for p in pieces]),
        out_shape=jax.ShapeDtypeStruct((2, size, tokens), jnp.float32),
        grid_spec=pltpu.PrefetchScalarGridSpec(
            num_scalar_prefetch=1,
            grid=(lat_rows // several,),
            in_specs=[resident(ids.shape)]
            + [pl.BlockSpec((1, several, width), lambda i, s, n=n: (0, i, s[n + 1])) for n in range(len(pieces))]
            + [resident(p.shape) for p in flat],
            out_specs=resident((2, size, tokens)),
        ),
        compiler_params=params(),
        cost_estimate=cost(lat_rows, len(pieces) * width, tokens),
        name="code_grad",
    )(scalars, ids, *[decoder] * len(pieces), *flat)


def decoder_kernel(size, shape, skip, scalar_ref, ids_ref, codes_ref, *refs):
    refs = refs[skip:]
    pieces, (out_ref, now, codes) = refs[:-3], refs[-3:]
    at = 0
    for i, count in enumerate(shape):

        @pl.when(pl.program_id(0) == i)
        def _(at=at, count=count):
            now[...] = lanes_of(pieces[at:at + count])

        at += count

    @pl.when(pl.program_id(0) == 0)
    def _():
        spread_into(codes, ids_ref, [codes_ref.at[0], codes_ref.at[1]], scalar_ref[0], size)

    several = 8 * size if codes.shape[0] % (8 * size) == 0 else size

    def step(i, carry):
        rows = pl.ds(pl.multiple_of(i * several, several), several)
        out_ref[rows, :] = jnp.dot(codes[rows, :], now[...], preferred_element_type=jnp.float32).astype(jnp.bfloat16)
        return carry

    lax.fori_loop(0, codes.shape[0] // several, step, 0)


def decoder_part(pieces, ids, code_lanes, first, columns, lat_rows, half, held):
    _, size, tokens = code_lanes.shape
    width = sum(p.shape[1] for p in pieces[0])
    scalars = jnp.concatenate([first[None], columns]).astype(jnp.int32)
    flat = [p for piece in pieces for p in piece]
    onto = [] if held is None else [held]
    return pl.pallas_call(
        functools.partial(decoder_kernel, size, [len(p) for p in pieces], len(onto)),
        out_shape=jax.ShapeDtypeStruct((lat_rows, half), jnp.bfloat16),
        grid_spec=pltpu.PrefetchScalarGridSpec(
            num_scalar_prefetch=1,
            grid=(len(pieces),),
            in_specs=[resident(ids.shape), resident(code_lanes.shape)]
            + [pl.BlockSpec(memory_space=pl.ANY) for _ in onto]
            + [resident(p.shape) for p in flat],
            out_specs=pl.BlockSpec((lat_rows, width), lambda i, s: (0, s[i + 1])),
            scratch_shapes=[
                pltpu.VMEM((tokens, width), jnp.bfloat16),
                pltpu.VMEM((lat_rows, tokens), jnp.bfloat16),
            ],
        ),
        compiler_params=params(),
        input_output_aliases={3: 0} if onto else {},
        cost_estimate=cost(lat_rows, tokens, len(pieces) * width),
        name="decoder_part",
    )(scalars, ids, code_lanes, *onto, *flat)


def pre_grad_kernel(size, tok, scalar_ref, ids_ref, pre_ref, own_ref, theirs_ref, out_ref, rows):
    for j in range(2):
        for at in range(0, pre_ref.shape[2], 2 * tok):
            for core in range(2):
                here = slice(at + core * tok, at + (core + 1) * tok)
                there = slice(at + (1 - core) * tok, at + (2 - core) * tok)
                total = own_ref[j, :, here] + theirs_ref[j, :, there]
                rows[j, :, here] = jnp.where(pre_ref[j, :, here].astype(jnp.float32) > 0, total, 0.0).astype(jnp.bfloat16)
    spread_into(out_ref, ids_ref, [rows.at[0], rows.at[1]], scalar_ref[0], size)


def pre_grad_spread(own, theirs, ids, pre_lanes, first, lat_rows, tok):
    _, size, tokens = pre_lanes.shape
    scalars = first[None].astype(jnp.int32)
    return pl.pallas_call(
        functools.partial(pre_grad_kernel, size, tok),
        out_shape=jax.ShapeDtypeStruct((lat_rows, tokens), jnp.bfloat16),
        grid_spec=pltpu.PrefetchScalarGridSpec(
            num_scalar_prefetch=1,
            grid=(1,),
            in_specs=[resident(ids.shape)] + [resident(pre_lanes.shape)] * 3,
            out_specs=resident((lat_rows, tokens)),
            scratch_shapes=[pltpu.VMEM((2, size, tokens), jnp.bfloat16)],
        ),
        compiler_params=params(),
        cost_estimate=cost(lat_rows, 2, tokens),
        name="pre_grad_spread",
    )(scalars, ids, pre_lanes, own, theirs)


def dense_plan(pre_codes, block_ids, activations, target, decoder):
    lay_count = lax.axis_size("layer")
    lat_count = lax.axis_size("latent")
    dp_count = lax.axis_size("dp")
    lay_here = lax.axis_index("layer")
    lat_here = lax.axis_index("latent")
    dp_here = lax.axis_index("dp")
    tok_count = activations.shape[1]
    model_width = activations.shape[2]
    active_count = block_ids.shape[2]
    block_size = pre_codes.shape[3]
    lat_rows = decoder.shape[1]
    local_blocks = lat_rows // block_size
    half = model_width // dp_count
    group = dp_count * tok_count
    tokens = lat_count * group
    width = half // (PAIRS * lay_count)
    side = width // 2
    f32, bf16 = jnp.float32, jnp.bfloat16
    first = lat_here * local_blocks

    def columns(rows, which):
        return lax.dynamic_slice_in_dim(rows, which * half, half, axis=1)

    pre_rows = jnp.swapaxes(pre_codes[0], 0, 1).reshape(active_count * tok_count, block_size)
    id_rows = jnp.pad(block_ids[0].T, ((0, 16 - active_count), (0, 0))).astype(bf16)
    own = jnp.concatenate([pre_rows, id_rows], axis=0)
    message = jnp.stack([own] + [flip(own, "latent", r) for r in range(1, lat_count)])

    acts = jnp.concatenate(
        [columns(activations[0], dp_here), flip(columns(activations[0], 1 - dp_here), "dp", 1)]
    )
    up, down = [acts], [acts]

    def next_hops():
        step = len(up)
        up.append(hop(up[-1], "latent", 1, step - 1))
        down.append(hop(down[-1], "latent", -1, step - 1))

    next_hops()
    message = jnp.stack([message, flip(message, "dp", 1)], axis=1)
    message = message.reshape(lat_count * dp_count, own.shape[0], block_size)

    goal = target.reshape(tok_count, dp_count, PAIRS, lay_count, width)

    def goal_of(which):
        cut = lax.dynamic_index_in_dim(goal, which, 1, False)
        return lax.dynamic_index_in_dim(cut, lay_here, 2, False)

    goals = jnp.concatenate([goal_of(dp_here), flip(goal_of(1 - dp_here), "dp", 1)])

    def places(pair, names, offset):
        return jnp.stack([offset + pair * lay_count + (lay_here ^ r) for r in names])

    def weight_places(pair, names):
        return places(pair, names, dp_here * (half // width))

    parts = [forward(message, decoder, first, weight_places(p, (3, 1, 2, 0)), width) for p in range(PAIRS)]
    got = [(flip(parts[p][0], "layer", 1), flip(parts[p][2], "layer", 2)) for p in range(PAIRS)]
    up[1], down[1], got[0] = lax.optimization_barrier((up[1], down[1], got[0]))

    def add(one, two):
        return (one.astype(f32) + two.astype(f32)).astype(bf16)

    lat_bits = [1 << i for i in range(lat_count.bit_length() - 1)]
    own_errors = []
    for p in range(PAIRS):
        kept = parts[p][1], parts[p][3]
        far = [flip(add(got[p][n][1:], kept[n][1:]), "layer", 2 - n) for n in range(2)]
        sent, held = layer_sum((got[p][0], kept[0], far[0]), (got[p][1], kept[1], far[1]), lat_count)
        near = flip(sent, "latent", 1)
        terms = [held, near]
        for bit in lat_bits[1:]:
            cut = [t.reshape((-1, 2) + t.shape[1:]) for t in terms]
            out = sum(c[:, 1].astype(f32) for c in cut).astype(bf16)
            terms = [c[:, 0] for c in cut] + [flip(out, "latent", bit)]
        total = sum(t[0].astype(f32) for t in terms)
        own_errors.append(((total - goals[:, p].astype(f32)) / tok_count).astype(bf16))

    if lat_count > 2:
        up[1], down[1], own_errors[-1] = lax.optimization_barrier((up[1], down[1], own_errors[-1]))
    while len(up) < lat_count:
        next_hops()

    pieces = []
    for p in range(PAIRS):
        rows = own_errors[p][None]
        for bit in lat_bits[:0:-1]:
            rows = jnp.stack([rows, flip(rows, "latent", bit)], axis=1).reshape((-1,) + rows.shape[1:])
        rows = jnp.stack([rows, flip(rows, "latent", 1)], axis=1).reshape(tokens, width)
        one, two = flip(rows, "layer", 1), flip(rows, "layer", 2)
        three = (flip(two[:, :side], "layer", 1), flip(one[:, side:], "layer", 2))
        pieces.append([(rows,), (one,), (two,), three])

    cut = message.reshape(tokens // tok_count, own.shape[0], block_size)
    pre_lanes = cut[:, :active_count * tok_count].reshape(-1, active_count, tok_count, block_size)
    pre_lanes = jnp.transpose(pre_lanes, (1, 3, 0, 2)).reshape(active_count, block_size, tokens)
    code_lanes = jnp.maximum(pre_lanes, jnp.zeros((), bf16))
    ids = cut[:, active_count * tok_count:active_count * tok_count + active_count]
    ids = jnp.swapaxes(ids, 0, 1).reshape(active_count, tokens)
    ids_wide = jnp.broadcast_to(ids[:, None, :], (active_count, 16, tokens))
    ids = ids.astype(f32)

    grads = []
    dec = None
    for p in range(PAIRS):
        for names in ((0, 1, 2, 3),) if p < PAIRS - 1 else ((0, 1, 2), (3,)):
            here = [pieces[p][r] for r in names]
            grads.append(code_grad(here, ids, decoder, first, weight_places(p, names), block_size))
            dec = decoder_part(here, ids_wide, code_lanes, first, places(p, names, 0), lat_rows, half, dec)
    grad = sum(grads)
    pre_grad = pre_grad_spread(grad, flip(grad, "dp", 1), ids_wide, pre_lanes, first, lat_rows, tok_count)
    along = [acts] + [down[k] + up[lat_count - k] for k in range(1, lat_count)]
    along = jnp.stack(along)
    along = [lax.dynamic_index_in_dim(along, lax.rem((lat_here ^ r) - lat_here + lat_count, lat_count), 0, False) for r in range(lat_count)]
    enc = jnp.dot(pre_grad, jnp.concatenate(along), preferred_element_type=f32).astype(bf16)
    return dec[None], enc[None]


def per_device(pre_codes, block_ids, activations, target, decoder):
    lat_count = lax.axis_size("latent")
    lay_count = lax.axis_size("layer")
    dp_count = lax.axis_size("dp")
    tok_count = activations.shape[1]
    model_width = activations.shape[2]
    active_count = block_ids.shape[2]
    block_size = pre_codes.shape[3]
    all_blocks = decoder.shape[1] // block_size * lat_count
    slots = 2 * tok_count * active_count // lat_count
    dense = (
        slots >= tok_count
        and dp_count == 2
        and active_count == 2
        and lay_count == 4
        and lat_count > 1
        and lat_count & (lat_count - 1) == 0
        and tok_count == block_size
        and lat_count * dp_count * 16 <= tok_count
        and model_width % (dp_count * 2 * PAIRS * lay_count * 128) == 0
        and all_blocks <= 256
    )
    plan = dense_plan if dense else slot_plan
    return plan(pre_codes, block_ids, activations, target, decoder)


def solution(mesh):
    placed = (
        P("layer", ("latent", "dp"), None, None),
        P("layer", ("latent", "dp"), None),
        P("layer", ("latent", "dp"), None),
        P(("latent", "dp"), None),
        P("layer", "latent", None),
    )
    return jax.shard_map(
        per_device,
        mesh=mesh,
        in_specs=placed,
        out_specs=(P("layer", "latent", "dp"), P("layer", "latent", "dp")),
        check_vma=False,
    )
```

```python
import functools

import jax
import jax.numpy as jnp
from jax import lax
from jax.experimental import pallas as pl
from jax.experimental.pallas import tpu as pltpu
from jax.sharding import PartitionSpec as P

PAIRS = 2
VMEM_BYTES = 40 * 1024 * 1024


def local_contrib(received_pre, weights, lat_count, local_blocks):
    code_vals = jnp.maximum(received_pre, jnp.zeros((), received_pre.dtype))
    slot_span = received_pre.shape[1]
    block_size = received_pre.shape[2]
    grouped = code_vals.reshape(lat_count, local_blocks, slot_span, block_size)
    contrib = jnp.einsum("sbcl,bld->sbcd", grouped, weights, preferred_element_type=jnp.float32)
    contrib = contrib.astype(jnp.bfloat16).reshape(
        lat_count * local_blocks, slot_span, weights.shape[2]
    )
    return lax.all_to_all(contrib, "latent", split_axis=0, concat_axis=0, tiled=True)


def slot_plan(pre_codes, block_ids, activations, target, decoder):
    lat_count = lax.axis_size("latent")
    tok_count = activations.shape[1]
    model_width = activations.shape[2]
    active_count = block_ids.shape[2]
    block_size = pre_codes.shape[3]
    lat_rows = decoder.shape[1]
    local_blocks = lat_rows // block_size
    all_blocks = local_blocks * lat_count
    capacity = 2 * tok_count * active_count // all_blocks
    slot_count = all_blocks * capacity
    pair_count = tok_count * active_count
    pair_block = block_ids[0].T.reshape(pair_count)
    member = (pair_block[:, None] == jnp.arange(all_blocks, dtype=jnp.int32)[None, :]).astype(
        jnp.int32
    )
    before = jnp.cumsum(member, axis=0) - member
    pair_rank = jnp.sum(before * member, axis=1)
    target_slot = pair_block * capacity + pair_rank
    slot_pair = (jnp.arange(slot_count, dtype=jnp.int32)[:, None] == target_slot[None, :]).astype(
        jnp.bfloat16
    )
    slot_token = jnp.sum(slot_pair.reshape(slot_count, active_count, tok_count), axis=1)
    pre_pairs = jnp.transpose(pre_codes[0], (1, 0, 2)).reshape(pair_count, block_size)
    pre_slots = jnp.dot(slot_pair, pre_pairs, preferred_element_type=jnp.float32).astype(
        jnp.bfloat16
    )
    pre_slots = pre_slots.reshape(all_blocks, capacity, block_size)
    inputs = activations[0]
    weights = decoder[0].reshape(local_blocks, block_size, model_width)
    input_slots = jnp.dot(slot_token, inputs, preferred_element_type=jnp.float32).astype(
        jnp.bfloat16
    )
    input_slots = input_slots.reshape(all_blocks, capacity, model_width)
    pieces = (
        lax.all_to_all(pre_slots, "latent", split_axis=0, concat_axis=0, tiled=True),
        lax.all_to_all(input_slots, "latent", split_axis=0, concat_axis=0, tiled=True),
    )
    returned = local_contrib(pieces[0], weights, lat_count, local_blocks)
    returned, received_pre, received_inputs = (returned, pieces[0], pieces[1])
    part_sum = jnp.einsum(
        "st,sd->td",
        slot_token,
        returned.reshape(slot_count, model_width),
        preferred_element_type=jnp.float32,
    )
    rebuilt = lax.psum(part_sum, "layer")
    errors = ((rebuilt - target.astype(jnp.float32)) / tok_count).astype(jnp.bfloat16)
    error_slots = jnp.dot(slot_token, errors, preferred_element_type=jnp.float32).astype(
        jnp.bfloat16
    )
    error_slots = error_slots.reshape(all_blocks, capacity, model_width)
    received_errors = lax.all_to_all(error_slots, "latent", split_axis=0, concat_axis=0, tiled=True)
    pre_blocks = received_pre.reshape(lat_count, local_blocks, capacity, block_size)
    code_blocks = jnp.maximum(pre_blocks, jnp.zeros((), pre_blocks.dtype))
    error_blocks = received_errors.reshape(lat_count, local_blocks, capacity, model_width)
    input_blocks = received_inputs.reshape(lat_count, local_blocks, capacity, model_width)
    code_grad = jnp.einsum(
        "sbcd,bld->sbcl", error_blocks, weights, preferred_element_type=jnp.float32
    )
    pre_grad = jnp.where(pre_blocks > 0, code_grad, jnp.zeros((), jnp.float32)).astype(jnp.bfloat16)
    dec_term = jnp.einsum(
        "sbcl,sbcd->bld", code_blocks, error_blocks, preferred_element_type=jnp.float32
    )
    enc_term = jnp.einsum(
        "sbcl,sbcd->bld", pre_grad, input_blocks, preferred_element_type=jnp.float32
    )
    dec_term = dec_term.reshape(lat_rows, model_width)
    enc_term = enc_term.reshape(lat_rows, model_width)
    dec_half, enc_half = (
        lax.psum_scatter(dec_term, "dp", scatter_dimension=1, tiled=True),
        lax.psum_scatter(enc_term, "dp", scatter_dimension=1, tiled=True),
    )
    return (dec_half.astype(jnp.bfloat16)[None], enc_half.astype(jnp.bfloat16)[None])


def flip(value, axis, bit):
    count = lax.axis_size(axis)
    return lax.ppermute(value, axis, [(i, i ^ bit) for i in range(count)])


def hop(value, axis, step, least):
    count = lax.axis_size(axis)
    if step > 0:
        pairs = [(i, i + 1) for i in range(least, count - 1)]
    else:
        pairs = [(i, i - 1) for i in range(1, count - least)]
    return lax.ppermute(value, axis, pairs)


def after(value, *others):
    return lax.optimization_barrier((value,) + others)[0]


def params():
    return pltpu.CompilerParams(vmem_limit_bytes=VMEM_BYTES)


def cost(rows, depth, columns):
    return pl.CostEstimate(
        flops=rows * depth * columns // 2,
        bytes_accessed=(rows * depth + depth * columns + rows * columns) // 2,
        transcendentals=0,
    )


def resident(shape):
    return pl.BlockSpec(shape, lambda i, s: (0,) * len(shape))


def gather_kernel(scalar_ref, source_ref, out_ref):
    out_ref[...] = source_ref[...].reshape(out_ref.shape)


def gather_columns(source, columns, width):
    rows = source.shape[-2]
    lead = (1,) * (source.ndim - 2)
    count = columns.shape[0]
    return pl.pallas_call(
        gather_kernel,
        out_shape=jax.ShapeDtypeStruct((rows, count * width), source.dtype),
        grid_spec=pltpu.PrefetchScalarGridSpec(
            num_scalar_prefetch=1,
            grid=(count,),
            in_specs=[pl.BlockSpec(lead + (rows, width), lambda i, s: (0,) * len(lead) + (0, s[i]))],
            out_specs=pl.BlockSpec((rows, width), lambda i, s: (0, i)),
        ),
        compiler_params=params(),
        cost_estimate=cost(rows, 1, count * width),
        name="gather_columns",
    )(columns.astype(jnp.int32), source)


def codes_kernel(groups, blocks, scalar_ref, message_ref, codes, id_map, pre):
    tok = message_ref.shape[2]
    pad = message_ref.shape[1] - 2 * tok
    first = scalar_ref[0].astype(jnp.float32)
    rows = [message_ref[g, 2 * tok:2 * tok + pad, :].astype(jnp.float32) for g in range(groups)]
    fill = tok - groups * pad
    if fill:
        rows.append(jnp.zeros((fill, tok), jnp.float32))
    table = jnp.concatenate(rows, axis=0).T - first
    for g in range(groups):
        pre[g] = jnp.maximum(message_ref[g, 0:2 * tok, :], jnp.zeros((), jnp.bfloat16))
        for j in range(2):
            at = g * pad + j
            wide = jnp.broadcast_to(table[:, at:at + 1], (tok, tok))
            id_map[g, j * tok:(j + 1) * tok, :] = wide.astype(jnp.bfloat16)

    def block_step(b, carry):
        block = b.astype(jnp.float32).astype(jnp.bfloat16)
        at = pl.multiple_of(b * tok, tok)
        for g in range(groups):
            value = jnp.where(id_map[g, tok:2 * tok, :] == block, pre[g, tok:2 * tok, :], jnp.zeros((), jnp.bfloat16))
            value = jnp.where(id_map[g, 0:tok, :] == block, pre[g, 0:tok, :], value)
            codes[g * tok:(g + 1) * tok, pl.ds(at, tok)] = value
        return carry

    lax.fori_loop(0, blocks, block_step, 0)


def spread_codes(message, first, lat_rows):
    groups, _, tok = message.shape
    rows = groups * tok
    return pl.pallas_call(
        functools.partial(codes_kernel, groups, lat_rows // tok),
        out_shape=jax.ShapeDtypeStruct((rows, lat_rows), jnp.bfloat16),
        grid_spec=pltpu.PrefetchScalarGridSpec(
            num_scalar_prefetch=1,
            grid=(1,),
            in_specs=[resident(message.shape)],
            out_specs=resident((rows, lat_rows)),
            scratch_shapes=[
                pltpu.VMEM((groups, 2 * tok, tok), jnp.bfloat16),
                pltpu.VMEM((groups, 2 * tok, tok), jnp.bfloat16),
            ],
        ),
        compiler_params=params(),
        cost_estimate=cost(rows, 1, lat_rows),
        name="spread_codes",
    )(first[None].astype(jnp.int32), message)


def layer_sum_kernel(got_a, kept_a, far_a, got_b, kept_b, far_b, sent_ref, held_ref):
    half = far_a.shape[1]
    rows = sent_ref.shape[1]
    for side, (got, kept, far) in enumerate(((got_a, kept_a, far_a), (got_b, kept_b, far_b))):
        lanes = slice(side * half, (side + 1) * half)
        for n in range(2 * sent_ref.shape[0]):
            at = slice(n * rows, (n + 1) * rows)
            total = got[at, :half].astype(jnp.float32) + kept[at, :half].astype(jnp.float32)
            total = total + far[at, :].astype(jnp.float32)
            if n % 2:
                sent_ref[n // 2, :, lanes] = total.astype(jnp.bfloat16)
            else:
                held_ref[n // 2, :, lanes] = total


def layer_sum(terms_a, terms_b, blocks):
    rows, half = terms_a[2].shape
    cut = (blocks // 2, rows // blocks, 2 * half)
    return pl.pallas_call(
        layer_sum_kernel,
        out_shape=[jax.ShapeDtypeStruct(cut, jnp.bfloat16), jax.ShapeDtypeStruct(cut, jnp.float32)],
        grid=(1,),
        in_specs=[pl.BlockSpec((rows, half), lambda i: (0, 0)) for _ in range(6)],
        out_specs=[pl.BlockSpec(cut, lambda i: (0, 0, 0))] * 2,
        compiler_params=params(),
        cost_estimate=cost(rows, 4, half),
        name="layer_sum",
    )(*terms_a, *terms_b)


def spread_into(target, ids_ref, rows_refs, first, size):
    low = ids_ref.shape[1]

    def build(b, carry):
        at = pl.multiple_of(b * size, size)
        block = (first + b).astype(jnp.float32).astype(jnp.bfloat16)
        here = [ids_ref[j] == block for j in range(2)]
        for n in range(size // low):
            rows = slice(n * low, (n + 1) * low)
            value = jnp.where(here[1], rows_refs[1][rows, :], jnp.zeros((), jnp.bfloat16))
            target[pl.ds(at + n * low, low), :] = jnp.where(here[0], rows_refs[0][rows, :], value)
        return carry

    lax.fori_loop(0, target.shape[0] // size, build, 0)


def lanes_of(refs):
    return refs[0][...] if len(refs) == 1 else jnp.concatenate([r[...] for r in refs], axis=1)


def code_grad_kernel(size, shape, scalar_ref, ids_ref, *refs):
    grad_ref = refs[-1]
    weights, pieces = refs[:len(shape)], refs[len(shape):-1]

    @pl.when(pl.program_id(0) == 0)
    def _():
        grad_ref[...] = jnp.zeros_like(grad_ref)

    weight = jnp.concatenate([w[0] for w in weights], axis=1)
    grad = lax.dot_general(
        weight, lanes_of(pieces), (((1,), (1,)), ((), ())), preferred_element_type=jnp.float32
    )
    several = weight.shape[0] // size
    add0, add1 = 0.0, 0.0
    for n in range(several):
        block = (scalar_ref[0] + pl.program_id(0) * several + n).astype(jnp.float32)
        part = grad[n * size:(n + 1) * size]
        add0 = jnp.where(ids_ref[0:1] == block, part, add0)
        add1 = jnp.where(ids_ref[1:2] == block, part, add1)
    grad_ref[0] += add0
    grad_ref[1] += add1


def code_grad(pieces, ids, decoder, first, columns, size):
    lat_rows = decoder.shape[1]
    tokens = pieces[0][0].shape[0]
    width = sum(p.shape[1] for p in pieces[0])
    scalars = jnp.concatenate([first[None], columns]).astype(jnp.int32)
    flat = [p for piece in pieces for p in piece]
    several = 4 * size if lat_rows % (4 * size) == 0 else size
    return pl.pallas_call(
        functools.partial(code_grad_kernel, size, [len(p) for p in pieces]),
        out_shape=jax.ShapeDtypeStruct((2, size, tokens), jnp.float32),
        grid_spec=pltpu.PrefetchScalarGridSpec(
            num_scalar_prefetch=1,
            grid=(lat_rows // several,),
            in_specs=[resident(ids.shape)]
            + [pl.BlockSpec((1, several, width), lambda i, s, n=n: (0, i, s[n + 1])) for n in range(len(pieces))]
            + [resident(p.shape) for p in flat],
            out_specs=resident((2, size, tokens)),
        ),
        compiler_params=params(),
        cost_estimate=cost(lat_rows, len(pieces) * width, tokens),
        name="code_grad",
    )(scalars, ids, *[decoder] * len(pieces), *flat)


def decoder_kernel(size, shape, skip, scalar_ref, ids_ref, codes_ref, *refs):
    refs = refs[skip:]
    pieces, (out_ref, now, codes) = refs[:-3], refs[-3:]
    at = 0
    for i, count in enumerate(shape):

        @pl.when(pl.program_id(0) == i)
        def _(at=at, count=count):
            now[...] = lanes_of(pieces[at:at + count])

        at += count

    @pl.when(pl.program_id(0) == 0)
    def _():
        spread_into(codes, ids_ref, [codes_ref.at[0], codes_ref.at[1]], scalar_ref[0], size)

    several = 8 * size if codes.shape[0] % (8 * size) == 0 else size

    def step(i, carry):
        rows = pl.ds(pl.multiple_of(i * several, several), several)
        out_ref[rows, :] = jnp.dot(codes[rows, :], now[...], preferred_element_type=jnp.float32).astype(jnp.bfloat16)
        return carry

    lax.fori_loop(0, codes.shape[0] // several, step, 0)


def decoder_part(pieces, ids, code_lanes, first, columns, lat_rows, half, held):
    _, size, tokens = code_lanes.shape
    width = sum(p.shape[1] for p in pieces[0])
    scalars = jnp.concatenate([first[None], columns]).astype(jnp.int32)
    flat = [p for piece in pieces for p in piece]
    onto = [] if held is None else [held]
    return pl.pallas_call(
        functools.partial(decoder_kernel, size, [len(p) for p in pieces], len(onto)),
        out_shape=jax.ShapeDtypeStruct((lat_rows, half), jnp.bfloat16),
        grid_spec=pltpu.PrefetchScalarGridSpec(
            num_scalar_prefetch=1,
            grid=(len(pieces),),
            in_specs=[resident(ids.shape), resident(code_lanes.shape)]
            + [pl.BlockSpec(memory_space=pl.ANY) for _ in onto]
            + [resident(p.shape) for p in flat],
            out_specs=pl.BlockSpec((lat_rows, width), lambda i, s: (0, s[i + 1])),
            scratch_shapes=[
                pltpu.VMEM((tokens, width), jnp.bfloat16),
                pltpu.VMEM((lat_rows, tokens), jnp.bfloat16),
            ],
        ),
        compiler_params=params(),
        input_output_aliases={3: 0} if onto else {},
        cost_estimate=cost(lat_rows, tokens, len(pieces) * width),
        name="decoder_part",
    )(scalars, ids, code_lanes, *onto, *flat)


def pre_grad_kernel(size, tok, scalar_ref, ids_ref, pre_ref, own_ref, theirs_ref, out_ref, rows):
    for j in range(2):
        for at in range(0, pre_ref.shape[2], 2 * tok):
            for core in range(2):
                here = slice(at + core * tok, at + (core + 1) * tok)
                there = slice(at + (1 - core) * tok, at + (2 - core) * tok)
                total = own_ref[j, :, here] + theirs_ref[j, :, there]
                rows[j, :, here] = jnp.where(pre_ref[j, :, here].astype(jnp.float32) > 0, total, 0.0).astype(jnp.bfloat16)
    spread_into(out_ref, ids_ref, [rows.at[0], rows.at[1]], scalar_ref[0], size)


def pre_grad_spread(own, theirs, ids, pre_lanes, first, lat_rows, tok):
    _, size, tokens = pre_lanes.shape
    scalars = first[None].astype(jnp.int32)
    return pl.pallas_call(
        functools.partial(pre_grad_kernel, size, tok),
        out_shape=jax.ShapeDtypeStruct((lat_rows, tokens), jnp.bfloat16),
        grid_spec=pltpu.PrefetchScalarGridSpec(
            num_scalar_prefetch=1,
            grid=(1,),
            in_specs=[resident(ids.shape)] + [resident(pre_lanes.shape)] * 3,
            out_specs=resident((lat_rows, tokens)),
            scratch_shapes=[pltpu.VMEM((2, size, tokens), jnp.bfloat16)],
        ),
        compiler_params=params(),
        cost_estimate=cost(lat_rows, 2, tokens),
        name="pre_grad_spread",
    )(scalars, ids, pre_lanes, own, theirs)


def dense_plan(pre_codes, block_ids, activations, target, decoder):
    lay_count = lax.axis_size("layer")
    lat_count = lax.axis_size("latent")
    dp_count = lax.axis_size("dp")
    lay_here = lax.axis_index("layer")
    lat_here = lax.axis_index("latent")
    dp_here = lax.axis_index("dp")
    tok_count = activations.shape[1]
    model_width = activations.shape[2]
    active_count = block_ids.shape[2]
    block_size = pre_codes.shape[3]
    lat_rows = decoder.shape[1]
    local_blocks = lat_rows // block_size
    half = model_width // dp_count
    group = dp_count * tok_count
    tokens = lat_count * group
    width = half // (PAIRS * lay_count)
    side = width // 2
    f32, bf16 = jnp.float32, jnp.bfloat16
    first = lat_here * local_blocks

    def columns(rows, which):
        return lax.dynamic_slice_in_dim(rows, which * half, half, axis=1)

    pre_rows = jnp.swapaxes(pre_codes[0], 0, 1).reshape(active_count * tok_count, block_size)
    id_rows = jnp.pad(block_ids[0].T, ((0, 16 - active_count), (0, 0))).astype(bf16)
    own = jnp.concatenate([pre_rows, id_rows], axis=0)
    message = jnp.stack([own] + [flip(own, "latent", r) for r in range(1, lat_count)])

    acts = jnp.concatenate(
        [columns(activations[0], dp_here), flip(columns(activations[0], 1 - dp_here), "dp", 1)]
    )
    up, down = [acts], [acts]

    def next_hops():
        step = len(up)
        up.append(hop(up[-1], "latent", 1, step - 1))
        down.append(hop(down[-1], "latent", -1, step - 1))

    def places(pair, names, offset, fine=1, sub=0):
        return [(offset + pair * lay_count + (lay_here ^ r)) * fine + sub for r in names]

    def weight_places(pair, names):
        return jnp.stack(places(pair, names, dp_here * (half // width)))

    wanted = [((1, 3), 0), ((2, 3), 1), ((0, 2), 0), ((0, 1), 1)]
    at = [
        c for p in range(PAIRS) for names, n in wanted for c in places(p, names, dp_here * (half // width), 2, n)
    ]
    weights = gather_columns(decoder, jnp.stack(at), side)
    goal_at = [which * (half // width) + p * lay_count + lay_here for which in (dp_here, 1 - dp_here) for p in range(PAIRS)]
    goals = gather_columns(target, jnp.stack(goal_at), width)
    span = PAIRS * width
    goals = jnp.concatenate([goals[:, :span], flip(goals[:, span:], "dp", 1)])

    message = jnp.stack([message, flip(message, "dp", 1)], axis=1)
    message = message.reshape(lat_count * dp_count, own.shape[0], block_size)
    message, acts_now, weights = lax.optimization_barrier((message, acts, weights))
    up, down = [acts_now], [acts_now]
    next_hops()

    codes = spread_codes(message, first, lat_rows)

    def rows_for(spread, pair, n):
        cols = weights[:, (4 * pair + n) * width:(4 * pair + n + 1) * width]
        return jnp.dot(spread, cols, preferred_element_type=f32).astype(bf16)

    parts, got = [], []
    for p in range(PAIRS):
        if p == 1:
            codes, up[1], down[1] = lax.optimization_barrier((codes, up[1], down[1]))
            if lat_count > 2:
                next_hops()
        sent = rows_for(codes, p, 0), rows_for(codes, p, 1)
        got.append((flip(sent[0], "layer", 1), flip(sent[1], "layer", 2)))
        parts.append((rows_for(codes, p, 2), rows_for(codes, p, 3)))

    def add(one, two):
        return (one[:, side:].astype(f32) + two[:, side:].astype(f32)).astype(bf16)

    lat_bits = [1 << i for i in range(lat_count.bit_length() - 1)]
    own_errors = []
    for p in range(PAIRS):
        kept = parts[p]
        far = [flip(add(got[p][n], kept[n]), "layer", 2 - n) for n in range(2)]
        if p == 0 and len(up) > 2:
            up[2], down[2], far[0] = lax.optimization_barrier((up[2], down[2], far[0]))
        sent, held = layer_sum((got[p][0], kept[0], far[0]), (got[p][1], kept[1], far[1]), lat_count)
        near = flip(sent, "latent", 1)
        terms = [held, near]
        for bit in lat_bits[1:]:
            cut = [t.reshape((-1, 2) + t.shape[1:]) for t in terms]
            out = sum(c[:, 1].astype(f32) for c in cut).astype(bf16)
            terms = [c[:, 0] for c in cut] + [flip(out, "latent", bit)]
        total = sum(t[0].astype(f32) for t in terms)
        own_errors.append(((total - goals[:, p * width:(p + 1) * width].astype(f32)) / tok_count).astype(bf16))

    gathered = []
    for p in range(PAIRS):
        rows = own_errors[p][None]
        for bit in lat_bits[:0:-1]:
            rows = jnp.stack([rows, flip(rows, "latent", bit)], axis=1).reshape((-1,) + rows.shape[1:])
        gathered.append(jnp.stack([rows, flip(rows, "latent", 1)], axis=1).reshape(tokens, width))
    if len(up) < lat_count:
        up[-1], down[-1], gathered[-1] = lax.optimization_barrier((up[-1], down[-1], gathered[-1]))
    while len(up) < lat_count:
        next_hops()

    pieces = []
    for rows in gathered:
        one, two = flip(rows, "layer", 1), flip(rows, "layer", 2)
        one, two = lax.optimization_barrier((one, two))
        three = (flip(two[:, :side], "layer", 1), flip(one[:, side:], "layer", 2))
        pieces.append([(rows,), (one,), (two,), lax.optimization_barrier(three)])

    cut = message.reshape(tokens // tok_count, own.shape[0], block_size)
    pre_lanes = cut[:, :active_count * tok_count].reshape(-1, active_count, tok_count, block_size)
    pre_lanes = jnp.transpose(pre_lanes, (1, 3, 0, 2)).reshape(active_count, block_size, tokens)
    code_lanes = jnp.maximum(pre_lanes, jnp.zeros((), bf16))
    ids = cut[:, active_count * tok_count:active_count * tok_count + active_count]
    ids = jnp.swapaxes(ids, 0, 1).reshape(active_count, tokens)
    ids_wide = jnp.broadcast_to(ids[:, None, :], (active_count, 16, tokens))
    ids = ids.astype(f32)

    grads = []
    dec = None
    for p in range(PAIRS):
        for names in ((0, 1, 2, 3),) if p < PAIRS - 1 else ((0, 1, 2), (3,)):
            here = [pieces[p][r] for r in names]
            grads.append(code_grad(here, ids, decoder, first, weight_places(p, names), block_size))
            dec = decoder_part(here, ids_wide, code_lanes, first, jnp.stack(places(p, names, 0)), lat_rows, half, dec)
            if p + 1 < PAIRS:
                pieces[p + 1][3], grads[-1], dec = lax.optimization_barrier((pieces[p + 1][3], grads[-1], dec))
    grad = sum(grads)
    pre_grad = pre_grad_spread(grad, flip(grad, "dp", 1), ids_wide, pre_lanes, first, lat_rows, tok_count)
    along = [acts] + [down[k] + up[lat_count - k] for k in range(1, lat_count)]
    along = jnp.stack(along)
    along = [lax.dynamic_index_in_dim(along, lax.rem((lat_here ^ r) - lat_here + lat_count, lat_count), 0, False) for r in range(lat_count)]
    enc = jnp.dot(pre_grad, jnp.concatenate(along), preferred_element_type=f32).astype(bf16)
    return dec[None], enc[None]


def per_device(pre_codes, block_ids, activations, target, decoder):
    lat_count = lax.axis_size("latent")
    lay_count = lax.axis_size("layer")
    dp_count = lax.axis_size("dp")
    tok_count = activations.shape[1]
    model_width = activations.shape[2]
    active_count = block_ids.shape[2]
    block_size = pre_codes.shape[3]
    all_blocks = decoder.shape[1] // block_size * lat_count
    slots = 2 * tok_count * active_count // lat_count
    dense = (
        slots >= tok_count
        and dp_count == 2
        and active_count == 2
        and lay_count == 4
        and lat_count > 1
        and lat_count & (lat_count - 1) == 0
        and tok_count == block_size
        and lat_count * dp_count * 16 <= tok_count
        and model_width % (dp_count * 2 * PAIRS * lay_count * 128) == 0
        and all_blocks <= 256
    )
    plan = dense_plan if dense else slot_plan
    return plan(pre_codes, block_ids, activations, target, decoder)


def solution(mesh):
    placed = (
        P("layer", ("latent", "dp"), None, None),
        P("layer", ("latent", "dp"), None),
        P("layer", ("latent", "dp"), None),
        P(("latent", "dp"), None),
        P("layer", "latent", None),
    )
    return jax.shard_map(
        per_device,
        mesh=mesh,
        in_specs=placed,
        out_specs=(P("layer", "latent", "dp"), P("layer", "latent", "dp")),
        check_vma=False,
    )
```

```python
import functools

import jax
import jax.numpy as jnp
from jax import lax
from jax.experimental import pallas as pl
from jax.experimental.pallas import tpu as pltpu
from jax.sharding import PartitionSpec as P

VMEM_BYTES = 40 * 1024 * 1024


def local_contrib(received_pre, weights, lat_count, local_blocks):
    code_vals = jnp.maximum(received_pre, jnp.zeros((), received_pre.dtype))
    slot_span = received_pre.shape[1]
    block_size = received_pre.shape[2]
    grouped = code_vals.reshape(lat_count, local_blocks, slot_span, block_size)
    contrib = jnp.einsum("sbcl,bld->sbcd", grouped, weights, preferred_element_type=jnp.float32)
    contrib = contrib.astype(jnp.bfloat16).reshape(
        lat_count * local_blocks, slot_span, weights.shape[2]
    )
    return lax.all_to_all(contrib, "latent", split_axis=0, concat_axis=0, tiled=True)


def slot_plan(pre_codes, block_ids, activations, target, decoder):
    lat_count = lax.axis_size("latent")
    tok_count = activations.shape[1]
    model_width = activations.shape[2]
    active_count = block_ids.shape[2]
    block_size = pre_codes.shape[3]
    lat_rows = decoder.shape[1]
    local_blocks = lat_rows // block_size
    all_blocks = local_blocks * lat_count
    capacity = 2 * tok_count * active_count // all_blocks
    slot_count = all_blocks * capacity
    pair_count = tok_count * active_count
    pair_block = block_ids[0].T.reshape(pair_count)
    member = (pair_block[:, None] == jnp.arange(all_blocks, dtype=jnp.int32)[None, :]).astype(
        jnp.int32
    )
    before = jnp.cumsum(member, axis=0) - member
    pair_rank = jnp.sum(before * member, axis=1)
    target_slot = pair_block * capacity + pair_rank
    slot_pair = (jnp.arange(slot_count, dtype=jnp.int32)[:, None] == target_slot[None, :]).astype(
        jnp.bfloat16
    )
    slot_token = jnp.sum(slot_pair.reshape(slot_count, active_count, tok_count), axis=1)
    pre_pairs = jnp.transpose(pre_codes[0], (1, 0, 2)).reshape(pair_count, block_size)
    pre_slots = jnp.dot(slot_pair, pre_pairs, preferred_element_type=jnp.float32).astype(
        jnp.bfloat16
    )
    pre_slots = pre_slots.reshape(all_blocks, capacity, block_size)
    inputs = activations[0]
    weights = decoder[0].reshape(local_blocks, block_size, model_width)
    input_slots = jnp.dot(slot_token, inputs, preferred_element_type=jnp.float32).astype(
        jnp.bfloat16
    )
    input_slots = input_slots.reshape(all_blocks, capacity, model_width)
    pieces = (
        lax.all_to_all(pre_slots, "latent", split_axis=0, concat_axis=0, tiled=True),
        lax.all_to_all(input_slots, "latent", split_axis=0, concat_axis=0, tiled=True),
    )
    returned = local_contrib(pieces[0], weights, lat_count, local_blocks)
    returned, received_pre, received_inputs = (returned, pieces[0], pieces[1])
    part_sum = jnp.einsum(
        "st,sd->td",
        slot_token,
        returned.reshape(slot_count, model_width),
        preferred_element_type=jnp.float32,
    )
    rebuilt = lax.psum(part_sum, "layer")
    errors = ((rebuilt - target.astype(jnp.float32)) / tok_count).astype(jnp.bfloat16)
    error_slots = jnp.dot(slot_token, errors, preferred_element_type=jnp.float32).astype(
        jnp.bfloat16
    )
    error_slots = error_slots.reshape(all_blocks, capacity, model_width)
    received_errors = lax.all_to_all(error_slots, "latent", split_axis=0, concat_axis=0, tiled=True)
    pre_blocks = received_pre.reshape(lat_count, local_blocks, capacity, block_size)
    code_blocks = jnp.maximum(pre_blocks, jnp.zeros((), pre_blocks.dtype))
    error_blocks = received_errors.reshape(lat_count, local_blocks, capacity, model_width)
    input_blocks = received_inputs.reshape(lat_count, local_blocks, capacity, model_width)
    code_grad = jnp.einsum(
        "sbcd,bld->sbcl", error_blocks, weights, preferred_element_type=jnp.float32
    )
    pre_grad = jnp.where(pre_blocks > 0, code_grad, jnp.zeros((), jnp.float32)).astype(jnp.bfloat16)
    dec_term = jnp.einsum(
        "sbcl,sbcd->bld", code_blocks, error_blocks, preferred_element_type=jnp.float32
    )
    enc_term = jnp.einsum(
        "sbcl,sbcd->bld", pre_grad, input_blocks, preferred_element_type=jnp.float32
    )
    dec_term = dec_term.reshape(lat_rows, model_width)
    enc_term = enc_term.reshape(lat_rows, model_width)
    dec_half, enc_half = (
        lax.psum_scatter(dec_term, "dp", scatter_dimension=1, tiled=True),
        lax.psum_scatter(enc_term, "dp", scatter_dimension=1, tiled=True),
    )
    return (dec_half.astype(jnp.bfloat16)[None], enc_half.astype(jnp.bfloat16)[None])


def flip(value, axis, bit):
    count = lax.axis_size(axis)
    return lax.ppermute(value, axis, [(i, i ^ bit) for i in range(count)])


def hop(value, axis, step, least):
    count = lax.axis_size(axis)
    if step > 0:
        pairs = [(i, i + 1) for i in range(least, count - 1)]
    else:
        pairs = [(i, i - 1) for i in range(1, count - least)]
    return lax.ppermute(value, axis, pairs)


def params():
    return pltpu.CompilerParams(vmem_limit_bytes=VMEM_BYTES)


def cost(rows, depth, columns):
    return pl.CostEstimate(
        flops=rows * depth * columns // 2,
        bytes_accessed=(rows * depth + depth * columns + rows * columns) // 2,
        transcendentals=0,
    )


def resident(shape):
    return pl.BlockSpec(shape, lambda i, s: (0,) * len(shape))


def gather_kernel(scalar_ref, source_ref, out_ref):
    out_ref[...] = source_ref[...].reshape(out_ref.shape)


def gather_columns(source, columns, width):
    rows = source.shape[-2]
    lead = (1,) * (source.ndim - 2)
    count = columns.shape[0]
    return pl.pallas_call(
        gather_kernel,
        out_shape=jax.ShapeDtypeStruct((rows, count * width), source.dtype),
        grid_spec=pltpu.PrefetchScalarGridSpec(
            num_scalar_prefetch=1,
            grid=(count,),
            in_specs=[pl.BlockSpec(lead + (rows, width), lambda i, s: (0,) * len(lead) + (0, s[i]))],
            out_specs=pl.BlockSpec((rows, width), lambda i, s: (0, i)),
        ),
        compiler_params=params(),
        cost_estimate=cost(rows, 1, count * width),
        name="gather_columns",
    )(columns.astype(jnp.int32), source)


def codes_kernel(groups, blocks, scalar_ref, message_ref, codes, id_map, pre):
    tok = message_ref.shape[2]
    pad = message_ref.shape[1] - 2 * tok
    first = scalar_ref[0].astype(jnp.float32)
    rows = [message_ref[g, 2 * tok:2 * tok + pad, :].astype(jnp.float32) for g in range(groups)]
    fill = tok - groups * pad
    if fill:
        rows.append(jnp.zeros((fill, tok), jnp.float32))
    table = jnp.concatenate(rows, axis=0).T - first
    for g in range(groups):
        pre[g] = jnp.maximum(message_ref[g, 0:2 * tok, :], jnp.zeros((), jnp.bfloat16))
        for j in range(2):
            at = g * pad + j
            wide = jnp.broadcast_to(table[:, at:at + 1], (tok, tok))
            id_map[g, j * tok:(j + 1) * tok, :] = wide.astype(jnp.bfloat16)

    def block_step(b, carry):
        block = b.astype(jnp.float32).astype(jnp.bfloat16)
        at = pl.multiple_of(b * tok, tok)
        for g in range(groups):
            value = jnp.where(id_map[g, tok:2 * tok, :] == block, pre[g, tok:2 * tok, :], jnp.zeros((), jnp.bfloat16))
            value = jnp.where(id_map[g, 0:tok, :] == block, pre[g, 0:tok, :], value)
            codes[g * tok:(g + 1) * tok, pl.ds(at, tok)] = value
        return carry

    lax.fori_loop(0, blocks, block_step, 0)


def spread_codes(message, first, lat_rows):
    groups, _, tok = message.shape
    rows = groups * tok
    return pl.pallas_call(
        functools.partial(codes_kernel, groups, lat_rows // tok),
        out_shape=jax.ShapeDtypeStruct((rows, lat_rows), jnp.bfloat16),
        grid_spec=pltpu.PrefetchScalarGridSpec(
            num_scalar_prefetch=1,
            grid=(1,),
            in_specs=[resident(message.shape)],
            out_specs=resident((rows, lat_rows)),
            scratch_shapes=[
                pltpu.VMEM((groups, 2 * tok, tok), jnp.bfloat16),
                pltpu.VMEM((groups, 2 * tok, tok), jnp.bfloat16),
            ],
        ),
        compiler_params=params(),
        cost_estimate=cost(rows, 1, lat_rows),
        name="spread_codes",
    )(first[None].astype(jnp.int32), message)


def layer_sum_kernel(got_a, kept_a, far_a, got_b, kept_b, far_b, own_ref, *sent_refs):
    half = far_a.shape[1]
    rows = own_ref.shape[0]
    for side, (got, kept, far) in enumerate(((got_a, kept_a, far_a), (got_b, kept_b, far_b))):
        lanes = slice(side * half, (side + 1) * half)
        for n in range(1 + len(sent_refs)):
            at = slice(n * rows, (n + 1) * rows)
            total = got[at, :half].astype(jnp.float32) + kept[at, :half].astype(jnp.float32)
            total = total + far[at, :].astype(jnp.float32)
            if n:
                sent_refs[n - 1][:, lanes] = total.astype(jnp.bfloat16)
            else:
                own_ref[:, lanes] = total


def layer_sum(terms_a, terms_b, blocks):
    rows, half = terms_a[2].shape
    cut = (rows // blocks, 2 * half)
    return pl.pallas_call(
        layer_sum_kernel,
        out_shape=[jax.ShapeDtypeStruct(cut, jnp.float32)] + [jax.ShapeDtypeStruct(cut, jnp.bfloat16)] * (blocks - 1),
        grid=(1,),
        in_specs=[pl.BlockSpec((rows, half), lambda i: (0, 0)) for _ in range(6)],
        out_specs=[pl.BlockSpec(cut, lambda i: (0, 0))] * blocks,
        compiler_params=params(),
        cost_estimate=cost(rows, 4, half),
        name="layer_sum",
    )(*terms_a, *terms_b)


def spread_into(target, ids_ref, rows_refs, first, size):
    low = ids_ref.shape[1]

    def build(b, carry):
        at = pl.multiple_of(b * size, size)
        block = (first + b).astype(jnp.float32).astype(jnp.bfloat16)
        here = [ids_ref[j] == block for j in range(2)]
        for n in range(size // low):
            rows = slice(n * low, (n + 1) * low)
            value = jnp.where(here[1], rows_refs[1][rows, :], jnp.zeros((), jnp.bfloat16))
            target[pl.ds(at + n * low, low), :] = jnp.where(here[0], rows_refs[0][rows, :], value)
        return carry

    lax.fori_loop(0, target.shape[0] // size, build, 0)


def lanes_of(refs):
    return refs[0][...] if len(refs) == 1 else jnp.concatenate([r[...] for r in refs], axis=1)


def code_grad_kernel(size, shape, scalar_ref, ids_ref, *refs):
    grad_ref = refs[-1]
    weights, pieces = refs[:len(shape)], refs[len(shape):-1]

    @pl.when(pl.program_id(0) == 0)
    def _():
        grad_ref[...] = jnp.zeros_like(grad_ref)

    weight = jnp.concatenate([w[0] for w in weights], axis=1)
    grad = lax.dot_general(
        weight, lanes_of(pieces), (((1,), (1,)), ((), ())), preferred_element_type=jnp.float32
    )
    several = weight.shape[0] // size
    add0, add1 = 0.0, 0.0
    for n in range(several):
        block = (scalar_ref[0] + pl.program_id(0) * several + n).astype(jnp.float32)
        part = grad[n * size:(n + 1) * size]
        add0 = jnp.where(ids_ref[0:1] == block, part, add0)
        add1 = jnp.where(ids_ref[1:2] == block, part, add1)
    grad_ref[0] += add0
    grad_ref[1] += add1


def code_grad(pieces, ids, decoder, first, columns, size):
    lat_rows = decoder.shape[1]
    tokens = pieces[0][0].shape[0]
    width = sum(p.shape[1] for p in pieces[0])
    scalars = jnp.concatenate([first[None], columns]).astype(jnp.int32)
    flat = [p for piece in pieces for p in piece]
    several = 4 * size if lat_rows % (4 * size) == 0 else size
    return pl.pallas_call(
        functools.partial(code_grad_kernel, size, [len(p) for p in pieces]),
        out_shape=jax.ShapeDtypeStruct((2, size, tokens), jnp.float32),
        grid_spec=pltpu.PrefetchScalarGridSpec(
            num_scalar_prefetch=1,
            grid=(lat_rows // several,),
            in_specs=[resident(ids.shape)]
            + [pl.BlockSpec((1, several, width), lambda i, s, n=n: (0, i, s[n + 1])) for n in range(len(pieces))]
            + [resident(p.shape) for p in flat],
            out_specs=resident((2, size, tokens)),
        ),
        compiler_params=params(),
        cost_estimate=cost(lat_rows, len(pieces) * width, tokens),
        name="code_grad",
    )(scalars, ids, *[decoder] * len(pieces), *flat)


def decoder_kernel(size, shape, skip, scalar_ref, ids_ref, codes_ref, *refs):
    refs = refs[skip:]
    pieces, (out_ref, now, codes) = refs[:-3], refs[-3:]
    at = 0
    for i, count in enumerate(shape):

        @pl.when(pl.program_id(0) == i)
        def _(at=at, count=count):
            now[...] = lanes_of(pieces[at:at + count])

        at += count

    @pl.when(pl.program_id(0) == 0)
    def _():
        spread_into(codes, ids_ref, [codes_ref.at[0], codes_ref.at[1]], scalar_ref[0], size)

    several = 8 * size if codes.shape[0] % (8 * size) == 0 else size

    def step(i, carry):
        rows = pl.ds(pl.multiple_of(i * several, several), several)
        out_ref[rows, :] = jnp.dot(codes[rows, :], now[...], preferred_element_type=jnp.float32).astype(jnp.bfloat16)
        return carry

    lax.fori_loop(0, codes.shape[0] // several, step, 0)


def decoder_part(pieces, ids, code_lanes, first, columns, lat_rows, half, held):
    _, size, tokens = code_lanes.shape
    width = sum(p.shape[1] for p in pieces[0])
    scalars = jnp.concatenate([first[None], columns]).astype(jnp.int32)
    flat = [p for piece in pieces for p in piece]
    onto = [] if held is None else [held]
    return pl.pallas_call(
        functools.partial(decoder_kernel, size, [len(p) for p in pieces], len(onto)),
        out_shape=jax.ShapeDtypeStruct((lat_rows, half), jnp.bfloat16),
        grid_spec=pltpu.PrefetchScalarGridSpec(
            num_scalar_prefetch=1,
            grid=(len(pieces),),
            in_specs=[resident(ids.shape), resident(code_lanes.shape)]
            + [pl.BlockSpec(memory_space=pl.ANY) for _ in onto]
            + [resident(p.shape) for p in flat],
            out_specs=pl.BlockSpec((lat_rows, width), lambda i, s: (0, s[i + 1])),
            scratch_shapes=[
                pltpu.VMEM((tokens, width), jnp.bfloat16),
                pltpu.VMEM((lat_rows, tokens), jnp.bfloat16),
            ],
        ),
        compiler_params=params(),
        input_output_aliases={3: 0} if onto else {},
        cost_estimate=cost(lat_rows, tokens, len(pieces) * width),
        name="decoder_part",
    )(scalars, ids, code_lanes, *onto, *flat)


def pre_grad_kernel(size, tok, scalar_ref, ids_ref, pre_ref, own_ref, theirs_ref, out_ref, rows):
    for j in range(2):
        for at in range(0, pre_ref.shape[2], 2 * tok):
            for core in range(2):
                here = slice(at + core * tok, at + (core + 1) * tok)
                there = slice(at + (1 - core) * tok, at + (2 - core) * tok)
                total = own_ref[j, :, here] + theirs_ref[j, :, there]
                rows[j, :, here] = jnp.where(pre_ref[j, :, here].astype(jnp.float32) > 0, total, 0.0).astype(jnp.bfloat16)
    spread_into(out_ref, ids_ref, [rows.at[0], rows.at[1]], scalar_ref[0], size)


def pre_grad_spread(own, theirs, ids, pre_lanes, first, lat_rows, tok):
    _, size, tokens = pre_lanes.shape
    scalars = first[None].astype(jnp.int32)
    return pl.pallas_call(
        functools.partial(pre_grad_kernel, size, tok),
        out_shape=jax.ShapeDtypeStruct((lat_rows, tokens), jnp.bfloat16),
        grid_spec=pltpu.PrefetchScalarGridSpec(
            num_scalar_prefetch=1,
            grid=(1,),
            in_specs=[resident(ids.shape)] + [resident(pre_lanes.shape)] * 3,
            out_specs=resident((lat_rows, tokens)),
            scratch_shapes=[pltpu.VMEM((2, size, tokens), jnp.bfloat16)],
        ),
        compiler_params=params(),
        cost_estimate=cost(lat_rows, 2, tokens),
        name="pre_grad_spread",
    )(scalars, ids, pre_lanes, own, theirs)


def dense_plan(pre_codes, block_ids, activations, target, decoder):
    lay_count = lax.axis_size("layer")
    lat_count = lax.axis_size("latent")
    dp_count = lax.axis_size("dp")
    lay_here = lax.axis_index("layer")
    lat_here = lax.axis_index("latent")
    dp_here = lax.axis_index("dp")
    tok_count = activations.shape[1]
    model_width = activations.shape[2]
    active_count = block_ids.shape[2]
    block_size = pre_codes.shape[3]
    lat_rows = decoder.shape[1]
    local_blocks = lat_rows // block_size
    half = model_width // dp_count
    group = dp_count * tok_count
    tokens = lat_count * group
    width = half // lay_count
    side = width // 2
    f32, bf16 = jnp.float32, jnp.bfloat16
    first = lat_here * local_blocks

    def columns(rows, which):
        return lax.dynamic_slice_in_dim(rows, which * half, half, axis=1)

    def places(names, offset, fine=1, sub=0):
        return [(offset + (lay_here ^ r)) * fine + sub for r in names]

    def weight_places(names):
        return jnp.stack(places(names, dp_here * lay_count))

    pre_rows = jnp.swapaxes(pre_codes[0], 0, 1).reshape(active_count * tok_count, block_size)
    id_rows = jnp.pad(block_ids[0].T, ((0, 16 - active_count), (0, 0))).astype(bf16)
    own = jnp.concatenate([pre_rows, id_rows], axis=0)
    message = jnp.stack([own] + [flip(own, "latent", r) for r in range(1, lat_count)])

    at = places((1, 3), dp_here * lay_count, 2, 0) + places((2, 3), dp_here * lay_count, 2, 1)
    send_weights = gather_columns(decoder, jnp.stack(at), side)

    acts = jnp.concatenate(
        [columns(activations[0], dp_here), flip(columns(activations[0], 1 - dp_here), "dp", 1)]
    )
    message, acts, send_weights = lax.optimization_barrier((message, acts, send_weights))
    up, down = [acts], [acts]

    def next_hops():
        step = len(up)
        up.append(hop(up[-1], "latent", 1, step - 1))
        down.append(hop(down[-1], "latent", -1, step - 1))

    message = jnp.stack([message, flip(message, "dp", 1)], axis=1)
    message = message.reshape(lat_count * dp_count, own.shape[0], block_size)
    next_hops()

    at = places((0, 2), dp_here * lay_count, 2, 0) + places((0, 1), dp_here * lay_count, 2, 1)
    keep_weights = gather_columns(decoder, jnp.stack(at), side)
    goals = gather_columns(target, jnp.stack([which * lay_count + lay_here for which in (dp_here, 1 - dp_here)]), width)
    goals = jnp.concatenate([goals[:, :width], flip(goals[:, width:], "dp", 1)])

    codes = spread_codes(message, first, lat_rows)

    def rows_for(spread, weights, n):
        return jnp.dot(spread, weights[:, n * width:(n + 1) * width], preferred_element_type=f32).astype(bf16)

    got = flip(rows_for(codes, send_weights, 0), "layer", 1), flip(rows_for(codes, send_weights, 1), "layer", 2)
    keep_codes = codes
    if lat_count > 2:
        keep_codes, up[1], down[1] = lax.optimization_barrier((codes, up[1], down[1]))
        next_hops()
    kept = rows_for(keep_codes, keep_weights, 0), rows_for(keep_codes, keep_weights, 1)

    def add(one, two):
        return (one[:, side:].astype(f32) + two[:, side:].astype(f32)).astype(bf16)

    far = [flip(add(got[n], kept[n]), "layer", 2 - n) for n in range(2)]
    far, goals, up[-1], down[-1] = lax.optimization_barrier((far, goals, up[-1], down[-1]))

    total, *sent = layer_sum((got[0], kept[0], far[0]), (got[1], kept[1], far[1]), lat_count)
    for r in range(1, lat_count):
        total = total + flip(sent[r - 1], "latent", r).astype(f32)
    errors = ((total - goals.astype(f32)) / tok_count).astype(bf16)
    rows = jnp.concatenate([errors] + [flip(errors, "latent", r) for r in range(1, lat_count)])
    rows, up[-1], down[-1] = lax.optimization_barrier((rows, up[-1], down[-1]))
    while len(up) < lat_count:
        next_hops()
    one, two = flip(rows, "layer", 1), flip(rows, "layer", 2)

    cut = message.reshape(tokens // tok_count, own.shape[0], block_size)
    pre_lanes = cut[:, :active_count * tok_count].reshape(-1, active_count, tok_count, block_size)
    pre_lanes = jnp.transpose(pre_lanes, (1, 3, 0, 2)).reshape(active_count, block_size, tokens)
    code_lanes = jnp.maximum(pre_lanes, jnp.zeros((), bf16))
    ids = cut[:, active_count * tok_count:active_count * tok_count + active_count]
    ids = jnp.swapaxes(ids, 0, 1).reshape(active_count, tokens)
    ids_wide = jnp.broadcast_to(ids[:, None, :], (active_count, 16, tokens))
    ids = ids.astype(f32)

    def grads_of(here, names, dec):
        grad = code_grad(here, ids, decoder, first, weight_places(names), block_size)
        where = jnp.stack(places(names, 0))
        return grad, decoder_part(here, ids_wide, code_lanes, first, where, lat_rows, half, dec)

    grad, dec = grads_of([(rows,)], (0,), None)
    one, two, grad, dec, up[-1], down[-1] = lax.optimization_barrier((one, two, grad, dec, up[-1], down[-1]))
    three = flip(two[:, :side], "layer", 1), flip(one[:, side:], "layer", 2)
    along = [acts] + [down[k] + up[lat_count - k] for k in range(1, lat_count)]
    along = jnp.stack(along)
    along = [
        lax.dynamic_index_in_dim(along, lax.rem((lat_here ^ r) - lat_here + lat_count, lat_count), 0, False)
        for r in range(lat_count)
    ]
    along = jnp.concatenate(along)
    more, dec = grads_of([(one,), (two,)], (1, 2), dec)
    three, more, dec, along = lax.optimization_barrier((three, more, dec, along))
    last, dec = grads_of([three], (3,), dec)
    grad = grad + more + last
    pre_grad = pre_grad_spread(grad, flip(grad, "dp", 1), ids_wide, pre_lanes, first, lat_rows, tok_count)
    enc = jnp.dot(pre_grad, along, preferred_element_type=f32).astype(bf16)
    return dec[None], enc[None]


def per_device(pre_codes, block_ids, activations, target, decoder):
    lat_count = lax.axis_size("latent")
    lay_count = lax.axis_size("layer")
    dp_count = lax.axis_size("dp")
    tok_count = activations.shape[1]
    model_width = activations.shape[2]
    active_count = block_ids.shape[2]
    block_size = pre_codes.shape[3]
    all_blocks = decoder.shape[1] // block_size * lat_count
    slots = 2 * tok_count * active_count // lat_count
    dense = (
        slots >= tok_count
        and dp_count == 2
        and active_count == 2
        and lay_count == 4
        and lat_count > 1
        and lat_count & (lat_count - 1) == 0
        and tok_count == block_size
        and lat_count * dp_count * 16 <= tok_count
        and model_width % (dp_count * 2 * lay_count * 128) == 0
        and all_blocks <= 256
    )
    plan = dense_plan if dense else slot_plan
    return plan(pre_codes, block_ids, activations, target, decoder)


def solution(mesh):
    placed = (
        P("layer", ("latent", "dp"), None, None),
        P("layer", ("latent", "dp"), None),
        P("layer", ("latent", "dp"), None),
        P(("latent", "dp"), None),
        P("layer", "latent", None),
    )
    return jax.shard_map(
        per_device,
        mesh=mesh,
        in_specs=placed,
        out_specs=(P("layer", "latent", "dp"), P("layer", "latent", "dp")),
        check_vma=False,
    )
```

```python
import functools

import jax
import jax.numpy as jnp
from jax import lax
from jax.experimental import pallas as pl
from jax.experimental.pallas import tpu as pltpu
from jax.sharding import PartitionSpec as P

VMEM_BYTES = 40 * 1024 * 1024


def local_contrib(received_pre, weights, lat_count, local_blocks):
    code_vals = jnp.maximum(received_pre, jnp.zeros((), received_pre.dtype))
    slot_span = received_pre.shape[1]
    block_size = received_pre.shape[2]
    grouped = code_vals.reshape(lat_count, local_blocks, slot_span, block_size)
    contrib = jnp.einsum("sbcl,bld->sbcd", grouped, weights, preferred_element_type=jnp.float32)
    contrib = contrib.astype(jnp.bfloat16).reshape(
        lat_count * local_blocks, slot_span, weights.shape[2]
    )
    return lax.all_to_all(contrib, "latent", split_axis=0, concat_axis=0, tiled=True)


def slot_plan(pre_codes, block_ids, activations, target, decoder):
    lat_count = lax.axis_size("latent")
    tok_count = activations.shape[1]
    model_width = activations.shape[2]
    active_count = block_ids.shape[2]
    block_size = pre_codes.shape[3]
    lat_rows = decoder.shape[1]
    local_blocks = lat_rows // block_size
    all_blocks = local_blocks * lat_count
    capacity = 2 * tok_count * active_count // all_blocks
    slot_count = all_blocks * capacity
    pair_count = tok_count * active_count
    pair_block = block_ids[0].T.reshape(pair_count)
    member = (pair_block[:, None] == jnp.arange(all_blocks, dtype=jnp.int32)[None, :]).astype(
        jnp.int32
    )
    before = jnp.cumsum(member, axis=0) - member
    pair_rank = jnp.sum(before * member, axis=1)
    target_slot = pair_block * capacity + pair_rank
    slot_pair = (jnp.arange(slot_count, dtype=jnp.int32)[:, None] == target_slot[None, :]).astype(
        jnp.bfloat16
    )
    slot_token = jnp.sum(slot_pair.reshape(slot_count, active_count, tok_count), axis=1)
    pre_pairs = jnp.transpose(pre_codes[0], (1, 0, 2)).reshape(pair_count, block_size)
    pre_slots = jnp.dot(slot_pair, pre_pairs, preferred_element_type=jnp.float32).astype(
        jnp.bfloat16
    )
    pre_slots = pre_slots.reshape(all_blocks, capacity, block_size)
    inputs = activations[0]
    weights = decoder[0].reshape(local_blocks, block_size, model_width)
    input_slots = jnp.dot(slot_token, inputs, preferred_element_type=jnp.float32).astype(
        jnp.bfloat16
    )
    input_slots = input_slots.reshape(all_blocks, capacity, model_width)
    pieces = (
        lax.all_to_all(pre_slots, "latent", split_axis=0, concat_axis=0, tiled=True),
        lax.all_to_all(input_slots, "latent", split_axis=0, concat_axis=0, tiled=True),
    )
    returned = local_contrib(pieces[0], weights, lat_count, local_blocks)
    returned, received_pre, received_inputs = (returned, pieces[0], pieces[1])
    part_sum = jnp.einsum(
        "st,sd->td",
        slot_token,
        returned.reshape(slot_count, model_width),
        preferred_element_type=jnp.float32,
    )
    rebuilt = lax.psum(part_sum, "layer")
    errors = ((rebuilt - target.astype(jnp.float32)) / tok_count).astype(jnp.bfloat16)
    error_slots = jnp.dot(slot_token, errors, preferred_element_type=jnp.float32).astype(
        jnp.bfloat16
    )
    error_slots = error_slots.reshape(all_blocks, capacity, model_width)
    received_errors = lax.all_to_all(error_slots, "latent", split_axis=0, concat_axis=0, tiled=True)
    pre_blocks = received_pre.reshape(lat_count, local_blocks, capacity, block_size)
    code_blocks = jnp.maximum(pre_blocks, jnp.zeros((), pre_blocks.dtype))
    error_blocks = received_errors.reshape(lat_count, local_blocks, capacity, model_width)
    input_blocks = received_inputs.reshape(lat_count, local_blocks, capacity, model_width)
    code_grad = jnp.einsum(
        "sbcd,bld->sbcl", error_blocks, weights, preferred_element_type=jnp.float32
    )
    pre_grad = jnp.where(pre_blocks > 0, code_grad, jnp.zeros((), jnp.float32)).astype(jnp.bfloat16)
    dec_term = jnp.einsum(
        "sbcl,sbcd->bld", code_blocks, error_blocks, preferred_element_type=jnp.float32
    )
    enc_term = jnp.einsum(
        "sbcl,sbcd->bld", pre_grad, input_blocks, preferred_element_type=jnp.float32
    )
    dec_term = dec_term.reshape(lat_rows, model_width)
    enc_term = enc_term.reshape(lat_rows, model_width)
    dec_half, enc_half = (
        lax.psum_scatter(dec_term, "dp", scatter_dimension=1, tiled=True),
        lax.psum_scatter(enc_term, "dp", scatter_dimension=1, tiled=True),
    )
    return (dec_half.astype(jnp.bfloat16)[None], enc_half.astype(jnp.bfloat16)[None])


def flip(value, axis, bit):
    count = lax.axis_size(axis)
    return lax.ppermute(value, axis, [(i, i ^ bit) for i in range(count)])


def hop(value, axis, step, least):
    count = lax.axis_size(axis)
    if step > 0:
        pairs = [(i, i + 1) for i in range(least, count - 1)]
    else:
        pairs = [(i, i - 1) for i in range(1, count - least)]
    return lax.ppermute(value, axis, pairs)


def params():
    return pltpu.CompilerParams(vmem_limit_bytes=VMEM_BYTES)


def cost(rows, depth, columns):
    return pl.CostEstimate(
        flops=rows * depth * columns // 2,
        bytes_accessed=(rows * depth + depth * columns + rows * columns) // 2,
        transcendentals=0,
    )


def resident(shape):
    return pl.BlockSpec(shape, lambda i, s: (0,) * len(shape))


def gather_kernel(scalar_ref, source_ref, out_ref):
    out_ref[...] = source_ref[...].reshape(out_ref.shape)


def gather_columns(source, columns, width):
    rows = source.shape[-2]
    lead = (1,) * (source.ndim - 2)
    count = columns.shape[0]
    return pl.pallas_call(
        gather_kernel,
        out_shape=jax.ShapeDtypeStruct((rows, count * width), source.dtype),
        grid_spec=pltpu.PrefetchScalarGridSpec(
            num_scalar_prefetch=1,
            grid=(count,),
            in_specs=[pl.BlockSpec(lead + (rows, width), lambda i, s: (0,) * len(lead) + (0, s[i]))],
            out_specs=pl.BlockSpec((rows, width), lambda i, s: (0, i)),
        ),
        compiler_params=params(),
        cost_estimate=cost(rows, 1, count * width),
        name="gather_columns",
    )(columns.astype(jnp.int32), source)


def codes_kernel(groups, blocks, scalar_ref, message_ref, codes, id_map, pre):
    tok = message_ref.shape[2]
    pad = message_ref.shape[1] - 2 * tok
    first = scalar_ref[0].astype(jnp.float32)
    rows = [message_ref[g, 2 * tok:2 * tok + pad, :].astype(jnp.float32) for g in range(groups)]
    fill = tok - groups * pad
    if fill:
        rows.append(jnp.zeros((fill, tok), jnp.float32))
    table = jnp.concatenate(rows, axis=0).T - first
    for g in range(groups):
        pre[g] = jnp.maximum(message_ref[g, 0:2 * tok, :], jnp.zeros((), jnp.bfloat16))
        for j in range(2):
            at = g * pad + j
            wide = jnp.broadcast_to(table[:, at:at + 1], (tok, tok))
            id_map[g, j * tok:(j + 1) * tok, :] = wide.astype(jnp.bfloat16)

    def block_step(b, carry):
        block = b.astype(jnp.float32).astype(jnp.bfloat16)
        at = pl.multiple_of(b * tok, tok)
        for g in range(groups):
            value = jnp.where(id_map[g, tok:2 * tok, :] == block, pre[g, tok:2 * tok, :], jnp.zeros((), jnp.bfloat16))
            value = jnp.where(id_map[g, 0:tok, :] == block, pre[g, 0:tok, :], value)
            codes[g * tok:(g + 1) * tok, pl.ds(at, tok)] = value
        return carry

    lax.fori_loop(0, blocks, block_step, 0)


def spread_codes(message, first, lat_rows):
    groups, _, tok = message.shape
    rows = groups * tok
    return pl.pallas_call(
        functools.partial(codes_kernel, groups, lat_rows // tok),
        out_shape=jax.ShapeDtypeStruct((rows, lat_rows), jnp.bfloat16),
        grid_spec=pltpu.PrefetchScalarGridSpec(
            num_scalar_prefetch=1,
            grid=(1,),
            in_specs=[resident(message.shape)],
            out_specs=resident((rows, lat_rows)),
            scratch_shapes=[
                pltpu.VMEM((groups, 2 * tok, tok), jnp.bfloat16),
                pltpu.VMEM((groups, 2 * tok, tok), jnp.bfloat16),
            ],
        ),
        compiler_params=params(),
        cost_estimate=cost(rows, 1, lat_rows),
        name="spread_codes",
    )(first[None].astype(jnp.int32), message)


def layer_sum_kernel(got_a, kept_a, far_a, got_b, kept_b, far_b, own_ref, *sent_refs):
    half = far_a.shape[1]
    rows = own_ref.shape[0]
    for side, (got, kept, far) in enumerate(((got_a, kept_a, far_a), (got_b, kept_b, far_b))):
        lanes = slice(side * half, (side + 1) * half)
        for n in range(1 + len(sent_refs)):
            at = slice(n * rows, (n + 1) * rows)
            total = got[at, :half].astype(jnp.float32) + kept[at, :half].astype(jnp.float32)
            total = total + far[at, :].astype(jnp.float32)
            if n:
                sent_refs[n - 1][:, lanes] = total.astype(jnp.bfloat16)
            else:
                own_ref[:, lanes] = total


def layer_sum(terms_a, terms_b, blocks):
    rows, half = terms_a[2].shape
    cut = (rows // blocks, 2 * half)
    return pl.pallas_call(
        layer_sum_kernel,
        out_shape=[jax.ShapeDtypeStruct(cut, jnp.float32)] + [jax.ShapeDtypeStruct(cut, jnp.bfloat16)] * (blocks - 1),
        grid=(1,),
        in_specs=[pl.BlockSpec((rows, half), lambda i: (0, 0)) for _ in range(6)],
        out_specs=[pl.BlockSpec(cut, lambda i: (0, 0))] * blocks,
        compiler_params=params(),
        cost_estimate=cost(rows, 4, half),
        name="layer_sum",
    )(*terms_a, *terms_b)


def slots_kernel(groups, blocks, cap, scalar_ref, message_ref, hot_ref, pre_ref, code_ref):
    tok = message_ref.shape[2]
    pad = message_ref.shape[1] - 2 * tok
    f32, bf16 = jnp.float32, jnp.bfloat16
    first = scalar_ref[0].astype(f32)
    rows = [message_ref[g, 2 * tok:2 * tok + pad, :].astype(f32) for g in range(groups)]
    fill = tok - groups * pad
    table = jnp.concatenate(rows + ([jnp.zeros((fill, tok), f32)] if fill else []), axis=0).T
    earlier = lax.broadcasted_iota(jnp.int32, (tok, tok), 0) < lax.broadcasted_iota(jnp.int32, (tok, tok), 1)
    per = 2 * cap
    for z in range(groups // 2):
        pre = 0.0
        hot = []
        for core in range(2):
            g = 2 * z + core
            lanes = [rows[g][j:j + 1] for j in range(2)]
            down = [table[:, g * pad + j:g * pad + j + 1] for j in range(2)]
            same = [jnp.where((down[j] == lanes[j]) & earlier, 1.0, 0.0) for j in range(2)]
            cross = jnp.where(down[0] == lanes[1], 1.0, 0.0)
            rank = [jnp.sum(same[0], axis=0, keepdims=True), jnp.sum(same[1] + cross, axis=0, keepdims=True)]
            here = []
            for j in range(2):
                block = lanes[j] - first
                slot = block * per + (core * cap + rank[j])
                slot = jnp.where((block >= 0) & (block < blocks), slot, -1.0)
                number = lax.broadcasted_iota(jnp.int32, (blocks * per, tok), 0).astype(f32)
                here.append(jnp.where(number == slot, 1.0, 0.0).astype(bf16))
                pre = pre + jnp.dot(
                    here[j], message_ref[g, j * tok:(j + 1) * tok, :], preferred_element_type=f32
                )
            hot.append(here[0] + here[1])
        hot_ref[z] = jnp.concatenate(hot, axis=1)
        for b in range(blocks):
            pre_ref[b, z * per:(z + 1) * per, :] = pre[b * per:(b + 1) * per].astype(bf16)
    for b in range(blocks):
        code_ref[b] = jnp.maximum(pre_ref[b].astype(f32), 0.0).T.astype(bf16)


def make_slots(message, first, lat_rows, cap):
    groups, _, tok = message.shape
    blocks = lat_rows // tok
    per = 2 * cap
    shards = groups // 2
    shapes = [(shards, blocks * per, 2 * tok), (blocks, shards * per, tok), (blocks, tok, shards * per)]
    return pl.pallas_call(
        functools.partial(slots_kernel, groups, blocks, cap),
        out_shape=[jax.ShapeDtypeStruct(shape, jnp.bfloat16) for shape in shapes],
        grid_spec=pltpu.PrefetchScalarGridSpec(
            num_scalar_prefetch=1,
            grid=(1,),
            in_specs=[resident(message.shape)],
            out_specs=[resident(shape) for shape in shapes],
        ),
        compiler_params=params(),
        cost_estimate=cost(groups * tok, 2 * tok, tok),
        name="make_slots",
    )(first[None].astype(jnp.int32), message)


def into_slots(hot, rows, out, z):
    per = out.shape[1] // hot.shape[0]
    value = jnp.dot(hot[z], rows, preferred_element_type=jnp.float32).astype(jnp.bfloat16)
    for b in range(out.shape[0]):
        out[b, z * per:(z + 1) * per, :] = value[b * per:(b + 1) * per]


def lanes_of(refs, rows):
    parts = [r[rows, :] for r in refs]
    return parts[0] if len(parts) == 1 else jnp.concatenate(parts, axis=1)


def piece_grad_kernel(layout, scalar_ref, hot_ref, weight_ref, *refs):
    parts, (slots_ref, grad_ref) = refs[:-2], refs[-2:]
    blocks, _, size = grad_ref.shape
    group = hot_ref.shape[2]
    step = pl.program_id(0)

    @pl.when(step == 0)
    def _():
        grad_ref[...] = jnp.zeros_like(grad_ref)

    at = 0
    for i, piece in enumerate(layout):
        z = 0
        for lanes in piece:
            here = parts[at:at + lanes]
            at += lanes
            for n in range(here[0].shape[0] // group):

                @pl.when(step == i)
                def _(z=z, n=n, here=here):
                    into_slots(hot_ref, lanes_of(here, slice(n * group, (n + 1) * group)), slots_ref.at[0], z)

                z += 1
    for b in range(blocks):
        grad_ref[b] += lax.dot_general(
            slots_ref[0, b],
            weight_ref[0, b * size:(b + 1) * size, :],
            (((1,), (1,)), ((), ())),
            preferred_element_type=jnp.float32,
        )


def piece_grad(pieces, hot, decoder, columns, size):
    lat_rows = decoder.shape[1]
    blocks = lat_rows // size
    slots = hot.shape[0] * hot.shape[1] // blocks
    width = sum(p.shape[1] for p in pieces[0][0])
    flat = [p for piece in pieces for row in piece for p in row]
    return pl.pallas_call(
        functools.partial(piece_grad_kernel, [[len(row) for row in piece] for piece in pieces]),
        out_shape=[
            jax.ShapeDtypeStruct((len(pieces), blocks, slots, width), jnp.bfloat16),
            jax.ShapeDtypeStruct((blocks, slots, size), jnp.float32),
        ],
        grid_spec=pltpu.PrefetchScalarGridSpec(
            num_scalar_prefetch=1,
            grid=(len(pieces),),
            in_specs=[resident(hot.shape), pl.BlockSpec((1, lat_rows, width), lambda i, s: (0, 0, s[i]))]
            + [resident(p.shape) for p in flat],
            out_specs=[
                pl.BlockSpec((1, blocks, slots, width), lambda i, s: (i, 0, 0, 0)),
                resident((blocks, slots, size)),
            ],
        ),
        compiler_params=params(),
        cost_estimate=cost(lat_rows, 256, len(pieces) * width),
        name="piece_grad",
    )(columns.astype(jnp.int32), hot, decoder, *flat)


def decoder_kernel(skip, scalar_ref, code_ref, slots_ref, *refs):
    out_ref = refs[skip]
    size = code_ref.shape[1]
    for b in range(code_ref.shape[0]):
        out_ref[b * size:(b + 1) * size, :] = jnp.dot(
            code_ref[b], slots_ref[0, b], preferred_element_type=jnp.float32
        ).astype(jnp.bfloat16)


def decoder_part(slots, codes, columns, half, held):
    count, blocks, _, width = slots.shape
    lat_rows = blocks * codes.shape[1]
    onto = [] if held is None else [held]
    return pl.pallas_call(
        functools.partial(decoder_kernel, len(onto)),
        out_shape=jax.ShapeDtypeStruct((lat_rows, half), jnp.bfloat16),
        grid_spec=pltpu.PrefetchScalarGridSpec(
            num_scalar_prefetch=1,
            grid=(count,),
            in_specs=[resident(codes.shape), pl.BlockSpec((1,) + slots.shape[1:], lambda i, s: (i, 0, 0, 0))]
            + [pl.BlockSpec(memory_space=pl.ANY) for _ in onto],
            out_specs=pl.BlockSpec((lat_rows, width), lambda i, s: (0, s[i])),
        ),
        compiler_params=params(),
        input_output_aliases={3: 0} if onto else {},
        cost_estimate=cost(lat_rows, 256, count * width),
        name="decoder_part",
    )(columns.astype(jnp.int32), codes, slots, *onto)


def act_slots_kernel(hot_ref, *refs):
    out_ref = refs[-1]
    for z, act in enumerate(refs[:-1]):
        into_slots(hot_ref, act[...], out_ref, z)


def act_slots(acts, hot, blocks):
    group, half = acts[0].shape
    slots = hot.shape[0] * hot.shape[1] // blocks
    tile = half // 4
    return pl.pallas_call(
        act_slots_kernel,
        out_shape=jax.ShapeDtypeStruct((blocks, slots, half), jnp.bfloat16),
        grid=(4,),
        in_specs=[pl.BlockSpec(hot.shape, lambda i: (0, 0, 0))]
        + [pl.BlockSpec((group, tile), lambda i: (0, i)) for _ in acts],
        out_specs=pl.BlockSpec((blocks, slots, tile), lambda i: (0, 0, i)),
        compiler_params=params(),
        cost_estimate=cost(blocks * slots, group, half),
        name="act_slots",
    )(hot, *acts)


def encoder_kernel(cap, shared, pre_ref, own_ref, theirs_ref, act_ref, out_ref):
    size = pre_ref.shape[2]
    for n in range(shared):
        parts = []
        for at in range(0, own_ref.shape[1], 2 * cap):
            for core in range(2):
                here = slice(at + core * cap, at + (core + 1) * cap)
                there = slice(at + (1 - core) * cap, at + (2 - core) * cap)
                parts.append(own_ref[n, here, :] + theirs_ref[n, there, :])
        total = jnp.concatenate(parts, axis=0)
        grad = jnp.where(pre_ref[n].astype(jnp.float32) > 0, total, 0.0).T.astype(jnp.bfloat16)
        out_ref[n * size:(n + 1) * size, :] = jnp.dot(
            grad, act_ref[n], preferred_element_type=jnp.float32
        ).astype(jnp.bfloat16)


def encoder_part(pre, own, theirs, acts, cap):
    blocks, slots, size = pre.shape
    half = acts.shape[2]
    shared = 2 if blocks % 2 == 0 else 1
    block = pl.BlockSpec((shared, slots, size), lambda i: (i, 0, 0))
    return pl.pallas_call(
        functools.partial(encoder_kernel, cap, shared),
        out_shape=jax.ShapeDtypeStruct((blocks * size, half), jnp.bfloat16),
        grid=(blocks // shared,),
        in_specs=[block, block, block, pl.BlockSpec((shared, slots, half), lambda i: (i, 0, 0))],
        out_specs=pl.BlockSpec((shared * size, half), lambda i: (i, 0)),
        compiler_params=params(),
        cost_estimate=cost(blocks * size, 256, half),
        name="encoder_part",
    )(pre, own, theirs, acts)


def dense_plan(pre_codes, block_ids, activations, target, decoder):
    lay_count = lax.axis_size("layer")
    lat_count = lax.axis_size("latent")
    dp_count = lax.axis_size("dp")
    lay_here = lax.axis_index("layer")
    lat_here = lax.axis_index("latent")
    dp_here = lax.axis_index("dp")
    tok_count = activations.shape[1]
    model_width = activations.shape[2]
    active_count = block_ids.shape[2]
    block_size = pre_codes.shape[3]
    lat_rows = decoder.shape[1]
    local_blocks = lat_rows // block_size
    half = model_width // dp_count
    group = dp_count * tok_count
    tokens = lat_count * group
    width = half // lay_count
    side = width // 2
    f32, bf16 = jnp.float32, jnp.bfloat16
    first = lat_here * local_blocks
    capacity = 2 * tok_count * active_count // (local_blocks * lat_count)

    def columns(rows, which):
        return lax.dynamic_slice_in_dim(rows, which * half, half, axis=1)

    def places(names, offset, fine=1, sub=0):
        return [(offset + (lay_here ^ r)) * fine + sub for r in names]

    def weight_places(names):
        return jnp.stack(places(names, dp_here * lay_count))

    pre_rows = jnp.swapaxes(pre_codes[0], 0, 1).reshape(active_count * tok_count, block_size)
    id_rows = jnp.pad(block_ids[0].T, ((0, 16 - active_count), (0, 0))).astype(bf16)
    own = jnp.concatenate([pre_rows, id_rows], axis=0)
    message = jnp.stack([own] + [flip(own, "latent", r) for r in range(1, lat_count)])

    at = places((1, 3), dp_here * lay_count, 2, 0) + places((2, 3), dp_here * lay_count, 2, 1)
    send_weights = gather_columns(decoder, jnp.stack(at), side)

    acts = jnp.concatenate(
        [columns(activations[0], dp_here), flip(columns(activations[0], 1 - dp_here), "dp", 1)]
    )
    message, acts, send_weights = lax.optimization_barrier((message, acts, send_weights))
    up, down = [acts], [acts]

    def next_hops():
        step = len(up)
        up.append(hop(up[-1], "latent", 1, step - 1))
        down.append(hop(down[-1], "latent", -1, step - 1))

    message = jnp.stack([message, flip(message, "dp", 1)], axis=1)
    message = message.reshape(lat_count * dp_count, own.shape[0], block_size)
    next_hops()

    codes = spread_codes(message, first, lat_rows)
    at = places((0, 2), dp_here * lay_count, 2, 0) + places((0, 1), dp_here * lay_count, 2, 1)
    at, codes, target = lax.optimization_barrier((jnp.stack(at), codes, target))
    keep_weights = gather_columns(decoder, at, side)
    goals = gather_columns(target, jnp.stack([which * lay_count + lay_here for which in (dp_here, 1 - dp_here)]), width)
    goals = jnp.concatenate([goals[:, :width], flip(goals[:, width:], "dp", 1)])

    def rows_for(spread, weights, n):
        return jnp.dot(spread, weights[:, n * width:(n + 1) * width], preferred_element_type=f32).astype(bf16)

    got = flip(rows_for(codes, send_weights, 0), "layer", 1), flip(rows_for(codes, send_weights, 1), "layer", 2)
    keep_codes = codes
    if lat_count > 2:
        keep_codes, up[1], down[1] = lax.optimization_barrier((codes, up[1], down[1]))
        next_hops()
    kept = rows_for(keep_codes, keep_weights, 0), rows_for(keep_codes, keep_weights, 1)

    def add(one, two):
        return (one[:, side:].astype(f32) + two[:, side:].astype(f32)).astype(bf16)

    far = [flip(add(got[n], kept[n]), "layer", 2 - n) for n in range(2)]
    far, goals, up[-1], down[-1] = lax.optimization_barrier((far, goals, up[-1], down[-1]))

    total, *sent = layer_sum((got[0], kept[0], far[0]), (got[1], kept[1], far[1]), lat_count)
    for r in range(1, lat_count):
        total = total + flip(sent[r - 1], "latent", r).astype(f32)
    errors = ((total - goals.astype(f32)) / tok_count).astype(bf16)
    blocks_of = [errors] + [flip(errors, "latent", r) for r in range(1, lat_count)]
    near = jnp.concatenate(blocks_of[:lat_count // 2])
    one_near, two_near = flip(near, "layer", 1), flip(near, "layer", 2)
    one_near, two_near, far_blocks, up[-1], down[-1] = lax.optimization_barrier(
        (one_near, two_near, blocks_of[lat_count // 2:], up[-1], down[-1])
    )
    while len(up) < lat_count:
        next_hops()
    distant = jnp.concatenate(far_blocks)
    one_far, two_far = flip(distant, "layer", 1), flip(distant, "layer", 2)
    three_near = flip(two_near[:, :side], "layer", 1), flip(one_near[:, side:], "layer", 2)

    hot, pre_slots, code_slots = make_slots(message, first, lat_rows, capacity)

    def grads_of(here, names, dec):
        slots, grad = piece_grad(here, hot, decoder, weight_places(names), block_size)
        return grad, decoder_part(slots, code_slots, jnp.stack(places(names, 0)), half, dec)

    grad, dec = grads_of([[(near,), (distant,)]], (0,), None)
    one_far, two_far, three_near, grad, dec = lax.optimization_barrier((one_far, two_far, three_near, grad, dec))
    three_far = flip(two_far[:, :side], "layer", 1), flip(one_far[:, side:], "layer", 2)
    along = [acts] + [down[k] + up[lat_count - k] for k in range(1, lat_count)]
    along = jnp.stack(along)
    along = [
        lax.dynamic_index_in_dim(along, lax.rem((lat_here ^ r) - lat_here + lat_count, lat_count), 0, False)
        for r in range(lat_count)
    ]
    along = act_slots(along, hot, local_blocks)
    more, dec = grads_of([[(one_near,), (one_far,)], [(two_near,), (two_far,)]], (1, 2), dec)
    three_far, more, dec = lax.optimization_barrier((three_far, more, dec))
    last, dec = grads_of([[three_near, three_far]], (3,), dec)
    grad = grad + more + last
    enc = encoder_part(pre_slots, grad, flip(grad, "dp", 1), along, capacity)
    return dec[None], enc[None]


def per_device(pre_codes, block_ids, activations, target, decoder):
    lat_count = lax.axis_size("latent")
    lay_count = lax.axis_size("layer")
    dp_count = lax.axis_size("dp")
    tok_count = activations.shape[1]
    model_width = activations.shape[2]
    active_count = block_ids.shape[2]
    block_size = pre_codes.shape[3]
    all_blocks = decoder.shape[1] // block_size * lat_count
    slots = 2 * tok_count * active_count // lat_count
    dense = (
        slots >= tok_count
        and dp_count == 2
        and active_count == 2
        and lay_count == 4
        and lat_count > 1
        and lat_count & (lat_count - 1) == 0
        and tok_count == block_size
        and lat_count * dp_count * 16 <= tok_count
        and model_width % (dp_count * 2 * lay_count * 128) == 0
        and all_blocks <= 256
        and 2 * tok_count * active_count == 8 * all_blocks
    )
    plan = dense_plan if dense else slot_plan
    return plan(pre_codes, block_ids, activations, target, decoder)


def solution(mesh):
    placed = (
        P("layer", ("latent", "dp"), None, None),
        P("layer", ("latent", "dp"), None),
        P("layer", ("latent", "dp"), None),
        P(("latent", "dp"), None),
        P("layer", "latent", None),
    )
    return jax.shard_map(
        per_device,
        mesh=mesh,
        in_specs=placed,
        out_specs=(P("layer", "latent", "dp"), P("layer", "latent", "dp")),
        check_vma=False,
    )
```

```python
import functools

import jax
import jax.numpy as jnp
from jax import lax
from jax.experimental import pallas as pl
from jax.experimental.pallas import tpu as pltpu
from jax.sharding import PartitionSpec as P

VMEM_BYTES = 40 * 1024 * 1024


def local_contrib(received_pre, weights, lat_count, local_blocks):
    code_vals = jnp.maximum(received_pre, jnp.zeros((), received_pre.dtype))
    slot_span = received_pre.shape[1]
    block_size = received_pre.shape[2]
    grouped = code_vals.reshape(lat_count, local_blocks, slot_span, block_size)
    contrib = jnp.einsum("sbcl,bld->sbcd", grouped, weights, preferred_element_type=jnp.float32)
    contrib = contrib.astype(jnp.bfloat16).reshape(
        lat_count * local_blocks, slot_span, weights.shape[2]
    )
    return lax.all_to_all(contrib, "latent", split_axis=0, concat_axis=0, tiled=True)


def slot_plan(pre_codes, block_ids, activations, target, decoder):
    lat_count = lax.axis_size("latent")
    tok_count = activations.shape[1]
    model_width = activations.shape[2]
    active_count = block_ids.shape[2]
    block_size = pre_codes.shape[3]
    lat_rows = decoder.shape[1]
    local_blocks = lat_rows // block_size
    all_blocks = local_blocks * lat_count
    capacity = 2 * tok_count * active_count // all_blocks
    slot_count = all_blocks * capacity
    pair_count = tok_count * active_count
    pair_block = block_ids[0].T.reshape(pair_count)
    member = (pair_block[:, None] == jnp.arange(all_blocks, dtype=jnp.int32)[None, :]).astype(
        jnp.int32
    )
    before = jnp.cumsum(member, axis=0) - member
    pair_rank = jnp.sum(before * member, axis=1)
    target_slot = pair_block * capacity + pair_rank
    slot_pair = (jnp.arange(slot_count, dtype=jnp.int32)[:, None] == target_slot[None, :]).astype(
        jnp.bfloat16
    )
    slot_token = jnp.sum(slot_pair.reshape(slot_count, active_count, tok_count), axis=1)
    pre_pairs = jnp.transpose(pre_codes[0], (1, 0, 2)).reshape(pair_count, block_size)
    pre_slots = jnp.dot(slot_pair, pre_pairs, preferred_element_type=jnp.float32).astype(
        jnp.bfloat16
    )
    pre_slots = pre_slots.reshape(all_blocks, capacity, block_size)
    inputs = activations[0]
    weights = decoder[0].reshape(local_blocks, block_size, model_width)
    input_slots = jnp.dot(slot_token, inputs, preferred_element_type=jnp.float32).astype(
        jnp.bfloat16
    )
    input_slots = input_slots.reshape(all_blocks, capacity, model_width)
    pieces = (
        lax.all_to_all(pre_slots, "latent", split_axis=0, concat_axis=0, tiled=True),
        lax.all_to_all(input_slots, "latent", split_axis=0, concat_axis=0, tiled=True),
    )
    returned = local_contrib(pieces[0], weights, lat_count, local_blocks)
    returned, received_pre, received_inputs = (returned, pieces[0], pieces[1])
    part_sum = jnp.einsum(
        "st,sd->td",
        slot_token,
        returned.reshape(slot_count, model_width),
        preferred_element_type=jnp.float32,
    )
    rebuilt = lax.psum(part_sum, "layer")
    errors = ((rebuilt - target.astype(jnp.float32)) / tok_count).astype(jnp.bfloat16)
    error_slots = jnp.dot(slot_token, errors, preferred_element_type=jnp.float32).astype(
        jnp.bfloat16
    )
    error_slots = error_slots.reshape(all_blocks, capacity, model_width)
    received_errors = lax.all_to_all(error_slots, "latent", split_axis=0, concat_axis=0, tiled=True)
    pre_blocks = received_pre.reshape(lat_count, local_blocks, capacity, block_size)
    code_blocks = jnp.maximum(pre_blocks, jnp.zeros((), pre_blocks.dtype))
    error_blocks = received_errors.reshape(lat_count, local_blocks, capacity, model_width)
    input_blocks = received_inputs.reshape(lat_count, local_blocks, capacity, model_width)
    code_grad = jnp.einsum(
        "sbcd,bld->sbcl", error_blocks, weights, preferred_element_type=jnp.float32
    )
    pre_grad = jnp.where(pre_blocks > 0, code_grad, jnp.zeros((), jnp.float32)).astype(jnp.bfloat16)
    dec_term = jnp.einsum(
        "sbcl,sbcd->bld", code_blocks, error_blocks, preferred_element_type=jnp.float32
    )
    enc_term = jnp.einsum(
        "sbcl,sbcd->bld", pre_grad, input_blocks, preferred_element_type=jnp.float32
    )
    dec_term = dec_term.reshape(lat_rows, model_width)
    enc_term = enc_term.reshape(lat_rows, model_width)
    dec_half, enc_half = (
        lax.psum_scatter(dec_term, "dp", scatter_dimension=1, tiled=True),
        lax.psum_scatter(enc_term, "dp", scatter_dimension=1, tiled=True),
    )
    return (dec_half.astype(jnp.bfloat16)[None], enc_half.astype(jnp.bfloat16)[None])


def flip(value, axis, bit):
    count = lax.axis_size(axis)
    return lax.ppermute(value, axis, [(i, i ^ bit) for i in range(count)])


def hop(value, axis, step, least):
    count = lax.axis_size(axis)
    if step > 0:
        pairs = [(i, i + 1) for i in range(least, count - 1)]
    else:
        pairs = [(i, i - 1) for i in range(1, count - least)]
    return lax.ppermute(value, axis, pairs)


def params():
    return pltpu.CompilerParams(vmem_limit_bytes=VMEM_BYTES)


def cost(rows, depth, columns):
    return pl.CostEstimate(
        flops=rows * depth * columns // 2,
        bytes_accessed=(rows * depth + depth * columns + rows * columns) // 2,
        transcendentals=0,
    )


def resident(shape):
    return pl.BlockSpec(shape, lambda i, s: (0,) * len(shape))


def gather_kernel(scalar_ref, source_ref, out_ref):
    out_ref[...] = source_ref[...].reshape(out_ref.shape)


def gather_columns(source, columns, width):
    rows = source.shape[-2]
    lead = (1,) * (source.ndim - 2)
    count = columns.shape[0]
    return pl.pallas_call(
        gather_kernel,
        out_shape=jax.ShapeDtypeStruct((rows, count * width), source.dtype),
        grid_spec=pltpu.PrefetchScalarGridSpec(
            num_scalar_prefetch=1,
            grid=(count,),
            in_specs=[pl.BlockSpec(lead + (rows, width), lambda i, s: (0,) * len(lead) + (0, s[i]))],
            out_specs=pl.BlockSpec((rows, width), lambda i, s: (0, i)),
        ),
        compiler_params=params(),
        cost_estimate=cost(rows, 1, count * width),
        name="gather_columns",
    )(columns.astype(jnp.int32), source)


def codes_kernel(groups, blocks, scalar_ref, message_ref, codes, id_map, pre):
    tok = message_ref.shape[2]
    pad = message_ref.shape[1] - 2 * tok
    first = scalar_ref[0].astype(jnp.float32)
    rows = [message_ref[g, 2 * tok:2 * tok + pad, :].astype(jnp.float32) for g in range(groups)]
    fill = tok - groups * pad
    if fill:
        rows.append(jnp.zeros((fill, tok), jnp.float32))
    table = jnp.concatenate(rows, axis=0).T - first
    for g in range(groups):
        pre[g] = jnp.maximum(message_ref[g, 0:2 * tok, :], jnp.zeros((), jnp.bfloat16))
        for j in range(2):
            at = g * pad + j
            wide = jnp.broadcast_to(table[:, at:at + 1], (tok, tok))
            id_map[g, j * tok:(j + 1) * tok, :] = wide.astype(jnp.bfloat16)

    def block_step(b, carry):
        block = b.astype(jnp.float32).astype(jnp.bfloat16)
        at = pl.multiple_of(b * tok, tok)
        for g in range(groups):
            value = jnp.where(id_map[g, tok:2 * tok, :] == block, pre[g, tok:2 * tok, :], jnp.zeros((), jnp.bfloat16))
            value = jnp.where(id_map[g, 0:tok, :] == block, pre[g, 0:tok, :], value)
            codes[g * tok:(g + 1) * tok, pl.ds(at, tok)] = value
        return carry

    lax.fori_loop(0, blocks, block_step, 0)


def spread_codes(message, first, lat_rows):
    groups, _, tok = message.shape
    rows = groups * tok
    return pl.pallas_call(
        functools.partial(codes_kernel, groups, lat_rows // tok),
        out_shape=jax.ShapeDtypeStruct((rows, lat_rows), jnp.bfloat16),
        grid_spec=pltpu.PrefetchScalarGridSpec(
            num_scalar_prefetch=1,
            grid=(1,),
            in_specs=[resident(message.shape)],
            out_specs=resident((rows, lat_rows)),
            scratch_shapes=[
                pltpu.VMEM((groups, 2 * tok, tok), jnp.bfloat16),
                pltpu.VMEM((groups, 2 * tok, tok), jnp.bfloat16),
            ],
        ),
        compiler_params=params(),
        cost_estimate=cost(rows, 1, lat_rows),
        name="spread_codes",
    )(first[None].astype(jnp.int32), message)


def layer_sum_kernel(got_a, kept_a, far_a, got_b, kept_b, far_b, own_ref, *sent_refs):
    half = far_a.shape[1]
    rows = own_ref.shape[0]
    for side, (got, kept, far) in enumerate(((got_a, kept_a, far_a), (got_b, kept_b, far_b))):
        lanes = slice(side * half, (side + 1) * half)
        for n in range(1 + len(sent_refs)):
            at = slice(n * rows, (n + 1) * rows)
            total = got[at, :half].astype(jnp.float32) + kept[at, :half].astype(jnp.float32)
            total = total + far[at, :].astype(jnp.float32)
            if n:
                sent_refs[n - 1][:, lanes] = total.astype(jnp.bfloat16)
            else:
                own_ref[:, lanes] = total


def layer_sum(terms_a, terms_b, blocks):
    rows, half = terms_a[2].shape
    cut = (rows // blocks, 2 * half)
    return pl.pallas_call(
        layer_sum_kernel,
        out_shape=[jax.ShapeDtypeStruct(cut, jnp.float32)] + [jax.ShapeDtypeStruct(cut, jnp.bfloat16)] * (blocks - 1),
        grid=(1,),
        in_specs=[pl.BlockSpec((rows, half), lambda i: (0, 0)) for _ in range(6)],
        out_specs=[pl.BlockSpec(cut, lambda i: (0, 0))] * blocks,
        compiler_params=params(),
        cost_estimate=cost(rows, 4, half),
        name="layer_sum",
    )(*terms_a, *terms_b)


def slots_kernel(groups, blocks, cap, scalar_ref, message_ref, hot_ref, pre_ref, code_ref):
    tok = message_ref.shape[2]
    pad = message_ref.shape[1] - 2 * tok
    f32, bf16 = jnp.float32, jnp.bfloat16
    first = scalar_ref[0].astype(f32)
    rows = [message_ref[g, 2 * tok:2 * tok + pad, :].astype(f32) for g in range(groups)]
    fill = tok - groups * pad
    table = jnp.concatenate(rows + ([jnp.zeros((fill, tok), f32)] if fill else []), axis=0).T
    earlier = lax.broadcasted_iota(jnp.int32, (tok, tok), 0) < lax.broadcasted_iota(jnp.int32, (tok, tok), 1)
    per = 2 * cap
    for z in range(groups // 2):
        pre = 0.0
        hot = []
        for core in range(2):
            g = 2 * z + core
            lanes = [rows[g][j:j + 1] for j in range(2)]
            down = [table[:, g * pad + j:g * pad + j + 1] for j in range(2)]
            same = [jnp.where((down[j] == lanes[j]) & earlier, 1.0, 0.0) for j in range(2)]
            cross = jnp.where(down[0] == lanes[1], 1.0, 0.0)
            rank = [jnp.sum(same[0], axis=0, keepdims=True), jnp.sum(same[1] + cross, axis=0, keepdims=True)]
            here = []
            for j in range(2):
                block = lanes[j] - first
                slot = block * per + (core * cap + rank[j])
                slot = jnp.where((block >= 0) & (block < blocks), slot, -1.0)
                number = lax.broadcasted_iota(jnp.int32, (blocks * per, tok), 0).astype(f32)
                here.append(jnp.where(number == slot, 1.0, 0.0).astype(bf16))
                pre = pre + jnp.dot(
                    here[j], message_ref[g, j * tok:(j + 1) * tok, :], preferred_element_type=f32
                )
            hot.append(here[0] + here[1])
        hot_ref[z] = jnp.concatenate(hot, axis=1)
        for b in range(blocks):
            pre_ref[b, z * per:(z + 1) * per, :] = pre[b * per:(b + 1) * per].astype(bf16)
    for b in range(blocks):
        code_ref[b] = jnp.maximum(pre_ref[b].astype(f32), 0.0).T.astype(bf16)


def make_slots(message, first, lat_rows, cap):
    groups, _, tok = message.shape
    blocks = lat_rows // tok
    per = 2 * cap
    shards = groups // 2
    shapes = [(shards, blocks * per, 2 * tok), (blocks, shards * per, tok), (blocks, tok, shards * per)]
    return pl.pallas_call(
        functools.partial(slots_kernel, groups, blocks, cap),
        out_shape=[jax.ShapeDtypeStruct(shape, jnp.bfloat16) for shape in shapes],
        grid_spec=pltpu.PrefetchScalarGridSpec(
            num_scalar_prefetch=1,
            grid=(1,),
            in_specs=[resident(message.shape)],
            out_specs=[resident(shape) for shape in shapes],
        ),
        compiler_params=params(),
        cost_estimate=cost(groups * tok, 2 * tok, tok),
        name="make_slots",
    )(first[None].astype(jnp.int32), message)


def into_slots(hot, rows, out, z):
    per = out.shape[1] // hot.shape[0]
    value = jnp.dot(hot[z], rows, preferred_element_type=jnp.float32).astype(jnp.bfloat16)
    for b in range(out.shape[0]):
        out[b, z * per:(z + 1) * per, :] = value[b * per:(b + 1) * per]


def lanes_of(refs, rows):
    parts = [r[rows, :] for r in refs]
    return parts[0] if len(parts) == 1 else jnp.concatenate(parts, axis=1)


def piece_grad_kernel(layout, scalar_ref, hot_ref, weight_ref, *refs):
    parts, (slots_ref, grad_ref) = refs[:-2], refs[-2:]
    blocks, _, size = grad_ref.shape
    group = hot_ref.shape[2]
    step = pl.program_id(0)

    @pl.when(step == 0)
    def _():
        grad_ref[...] = jnp.zeros_like(grad_ref)

    at = 0
    for i, piece in enumerate(layout):
        z = 0
        for lanes in piece:
            here = parts[at:at + lanes]
            at += lanes
            for n in range(here[0].shape[0] // group):

                @pl.when(step == i)
                def _(z=z, n=n, here=here):
                    into_slots(hot_ref, lanes_of(here, slice(n * group, (n + 1) * group)), slots_ref.at[0], z)

                z += 1
    for b in range(blocks):
        grad_ref[b] += lax.dot_general(
            slots_ref[0, b],
            weight_ref[0, b * size:(b + 1) * size, :],
            (((1,), (1,)), ((), ())),
            preferred_element_type=jnp.float32,
        )


def piece_grad(pieces, hot, decoder, columns, size):
    lat_rows = decoder.shape[1]
    blocks = lat_rows // size
    slots = hot.shape[0] * hot.shape[1] // blocks
    width = sum(p.shape[1] for p in pieces[0][0])
    flat = [p for piece in pieces for row in piece for p in row]
    return pl.pallas_call(
        functools.partial(piece_grad_kernel, [[len(row) for row in piece] for piece in pieces]),
        out_shape=[
            jax.ShapeDtypeStruct((len(pieces), blocks, slots, width), jnp.bfloat16),
            jax.ShapeDtypeStruct((blocks, slots, size), jnp.float32),
        ],
        grid_spec=pltpu.PrefetchScalarGridSpec(
            num_scalar_prefetch=1,
            grid=(len(pieces),),
            in_specs=[resident(hot.shape), pl.BlockSpec((1, lat_rows, width), lambda i, s: (0, 0, s[i]))]
            + [resident(p.shape) for p in flat],
            out_specs=[
                pl.BlockSpec((1, blocks, slots, width), lambda i, s: (i, 0, 0, 0)),
                resident((blocks, slots, size)),
            ],
        ),
        compiler_params=params(),
        cost_estimate=cost(lat_rows, 256, len(pieces) * width),
        name="piece_grad",
    )(columns.astype(jnp.int32), hot, decoder, *flat)


def decoder_kernel(skip, scalar_ref, code_ref, slots_ref, *refs):
    out_ref = refs[skip]
    size = code_ref.shape[1]
    for b in range(code_ref.shape[0]):
        out_ref[b * size:(b + 1) * size, :] = jnp.dot(
            code_ref[b], slots_ref[0, b], preferred_element_type=jnp.float32
        ).astype(jnp.bfloat16)


def decoder_part(slots, codes, columns, half, held):
    count, blocks, _, width = slots.shape
    lat_rows = blocks * codes.shape[1]
    onto = [] if held is None else [held]
    return pl.pallas_call(
        functools.partial(decoder_kernel, len(onto)),
        out_shape=jax.ShapeDtypeStruct((lat_rows, half), jnp.bfloat16),
        grid_spec=pltpu.PrefetchScalarGridSpec(
            num_scalar_prefetch=1,
            grid=(count,),
            in_specs=[resident(codes.shape), pl.BlockSpec((1,) + slots.shape[1:], lambda i, s: (i, 0, 0, 0))]
            + [pl.BlockSpec(memory_space=pl.ANY) for _ in onto],
            out_specs=pl.BlockSpec((lat_rows, width), lambda i, s: (0, s[i])),
        ),
        compiler_params=params(),
        input_output_aliases={3: 0} if onto else {},
        cost_estimate=cost(lat_rows, 256, count * width),
        name="decoder_part",
    )(columns.astype(jnp.int32), codes, slots, *onto)


def act_slots_kernel(counts, skip, scalar_ref, hot_ref, *refs):
    refs = refs[skip:]
    out_ref = refs[-1]
    per = out_ref.shape[2]
    at = 0
    for i, layout in enumerate(counts):
        mine = refs[at:at + sum(layout)]
        at += sum(layout)

        @pl.when(pl.program_id(1) == i)
        def _(i=i, layout=layout, mine=mine):
            rows = []
            n = 0
            for count in layout:
                part = mine[n][...]
                for more in mine[n + 1:n + count]:
                    part = part + more[...]
                rows.append(part)
                n += count
            rows = rows[0] if len(rows) == 1 else jnp.concatenate(rows, axis=0)
            value = jnp.dot(hot_ref[scalar_ref[i]], rows, preferred_element_type=jnp.float32).astype(jnp.bfloat16)
            for b in range(out_ref.shape[1]):
                out_ref[0, b] = value[b * per:(b + 1) * per]


def act_slots(blocks_of, places, hot, count, held):
    group, half = hot.shape[2], blocks_of[0][0][0].shape[1]
    shards, per = hot.shape[0], hot.shape[1] // count
    tile = half // 4
    onto = [] if held is None else [held]
    flat = [part for parts in blocks_of for row in parts for part in row]
    out = pl.BlockSpec((1, count, per, tile), lambda i, j, s: (s[j], 0, 0, i))
    return pl.pallas_call(
        functools.partial(act_slots_kernel, [[len(row) for row in parts] for parts in blocks_of], len(onto)),
        out_shape=jax.ShapeDtypeStruct((shards, count, per, half), jnp.bfloat16),
        grid_spec=pltpu.PrefetchScalarGridSpec(
            num_scalar_prefetch=1,
            grid=(4, len(blocks_of)),
            in_specs=[pl.BlockSpec(hot.shape, lambda i, j, s: (0, 0, 0))]
            + [pl.BlockSpec(memory_space=pl.ANY) for _ in onto]
            + [pl.BlockSpec((part.shape[0], tile), lambda i, j, s: (0, i)) for part in flat],
            out_specs=out,
        ),
        compiler_params=params(),
        cost_estimate=cost(count * per, group, half),
        name="act_slots",
        input_output_aliases={2: 0} if onto else {},
    )(jnp.stack(places).astype(jnp.int32), hot, *onto, *flat)


def encoder_kernel(cap, shared, pre_ref, own_ref, theirs_ref, act_ref, out_ref):
    size = pre_ref.shape[2]
    for n in range(shared):
        parts = []
        for at in range(0, own_ref.shape[1], 2 * cap):
            for core in range(2):
                here = slice(at + core * cap, at + (core + 1) * cap)
                there = slice(at + (1 - core) * cap, at + (2 - core) * cap)
                parts.append(own_ref[n, here, :] + theirs_ref[n, there, :])
        total = jnp.concatenate(parts, axis=0)
        grad = jnp.where(pre_ref[n].astype(jnp.float32) > 0, total, 0.0).T.astype(jnp.bfloat16)
        act = jnp.concatenate([act_ref[z, n] for z in range(act_ref.shape[0])], axis=0)
        out_ref[n * size:(n + 1) * size, :] = jnp.dot(
            grad, act, preferred_element_type=jnp.float32
        ).astype(jnp.bfloat16)


def encoder_part(pre, own, theirs, acts, cap):
    blocks, slots, size = pre.shape
    half = acts.shape[3]
    shared = 2 if blocks % 2 == 0 else 1
    block = pl.BlockSpec((shared, slots, size), lambda i: (i, 0, 0))
    return pl.pallas_call(
        functools.partial(encoder_kernel, cap, shared),
        out_shape=jax.ShapeDtypeStruct((blocks * size, half), jnp.bfloat16),
        grid=(blocks // shared,),
        in_specs=[block, block, block, pl.BlockSpec((acts.shape[0], shared) + acts.shape[2:], lambda i: (0, i, 0, 0))],
        out_specs=pl.BlockSpec((shared * size, half), lambda i: (i, 0)),
        compiler_params=params(),
        cost_estimate=cost(blocks * size, 256, half),
        name="encoder_part",
    )(pre, own, theirs, acts)


def dense_plan(pre_codes, block_ids, activations, target, decoder):
    lay_count = lax.axis_size("layer")
    lat_count = lax.axis_size("latent")
    dp_count = lax.axis_size("dp")
    lay_here = lax.axis_index("layer")
    lat_here = lax.axis_index("latent")
    dp_here = lax.axis_index("dp")
    tok_count = activations.shape[1]
    model_width = activations.shape[2]
    active_count = block_ids.shape[2]
    block_size = pre_codes.shape[3]
    lat_rows = decoder.shape[1]
    local_blocks = lat_rows // block_size
    half = model_width // dp_count
    group = dp_count * tok_count
    tokens = lat_count * group
    width = half // lay_count
    side = width // 2
    f32, bf16 = jnp.float32, jnp.bfloat16
    first = lat_here * local_blocks
    capacity = 2 * tok_count * active_count // (local_blocks * lat_count)

    def columns(rows, which):
        return lax.dynamic_slice_in_dim(rows, which * half, half, axis=1)

    def places(names, offset, fine=1, sub=0):
        return [(offset + (lay_here ^ r)) * fine + sub for r in names]

    def weight_places(names):
        return jnp.stack(places(names, dp_here * lay_count))

    pre_rows = jnp.swapaxes(pre_codes[0], 0, 1).reshape(active_count * tok_count, block_size)
    id_rows = jnp.pad(block_ids[0].T, ((0, 16 - active_count), (0, 0))).astype(bf16)
    own = jnp.concatenate([pre_rows, id_rows], axis=0)
    message = jnp.stack([own] + [flip(own, "latent", r) for r in range(1, lat_count)])

    at = places((1, 3), dp_here * lay_count, 2, 0) + places((2, 3), dp_here * lay_count, 2, 1)
    send_weights = gather_columns(decoder, jnp.stack(at), side)

    own, inputs = lax.optimization_barrier((own, activations[0]))
    acts = jnp.concatenate([columns(inputs, dp_here), flip(columns(inputs, 1 - dp_here), "dp", 1)])
    corner = send_weights[:16, :128]
    message, corner, acts = lax.optimization_barrier((message, corner, acts))
    up, down = [acts], [acts]

    def next_hops():
        step = len(up)
        up.append(hop(up[-1], "latent", 1, step - 1))
        down.append(hop(down[-1], "latent", -1, step - 1))

    message = jnp.stack([message, flip(message, "dp", 1)], axis=1)
    message = message.reshape(lat_count * dp_count, own.shape[0], block_size)
    next_hops()

    codes = spread_codes(message, first, lat_rows)
    at = places((0, 2), dp_here * lay_count, 2, 0) + places((0, 1), dp_here * lay_count, 2, 1)
    at, codes, target = lax.optimization_barrier((jnp.stack(at), codes, target))
    keep_weights = gather_columns(decoder, at, side)
    goals = gather_columns(target, jnp.stack([which * lay_count + lay_here for which in (dp_here, 1 - dp_here)]), width)
    goals = jnp.concatenate([goals[:, :width], flip(goals[:, width:], "dp", 1)])

    codes = spread_codes(message, first, lat_rows)
    at = places((0, 2), dp_here * lay_count, 2, 0) + places((0, 1), dp_here * lay_count, 2, 1)
    at, codes, target = lax.optimization_barrier((jnp.stack(at), codes, target))
    keep_weights = gather_columns(decoder, at, side)
    goals = gather_columns(target, jnp.stack([which * lay_count + lay_here for which in (dp_here, 1 - dp_here)]), width)
    goals = jnp.concatenate([goals[:, :width], flip(goals[:, width:], "dp", 1)])

    def rows_for(spread, weights, n):
        return jnp.dot(spread, weights[:, n * width:(n + 1) * width], preferred_element_type=f32).astype(bf16)

    got = flip(rows_for(codes, send_weights, 0), "layer", 1), flip(rows_for(codes, send_weights, 1), "layer", 2)
    keep_codes, up[1], down[1] = lax.optimization_barrier((codes, up[1], down[1]))
    early = group * 11 // 16
    ups, downs = ([up[1][:early], up[1][early:]], [down[1][:early], down[1][early:]])
    ups, downs = [[part] for part in ups], [[part] for part in downs]

    def next_hop(part):
        step = len(ups[part])
        ups[part].append(hop(ups[part][-1], "latent", 1, step))
        downs[part].append(hop(downs[part][-1], "latent", -1, step))

    if lat_count > 2:
        next_hop(0)
    kept = rows_for(keep_codes, keep_weights, 0), rows_for(keep_codes, keep_weights, 1)

    def add(one, two):
        return (one[:, side:].astype(f32) + two[:, side:].astype(f32)).astype(bf16)

    far = [flip(add(got[n], kept[n]), "layer", 2 - n) for n in range(2)]
    far, goals, ups[0][-1], downs[0][-1] = lax.optimization_barrier((far, goals, ups[0][-1], downs[0][-1]))

    total, *sent = layer_sum((got[0], kept[0], far[0]), (got[1], kept[1], far[1]), lat_count)
    for r in range(1, lat_count):
        total = total + flip(sent[r - 1], "latent", r).astype(f32)
    errors = ((total - goals.astype(f32)) / tok_count).astype(bf16)
    others = [flip(errors, "latent", r) for r in range(1, lat_count)]
    one_near, two_near = flip(errors, "layer", 1), flip(errors, "layer", 2)
    one_near, two_near, others, ups, downs = lax.optimization_barrier((one_near, two_near, others, ups, downs))
    distant = jnp.concatenate(others)
    one_far, two_far = flip(distant, "layer", 1), flip(distant, "layer", 2)
    three_near = flip(two_near[:, :side], "layer", 1), flip(one_near[:, side:], "layer", 2)
    while len(ups[0]) < lat_count - 1:
        next_hop(0)
    while len(ups[1]) < lat_count - 2:
        next_hop(1)

    hot, pre_slots, code_slots = make_slots(message, first, lat_rows, capacity)

    def grads_of(here, names, dec):
        slots, grad = piece_grad(here, hot, decoder, weight_places(names), block_size)
        return grad, decoder_part(slots, code_slots, jnp.stack(places(names, 0)), half, dec)

    grad, dec = grads_of([[(errors,), (distant,)]], (0,), None)
    one_far, two_far, three_near, grad, dec, ups, downs = lax.optimization_barrier(
        (one_far, two_far, three_near, grad, dec, ups, downs)
    )
    while len(ups[1]) < lat_count - 1:
        next_hop(1)
    three_far = flip(two_far[:, :side], "layer", 1), flip(one_far[:, side:], "layer", 2)
    more, dec = grads_of([[(one_near,), (one_far,)], [(two_near,), (two_far,)]], (1, 2), dec)
    three_far, more, dec = lax.optimization_barrier((three_far, more, dec))
    last, dec = grads_of([[three_near, three_far]], (3,), dec)
    grad = grad + more + last

    shards = [lax.rem(lat_here + k, lat_count) ^ lat_here for k in range(lat_count)]
    along = [[(acts,)]] + [
        [(downs[n][k - 1], ups[n][lat_count - k - 1]) for n in range(2)] for k in range(1, lat_count)
    ]
    middle = [k for k in range(lat_count) if k == 0 or 2 * k == lat_count]
    others = [k for k in range(lat_count) if k not in middle]
    slotted = None
    for names in (middle, others):
        if names:
            here = [along[k] for k in names]
            slotted = act_slots(here, [shards[k] for k in names], hot, local_blocks, slotted)
    enc = encoder_part(pre_slots, grad, flip(grad, "dp", 1), slotted, capacity)
    return dec[None], enc[None]


def per_device(pre_codes, block_ids, activations, target, decoder):
    lat_count = lax.axis_size("latent")
    lay_count = lax.axis_size("layer")
    dp_count = lax.axis_size("dp")
    tok_count = activations.shape[1]
    model_width = activations.shape[2]
    active_count = block_ids.shape[2]
    block_size = pre_codes.shape[3]
    all_blocks = decoder.shape[1] // block_size * lat_count
    slots = 2 * tok_count * active_count // lat_count
    dense = (
        slots >= tok_count
        and dp_count == 2
        and active_count == 2
        and lay_count == 4
        and lat_count > 1
        and lat_count & (lat_count - 1) == 0
        and tok_count == block_size
        and lat_count * dp_count * 16 <= tok_count
        and model_width % (dp_count * 2 * lay_count * 128) == 0
        and all_blocks <= 256
        and 2 * tok_count * active_count == 8 * all_blocks
    )
    plan = dense_plan if dense else slot_plan
    return plan(pre_codes, block_ids, activations, target, decoder)


def solution(mesh):
    placed = (
        P("layer", ("latent", "dp"), None, None),
        P("layer", ("latent", "dp"), None),
        P("layer", ("latent", "dp"), None),
        P(("latent", "dp"), None),
        P("layer", "latent", None),
    )
    return jax.shard_map(
        per_device,
        mesh=mesh,
        in_specs=placed,
        out_specs=(P("layer", "latent", "dp"), P("layer", "latent", "dp")),
        check_vma=False,
    )
```

```python
import functools

import jax
import jax.numpy as jnp
from jax import lax
from jax.experimental import pallas as pl
from jax.experimental.pallas import tpu as pltpu
from jax.sharding import PartitionSpec as P

VMEM_BYTES = 40 * 1024 * 1024


def local_contrib(received_pre, weights, lat_count, local_blocks):
    code_vals = jnp.maximum(received_pre, jnp.zeros((), received_pre.dtype))
    slot_span = received_pre.shape[1]
    block_size = received_pre.shape[2]
    grouped = code_vals.reshape(lat_count, local_blocks, slot_span, block_size)
    contrib = jnp.einsum("sbcl,bld->sbcd", grouped, weights, preferred_element_type=jnp.float32)
    contrib = contrib.astype(jnp.bfloat16).reshape(
        lat_count * local_blocks, slot_span, weights.shape[2]
    )
    return lax.all_to_all(contrib, "latent", split_axis=0, concat_axis=0, tiled=True)


def slot_plan(pre_codes, block_ids, activations, target, decoder):
    lat_count = lax.axis_size("latent")
    tok_count = activations.shape[1]
    model_width = activations.shape[2]
    active_count = block_ids.shape[2]
    block_size = pre_codes.shape[3]
    lat_rows = decoder.shape[1]
    local_blocks = lat_rows // block_size
    all_blocks = local_blocks * lat_count
    capacity = 2 * tok_count * active_count // all_blocks
    slot_count = all_blocks * capacity
    pair_count = tok_count * active_count
    pair_block = block_ids[0].T.reshape(pair_count)
    member = (pair_block[:, None] == jnp.arange(all_blocks, dtype=jnp.int32)[None, :]).astype(
        jnp.int32
    )
    before = jnp.cumsum(member, axis=0) - member
    pair_rank = jnp.sum(before * member, axis=1)
    target_slot = pair_block * capacity + pair_rank
    slot_pair = (jnp.arange(slot_count, dtype=jnp.int32)[:, None] == target_slot[None, :]).astype(
        jnp.bfloat16
    )
    slot_token = jnp.sum(slot_pair.reshape(slot_count, active_count, tok_count), axis=1)
    pre_pairs = jnp.transpose(pre_codes[0], (1, 0, 2)).reshape(pair_count, block_size)
    pre_slots = jnp.dot(slot_pair, pre_pairs, preferred_element_type=jnp.float32).astype(
        jnp.bfloat16
    )
    pre_slots = pre_slots.reshape(all_blocks, capacity, block_size)
    inputs = activations[0]
    weights = decoder[0].reshape(local_blocks, block_size, model_width)
    input_slots = jnp.dot(slot_token, inputs, preferred_element_type=jnp.float32).astype(
        jnp.bfloat16
    )
    input_slots = input_slots.reshape(all_blocks, capacity, model_width)
    pieces = (
        lax.all_to_all(pre_slots, "latent", split_axis=0, concat_axis=0, tiled=True),
        lax.all_to_all(input_slots, "latent", split_axis=0, concat_axis=0, tiled=True),
    )
    returned = local_contrib(pieces[0], weights, lat_count, local_blocks)
    returned, received_pre, received_inputs = (returned, pieces[0], pieces[1])
    part_sum = jnp.einsum(
        "st,sd->td",
        slot_token,
        returned.reshape(slot_count, model_width),
        preferred_element_type=jnp.float32,
    )
    rebuilt = lax.psum(part_sum, "layer")
    errors = ((rebuilt - target.astype(jnp.float32)) / tok_count).astype(jnp.bfloat16)
    error_slots = jnp.dot(slot_token, errors, preferred_element_type=jnp.float32).astype(
        jnp.bfloat16
    )
    error_slots = error_slots.reshape(all_blocks, capacity, model_width)
    received_errors = lax.all_to_all(error_slots, "latent", split_axis=0, concat_axis=0, tiled=True)
    pre_blocks = received_pre.reshape(lat_count, local_blocks, capacity, block_size)
    code_blocks = jnp.maximum(pre_blocks, jnp.zeros((), pre_blocks.dtype))
    error_blocks = received_errors.reshape(lat_count, local_blocks, capacity, model_width)
    input_blocks = received_inputs.reshape(lat_count, local_blocks, capacity, model_width)
    code_grad = jnp.einsum(
        "sbcd,bld->sbcl", error_blocks, weights, preferred_element_type=jnp.float32
    )
    pre_grad = jnp.where(pre_blocks > 0, code_grad, jnp.zeros((), jnp.float32)).astype(jnp.bfloat16)
    dec_term = jnp.einsum(
        "sbcl,sbcd->bld", code_blocks, error_blocks, preferred_element_type=jnp.float32
    )
    enc_term = jnp.einsum(
        "sbcl,sbcd->bld", pre_grad, input_blocks, preferred_element_type=jnp.float32
    )
    dec_term = dec_term.reshape(lat_rows, model_width)
    enc_term = enc_term.reshape(lat_rows, model_width)
    dec_half, enc_half = (
        lax.psum_scatter(dec_term, "dp", scatter_dimension=1, tiled=True),
        lax.psum_scatter(enc_term, "dp", scatter_dimension=1, tiled=True),
    )
    return (dec_half.astype(jnp.bfloat16)[None], enc_half.astype(jnp.bfloat16)[None])


def flip(value, axis, bit):
    count = lax.axis_size(axis)
    return lax.ppermute(value, axis, [(i, i ^ bit) for i in range(count)])


def hop(value, axis, step, least):
    count = lax.axis_size(axis)
    if step > 0:
        pairs = [(i, i + 1) for i in range(least, count - 1)]
    else:
        pairs = [(i, i - 1) for i in range(1, count - least)]
    return lax.ppermute(value, axis, pairs)


def params():
    return pltpu.CompilerParams(vmem_limit_bytes=VMEM_BYTES)


def cost(rows, depth, columns):
    return pl.CostEstimate(
        flops=rows * depth * columns // 2,
        bytes_accessed=(rows * depth + depth * columns + rows * columns) // 2,
        transcendentals=0,
    )


def resident(shape):
    return pl.BlockSpec(shape, lambda i, s: (0,) * len(shape))


def gather_kernel(scalar_ref, source_ref, out_ref):
    out_ref[...] = source_ref[...].reshape(out_ref.shape)


def gather_columns(source, columns, width):
    rows = source.shape[-2]
    lead = (1,) * (source.ndim - 2)
    count = columns.shape[0]
    return pl.pallas_call(
        gather_kernel,
        out_shape=jax.ShapeDtypeStruct((rows, count * width), source.dtype),
        grid_spec=pltpu.PrefetchScalarGridSpec(
            num_scalar_prefetch=1,
            grid=(count,),
            in_specs=[pl.BlockSpec(lead + (rows, width), lambda i, s: (0,) * len(lead) + (0, s[i]))],
            out_specs=pl.BlockSpec((rows, width), lambda i, s: (0, i)),
        ),
        compiler_params=params(),
        cost_estimate=cost(rows, 1, count * width),
        name="gather_columns",
    )(columns.astype(jnp.int32), source)


def codes_kernel(groups, blocks, scalar_ref, message_ref, codes, id_map, pre):
    tok = message_ref.shape[2]
    pad = message_ref.shape[1] - 2 * tok
    first = scalar_ref[0].astype(jnp.float32)
    rows = [message_ref[g, 2 * tok:2 * tok + pad, :].astype(jnp.float32) for g in range(groups)]
    fill = tok - groups * pad
    if fill:
        rows.append(jnp.zeros((fill, tok), jnp.float32))
    table = jnp.concatenate(rows, axis=0).T - first
    for g in range(groups):
        pre[g] = jnp.maximum(message_ref[g, 0:2 * tok, :], jnp.zeros((), jnp.bfloat16))
        for j in range(2):
            at = g * pad + j
            wide = jnp.broadcast_to(table[:, at:at + 1], (tok, tok))
            id_map[g, j * tok:(j + 1) * tok, :] = wide.astype(jnp.bfloat16)

    def block_step(b, carry):
        block = b.astype(jnp.float32).astype(jnp.bfloat16)
        at = pl.multiple_of(b * tok, tok)
        for g in range(groups):
            value = jnp.where(id_map[g, tok:2 * tok, :] == block, pre[g, tok:2 * tok, :], jnp.zeros((), jnp.bfloat16))
            value = jnp.where(id_map[g, 0:tok, :] == block, pre[g, 0:tok, :], value)
            codes[g * tok:(g + 1) * tok, pl.ds(at, tok)] = value
        return carry

    lax.fori_loop(0, blocks, block_step, 0)


def spread_codes(message, first, lat_rows):
    groups, _, tok = message.shape
    rows = groups * tok
    return pl.pallas_call(
        functools.partial(codes_kernel, groups, lat_rows // tok),
        out_shape=jax.ShapeDtypeStruct((rows, lat_rows), jnp.bfloat16),
        grid_spec=pltpu.PrefetchScalarGridSpec(
            num_scalar_prefetch=1,
            grid=(1,),
            in_specs=[resident(message.shape)],
            out_specs=resident((rows, lat_rows)),
            scratch_shapes=[
                pltpu.VMEM((groups, 2 * tok, tok), jnp.bfloat16),
                pltpu.VMEM((groups, 2 * tok, tok), jnp.bfloat16),
            ],
        ),
        compiler_params=params(),
        cost_estimate=cost(rows, 1, lat_rows),
        name="spread_codes",
    )(first[None].astype(jnp.int32), message)


def layer_sum_kernel(got_a, kept_a, far_a, got_b, kept_b, far_b, own_ref, *sent_refs):
    half = far_a.shape[1]
    rows = own_ref.shape[0]
    for side, (got, kept, far) in enumerate(((got_a, kept_a, far_a), (got_b, kept_b, far_b))):
        lanes = slice(side * half, (side + 1) * half)
        for n in range(1 + len(sent_refs)):
            at = slice(n * rows, (n + 1) * rows)
            total = got[at, :half].astype(jnp.float32) + kept[at, :half].astype(jnp.float32)
            total = total + far[at, :].astype(jnp.float32)
            if n:
                sent_refs[n - 1][:, lanes] = total.astype(jnp.bfloat16)
            else:
                own_ref[:, lanes] = total


def layer_sum(terms_a, terms_b, blocks):
    rows, half = terms_a[2].shape
    cut = (rows // blocks, 2 * half)
    return pl.pallas_call(
        layer_sum_kernel,
        out_shape=[jax.ShapeDtypeStruct(cut, jnp.float32)] + [jax.ShapeDtypeStruct(cut, jnp.bfloat16)] * (blocks - 1),
        grid=(1,),
        in_specs=[pl.BlockSpec((rows, half), lambda i: (0, 0)) for _ in range(6)],
        out_specs=[pl.BlockSpec(cut, lambda i: (0, 0))] * blocks,
        compiler_params=params(),
        cost_estimate=cost(rows, 4, half),
        name="layer_sum",
    )(*terms_a, *terms_b)


def slots_kernel(groups, blocks, cap, scalar_ref, message_ref, hot_ref, pre_ref, code_ref):
    tok = message_ref.shape[2]
    pad = message_ref.shape[1] - 2 * tok
    f32, bf16 = jnp.float32, jnp.bfloat16
    first = scalar_ref[0].astype(f32)
    rows = [message_ref[g, 2 * tok:2 * tok + pad, :].astype(f32) for g in range(groups)]
    fill = tok - groups * pad
    table = jnp.concatenate(rows + ([jnp.zeros((fill, tok), f32)] if fill else []), axis=0).T
    earlier = lax.broadcasted_iota(jnp.int32, (tok, tok), 0) < lax.broadcasted_iota(jnp.int32, (tok, tok), 1)
    per = 2 * cap
    for z in range(groups // 2):
        pre = 0.0
        hot = []
        for core in range(2):
            g = 2 * z + core
            lanes = [rows[g][j:j + 1] for j in range(2)]
            down = [table[:, g * pad + j:g * pad + j + 1] for j in range(2)]
            same = [jnp.where((down[j] == lanes[j]) & earlier, 1.0, 0.0) for j in range(2)]
            cross = jnp.where(down[0] == lanes[1], 1.0, 0.0)
            rank = [jnp.sum(same[0], axis=0, keepdims=True), jnp.sum(same[1] + cross, axis=0, keepdims=True)]
            here = []
            for j in range(2):
                block = lanes[j] - first
                slot = block * per + (core * cap + rank[j])
                slot = jnp.where((block >= 0) & (block < blocks), slot, -1.0)
                number = lax.broadcasted_iota(jnp.int32, (blocks * per, tok), 0).astype(f32)
                here.append(jnp.where(number == slot, 1.0, 0.0).astype(bf16))
                pre = pre + jnp.dot(
                    here[j], message_ref[g, j * tok:(j + 1) * tok, :], preferred_element_type=f32
                )
            hot.append(here[0] + here[1])
        hot_ref[z] = jnp.concatenate(hot, axis=1)
        for b in range(blocks):
            pre_ref[b, z * per:(z + 1) * per, :] = pre[b * per:(b + 1) * per].astype(bf16)
    for b in range(blocks):
        code_ref[b] = jnp.maximum(pre_ref[b].astype(f32), 0.0).T.astype(bf16)


def make_slots(message, first, lat_rows, cap):
    groups, _, tok = message.shape
    blocks = lat_rows // tok
    per = 2 * cap
    shards = groups // 2
    shapes = [(shards, blocks * per, 2 * tok), (blocks, shards * per, tok), (blocks, tok, shards * per)]
    return pl.pallas_call(
        functools.partial(slots_kernel, groups, blocks, cap),
        out_shape=[jax.ShapeDtypeStruct(shape, jnp.bfloat16) for shape in shapes],
        grid_spec=pltpu.PrefetchScalarGridSpec(
            num_scalar_prefetch=1,
            grid=(1,),
            in_specs=[resident(message.shape)],
            out_specs=[resident(shape) for shape in shapes],
        ),
        compiler_params=params(),
        cost_estimate=cost(groups * tok, 2 * tok, tok),
        name="make_slots",
    )(first[None].astype(jnp.int32), message)


def into_slots(hot, rows, out, z):
    per = out.shape[1] // hot.shape[0]
    value = jnp.dot(hot[z], rows, preferred_element_type=jnp.float32).astype(jnp.bfloat16)
    for b in range(out.shape[0]):
        out[b, z * per:(z + 1) * per, :] = value[b * per:(b + 1) * per]


def lanes_of(refs, rows):
    parts = [r[rows, :] for r in refs]
    return parts[0] if len(parts) == 1 else jnp.concatenate(parts, axis=1)


def piece_grad_kernel(layout, scalar_ref, hot_ref, weight_ref, *refs):
    parts, (slots_ref, grad_ref) = refs[:-2], refs[-2:]
    blocks, _, size = grad_ref.shape
    group = hot_ref.shape[2]
    step = pl.program_id(0)

    @pl.when(step == 0)
    def _():
        grad_ref[...] = jnp.zeros_like(grad_ref)

    at = 0
    for i, piece in enumerate(layout):
        z = 0
        for lanes in piece:
            here = parts[at:at + lanes]
            at += lanes
            for n in range(here[0].shape[0] // group):

                @pl.when(step == i)
                def _(z=z, n=n, here=here):
                    into_slots(hot_ref, lanes_of(here, slice(n * group, (n + 1) * group)), slots_ref.at[0], z)

                z += 1
    for b in range(blocks):
        grad_ref[b] += lax.dot_general(
            slots_ref[0, b],
            weight_ref[0, b * size:(b + 1) * size, :],
            (((1,), (1,)), ((), ())),
            preferred_element_type=jnp.float32,
        )


def piece_grad(pieces, hot, decoder, columns, size):
    lat_rows = decoder.shape[1]
    blocks = lat_rows // size
    slots = hot.shape[0] * hot.shape[1] // blocks
    width = sum(p.shape[1] for p in pieces[0][0])
    flat = [p for piece in pieces for row in piece for p in row]
    return pl.pallas_call(
        functools.partial(piece_grad_kernel, [[len(row) for row in piece] for piece in pieces]),
        out_shape=[
            jax.ShapeDtypeStruct((len(pieces), blocks, slots, width), jnp.bfloat16),
            jax.ShapeDtypeStruct((blocks, slots, size), jnp.float32),
        ],
        grid_spec=pltpu.PrefetchScalarGridSpec(
            num_scalar_prefetch=1,
            grid=(len(pieces),),
            in_specs=[resident(hot.shape), pl.BlockSpec((1, lat_rows, width), lambda i, s: (0, 0, s[i]))]
            + [resident(p.shape) for p in flat],
            out_specs=[
                pl.BlockSpec((1, blocks, slots, width), lambda i, s: (i, 0, 0, 0)),
                resident((blocks, slots, size)),
            ],
        ),
        compiler_params=params(),
        cost_estimate=cost(lat_rows, 256, len(pieces) * width),
        name="piece_grad",
    )(columns.astype(jnp.int32), hot, decoder, *flat)


def decoder_kernel(skip, scalar_ref, code_ref, slots_ref, *refs):
    out_ref = refs[skip]
    size = code_ref.shape[1]
    for b in range(code_ref.shape[0]):
        out_ref[b * size:(b + 1) * size, :] = jnp.dot(
            code_ref[b], slots_ref[0, b], preferred_element_type=jnp.float32
        ).astype(jnp.bfloat16)


def decoder_part(slots, codes, columns, half, held):
    count, blocks, _, width = slots.shape
    lat_rows = blocks * codes.shape[1]
    onto = [] if held is None else [held]
    return pl.pallas_call(
        functools.partial(decoder_kernel, len(onto)),
        out_shape=jax.ShapeDtypeStruct((lat_rows, half), jnp.bfloat16),
        grid_spec=pltpu.PrefetchScalarGridSpec(
            num_scalar_prefetch=1,
            grid=(count,),
            in_specs=[resident(codes.shape), pl.BlockSpec((1,) + slots.shape[1:], lambda i, s: (i, 0, 0, 0))]
            + [pl.BlockSpec(memory_space=pl.ANY) for _ in onto],
            out_specs=pl.BlockSpec((lat_rows, width), lambda i, s: (0, s[i])),
        ),
        compiler_params=params(),
        input_output_aliases={3: 0} if onto else {},
        cost_estimate=cost(lat_rows, 256, count * width),
        name="decoder_part",
    )(columns.astype(jnp.int32), codes, slots, *onto)


def act_slots_kernel(layouts, scalar_ref, hot_ref, *refs):
    out_ref = refs[-1]
    per = out_ref.shape[1] // hot_ref.shape[0]
    at = 0
    for i, layout in enumerate(layouts):
        z = scalar_ref[i]
        total = None
        for count in layout:
            rows = [ref[...] for ref in refs[at:at + count]]
            rows = rows[0] if count == 1 else jnp.concatenate(rows, axis=0)
            total = rows if total is None else total + rows
            at += count
        value = jnp.dot(hot_ref[z], total, preferred_element_type=jnp.float32).astype(jnp.bfloat16)
        to = pl.ds(pl.multiple_of(z * per, per), per)
        for b in range(out_ref.shape[0]):
            out_ref[b, to, :] = value[b * per:(b + 1) * per]


def act_slots(terms_of, places, hot, count):
    half = terms_of[0][0][0].shape[1]
    slots = hot.shape[0] * hot.shape[1] // count
    tile = half // 4
    flat = [part for terms in terms_of for term in terms for part in term]
    return pl.pallas_call(
        functools.partial(act_slots_kernel, [[len(term) for term in terms] for terms in terms_of]),
        out_shape=jax.ShapeDtypeStruct((count, slots, half), jnp.bfloat16),
        grid_spec=pltpu.PrefetchScalarGridSpec(
            num_scalar_prefetch=1,
            grid=(4,),
            in_specs=[resident(hot.shape)] + [pl.BlockSpec((part.shape[0], tile), lambda i, s: (0, i)) for part in flat],
            out_specs=pl.BlockSpec((count, slots, tile), lambda i, s: (0, 0, i)),
        ),
        compiler_params=params(),
        cost_estimate=cost(count * slots, 256, half),
        name="act_slots",
    )(jnp.stack(places).astype(jnp.int32), hot, *flat)


def encoder_kernel(cap, shared, pre_ref, own_ref, theirs_ref, act_ref, out_ref):
    size = pre_ref.shape[2]
    for n in range(shared):
        parts = []
        for at in range(0, own_ref.shape[1], 2 * cap):
            for core in range(2):
                here = slice(at + core * cap, at + (core + 1) * cap)
                there = slice(at + (1 - core) * cap, at + (2 - core) * cap)
                parts.append(own_ref[n, here, :] + theirs_ref[n, there, :])
        total = jnp.concatenate(parts, axis=0)
        grad = jnp.where(pre_ref[n].astype(jnp.float32) > 0, total, 0.0).T.astype(jnp.bfloat16)
        out_ref[n * size:(n + 1) * size, :] = jnp.dot(
            grad, act_ref[n], preferred_element_type=jnp.float32
        ).astype(jnp.bfloat16)


def encoder_part(pre, own, theirs, acts, cap):
    blocks, slots, size = pre.shape
    half = acts.shape[2]
    shared = 2 if blocks % 2 == 0 else 1
    block = pl.BlockSpec((shared, slots, size), lambda i: (i, 0, 0))
    return pl.pallas_call(
        functools.partial(encoder_kernel, cap, shared),
        out_shape=jax.ShapeDtypeStruct((blocks * size, half), jnp.bfloat16),
        grid=(blocks // shared,),
        in_specs=[block, block, block, pl.BlockSpec((shared, slots, half), lambda i: (i, 0, 0))],
        out_specs=pl.BlockSpec((shared * size, half), lambda i: (i, 0)),
        compiler_params=params(),
        cost_estimate=cost(blocks * size, 256, half),
        name="encoder_part",
    )(pre, own, theirs, acts)


def dense_plan(pre_codes, block_ids, activations, target, decoder):
    lay_count = lax.axis_size("layer")
    lat_count = lax.axis_size("latent")
    dp_count = lax.axis_size("dp")
    lay_here = lax.axis_index("layer")
    lat_here = lax.axis_index("latent")
    dp_here = lax.axis_index("dp")
    tok_count = activations.shape[1]
    model_width = activations.shape[2]
    active_count = block_ids.shape[2]
    block_size = pre_codes.shape[3]
    lat_rows = decoder.shape[1]
    local_blocks = lat_rows // block_size
    half = model_width // dp_count
    group = dp_count * tok_count
    tokens = lat_count * group
    width = half // lay_count
    side = width // 2
    f32, bf16 = jnp.float32, jnp.bfloat16
    first = lat_here * local_blocks
    capacity = 2 * tok_count * active_count // (local_blocks * lat_count)

    def columns(rows, which):
        return lax.dynamic_slice_in_dim(rows, which * half, half, axis=1)

    def places(names, offset, fine=1, sub=0):
        return [(offset + (lay_here ^ r)) * fine + sub for r in names]

    def weight_places(names):
        return jnp.stack(places(names, dp_here * lay_count))

    pre_rows = jnp.swapaxes(pre_codes[0], 0, 1).reshape(active_count * tok_count, block_size)
    id_rows = jnp.pad(block_ids[0].T, ((0, 16 - active_count), (0, 0))).astype(bf16)
    own = jnp.concatenate([pre_rows, id_rows], axis=0)
    at = places((1, 3), dp_here * lay_count, 2, 0) + places((2, 3), dp_here * lay_count, 2, 1)
    send_weights = gather_columns(decoder, jnp.stack(at), side)

    corner = send_weights[:16, :128]
    later, corner = lax.optimization_barrier((own, corner))
    message = [own, flip(later, "latent", 1)] + [flip(own, "latent", r) for r in range(2, lat_count)]
    message = jnp.stack(message)

    own, inputs = lax.optimization_barrier((own, activations[0]))
    acts = jnp.concatenate([columns(inputs, dp_here), flip(columns(inputs, 1 - dp_here), "dp", 1)])
    message, acts = lax.optimization_barrier((message, acts))
    up, down = [acts], [acts]

    def next_hops():
        step = len(up)
        up.append(hop(up[-1], "latent", 1, step - 1))
        down.append(hop(down[-1], "latent", -1, step - 1))

    message = jnp.stack([message, flip(message, "dp", 1)], axis=1)
    message = message.reshape(lat_count * dp_count, own.shape[0], block_size)
    next_hops()

    codes = spread_codes(message, first, lat_rows)
    at = places((0, 2), dp_here * lay_count, 2, 0) + places((0, 1), dp_here * lay_count, 2, 1)
    at, codes, target = lax.optimization_barrier((jnp.stack(at), codes, target))
    keep_weights = gather_columns(decoder, at, side)
    goals = gather_columns(target, jnp.stack([which * lay_count + lay_here for which in (dp_here, 1 - dp_here)]), width)
    goals = jnp.concatenate([goals[:, :width], flip(goals[:, width:], "dp", 1)])

    codes = spread_codes(message, first, lat_rows)
    at = places((0, 2), dp_here * lay_count, 2, 0) + places((0, 1), dp_here * lay_count, 2, 1)
    at, codes, target = lax.optimization_barrier((jnp.stack(at), codes, target))
    keep_weights = gather_columns(decoder, at, side)
    goals = gather_columns(target, jnp.stack([which * lay_count + lay_here for which in (dp_here, 1 - dp_here)]), width)
    goals = jnp.concatenate([goals[:, :width], flip(goals[:, width:], "dp", 1)])

    def rows_for(spread, weights, n):
        return jnp.dot(spread, weights[:, n * width:(n + 1) * width], preferred_element_type=f32).astype(bf16)

    got = flip(rows_for(codes, send_weights, 0), "layer", 1), flip(rows_for(codes, send_weights, 1), "layer", 2)
    keep_codes, up[1], down[1] = lax.optimization_barrier((codes, up[1], down[1]))
    if lat_count > 2:
        next_hops()
    kept = rows_for(keep_codes, keep_weights, 0), rows_for(keep_codes, keep_weights, 1)

    def add(one, two):
        return (one[:, side:].astype(f32) + two[:, side:].astype(f32)).astype(bf16)

    far = [flip(add(got[n], kept[n]), "layer", 2 - n) for n in range(2)]
    far, goals, up[-1], down[-1] = lax.optimization_barrier((far, goals, up[-1], down[-1]))

    total, *sent = layer_sum((got[0], kept[0], far[0]), (got[1], kept[1], far[1]), lat_count)
    for r in range(1, lat_count):
        total = total + flip(sent[r - 1], "latent", r).astype(f32)
    errors = ((total - goals.astype(f32)) / tok_count).astype(bf16)
    others = [flip(errors, "latent", r) for r in range(1, lat_count)]
    one_near, two_near = flip(errors, "layer", 1), flip(errors, "layer", 2)
    one_near, two_near, others, up[-1], down[-1] = lax.optimization_barrier(
        (one_near, two_near, others, up[-1], down[-1])
    )
    distant = jnp.concatenate(others)
    one_far, two_far = flip(distant, "layer", 1), flip(distant, "layer", 2)
    three_near = flip(two_near[:, :side], "layer", 1), flip(one_near[:, side:], "layer", 2)
    while len(up) < lat_count - 1:
        next_hops()
    early = group * 11 // 16
    ends = []
    if len(up) < lat_count:
        for rows in (slice(0, early), slice(early, group)):
            ends.append([hop(up[-1][rows], "latent", 1, len(up) - 1), hop(down[-1][rows], "latent", -1, len(up) - 1)])

    hot, pre_slots, code_slots = make_slots(message, first, lat_rows, capacity)

    def grads_of(here, names, dec):
        slots, grad = piece_grad(here, hot, decoder, weight_places(names), block_size)
        return grad, decoder_part(slots, code_slots, jnp.stack(places(names, 0)), half, dec)

    grad, dec = grads_of([[(errors,), (distant,)]], (0,), None)
    one_far, two_far, three_near, grad, dec, ends[:1] = lax.optimization_barrier(
        (one_far, two_far, three_near, grad, dec, ends[:1])
    )
    three_far = flip(two_far[:, :side], "layer", 1), flip(one_far[:, side:], "layer", 2)
    more, dec = grads_of([[(one_near,), (one_far,)], [(two_near,), (two_far,)]], (1, 2), dec)
    three_far, more, dec, ends = lax.optimization_barrier((three_far, more, dec, ends))
    last, dec = grads_of([[three_near, three_far]], (3,), dec)
    grad = grad + more + last

    ups, downs = [[part] for part in up], [[part] for part in down]
    if ends:
        ups.append([part[0] for part in ends])
        downs.append([part[1] for part in ends])
    terms_of = [[[acts]]] + [[downs[k], ups[lat_count - k]] for k in range(1, lat_count)]
    shards = [lax.rem(lat_here + k, lat_count) ^ lat_here for k in range(lat_count)]
    slotted = act_slots(terms_of, shards, hot, local_blocks)
    enc = encoder_part(pre_slots, grad, flip(grad, "dp", 1), slotted, capacity)
    return dec[None], enc[None]


def per_device(pre_codes, block_ids, activations, target, decoder):
    lat_count = lax.axis_size("latent")
    lay_count = lax.axis_size("layer")
    dp_count = lax.axis_size("dp")
    tok_count = activations.shape[1]
    model_width = activations.shape[2]
    active_count = block_ids.shape[2]
    block_size = pre_codes.shape[3]
    all_blocks = decoder.shape[1] // block_size * lat_count
    slots = 2 * tok_count * active_count // lat_count
    dense = (
        slots >= tok_count
        and dp_count == 2
        and active_count == 2
        and lay_count == 4
        and lat_count > 1
        and lat_count & (lat_count - 1) == 0
        and tok_count == block_size
        and lat_count * dp_count * 16 <= tok_count
        and model_width % (dp_count * 2 * lay_count * 128) == 0
        and all_blocks <= 256
        and 2 * tok_count * active_count == 8 * all_blocks
    )
    plan = dense_plan if dense else slot_plan
    return plan(pre_codes, block_ids, activations, target, decoder)


def solution(mesh):
    placed = (
        P("layer", ("latent", "dp"), None, None),
        P("layer", ("latent", "dp"), None),
        P("layer", ("latent", "dp"), None),
        P(("latent", "dp"), None),
        P("layer", "latent", None),
    )
    return jax.shard_map(
        per_device,
        mesh=mesh,
        in_specs=placed,
        out_specs=(P("layer", "latent", "dp"), P("layer", "latent", "dp")),
        check_vma=False,
    )
```

```python
import functools

import jax
import jax.numpy as jnp
from jax import lax
from jax.experimental import pallas as pl
from jax.experimental.pallas import tpu as pltpu
from jax.sharding import PartitionSpec as P

VMEM_BYTES = 40 * 1024 * 1024


def local_contrib(received_pre, weights, lat_count, local_blocks):
    code_vals = jnp.maximum(received_pre, jnp.zeros((), received_pre.dtype))
    slot_span = received_pre.shape[1]
    block_size = received_pre.shape[2]
    grouped = code_vals.reshape(lat_count, local_blocks, slot_span, block_size)
    contrib = jnp.einsum("sbcl,bld->sbcd", grouped, weights, preferred_element_type=jnp.float32)
    contrib = contrib.astype(jnp.bfloat16).reshape(
        lat_count * local_blocks, slot_span, weights.shape[2]
    )
    return lax.all_to_all(contrib, "latent", split_axis=0, concat_axis=0, tiled=True)


def slot_plan(pre_codes, block_ids, activations, target, decoder):
    lat_count = lax.axis_size("latent")
    tok_count = activations.shape[1]
    model_width = activations.shape[2]
    active_count = block_ids.shape[2]
    block_size = pre_codes.shape[3]
    lat_rows = decoder.shape[1]
    local_blocks = lat_rows // block_size
    all_blocks = local_blocks * lat_count
    capacity = 2 * tok_count * active_count // all_blocks
    slot_count = all_blocks * capacity
    pair_count = tok_count * active_count
    pair_block = block_ids[0].T.reshape(pair_count)
    member = (pair_block[:, None] == jnp.arange(all_blocks, dtype=jnp.int32)[None, :]).astype(
        jnp.int32
    )
    before = jnp.cumsum(member, axis=0) - member
    pair_rank = jnp.sum(before * member, axis=1)
    target_slot = pair_block * capacity + pair_rank
    slot_pair = (jnp.arange(slot_count, dtype=jnp.int32)[:, None] == target_slot[None, :]).astype(
        jnp.bfloat16
    )
    slot_token = jnp.sum(slot_pair.reshape(slot_count, active_count, tok_count), axis=1)
    pre_pairs = jnp.transpose(pre_codes[0], (1, 0, 2)).reshape(pair_count, block_size)
    pre_slots = jnp.dot(slot_pair, pre_pairs, preferred_element_type=jnp.float32).astype(
        jnp.bfloat16
    )
    pre_slots = pre_slots.reshape(all_blocks, capacity, block_size)
    inputs = activations[0]
    weights = decoder[0].reshape(local_blocks, block_size, model_width)
    input_slots = jnp.dot(slot_token, inputs, preferred_element_type=jnp.float32).astype(
        jnp.bfloat16
    )
    input_slots = input_slots.reshape(all_blocks, capacity, model_width)
    pieces = (
        lax.all_to_all(pre_slots, "latent", split_axis=0, concat_axis=0, tiled=True),
        lax.all_to_all(input_slots, "latent", split_axis=0, concat_axis=0, tiled=True),
    )
    returned = local_contrib(pieces[0], weights, lat_count, local_blocks)
    returned, received_pre, received_inputs = (returned, pieces[0], pieces[1])
    part_sum = jnp.einsum(
        "st,sd->td",
        slot_token,
        returned.reshape(slot_count, model_width),
        preferred_element_type=jnp.float32,
    )
    rebuilt = lax.psum(part_sum, "layer")
    errors = ((rebuilt - target.astype(jnp.float32)) / tok_count).astype(jnp.bfloat16)
    error_slots = jnp.dot(slot_token, errors, preferred_element_type=jnp.float32).astype(
        jnp.bfloat16
    )
    error_slots = error_slots.reshape(all_blocks, capacity, model_width)
    received_errors = lax.all_to_all(error_slots, "latent", split_axis=0, concat_axis=0, tiled=True)
    pre_blocks = received_pre.reshape(lat_count, local_blocks, capacity, block_size)
    code_blocks = jnp.maximum(pre_blocks, jnp.zeros((), pre_blocks.dtype))
    error_blocks = received_errors.reshape(lat_count, local_blocks, capacity, model_width)
    input_blocks = received_inputs.reshape(lat_count, local_blocks, capacity, model_width)
    code_grad = jnp.einsum(
        "sbcd,bld->sbcl", error_blocks, weights, preferred_element_type=jnp.float32
    )
    pre_grad = jnp.where(pre_blocks > 0, code_grad, jnp.zeros((), jnp.float32)).astype(jnp.bfloat16)
    dec_term = jnp.einsum(
        "sbcl,sbcd->bld", code_blocks, error_blocks, preferred_element_type=jnp.float32
    )
    enc_term = jnp.einsum(
        "sbcl,sbcd->bld", pre_grad, input_blocks, preferred_element_type=jnp.float32
    )
    dec_term = dec_term.reshape(lat_rows, model_width)
    enc_term = enc_term.reshape(lat_rows, model_width)
    dec_half, enc_half = (
        lax.psum_scatter(dec_term, "dp", scatter_dimension=1, tiled=True),
        lax.psum_scatter(enc_term, "dp", scatter_dimension=1, tiled=True),
    )
    return (dec_half.astype(jnp.bfloat16)[None], enc_half.astype(jnp.bfloat16)[None])


def flip(value, axis, bit):
    count = lax.axis_size(axis)
    return lax.ppermute(value, axis, [(i, i ^ bit) for i in range(count)])


def hop(value, axis, step, least):
    count = lax.axis_size(axis)
    if step > 0:
        pairs = [(i, i + 1) for i in range(least, count - 1)]
    else:
        pairs = [(i, i - 1) for i in range(1, count - least)]
    return lax.ppermute(value, axis, pairs)


def params():
    return pltpu.CompilerParams(vmem_limit_bytes=VMEM_BYTES)


def cost(microseconds):
    return pl.CostEstimate(flops=int(microseconds * 1.1e9), bytes_accessed=1, transcendentals=0)


def resident(shape):
    return pl.BlockSpec(shape, lambda i, s: (0,) * len(shape))


def gather_kernel(scalar_ref, source_ref, out_ref):
    out_ref[...] = source_ref[...].reshape(out_ref.shape)


def gather_columns(source, columns, width):
    rows = source.shape[-2]
    lead = (1,) * (source.ndim - 2)
    count = columns.shape[0]
    return pl.pallas_call(
        gather_kernel,
        out_shape=jax.ShapeDtypeStruct((rows, count * width), source.dtype),
        grid_spec=pltpu.PrefetchScalarGridSpec(
            num_scalar_prefetch=1,
            grid=(count,),
            in_specs=[pl.BlockSpec(lead + (rows, width), lambda i, s: (0,) * len(lead) + (0, s[i]))],
            out_specs=pl.BlockSpec((rows, width), lambda i, s: (0, i)),
        ),
        compiler_params=params(),
        cost_estimate=cost(0.9 * count),
        name="gather_columns",
    )(columns.astype(jnp.int32), source)


def codes_kernel(groups, blocks, scalar_ref, message_ref, codes, id_map, pre):
    tok = message_ref.shape[2]
    pad = message_ref.shape[1] - 2 * tok
    first = scalar_ref[0].astype(jnp.float32)
    rows = [message_ref[g, 2 * tok:2 * tok + pad, :].astype(jnp.float32) for g in range(groups)]
    fill = tok - groups * pad
    if fill:
        rows.append(jnp.zeros((fill, tok), jnp.float32))
    table = jnp.concatenate(rows, axis=0).T - first
    for g in range(groups):
        pre[g] = jnp.maximum(message_ref[g, 0:2 * tok, :], jnp.zeros((), jnp.bfloat16))
        for j in range(2):
            at = g * pad + j
            wide = jnp.broadcast_to(table[:, at:at + 1], (tok, tok))
            id_map[g, j * tok:(j + 1) * tok, :] = wide.astype(jnp.bfloat16)

    def block_step(b, carry):
        block = b.astype(jnp.float32).astype(jnp.bfloat16)
        at = pl.multiple_of(b * tok, tok)
        for g in range(groups):
            value = jnp.where(id_map[g, tok:2 * tok, :] == block, pre[g, tok:2 * tok, :], jnp.zeros((), jnp.bfloat16))
            value = jnp.where(id_map[g, 0:tok, :] == block, pre[g, 0:tok, :], value)
            codes[g * tok:(g + 1) * tok, pl.ds(at, tok)] = value
        return carry

    lax.fori_loop(0, blocks, block_step, 0)


def spread_codes(message, first, lat_rows):
    groups, _, tok = message.shape
    rows = groups * tok
    return pl.pallas_call(
        functools.partial(codes_kernel, groups, lat_rows // tok),
        out_shape=jax.ShapeDtypeStruct((rows, lat_rows), jnp.bfloat16),
        grid_spec=pltpu.PrefetchScalarGridSpec(
            num_scalar_prefetch=1,
            grid=(1,),
            in_specs=[resident(message.shape)],
            out_specs=resident((rows, lat_rows)),
            scratch_shapes=[
                pltpu.VMEM((groups, 2 * tok, tok), jnp.bfloat16),
                pltpu.VMEM((groups, 2 * tok, tok), jnp.bfloat16),
            ],
        ),
        compiler_params=params(),
        cost_estimate=cost(2.5),
        name="spread_codes",
    )(first[None].astype(jnp.int32), message)


def layer_sum_kernel(got_a, kept_a, far_a, got_b, kept_b, far_b, own_ref, *sent_refs):
    half = far_a.shape[1]
    rows = own_ref.shape[0]
    for side, (got, kept, far) in enumerate(((got_a, kept_a, far_a), (got_b, kept_b, far_b))):
        lanes = slice(side * half, (side + 1) * half)
        for n in range(1 + len(sent_refs)):
            at = slice(n * rows, (n + 1) * rows)
            total = got[at, :half].astype(jnp.float32) + kept[at, :half].astype(jnp.float32)
            total = total + far[at, :].astype(jnp.float32)
            if n:
                sent_refs[n - 1][:, lanes] = total.astype(jnp.bfloat16)
            else:
                own_ref[:, lanes] = total


def layer_sum(terms_a, terms_b, blocks):
    rows, half = terms_a[2].shape
    cut = (rows // blocks, 2 * half)
    return pl.pallas_call(
        layer_sum_kernel,
        out_shape=[jax.ShapeDtypeStruct(cut, jnp.float32)] + [jax.ShapeDtypeStruct(cut, jnp.bfloat16)] * (blocks - 1),
        grid=(1,),
        in_specs=[pl.BlockSpec((rows, half), lambda i: (0, 0)) for _ in range(6)],
        out_specs=[pl.BlockSpec(cut, lambda i: (0, 0))] * blocks,
        compiler_params=params(),
        cost_estimate=cost(0.5),
        name="layer_sum",
    )(*terms_a, *terms_b)


def join_kernel(*refs):
    out_ref = refs[-1]
    for i in range(out_ref.shape[0]):
        out_ref[i] = refs[i][...]


def join(parts, waited):
    shape = (len(parts),) + parts[0].shape
    vmem = pl.BlockSpec(memory_space=pltpu.VMEM)
    return pl.pallas_call(
        join_kernel,
        out_shape=jax.ShapeDtypeStruct(shape, parts[0].dtype),
        in_specs=[vmem] * len(parts) + [pl.BlockSpec(memory_space=pl.ANY)],
        out_specs=vmem,
        compiler_params=params(),
        cost_estimate=cost(0.3),
        name="join",
    )(*parts, waited)


def slots_kernel(groups, blocks, cap, scalar_ref, message_ref, hot_ref, pre_ref, code_ref):
    tok = message_ref.shape[2]
    pad = message_ref.shape[1] - 2 * tok
    f32, bf16 = jnp.float32, jnp.bfloat16
    first = scalar_ref[0].astype(f32)
    rows = [message_ref[g, 2 * tok:2 * tok + pad, :].astype(f32) for g in range(groups)]
    fill = tok - groups * pad
    table = jnp.concatenate(rows + ([jnp.zeros((fill, tok), f32)] if fill else []), axis=0).T
    earlier = lax.broadcasted_iota(jnp.int32, (tok, tok), 0) < lax.broadcasted_iota(jnp.int32, (tok, tok), 1)
    per = 2 * cap
    for z in range(groups // 2):
        pre = 0.0
        hot = []
        for core in range(2):
            g = 2 * z + core
            lanes = [rows[g][j:j + 1] for j in range(2)]
            down = [table[:, g * pad + j:g * pad + j + 1] for j in range(2)]
            same = [jnp.where((down[j] == lanes[j]) & earlier, 1.0, 0.0) for j in range(2)]
            cross = jnp.where(down[0] == lanes[1], 1.0, 0.0)
            rank = [jnp.sum(same[0], axis=0, keepdims=True), jnp.sum(same[1] + cross, axis=0, keepdims=True)]
            here = []
            for j in range(2):
                block = lanes[j] - first
                slot = block * per + (core * cap + rank[j])
                slot = jnp.where((block >= 0) & (block < blocks), slot, -1.0)
                number = lax.broadcasted_iota(jnp.int32, (blocks * per, tok), 0).astype(f32)
                here.append(jnp.where(number == slot, 1.0, 0.0).astype(bf16))
                pre = pre + jnp.dot(
                    here[j], message_ref[g, j * tok:(j + 1) * tok, :], preferred_element_type=f32
                )
            hot.append(here[0] + here[1])
        hot_ref[z] = jnp.concatenate(hot, axis=1)
        for b in range(blocks):
            pre_ref[b, z * per:(z + 1) * per, :] = pre[b * per:(b + 1) * per].astype(bf16)
    for b in range(blocks):
        code_ref[b] = jnp.maximum(pre_ref[b].astype(f32), 0.0).T.astype(bf16)


def make_slots(message, first, lat_rows, cap):
    groups, _, tok = message.shape
    blocks = lat_rows // tok
    per = 2 * cap
    shards = groups // 2
    shapes = [(shards, blocks * per, 2 * tok), (blocks, shards * per, tok), (blocks, tok, shards * per)]
    return pl.pallas_call(
        functools.partial(slots_kernel, groups, blocks, cap),
        out_shape=[jax.ShapeDtypeStruct(shape, jnp.bfloat16) for shape in shapes],
        grid_spec=pltpu.PrefetchScalarGridSpec(
            num_scalar_prefetch=1,
            grid=(1,),
            in_specs=[resident(message.shape)],
            out_specs=[resident(shape) for shape in shapes],
        ),
        compiler_params=params(),
        cost_estimate=cost(1),
        name="make_slots",
    )(first[None].astype(jnp.int32), message)


def into_slots(hot, rows, out, z):
    per = out.shape[1] // hot.shape[0]
    value = jnp.dot(hot[z], rows, preferred_element_type=jnp.float32).astype(jnp.bfloat16)
    for b in range(out.shape[0]):
        out[b, z * per:(z + 1) * per, :] = value[b * per:(b + 1) * per]


def lanes_of(refs, rows):
    parts = [r[rows, :] for r in refs]
    return parts[0] if len(parts) == 1 else jnp.concatenate(parts, axis=1)


def piece_grad_kernel(layout, onto, scalar_ref, hot_ref, weight_ref, *refs):
    parts, (slots_ref, grad_ref) = refs[onto:-2], refs[-2:]
    blocks, _, size = grad_ref.shape
    group = hot_ref.shape[2]
    step = pl.program_id(0)

    @pl.when(step == 0)
    def _():
        grad_ref[...] = refs[0][...] if onto else jnp.zeros_like(grad_ref)

    at = 0
    for i, piece in enumerate(layout):
        z = 0
        for lanes in piece:
            here = parts[at:at + lanes]
            at += lanes
            for n in range(here[0].shape[0] // group):

                @pl.when(step == i)
                def _(z=z, n=n, here=here):
                    into_slots(hot_ref, lanes_of(here, slice(n * group, (n + 1) * group)), slots_ref.at[0], z)

                z += 1
    for b in range(blocks):
        grad_ref[b] += lax.dot_general(
            slots_ref[0, b],
            weight_ref[0, b * size:(b + 1) * size, :],
            (((1,), (1,)), ((), ())),
            preferred_element_type=jnp.float32,
        )


def piece_grad(pieces, hot, decoder, columns, size, held):
    lat_rows = decoder.shape[1]
    blocks = lat_rows // size
    slots = hot.shape[0] * hot.shape[1] // blocks
    width = sum(p.shape[1] for p in pieces[0][0])
    flat = [p for piece in pieces for row in piece for p in row]
    onto = [] if held is None else [held]
    return pl.pallas_call(
        functools.partial(piece_grad_kernel, [[len(row) for row in piece] for piece in pieces], len(onto)),
        out_shape=[
            jax.ShapeDtypeStruct((len(pieces), blocks, slots, width), jnp.bfloat16),
            jax.ShapeDtypeStruct((blocks, slots, size), jnp.float32),
        ],
        grid_spec=pltpu.PrefetchScalarGridSpec(
            num_scalar_prefetch=1,
            grid=(len(pieces),),
            in_specs=[resident(hot.shape), pl.BlockSpec((1, lat_rows, width), lambda i, s: (0, 0, s[i]))]
            + [resident(p.shape) for p in onto + flat],
            out_specs=[
                pl.BlockSpec((1, blocks, slots, width), lambda i, s: (i, 0, 0, 0)),
                resident((blocks, slots, size)),
            ],
        ),
        compiler_params=params(),
        cost_estimate=cost(0.8 + 2 * len(pieces)),
        name="piece_grad",
    )(columns.astype(jnp.int32), hot, decoder, *onto, *flat)


def decoder_kernel(skip, scalar_ref, code_ref, slots_ref, *refs):
    out_ref = refs[skip]
    size = code_ref.shape[1]
    for b in range(code_ref.shape[0]):
        out_ref[b * size:(b + 1) * size, :] = jnp.dot(
            code_ref[b], slots_ref[0, b], preferred_element_type=jnp.float32
        ).astype(jnp.bfloat16)


def decoder_part(slots, codes, columns, half, held):
    count, blocks, _, width = slots.shape
    lat_rows = blocks * codes.shape[1]
    onto = [] if held is None else [held]
    return pl.pallas_call(
        functools.partial(decoder_kernel, len(onto)),
        out_shape=jax.ShapeDtypeStruct((lat_rows, half), jnp.bfloat16),
        grid_spec=pltpu.PrefetchScalarGridSpec(
            num_scalar_prefetch=1,
            grid=(count,),
            in_specs=[resident(codes.shape), pl.BlockSpec((1,) + slots.shape[1:], lambda i, s: (i, 0, 0, 0))]
            + [pl.BlockSpec(memory_space=pl.ANY) for _ in onto],
            out_specs=pl.BlockSpec((lat_rows, width), lambda i, s: (0, s[i])),
        ),
        compiler_params=params(),
        input_output_aliases={3: 0} if onto else {},
        cost_estimate=cost(0.7 + 1.3 * count),
        name="decoder_part",
    )(columns.astype(jnp.int32), codes, slots, *onto)


def act_slots_kernel(layouts, scalar_ref, hot_ref, *refs):
    out_ref = refs[-1]
    per = out_ref.shape[1] // hot_ref.shape[0]
    at = 0
    for i, layout in enumerate(layouts):
        z = scalar_ref[i]
        total = None
        for count in layout:
            rows = [ref[...] for ref in refs[at:at + count]]
            rows = rows[0] if count == 1 else jnp.concatenate(rows, axis=0)
            total = rows if total is None else total + rows
            at += count
        value = jnp.dot(hot_ref[z], total, preferred_element_type=jnp.float32).astype(jnp.bfloat16)
        to = pl.ds(pl.multiple_of(z * per, per), per)
        for b in range(out_ref.shape[0]):
            out_ref[b, to, :] = value[b * per:(b + 1) * per]


def act_slots(terms_of, places, hot, count):
    half = terms_of[0][0][0].shape[1]
    slots = hot.shape[0] * hot.shape[1] // count
    tile = half // 4
    flat = [part for terms in terms_of for term in terms for part in term]
    return pl.pallas_call(
        functools.partial(act_slots_kernel, [[len(term) for term in terms] for terms in terms_of]),
        out_shape=jax.ShapeDtypeStruct((count, slots, half), jnp.bfloat16),
        grid_spec=pltpu.PrefetchScalarGridSpec(
            num_scalar_prefetch=1,
            grid=(4,),
            in_specs=[resident(hot.shape)] + [pl.BlockSpec((part.shape[0], tile), lambda i, s: (0, i)) for part in flat],
            out_specs=pl.BlockSpec((count, slots, tile), lambda i, s: (0, 0, i)),
        ),
        compiler_params=params(),
        cost_estimate=cost(3.3),
        name="act_slots",
    )(jnp.stack(places).astype(jnp.int32), hot, *flat)


def encoder_kernel(cap, shared, pre_ref, own_ref, theirs_ref, act_ref, out_ref):
    size = pre_ref.shape[2]
    for n in range(shared):
        parts = []
        for at in range(0, own_ref.shape[1], 2 * cap):
            for core in range(2):
                here = slice(at + core * cap, at + (core + 1) * cap)
                there = slice(at + (1 - core) * cap, at + (2 - core) * cap)
                parts.append(own_ref[n, here, :] + theirs_ref[n, there, :])
        total = jnp.concatenate(parts, axis=0)
        grad = jnp.where(pre_ref[n].astype(jnp.float32) > 0, total, 0.0).T.astype(jnp.bfloat16)
        out_ref[n * size:(n + 1) * size, :] = jnp.dot(
            grad, act_ref[n], preferred_element_type=jnp.float32
        ).astype(jnp.bfloat16)


def encoder_part(pre, own, theirs, acts, cap):
    blocks, slots, size = pre.shape
    half = acts.shape[2]
    shared = 2 if blocks % 2 == 0 else 1
    block = pl.BlockSpec((shared, slots, size), lambda i: (i, 0, 0))
    return pl.pallas_call(
        functools.partial(encoder_kernel, cap, shared),
        out_shape=jax.ShapeDtypeStruct((blocks * size, half), jnp.bfloat16),
        grid=(blocks // shared,),
        in_specs=[block, block, block, pl.BlockSpec((shared, slots, half), lambda i: (i, 0, 0))],
        out_specs=pl.BlockSpec((shared * size, half), lambda i: (i, 0)),
        compiler_params=params(),
        cost_estimate=cost(6.5),
        name="encoder_part",
    )(pre, own, theirs, acts)


def dense_plan(pre_codes, block_ids, activations, target, decoder):
    lay_count = lax.axis_size("layer")
    lat_count = lax.axis_size("latent")
    dp_count = lax.axis_size("dp")
    lay_here = lax.axis_index("layer")
    lat_here = lax.axis_index("latent")
    dp_here = lax.axis_index("dp")
    tok_count = activations.shape[1]
    model_width = activations.shape[2]
    active_count = block_ids.shape[2]
    block_size = pre_codes.shape[3]
    lat_rows = decoder.shape[1]
    local_blocks = lat_rows // block_size
    half = model_width // dp_count
    group = dp_count * tok_count
    tokens = lat_count * group
    width = half // lay_count
    side = width // 2
    f32, bf16 = jnp.float32, jnp.bfloat16
    first = lat_here * local_blocks
    capacity = 2 * tok_count * active_count // (local_blocks * lat_count)

    def columns(rows, which):
        return lax.dynamic_slice_in_dim(rows, which * half, half, axis=1)

    def places(names, offset, fine=1, sub=0):
        return [(offset + (lay_here ^ r)) * fine + sub for r in names]

    def weight_places(names):
        return jnp.stack(places(names, dp_here * lay_count))

    pre_rows = jnp.swapaxes(pre_codes[0], 0, 1).reshape(active_count * tok_count, block_size)
    id_rows = jnp.pad(block_ids[0].T, ((0, 16 - active_count), (0, 0))).astype(bf16)
    own = jnp.concatenate([pre_rows, id_rows], axis=0)
    at = places((1, 3), dp_here * lay_count, 2, 0) + places((2, 3), dp_here * lay_count, 2, 1)
    send_weights = gather_columns(decoder, jnp.stack(at), side)

    message = [own] + [flip(own, "latent", r) for r in range(1, lat_count)]

    own, inputs = lax.optimization_barrier((own, activations[0]))
    acts = jnp.concatenate([columns(inputs, dp_here), flip(columns(inputs, 1 - dp_here), "dp", 1)])
    message, acts = lax.optimization_barrier((join(message, send_weights), acts))
    up, down = [acts], [acts]

    def next_hops():
        step = len(up)
        up.append(hop(up[-1], "latent", 1, step - 1))
        down.append(hop(down[-1], "latent", -1, step - 1))

    message = jnp.stack([message, flip(message, "dp", 1)], axis=1)
    message = message.reshape(lat_count * dp_count, own.shape[0], block_size)
    next_hops()

    codes = spread_codes(message, first, lat_rows)
    at = places((0, 2), dp_here * lay_count, 2, 0) + places((0, 1), dp_here * lay_count, 2, 1)
    at, codes, target = lax.optimization_barrier((jnp.stack(at), codes, target))
    keep_weights = gather_columns(decoder, at, side)
    goals = gather_columns(target, jnp.stack([which * lay_count + lay_here for which in (dp_here, 1 - dp_here)]), width)
    goals = jnp.concatenate([goals[:, :width], flip(goals[:, width:], "dp", 1)])

    codes = spread_codes(message, first, lat_rows)
    at = places((0, 2), dp_here * lay_count, 2, 0) + places((0, 1), dp_here * lay_count, 2, 1)
    at, codes, target = lax.optimization_barrier((jnp.stack(at), codes, target))
    keep_weights = gather_columns(decoder, at, side)
    goals = gather_columns(target, jnp.stack([which * lay_count + lay_here for which in (dp_here, 1 - dp_here)]), width)
    goals = jnp.concatenate([goals[:, :width], flip(goals[:, width:], "dp", 1)])

    def rows_for(spread, weights, n):
        return jnp.dot(spread, weights[:, n * width:(n + 1) * width], preferred_element_type=f32).astype(bf16)

    got = flip(rows_for(codes, send_weights, 0), "layer", 1), flip(rows_for(codes, send_weights, 1), "layer", 2)
    keep_codes, up[1], down[1] = lax.optimization_barrier((codes, up[1], down[1]))
    if lat_count > 2:
        next_hops()
    kept = rows_for(keep_codes, keep_weights, 0), rows_for(keep_codes, keep_weights, 1)

    def add(one, two):
        return (one[:, side:].astype(f32) + two[:, side:].astype(f32)).astype(bf16)

    far = [flip(add(got[n], kept[n]), "layer", 2 - n) for n in range(2)]
    far, goals, up[-1], down[-1] = lax.optimization_barrier((far, goals, up[-1], down[-1]))

    total, *sent = layer_sum((got[0], kept[0], far[0]), (got[1], kept[1], far[1]), lat_count)
    for r in range(1, lat_count):
        total = total + flip(sent[r - 1], "latent", r).astype(f32)
    errors = ((total - goals.astype(f32)) / tok_count).astype(bf16)
    others = [flip(errors, "latent", r) for r in range(1, lat_count)]
    one_near, two_near = flip(errors, "layer", 1), flip(errors, "layer", 2)
    made = make_slots(message, first, lat_rows, capacity)
    one_near, two_near, others, up[-1], down[-1], made = lax.optimization_barrier(
        (one_near, two_near, others, up[-1], down[-1], made)
    )
    hot, pre_slots, code_slots = made
    distant = jnp.concatenate(others)
    one_far, two_far = flip(distant, "layer", 1), flip(distant, "layer", 2)
    while len(up) < lat_count - 1:
        next_hops()
    early = group * 11 // 16
    ends = []
    if len(up) < lat_count:
        for rows in (slice(0, early), slice(early, group)):
            ends.append([hop(up[-1][rows], "latent", 1, len(up) - 1), hop(down[-1][rows], "latent", -1, len(up) - 1)])

    def grads_of(here, names, grad, dec):
        slots, grad = piece_grad(here, hot, decoder, weight_places(names), block_size, grad)
        return grad, decoder_part(slots, code_slots, jnp.stack(places(names, 0)), half, dec)

    grad, dec = grads_of([[(errors,), (distant,)]], (0,), None, None)
    one_far, two_far, grad, dec, ends[:1] = lax.optimization_barrier((one_far, two_far, grad, dec, ends[:1]))
    three_a = flip(jnp.concatenate([two_near[:, :side], two_far[:, :side]]), "layer", 1)
    three_b = flip(jnp.concatenate([one_near[:, side:], one_far[:, side:]]), "layer", 2)
    grad, dec = grads_of([[(one_near,), (one_far,)], [(two_near,), (two_far,)]], (1, 2), grad, dec)

    ups, downs = [[part] for part in up], [[part] for part in down]
    if ends:
        ups.append([part[0] for part in ends])
        downs.append([part[1] for part in ends])
    terms_of = [[[acts]]] + [[downs[k], ups[lat_count - k]] for k in range(1, lat_count)]
    shards = [lax.rem(lat_here + k, lat_count) ^ lat_here for k in range(lat_count)]
    slotted = act_slots(terms_of, shards, hot, local_blocks)
    three_a, three_b, grad, dec, slotted = lax.optimization_barrier((three_a, three_b, grad, dec, slotted))
    grad, dec = grads_of([[(three_a, three_b)]], (3,), grad, dec)
    enc = encoder_part(pre_slots, grad, flip(grad, "dp", 1), slotted, capacity)
    return dec[None], enc[None]


def per_device(pre_codes, block_ids, activations, target, decoder):
    lat_count = lax.axis_size("latent")
    lay_count = lax.axis_size("layer")
    dp_count = lax.axis_size("dp")
    tok_count = activations.shape[1]
    model_width = activations.shape[2]
    active_count = block_ids.shape[2]
    block_size = pre_codes.shape[3]
    all_blocks = decoder.shape[1] // block_size * lat_count
    slots = 2 * tok_count * active_count // lat_count
    dense = (
        slots >= tok_count
        and dp_count == 2
        and active_count == 2
        and lay_count == 4
        and lat_count > 1
        and lat_count & (lat_count - 1) == 0
        and tok_count == block_size
        and lat_count * dp_count * 16 <= tok_count
        and model_width % (dp_count * 2 * lay_count * 128) == 0
        and all_blocks <= 256
        and 2 * tok_count * active_count == 8 * all_blocks
    )
    plan = dense_plan if dense else slot_plan
    return plan(pre_codes, block_ids, activations, target, decoder)


def solution(mesh):
    placed = (
        P("layer", ("latent", "dp"), None, None),
        P("layer", ("latent", "dp"), None),
        P("layer", ("latent", "dp"), None),
        P(("latent", "dp"), None),
        P("layer", "latent", None),
    )
    return jax.shard_map(
        per_device,
        mesh=mesh,
        in_specs=placed,
        out_specs=(P("layer", "latent", "dp"), P("layer", "latent", "dp")),
        check_vma=False,
    )
```

```python
import functools

import jax
import jax.numpy as jnp
from jax import lax
from jax.experimental import pallas as pl
from jax.experimental.pallas import tpu as pltpu
from jax.sharding import PartitionSpec as P

VMEM_BYTES = 40 * 1024 * 1024


def local_contrib(received_pre, weights, lat_count, local_blocks):
    code_vals = jnp.maximum(received_pre, jnp.zeros((), received_pre.dtype))
    slot_span = received_pre.shape[1]
    block_size = received_pre.shape[2]
    grouped = code_vals.reshape(lat_count, local_blocks, slot_span, block_size)
    contrib = jnp.einsum("sbcl,bld->sbcd", grouped, weights, preferred_element_type=jnp.float32)
    contrib = contrib.astype(jnp.bfloat16).reshape(
        lat_count * local_blocks, slot_span, weights.shape[2]
    )
    return lax.all_to_all(contrib, "latent", split_axis=0, concat_axis=0, tiled=True)


def slot_plan(pre_codes, block_ids, activations, target, decoder):
    lat_count = lax.axis_size("latent")
    tok_count = activations.shape[1]
    model_width = activations.shape[2]
    active_count = block_ids.shape[2]
    block_size = pre_codes.shape[3]
    lat_rows = decoder.shape[1]
    local_blocks = lat_rows // block_size
    all_blocks = local_blocks * lat_count
    capacity = 2 * tok_count * active_count // all_blocks
    slot_count = all_blocks * capacity
    pair_count = tok_count * active_count
    pair_block = block_ids[0].T.reshape(pair_count)
    member = (pair_block[:, None] == jnp.arange(all_blocks, dtype=jnp.int32)[None, :]).astype(
        jnp.int32
    )
    before = jnp.cumsum(member, axis=0) - member
    pair_rank = jnp.sum(before * member, axis=1)
    target_slot = pair_block * capacity + pair_rank
    slot_pair = (jnp.arange(slot_count, dtype=jnp.int32)[:, None] == target_slot[None, :]).astype(
        jnp.bfloat16
    )
    slot_token = jnp.sum(slot_pair.reshape(slot_count, active_count, tok_count), axis=1)
    pre_pairs = jnp.transpose(pre_codes[0], (1, 0, 2)).reshape(pair_count, block_size)
    pre_slots = jnp.dot(slot_pair, pre_pairs, preferred_element_type=jnp.float32).astype(
        jnp.bfloat16
    )
    pre_slots = pre_slots.reshape(all_blocks, capacity, block_size)
    inputs = activations[0]
    weights = decoder[0].reshape(local_blocks, block_size, model_width)
    input_slots = jnp.dot(slot_token, inputs, preferred_element_type=jnp.float32).astype(
        jnp.bfloat16
    )
    input_slots = input_slots.reshape(all_blocks, capacity, model_width)
    pieces = (
        lax.all_to_all(pre_slots, "latent", split_axis=0, concat_axis=0, tiled=True),
        lax.all_to_all(input_slots, "latent", split_axis=0, concat_axis=0, tiled=True),
    )
    returned = local_contrib(pieces[0], weights, lat_count, local_blocks)
    returned, received_pre, received_inputs = (returned, pieces[0], pieces[1])
    part_sum = jnp.einsum(
        "st,sd->td",
        slot_token,
        returned.reshape(slot_count, model_width),
        preferred_element_type=jnp.float32,
    )
    rebuilt = lax.psum(part_sum, "layer")
    errors = ((rebuilt - target.astype(jnp.float32)) / tok_count).astype(jnp.bfloat16)
    error_slots = jnp.dot(slot_token, errors, preferred_element_type=jnp.float32).astype(
        jnp.bfloat16
    )
    error_slots = error_slots.reshape(all_blocks, capacity, model_width)
    received_errors = lax.all_to_all(error_slots, "latent", split_axis=0, concat_axis=0, tiled=True)
    pre_blocks = received_pre.reshape(lat_count, local_blocks, capacity, block_size)
    code_blocks = jnp.maximum(pre_blocks, jnp.zeros((), pre_blocks.dtype))
    error_blocks = received_errors.reshape(lat_count, local_blocks, capacity, model_width)
    input_blocks = received_inputs.reshape(lat_count, local_blocks, capacity, model_width)
    code_grad = jnp.einsum(
        "sbcd,bld->sbcl", error_blocks, weights, preferred_element_type=jnp.float32
    )
    pre_grad = jnp.where(pre_blocks > 0, code_grad, jnp.zeros((), jnp.float32)).astype(jnp.bfloat16)
    dec_term = jnp.einsum(
        "sbcl,sbcd->bld", code_blocks, error_blocks, preferred_element_type=jnp.float32
    )
    enc_term = jnp.einsum(
        "sbcl,sbcd->bld", pre_grad, input_blocks, preferred_element_type=jnp.float32
    )
    dec_term = dec_term.reshape(lat_rows, model_width)
    enc_term = enc_term.reshape(lat_rows, model_width)
    dec_half, enc_half = (
        lax.psum_scatter(dec_term, "dp", scatter_dimension=1, tiled=True),
        lax.psum_scatter(enc_term, "dp", scatter_dimension=1, tiled=True),
    )
    return (dec_half.astype(jnp.bfloat16)[None], enc_half.astype(jnp.bfloat16)[None])


def flip(value, axis, bit):
    count = lax.axis_size(axis)
    return lax.ppermute(value, axis, [(i, i ^ bit) for i in range(count)])


def hop(value, axis, step, least):
    count = lax.axis_size(axis)
    if step > 0:
        pairs = [(i, i + 1) for i in range(least, count - 1)]
    else:
        pairs = [(i, i - 1) for i in range(1, count - least)]
    return lax.ppermute(value, axis, pairs)


def params():
    return pltpu.CompilerParams(vmem_limit_bytes=VMEM_BYTES)


def cost(microseconds):
    return pl.CostEstimate(flops=int(microseconds * 1.1e9), bytes_accessed=1, transcendentals=0)


def resident(shape):
    return pl.BlockSpec(shape, lambda i, s: (0,) * len(shape))


def gather_kernel(scalar_ref, source_ref, out_ref, token_ref):
    out_ref[...] = source_ref[...].reshape(out_ref.shape)
    token_ref[...] = jnp.zeros_like(token_ref)


def gather_columns(source, columns, width):
    rows = source.shape[-2]
    lead = (1,) * (source.ndim - 2)
    count = columns.shape[0]
    return pl.pallas_call(
        gather_kernel,
        out_shape=[
            jax.ShapeDtypeStruct((rows, count * width), source.dtype),
            jax.ShapeDtypeStruct((8, 128), jnp.float32),
        ],
        grid_spec=pltpu.PrefetchScalarGridSpec(
            num_scalar_prefetch=1,
            grid=(count,),
            in_specs=[pl.BlockSpec(lead + (rows, width), lambda i, s: (0,) * len(lead) + (0, s[i]))],
            out_specs=[pl.BlockSpec((rows, width), lambda i, s: (0, i)), resident((8, 128))],
        ),
        compiler_params=params(),
        cost_estimate=cost(0.9 * count),
        name="gather_columns",
    )(columns.astype(jnp.int32), source)


def codes_kernel(groups, blocks, scalar_ref, message_ref, codes, id_map, pre):
    tok = message_ref.shape[2]
    pad = message_ref.shape[1] - 2 * tok
    first = scalar_ref[0].astype(jnp.float32)
    rows = [message_ref[g, 2 * tok:2 * tok + pad, :].astype(jnp.float32) for g in range(groups)]
    fill = tok - groups * pad
    if fill:
        rows.append(jnp.zeros((fill, tok), jnp.float32))
    table = jnp.concatenate(rows, axis=0).T - first
    for g in range(groups):
        pre[g] = jnp.maximum(message_ref[g, 0:2 * tok, :], jnp.zeros((), jnp.bfloat16))
        for j in range(2):
            at = g * pad + j
            wide = jnp.broadcast_to(table[:, at:at + 1], (tok, tok))
            id_map[g, j * tok:(j + 1) * tok, :] = wide.astype(jnp.bfloat16)

    def block_step(b, carry):
        block = b.astype(jnp.float32).astype(jnp.bfloat16)
        at = pl.multiple_of(b * tok, tok)
        for g in range(groups):
            value = jnp.where(id_map[g, tok:2 * tok, :] == block, pre[g, tok:2 * tok, :], jnp.zeros((), jnp.bfloat16))
            value = jnp.where(id_map[g, 0:tok, :] == block, pre[g, 0:tok, :], value)
            codes[g * tok:(g + 1) * tok, pl.ds(at, tok)] = value
        return carry

    lax.fori_loop(0, blocks, block_step, 0)


def spread_codes(message, first, lat_rows):
    groups, _, tok = message.shape
    rows = groups * tok
    return pl.pallas_call(
        functools.partial(codes_kernel, groups, lat_rows // tok),
        out_shape=jax.ShapeDtypeStruct((rows, lat_rows), jnp.bfloat16),
        grid_spec=pltpu.PrefetchScalarGridSpec(
            num_scalar_prefetch=1,
            grid=(1,),
            in_specs=[resident(message.shape)],
            out_specs=resident((rows, lat_rows)),
            scratch_shapes=[
                pltpu.VMEM((groups, 2 * tok, tok), jnp.bfloat16),
                pltpu.VMEM((groups, 2 * tok, tok), jnp.bfloat16),
            ],
        ),
        compiler_params=params(),
        cost_estimate=cost(2.5),
        name="spread_codes",
    )(first[None].astype(jnp.int32), message)


def layer_sum_kernel(got_a, kept_a, far_a, got_b, kept_b, far_b, own_ref, *sent_refs):
    half = far_a.shape[1]
    rows = own_ref.shape[0]
    for side, (got, kept, far) in enumerate(((got_a, kept_a, far_a), (got_b, kept_b, far_b))):
        lanes = slice(side * half, (side + 1) * half)
        for n in range(1 + len(sent_refs)):
            at = slice(n * rows, (n + 1) * rows)
            total = got[at, :half].astype(jnp.float32) + kept[at, :half].astype(jnp.float32)
            total = total + far[at, :].astype(jnp.float32)
            if n:
                sent_refs[n - 1][:, lanes] = total.astype(jnp.bfloat16)
            else:
                own_ref[:, lanes] = total


def layer_sum(terms_a, terms_b, blocks):
    rows, half = terms_a[2].shape
    cut = (rows // blocks, 2 * half)
    return pl.pallas_call(
        layer_sum_kernel,
        out_shape=[jax.ShapeDtypeStruct(cut, jnp.float32)] + [jax.ShapeDtypeStruct(cut, jnp.bfloat16)] * (blocks - 1),
        grid=(1,),
        in_specs=[pl.BlockSpec((rows, half), lambda i: (0, 0)) for _ in range(6)],
        out_specs=[pl.BlockSpec(cut, lambda i: (0, 0))] * blocks,
        compiler_params=params(),
        cost_estimate=cost(0.5),
        name="layer_sum",
    )(*terms_a, *terms_b)


def join_kernel(count, *refs):
    out_ref = refs[-1]
    rows = out_ref.shape[0] // count
    for i in range(count):
        out_ref[i * rows:(i + 1) * rows] = refs[i][...]


def join(parts, *waited):
    shape = (len(parts) * parts[0].shape[0],) + parts[0].shape[1:]
    vmem = pl.BlockSpec(memory_space=pltpu.VMEM)
    return pl.pallas_call(
        functools.partial(join_kernel, len(parts)),
        out_shape=jax.ShapeDtypeStruct(shape, parts[0].dtype),
        in_specs=[vmem] * (len(parts) + len(waited)),
        out_specs=vmem,
        compiler_params=params(),
        cost_estimate=cost(0.4),
        name="join",
    )(*parts, *waited)


def slots_kernel(groups, blocks, cap, scalar_ref, message_ref, hot_ref, pre_ref, code_ref):
    tok = message_ref.shape[2]
    pad = message_ref.shape[1] - 2 * tok
    f32, bf16 = jnp.float32, jnp.bfloat16
    first = scalar_ref[0].astype(f32)
    rows = [message_ref[g, 2 * tok:2 * tok + pad, :].astype(f32) for g in range(groups)]
    fill = tok - groups * pad
    table = jnp.concatenate(rows + ([jnp.zeros((fill, tok), f32)] if fill else []), axis=0).T
    earlier = lax.broadcasted_iota(jnp.int32, (tok, tok), 0) < lax.broadcasted_iota(jnp.int32, (tok, tok), 1)
    per = 2 * cap
    for z in range(groups // 2):
        pre = 0.0
        hot = []
        for core in range(2):
            g = 2 * z + core
            lanes = [rows[g][j:j + 1] for j in range(2)]
            down = [table[:, g * pad + j:g * pad + j + 1] for j in range(2)]
            same = [jnp.where((down[j] == lanes[j]) & earlier, 1.0, 0.0) for j in range(2)]
            cross = jnp.where(down[0] == lanes[1], 1.0, 0.0)
            rank = [jnp.sum(same[0], axis=0, keepdims=True), jnp.sum(same[1] + cross, axis=0, keepdims=True)]
            here = []
            for j in range(2):
                block = lanes[j] - first
                slot = block * per + (core * cap + rank[j])
                slot = jnp.where((block >= 0) & (block < blocks), slot, -1.0)
                number = lax.broadcasted_iota(jnp.int32, (blocks * per, tok), 0).astype(f32)
                here.append(jnp.where(number == slot, 1.0, 0.0).astype(bf16))
                pre = pre + jnp.dot(
                    here[j], message_ref[g, j * tok:(j + 1) * tok, :], preferred_element_type=f32
                )
            hot.append(here[0] + here[1])
        hot_ref[z] = jnp.concatenate(hot, axis=1)
        for b in range(blocks):
            pre_ref[b, z * per:(z + 1) * per, :] = pre[b * per:(b + 1) * per].astype(bf16)
    for b in range(blocks):
        code_ref[b] = jnp.maximum(pre_ref[b].astype(f32), 0.0).T.astype(bf16)


def make_slots(message, first, lat_rows, cap):
    groups, _, tok = message.shape
    blocks = lat_rows // tok
    per = 2 * cap
    shards = groups // 2
    shapes = [(shards, blocks * per, 2 * tok), (blocks, shards * per, tok), (blocks, tok, shards * per)]
    return pl.pallas_call(
        functools.partial(slots_kernel, groups, blocks, cap),
        out_shape=[jax.ShapeDtypeStruct(shape, jnp.bfloat16) for shape in shapes],
        grid_spec=pltpu.PrefetchScalarGridSpec(
            num_scalar_prefetch=1,
            grid=(1,),
            in_specs=[resident(message.shape)],
            out_specs=[resident(shape) for shape in shapes],
        ),
        compiler_params=params(),
        cost_estimate=cost(1),
        name="make_slots",
    )(first[None].astype(jnp.int32), message)


def into_slots(hot, rows, out, z):
    per = out.shape[1] // hot.shape[0]
    value = jnp.dot(hot[z], rows, preferred_element_type=jnp.float32).astype(jnp.bfloat16)
    for b in range(out.shape[0]):
        out[b, z * per:(z + 1) * per, :] = value[b * per:(b + 1) * per]


def lanes_of(refs, rows):
    parts = [r[rows, :] for r in refs]
    return parts[0] if len(parts) == 1 else jnp.concatenate(parts, axis=1)


def piece_grad_kernel(layout, onto, scalar_ref, hot_ref, weight_ref, *refs):
    parts, (slots_ref, grad_ref) = refs[onto:-2], refs[-2:]
    blocks, _, size = grad_ref.shape
    group = hot_ref.shape[2]
    step = pl.program_id(0)

    @pl.when(step == 0)
    def _():
        grad_ref[...] = refs[0][...] if onto else jnp.zeros_like(grad_ref)

    at = 0
    for i, piece in enumerate(layout):
        z = 0
        for lanes in piece:
            here = parts[at:at + lanes]
            at += lanes
            for n in range(here[0].shape[0] // group):

                @pl.when(step == i)
                def _(z=z, n=n, here=here):
                    into_slots(hot_ref, lanes_of(here, slice(n * group, (n + 1) * group)), slots_ref.at[0], z)

                z += 1
    for b in range(blocks):
        grad_ref[b] += lax.dot_general(
            slots_ref[0, b],
            weight_ref[0, b * size:(b + 1) * size, :],
            (((1,), (1,)), ((), ())),
            preferred_element_type=jnp.float32,
        )


def piece_grad(pieces, hot, decoder, columns, size, held):
    lat_rows = decoder.shape[1]
    blocks = lat_rows // size
    slots = hot.shape[0] * hot.shape[1] // blocks
    width = sum(p.shape[1] for p in pieces[0][0])
    flat = [p for piece in pieces for row in piece for p in row]
    onto = [] if held is None else [held]
    return pl.pallas_call(
        functools.partial(piece_grad_kernel, [[len(row) for row in piece] for piece in pieces], len(onto)),
        out_shape=[
            jax.ShapeDtypeStruct((len(pieces), blocks, slots, width), jnp.bfloat16),
            jax.ShapeDtypeStruct((blocks, slots, size), jnp.float32),
        ],
        grid_spec=pltpu.PrefetchScalarGridSpec(
            num_scalar_prefetch=1,
            grid=(len(pieces),),
            in_specs=[resident(hot.shape), pl.BlockSpec((1, lat_rows, width), lambda i, s: (0, 0, s[i]))]
            + [resident(p.shape) for p in onto + flat],
            out_specs=[
                pl.BlockSpec((1, blocks, slots, width), lambda i, s: (i, 0, 0, 0)),
                resident((blocks, slots, size)),
            ],
        ),
        compiler_params=params(),
        cost_estimate=cost(0.8 + 2 * len(pieces)),
        name="piece_grad",
    )(columns.astype(jnp.int32), hot, decoder, *onto, *flat)


def decoder_kernel(skip, scalar_ref, code_ref, slots_ref, *refs):
    out_ref = refs[skip]
    size = code_ref.shape[1]
    for b in range(code_ref.shape[0]):
        out_ref[b * size:(b + 1) * size, :] = jnp.dot(
            code_ref[b], slots_ref[0, b], preferred_element_type=jnp.float32
        ).astype(jnp.bfloat16)


def decoder_part(slots, codes, columns, half, held):
    count, blocks, _, width = slots.shape
    lat_rows = blocks * codes.shape[1]
    onto = [] if held is None else [held]
    return pl.pallas_call(
        functools.partial(decoder_kernel, len(onto)),
        out_shape=jax.ShapeDtypeStruct((lat_rows, half), jnp.bfloat16),
        grid_spec=pltpu.PrefetchScalarGridSpec(
            num_scalar_prefetch=1,
            grid=(count,),
            in_specs=[resident(codes.shape), pl.BlockSpec((1,) + slots.shape[1:], lambda i, s: (i, 0, 0, 0))]
            + [pl.BlockSpec(memory_space=pl.ANY) for _ in onto],
            out_specs=pl.BlockSpec((lat_rows, width), lambda i, s: (0, s[i])),
        ),
        compiler_params=params(),
        input_output_aliases={3: 0} if onto else {},
        cost_estimate=cost(0.7 + 1.3 * count),
        name="decoder_part",
    )(columns.astype(jnp.int32), codes, slots, *onto)


def act_slots_kernel(layouts, scalar_ref, hot_ref, *refs):
    out_ref = refs[-1]
    per = out_ref.shape[1] // hot_ref.shape[0]
    at = 0
    for i, layout in enumerate(layouts):
        z = scalar_ref[i]
        total = None
        for count in layout:
            rows = [ref[...] for ref in refs[at:at + count]]
            rows = rows[0] if count == 1 else jnp.concatenate(rows, axis=0)
            total = rows if total is None else total + rows
            at += count
        value = jnp.dot(hot_ref[z], total, preferred_element_type=jnp.float32).astype(jnp.bfloat16)
        to = pl.ds(pl.multiple_of(z * per, per), per)
        for b in range(out_ref.shape[0]):
            out_ref[b, to, :] = value[b * per:(b + 1) * per]


def act_slots(terms_of, places, hot, count):
    half = terms_of[0][0][0].shape[1]
    slots = hot.shape[0] * hot.shape[1] // count
    tile = half // 4
    flat = [part for terms in terms_of for term in terms for part in term]
    return pl.pallas_call(
        functools.partial(act_slots_kernel, [[len(term) for term in terms] for terms in terms_of]),
        out_shape=jax.ShapeDtypeStruct((count, slots, half), jnp.bfloat16),
        grid_spec=pltpu.PrefetchScalarGridSpec(
            num_scalar_prefetch=1,
            grid=(4,),
            in_specs=[resident(hot.shape)] + [pl.BlockSpec((part.shape[0], tile), lambda i, s: (0, i)) for part in flat],
            out_specs=pl.BlockSpec((count, slots, tile), lambda i, s: (0, 0, i)),
        ),
        compiler_params=params(),
        cost_estimate=cost(3.3),
        name="act_slots",
    )(jnp.stack(places).astype(jnp.int32), hot, *flat)


def encoder_kernel(cap, shared, pre_ref, own_ref, theirs_ref, act_ref, out_ref):
    size = pre_ref.shape[2]
    for n in range(shared):
        parts = []
        for at in range(0, own_ref.shape[1], 2 * cap):
            for core in range(2):
                here = slice(at + core * cap, at + (core + 1) * cap)
                there = slice(at + (1 - core) * cap, at + (2 - core) * cap)
                parts.append(own_ref[n, here, :] + theirs_ref[n, there, :])
        total = jnp.concatenate(parts, axis=0)
        grad = jnp.where(pre_ref[n].astype(jnp.float32) > 0, total, 0.0).T.astype(jnp.bfloat16)
        out_ref[n * size:(n + 1) * size, :] = jnp.dot(
            grad, act_ref[n], preferred_element_type=jnp.float32
        ).astype(jnp.bfloat16)


def encoder_part(pre, own, theirs, acts, cap):
    blocks, slots, size = pre.shape
    half = acts.shape[2]
    shared = 2 if blocks % 2 == 0 else 1
    block = pl.BlockSpec((shared, slots, size), lambda i: (i, 0, 0))
    return pl.pallas_call(
        functools.partial(encoder_kernel, cap, shared),
        out_shape=jax.ShapeDtypeStruct((blocks * size, half), jnp.bfloat16),
        grid=(blocks // shared,),
        in_specs=[block, block, block, pl.BlockSpec((shared, slots, half), lambda i: (i, 0, 0))],
        out_specs=pl.BlockSpec((shared * size, half), lambda i: (i, 0)),
        compiler_params=params(),
        cost_estimate=cost(6.5),
        name="encoder_part",
    )(pre, own, theirs, acts)


def dense_plan(pre_codes, block_ids, activations, target, decoder):
    lay_count = lax.axis_size("layer")
    lat_count = lax.axis_size("latent")
    dp_count = lax.axis_size("dp")
    lay_here = lax.axis_index("layer")
    lat_here = lax.axis_index("latent")
    dp_here = lax.axis_index("dp")
    tok_count = activations.shape[1]
    model_width = activations.shape[2]
    active_count = block_ids.shape[2]
    block_size = pre_codes.shape[3]
    lat_rows = decoder.shape[1]
    local_blocks = lat_rows // block_size
    half = model_width // dp_count
    group = dp_count * tok_count
    tokens = lat_count * group
    width = half // lay_count
    side = width // 2
    f32, bf16 = jnp.float32, jnp.bfloat16
    first = lat_here * local_blocks
    capacity = 2 * tok_count * active_count // (local_blocks * lat_count)

    def columns(rows, which):
        return lax.dynamic_slice_in_dim(rows, which * half, half, axis=1)

    def places(names, offset, fine=1, sub=0):
        return [(offset + (lay_here ^ r)) * fine + sub for r in names]

    def weight_places(names):
        return jnp.stack(places(names, dp_here * lay_count))

    pre_rows = jnp.swapaxes(pre_codes[0], 0, 1).reshape(active_count * tok_count, block_size)
    id_rows = jnp.pad(block_ids[0].T, ((0, 16 - active_count), (0, 0))).astype(bf16)
    own = jnp.concatenate([pre_rows, id_rows], axis=0)
    at = places((1, 3), dp_here * lay_count, 2, 0) + places((2, 3), dp_here * lay_count, 2, 1)
    send_weights, token = gather_columns(decoder, jnp.stack(at), side)

    message = [own] + [flip(own, "latent", r) for r in range(1, lat_count)]

    own, inputs = lax.optimization_barrier((own, activations[0]))
    ups = [[columns(inputs, dp_here)]]
    downs = [[ups[0][0]]]
    ups.append([flip(columns(inputs, 1 - dp_here), "dp", 1)])
    downs.append([ups[1][0]])

    def next_hop(part):
        step = len(ups[part])
        ups[part].append(hop(ups[part][-1], "latent", 1, step - 1))
        downs[part].append(hop(downs[part][-1], "latent", -1, step - 1))

    next_hop(0)
    message = join(message, token)
    message, ups, downs = lax.optimization_barrier((message, ups, downs))
    message = message.reshape((lat_count,) + own.shape)
    message = jnp.stack([message, flip(message, "dp", 1)], axis=1)
    message = message.reshape(lat_count * dp_count, own.shape[0], block_size)
    next_hop(1)
    for part in range(2):
        if lat_count > 2:
            next_hop(part)

    codes = spread_codes(message, first, lat_rows)
    at = places((0, 2), dp_here * lay_count, 2, 0) + places((0, 1), dp_here * lay_count, 2, 1)
    at, codes, target = lax.optimization_barrier((jnp.stack(at), codes, target))
    keep_weights, _ = gather_columns(decoder, at, side)
    goals, _ = gather_columns(target, jnp.stack([which * lay_count + lay_here for which in (dp_here, 1 - dp_here)]), width)
    goals = jnp.concatenate([goals[:, :width], flip(goals[:, width:], "dp", 1)])

    codes = spread_codes(message, first, lat_rows)
    at = places((0, 2), dp_here * lay_count, 2, 0) + places((0, 1), dp_here * lay_count, 2, 1)
    at, codes, target = lax.optimization_barrier((jnp.stack(at), codes, target))
    keep_weights, _ = gather_columns(decoder, at, side)
    goals, _ = gather_columns(target, jnp.stack([which * lay_count + lay_here for which in (dp_here, 1 - dp_here)]), width)
    goals = jnp.concatenate([goals[:, :width], flip(goals[:, width:], "dp", 1)])

    def rows_for(spread, weights, n):
        return jnp.dot(spread, weights[:, n * width:(n + 1) * width], preferred_element_type=f32).astype(bf16)

    got = flip(rows_for(codes, send_weights, 0), "layer", 1), flip(rows_for(codes, send_weights, 1), "layer", 2)
    keep_codes, ups, downs = lax.optimization_barrier((codes, ups, downs))
    for step in range(3, lat_count):
        next_hop(0)
    kept = rows_for(keep_codes, keep_weights, 0), rows_for(keep_codes, keep_weights, 1)

    def add(one, two):
        return (one[:, side:].astype(f32) + two[:, side:].astype(f32)).astype(bf16)

    far = [flip(add(got[n], kept[n]), "layer", 2 - n) for n in range(2)]
    far, goals, ups, downs = lax.optimization_barrier((far, goals, ups, downs))

    total, *sent = layer_sum((got[0], kept[0], far[0]), (got[1], kept[1], far[1]), lat_count)
    for r in range(1, lat_count):
        total = total + flip(sent[r - 1], "latent", r).astype(f32)
    errors = ((total - goals.astype(f32)) / tok_count).astype(bf16)
    others = [flip(errors, "latent", r) for r in range(1, lat_count)]
    one_near, two_near = flip(errors, "layer", 1), flip(errors, "layer", 2)
    made = make_slots(message, first, lat_rows, capacity)
    one_near, two_near, others, ups, downs, made = lax.optimization_barrier(
        (one_near, two_near, others, ups, downs, made)
    )
    hot, pre_slots, code_slots = made
    distant = join(others)
    one_far, two_far = flip(distant, "layer", 1), flip(distant, "layer", 2)
    for step in range(3, lat_count):
        next_hop(1)

    def grads_of(here, names, grad, dec):
        slots, grad = piece_grad(here, hot, decoder, weight_places(names), block_size, grad)
        return grad, decoder_part(slots, code_slots, jnp.stack(places(names, 0)), half, dec)

    grad, dec = grads_of([[(errors,), (distant,)]], (0,), None, None)
    one_far, two_far, grad, dec, ups, downs = lax.optimization_barrier((one_far, two_far, grad, dec, ups, downs))
    three_a = flip(jnp.concatenate([two_near[:, :side], two_far[:, :side]]), "layer", 1)
    three_b = flip(jnp.concatenate([one_near[:, side:], one_far[:, side:]]), "layer", 2)
    grad, dec = grads_of([[(one_near,), (one_far,)], [(two_near,), (two_far,)]], (1, 2), grad, dec)

    terms_of = [[[ups[0][0], ups[1][0]]]]
    for k in range(1, lat_count):
        terms_of.append([[downs[part][k] for part in range(2)], [ups[part][lat_count - k] for part in range(2)]])
    shards = [lax.rem(lat_here + k, lat_count) ^ lat_here for k in range(lat_count)]
    slotted = act_slots(terms_of, shards, hot, local_blocks)
    three_a, three_b, grad, dec, slotted = lax.optimization_barrier((three_a, three_b, grad, dec, slotted))
    grad, dec = grads_of([[(three_a, three_b)]], (3,), grad, dec)
    enc = encoder_part(pre_slots, grad, flip(grad, "dp", 1), slotted, capacity)
    return dec[None], enc[None]


def per_device(pre_codes, block_ids, activations, target, decoder):
    lat_count = lax.axis_size("latent")
    lay_count = lax.axis_size("layer")
    dp_count = lax.axis_size("dp")
    tok_count = activations.shape[1]
    model_width = activations.shape[2]
    active_count = block_ids.shape[2]
    block_size = pre_codes.shape[3]
    all_blocks = decoder.shape[1] // block_size * lat_count
    slots = 2 * tok_count * active_count // lat_count
    dense = (
        slots >= tok_count
        and dp_count == 2
        and active_count == 2
        and lay_count == 4
        and lat_count > 1
        and lat_count & (lat_count - 1) == 0
        and tok_count == block_size
        and lat_count * dp_count * 16 <= tok_count
        and model_width % (dp_count * 2 * lay_count * 128) == 0
        and all_blocks <= 256
        and 2 * tok_count * active_count == 8 * all_blocks
    )
    plan = dense_plan if dense else slot_plan
    return plan(pre_codes, block_ids, activations, target, decoder)


def solution(mesh):
    placed = (
        P("layer", ("latent", "dp"), None, None),
        P("layer", ("latent", "dp"), None),
        P("layer", ("latent", "dp"), None),
        P(("latent", "dp"), None),
        P("layer", "latent", None),
    )
    return jax.shard_map(
        per_device,
        mesh=mesh,
        in_specs=placed,
        out_specs=(P("layer", "latent", "dp"), P("layer", "latent", "dp")),
        check_vma=False,
    )
```

```python
import functools

import jax
import jax.numpy as jnp
from jax import lax
from jax.experimental import pallas as pl
from jax.experimental.pallas import tpu as pltpu
from jax.sharding import PartitionSpec as P

VMEM_BYTES = 40 * 1024 * 1024


def local_contrib(received_pre, weights, lat_count, local_blocks):
    code_vals = jnp.maximum(received_pre, jnp.zeros((), received_pre.dtype))
    slot_span = received_pre.shape[1]
    block_size = received_pre.shape[2]
    grouped = code_vals.reshape(lat_count, local_blocks, slot_span, block_size)
    contrib = jnp.einsum("sbcl,bld->sbcd", grouped, weights, preferred_element_type=jnp.float32)
    contrib = contrib.astype(jnp.bfloat16).reshape(
        lat_count * local_blocks, slot_span, weights.shape[2]
    )
    return lax.all_to_all(contrib, "latent", split_axis=0, concat_axis=0, tiled=True)


def slot_plan(pre_codes, block_ids, activations, target, decoder):
    lat_count = lax.axis_size("latent")
    tok_count = activations.shape[1]
    model_width = activations.shape[2]
    active_count = block_ids.shape[2]
    block_size = pre_codes.shape[3]
    lat_rows = decoder.shape[1]
    local_blocks = lat_rows // block_size
    all_blocks = local_blocks * lat_count
    capacity = 2 * tok_count * active_count // all_blocks
    slot_count = all_blocks * capacity
    pair_count = tok_count * active_count
    pair_block = block_ids[0].T.reshape(pair_count)
    member = (pair_block[:, None] == jnp.arange(all_blocks, dtype=jnp.int32)[None, :]).astype(
        jnp.int32
    )
    before = jnp.cumsum(member, axis=0) - member
    pair_rank = jnp.sum(before * member, axis=1)
    target_slot = pair_block * capacity + pair_rank
    slot_pair = (jnp.arange(slot_count, dtype=jnp.int32)[:, None] == target_slot[None, :]).astype(
        jnp.bfloat16
    )
    slot_token = jnp.sum(slot_pair.reshape(slot_count, active_count, tok_count), axis=1)
    pre_pairs = jnp.transpose(pre_codes[0], (1, 0, 2)).reshape(pair_count, block_size)
    pre_slots = jnp.dot(slot_pair, pre_pairs, preferred_element_type=jnp.float32).astype(
        jnp.bfloat16
    )
    pre_slots = pre_slots.reshape(all_blocks, capacity, block_size)
    inputs = activations[0]
    weights = decoder[0].reshape(local_blocks, block_size, model_width)
    input_slots = jnp.dot(slot_token, inputs, preferred_element_type=jnp.float32).astype(
        jnp.bfloat16
    )
    input_slots = input_slots.reshape(all_blocks, capacity, model_width)
    pieces = (
        lax.all_to_all(pre_slots, "latent", split_axis=0, concat_axis=0, tiled=True),
        lax.all_to_all(input_slots, "latent", split_axis=0, concat_axis=0, tiled=True),
    )
    returned = local_contrib(pieces[0], weights, lat_count, local_blocks)
    returned, received_pre, received_inputs = (returned, pieces[0], pieces[1])
    part_sum = jnp.einsum(
        "st,sd->td",
        slot_token,
        returned.reshape(slot_count, model_width),
        preferred_element_type=jnp.float32,
    )
    rebuilt = lax.psum(part_sum, "layer")
    errors = ((rebuilt - target.astype(jnp.float32)) / tok_count).astype(jnp.bfloat16)
    error_slots = jnp.dot(slot_token, errors, preferred_element_type=jnp.float32).astype(
        jnp.bfloat16
    )
    error_slots = error_slots.reshape(all_blocks, capacity, model_width)
    received_errors = lax.all_to_all(error_slots, "latent", split_axis=0, concat_axis=0, tiled=True)
    pre_blocks = received_pre.reshape(lat_count, local_blocks, capacity, block_size)
    code_blocks = jnp.maximum(pre_blocks, jnp.zeros((), pre_blocks.dtype))
    error_blocks = received_errors.reshape(lat_count, local_blocks, capacity, model_width)
    input_blocks = received_inputs.reshape(lat_count, local_blocks, capacity, model_width)
    code_grad = jnp.einsum(
        "sbcd,bld->sbcl", error_blocks, weights, preferred_element_type=jnp.float32
    )
    pre_grad = jnp.where(pre_blocks > 0, code_grad, jnp.zeros((), jnp.float32)).astype(jnp.bfloat16)
    dec_term = jnp.einsum(
        "sbcl,sbcd->bld", code_blocks, error_blocks, preferred_element_type=jnp.float32
    )
    enc_term = jnp.einsum(
        "sbcl,sbcd->bld", pre_grad, input_blocks, preferred_element_type=jnp.float32
    )
    dec_term = dec_term.reshape(lat_rows, model_width)
    enc_term = enc_term.reshape(lat_rows, model_width)
    dec_half, enc_half = (
        lax.psum_scatter(dec_term, "dp", scatter_dimension=1, tiled=True),
        lax.psum_scatter(enc_term, "dp", scatter_dimension=1, tiled=True),
    )
    return (dec_half.astype(jnp.bfloat16)[None], enc_half.astype(jnp.bfloat16)[None])


def flip(value, axis, bit):
    count = lax.axis_size(axis)
    return lax.ppermute(value, axis, [(i, i ^ bit) for i in range(count)])


def hop(value, axis, step, least):
    count = lax.axis_size(axis)
    if step > 0:
        pairs = [(i, i + 1) for i in range(least, count - 1)]
    else:
        pairs = [(i, i - 1) for i in range(1, count - least)]
    return lax.ppermute(value, axis, pairs)


def params():
    return pltpu.CompilerParams(vmem_limit_bytes=VMEM_BYTES)


def cost(microseconds):
    return pl.CostEstimate(flops=int(microseconds * 1.1e9), bytes_accessed=1, transcendentals=0)


def resident(shape):
    return pl.BlockSpec(shape, lambda i, s: (0,) * len(shape))


def gather_kernel(scalar_ref, source_ref, out_ref, token_ref):
    out_ref[...] = source_ref[...].reshape(out_ref.shape)
    token_ref[...] = jnp.zeros_like(token_ref)


def gather_columns(source, columns, width):
    rows = source.shape[-2]
    lead = (1,) * (source.ndim - 2)
    count = columns.shape[0]
    return pl.pallas_call(
        gather_kernel,
        out_shape=[
            jax.ShapeDtypeStruct((rows, count * width), source.dtype),
            jax.ShapeDtypeStruct((8, 128), jnp.float32),
        ],
        grid_spec=pltpu.PrefetchScalarGridSpec(
            num_scalar_prefetch=1,
            grid=(count,),
            in_specs=[pl.BlockSpec(lead + (rows, width), lambda i, s: (0,) * len(lead) + (0, s[i]))],
            out_specs=[pl.BlockSpec((rows, width), lambda i, s: (0, i)), resident((8, 128))],
        ),
        compiler_params=params(),
        cost_estimate=cost(0.9 * count),
        name="gather_columns",
    )(columns.astype(jnp.int32), source)


def codes_kernel(groups, blocks, scalar_ref, message_ref, codes, id_map, pre):
    tok = message_ref.shape[2]
    pad = message_ref.shape[1] - 2 * tok
    first = scalar_ref[0].astype(jnp.float32)
    rows = [message_ref[g, 2 * tok:2 * tok + pad, :].astype(jnp.float32) for g in range(groups)]
    fill = tok - groups * pad
    if fill:
        rows.append(jnp.zeros((fill, tok), jnp.float32))
    table = jnp.concatenate(rows, axis=0).T - first
    for g in range(groups):
        pre[g] = jnp.maximum(message_ref[g, 0:2 * tok, :], jnp.zeros((), jnp.bfloat16))
        for j in range(2):
            at = g * pad + j
            wide = jnp.broadcast_to(table[:, at:at + 1], (tok, tok))
            id_map[g, j * tok:(j + 1) * tok, :] = wide.astype(jnp.bfloat16)

    def block_step(b, carry):
        block = b.astype(jnp.float32).astype(jnp.bfloat16)
        at = pl.multiple_of(b * tok, tok)
        for g in range(groups):
            value = jnp.where(id_map[g, tok:2 * tok, :] == block, pre[g, tok:2 * tok, :], jnp.zeros((), jnp.bfloat16))
            value = jnp.where(id_map[g, 0:tok, :] == block, pre[g, 0:tok, :], value)
            codes[g * tok:(g + 1) * tok, pl.ds(at, tok)] = value
        return carry

    lax.fori_loop(0, blocks, block_step, 0)


def spread_codes(message, first, lat_rows):
    groups, _, tok = message.shape
    rows = groups * tok
    return pl.pallas_call(
        functools.partial(codes_kernel, groups, lat_rows // tok),
        out_shape=jax.ShapeDtypeStruct((rows, lat_rows), jnp.bfloat16),
        grid_spec=pltpu.PrefetchScalarGridSpec(
            num_scalar_prefetch=1,
            grid=(1,),
            in_specs=[resident(message.shape)],
            out_specs=resident((rows, lat_rows)),
            scratch_shapes=[
                pltpu.VMEM((groups, 2 * tok, tok), jnp.bfloat16),
                pltpu.VMEM((groups, 2 * tok, tok), jnp.bfloat16),
            ],
        ),
        compiler_params=params(),
        cost_estimate=cost(2.5),
        name="spread_codes",
    )(first[None].astype(jnp.int32), message)


def layer_sum_kernel(got_a, kept_a, far_a, got_b, kept_b, far_b, own_ref, *sent_refs):
    half = far_a.shape[1]
    rows = own_ref.shape[0]
    for side, (got, kept, far) in enumerate(((got_a, kept_a, far_a), (got_b, kept_b, far_b))):
        lanes = slice(side * half, (side + 1) * half)
        for n in range(1 + len(sent_refs)):
            at = slice(n * rows, (n + 1) * rows)
            total = got[at, :half].astype(jnp.float32) + kept[at, :half].astype(jnp.float32)
            total = total + far[at, :].astype(jnp.float32)
            if n:
                sent_refs[n - 1][:, lanes] = total.astype(jnp.bfloat16)
            else:
                own_ref[:, lanes] = total


def layer_sum(terms_a, terms_b, blocks):
    rows, half = terms_a[2].shape
    cut = (rows // blocks, 2 * half)
    return pl.pallas_call(
        layer_sum_kernel,
        out_shape=[jax.ShapeDtypeStruct(cut, jnp.float32)] + [jax.ShapeDtypeStruct(cut, jnp.bfloat16)] * (blocks - 1),
        grid=(1,),
        in_specs=[pl.BlockSpec((rows, half), lambda i: (0, 0)) for _ in range(6)],
        out_specs=[pl.BlockSpec(cut, lambda i: (0, 0))] * blocks,
        compiler_params=params(),
        cost_estimate=cost(0.5),
        name="layer_sum",
    )(*terms_a, *terms_b)


def join_kernel(count, *refs):
    out_ref = refs[-1]
    rows = out_ref.shape[0] // count
    for i in range(count):
        out_ref[i * rows:(i + 1) * rows] = refs[i][...]


def join(parts, *waited):
    shape = (len(parts) * parts[0].shape[0],) + parts[0].shape[1:]
    vmem = pl.BlockSpec(memory_space=pltpu.VMEM)
    return pl.pallas_call(
        functools.partial(join_kernel, len(parts)),
        out_shape=jax.ShapeDtypeStruct(shape, parts[0].dtype),
        in_specs=[vmem] * (len(parts) + len(waited)),
        out_specs=vmem,
        compiler_params=params(),
        cost_estimate=cost(0.4),
        name="join",
    )(*parts, *waited)


def slots_kernel(groups, blocks, cap, scalar_ref, message_ref, hot_ref, pre_ref, code_ref):
    tok = message_ref.shape[2]
    pad = message_ref.shape[1] - 2 * tok
    f32, bf16 = jnp.float32, jnp.bfloat16
    first = scalar_ref[0].astype(f32)
    rows = [message_ref[g, 2 * tok:2 * tok + pad, :].astype(f32) for g in range(groups)]
    fill = tok - groups * pad
    table = jnp.concatenate(rows + ([jnp.zeros((fill, tok), f32)] if fill else []), axis=0).T
    earlier = lax.broadcasted_iota(jnp.int32, (tok, tok), 0) < lax.broadcasted_iota(jnp.int32, (tok, tok), 1)
    per = 2 * cap
    for z in range(groups // 2):
        pre = 0.0
        hot = []
        for core in range(2):
            g = 2 * z + core
            lanes = [rows[g][j:j + 1] for j in range(2)]
            down = [table[:, g * pad + j:g * pad + j + 1] for j in range(2)]
            same = [jnp.where((down[j] == lanes[j]) & earlier, 1.0, 0.0) for j in range(2)]
            cross = jnp.where(down[0] == lanes[1], 1.0, 0.0)
            rank = [jnp.sum(same[0], axis=0, keepdims=True), jnp.sum(same[1] + cross, axis=0, keepdims=True)]
            here = []
            for j in range(2):
                block = lanes[j] - first
                slot = block * per + (core * cap + rank[j])
                slot = jnp.where((block >= 0) & (block < blocks), slot, -1.0)
                number = lax.broadcasted_iota(jnp.int32, (blocks * per, tok), 0).astype(f32)
                here.append(jnp.where(number == slot, 1.0, 0.0).astype(bf16))
                pre = pre + jnp.dot(
                    here[j], message_ref[g, j * tok:(j + 1) * tok, :], preferred_element_type=f32
                )
            hot.append(here[0] + here[1])
        hot_ref[z] = jnp.concatenate(hot, axis=1)
        for b in range(blocks):
            pre_ref[b, z * per:(z + 1) * per, :] = pre[b * per:(b + 1) * per].astype(bf16)
    for b in range(blocks):
        code_ref[b] = jnp.maximum(pre_ref[b].astype(f32), 0.0).T.astype(bf16)


def make_slots(message, first, lat_rows, cap):
    groups, _, tok = message.shape
    blocks = lat_rows // tok
    per = 2 * cap
    shards = groups // 2
    shapes = [(shards, blocks * per, 2 * tok), (blocks, shards * per, tok), (blocks, tok, shards * per)]
    return pl.pallas_call(
        functools.partial(slots_kernel, groups, blocks, cap),
        out_shape=[jax.ShapeDtypeStruct(shape, jnp.bfloat16) for shape in shapes],
        grid_spec=pltpu.PrefetchScalarGridSpec(
            num_scalar_prefetch=1,
            grid=(1,),
            in_specs=[resident(message.shape)],
            out_specs=[resident(shape) for shape in shapes],
        ),
        compiler_params=params(),
        cost_estimate=cost(1),
        name="make_slots",
    )(first[None].astype(jnp.int32), message)


def into_slots(hot, rows, out, z):
    per = out.shape[1] // hot.shape[0]
    value = jnp.dot(hot[z], rows, preferred_element_type=jnp.float32).astype(jnp.bfloat16)
    for b in range(out.shape[0]):
        out[b, z * per:(z + 1) * per, :] = value[b * per:(b + 1) * per]


def lanes_of(refs, rows):
    parts = [r[rows, :] for r in refs]
    return parts[0] if len(parts) == 1 else jnp.concatenate(parts, axis=1)


def piece_grad_kernel(layout, onto, scalar_ref, hot_ref, weight_ref, *refs):
    parts, (slots_ref, grad_ref) = refs[onto:-2], refs[-2:]
    blocks, _, size = grad_ref.shape
    group = hot_ref.shape[2]
    step = pl.program_id(0)

    @pl.when(step == 0)
    def _():
        grad_ref[...] = refs[0][...] if onto else jnp.zeros_like(grad_ref)

    at = 0
    for i, piece in enumerate(layout):
        z = 0
        for lanes in piece:
            here = parts[at:at + lanes]
            at += lanes
            for n in range(here[0].shape[0] // group):

                @pl.when(step == i)
                def _(z=z, n=n, here=here):
                    into_slots(hot_ref, lanes_of(here, slice(n * group, (n + 1) * group)), slots_ref.at[0], z)

                z += 1
    for b in range(blocks):
        grad_ref[b] += lax.dot_general(
            slots_ref[0, b],
            weight_ref[0, b * size:(b + 1) * size, :],
            (((1,), (1,)), ((), ())),
            preferred_element_type=jnp.float32,
        )


def piece_grad(pieces, hot, decoder, columns, size, held):
    lat_rows = decoder.shape[1]
    blocks = lat_rows // size
    slots = hot.shape[0] * hot.shape[1] // blocks
    width = sum(p.shape[1] for p in pieces[0][0])
    flat = [p for piece in pieces for row in piece for p in row]
    onto = [] if held is None else [held]
    return pl.pallas_call(
        functools.partial(piece_grad_kernel, [[len(row) for row in piece] for piece in pieces], len(onto)),
        out_shape=[
            jax.ShapeDtypeStruct((len(pieces), blocks, slots, width), jnp.bfloat16),
            jax.ShapeDtypeStruct((blocks, slots, size), jnp.float32),
        ],
        grid_spec=pltpu.PrefetchScalarGridSpec(
            num_scalar_prefetch=1,
            grid=(len(pieces),),
            in_specs=[resident(hot.shape), pl.BlockSpec((1, lat_rows, width), lambda i, s: (0, 0, s[i]))]
            + [resident(p.shape) for p in onto + flat],
            out_specs=[
                pl.BlockSpec((1, blocks, slots, width), lambda i, s: (i, 0, 0, 0)),
                resident((blocks, slots, size)),
            ],
        ),
        compiler_params=params(),
        cost_estimate=cost(0.8 + 2 * len(pieces)),
        name="piece_grad",
    )(columns.astype(jnp.int32), hot, decoder, *onto, *flat)


def decoder_kernel(skip, scalar_ref, code_ref, slots_ref, *refs):
    out_ref = refs[skip]
    size = code_ref.shape[1]
    for b in range(code_ref.shape[0]):
        out_ref[b * size:(b + 1) * size, :] = jnp.dot(
            code_ref[b], slots_ref[0, b], preferred_element_type=jnp.float32
        ).astype(jnp.bfloat16)


def decoder_part(slots, codes, columns, half, held):
    count, blocks, _, width = slots.shape
    lat_rows = blocks * codes.shape[1]
    onto = [] if held is None else [held]
    return pl.pallas_call(
        functools.partial(decoder_kernel, len(onto)),
        out_shape=jax.ShapeDtypeStruct((lat_rows, half), jnp.bfloat16),
        grid_spec=pltpu.PrefetchScalarGridSpec(
            num_scalar_prefetch=1,
            grid=(count,),
            in_specs=[resident(codes.shape), pl.BlockSpec((1,) + slots.shape[1:], lambda i, s: (i, 0, 0, 0))]
            + [pl.BlockSpec(memory_space=pl.ANY) for _ in onto],
            out_specs=pl.BlockSpec((lat_rows, width), lambda i, s: (0, s[i])),
        ),
        compiler_params=params(),
        input_output_aliases={3: 0} if onto else {},
        cost_estimate=cost(0.7 + 1.3 * count),
        name="decoder_part",
    )(columns.astype(jnp.int32), codes, slots, *onto)


def act_slots_kernel(layouts, scalar_ref, hot_ref, *refs):
    out_ref = refs[-1]
    per = out_ref.shape[1] // hot_ref.shape[0]
    at = 0
    for i, layout in enumerate(layouts):
        z = scalar_ref[i]
        total = None
        for count in layout:
            rows = [ref[...] for ref in refs[at:at + count]]
            rows = rows[0] if count == 1 else jnp.concatenate(rows, axis=0)
            total = rows if total is None else total + rows
            at += count
        value = jnp.dot(hot_ref[z], total, preferred_element_type=jnp.float32).astype(jnp.bfloat16)
        to = pl.ds(pl.multiple_of(z * per, per), per)
        for b in range(out_ref.shape[0]):
            out_ref[b, to, :] = value[b * per:(b + 1) * per]


def act_slots(terms_of, places, hot, count):
    half = terms_of[0][0][0].shape[1]
    slots = hot.shape[0] * hot.shape[1] // count
    tile = half // 4
    flat = [part for terms in terms_of for term in terms for part in term]
    return pl.pallas_call(
        functools.partial(act_slots_kernel, [[len(term) for term in terms] for terms in terms_of]),
        out_shape=jax.ShapeDtypeStruct((count, slots, half), jnp.bfloat16),
        grid_spec=pltpu.PrefetchScalarGridSpec(
            num_scalar_prefetch=1,
            grid=(4,),
            in_specs=[resident(hot.shape)] + [pl.BlockSpec((part.shape[0], tile), lambda i, s: (0, i)) for part in flat],
            out_specs=pl.BlockSpec((count, slots, tile), lambda i, s: (0, 0, i)),
        ),
        compiler_params=params(),
        cost_estimate=cost(3.3),
        name="act_slots",
    )(jnp.stack(places).astype(jnp.int32), hot, *flat)


def encoder_kernel(cap, shared, pre_ref, own_ref, theirs_ref, act_ref, out_ref):
    size = pre_ref.shape[2]
    for n in range(shared):
        parts = []
        for at in range(0, own_ref.shape[1], 2 * cap):
            for core in range(2):
                here = slice(at + core * cap, at + (core + 1) * cap)
                there = slice(at + (1 - core) * cap, at + (2 - core) * cap)
                parts.append(own_ref[n, here, :] + theirs_ref[n, there, :])
        total = jnp.concatenate(parts, axis=0)
        grad = jnp.where(pre_ref[n].astype(jnp.float32) > 0, total, 0.0).T.astype(jnp.bfloat16)
        out_ref[n * size:(n + 1) * size, :] = jnp.dot(
            grad, act_ref[n], preferred_element_type=jnp.float32
        ).astype(jnp.bfloat16)


def encoder_part(pre, own, theirs, acts, cap):
    blocks, slots, size = pre.shape
    half = acts.shape[2]
    shared = 2 if blocks % 2 == 0 else 1
    block = pl.BlockSpec((shared, slots, size), lambda i: (i, 0, 0))
    return pl.pallas_call(
        functools.partial(encoder_kernel, cap, shared),
        out_shape=jax.ShapeDtypeStruct((blocks * size, half), jnp.bfloat16),
        grid=(blocks // shared,),
        in_specs=[block, block, block, pl.BlockSpec((shared, slots, half), lambda i: (i, 0, 0))],
        out_specs=pl.BlockSpec((shared * size, half), lambda i: (i, 0)),
        compiler_params=params(),
        cost_estimate=cost(6.5),
        name="encoder_part",
    )(pre, own, theirs, acts)


def dense_plan(pre_codes, block_ids, activations, target, decoder):
    lay_count = lax.axis_size("layer")
    lat_count = lax.axis_size("latent")
    dp_count = lax.axis_size("dp")
    lay_here = lax.axis_index("layer")
    lat_here = lax.axis_index("latent")
    dp_here = lax.axis_index("dp")
    tok_count = activations.shape[1]
    model_width = activations.shape[2]
    active_count = block_ids.shape[2]
    block_size = pre_codes.shape[3]
    lat_rows = decoder.shape[1]
    local_blocks = lat_rows // block_size
    half = model_width // dp_count
    group = dp_count * tok_count
    tokens = lat_count * group
    width = half // lay_count
    side = width // 2
    f32, bf16 = jnp.float32, jnp.bfloat16
    first = lat_here * local_blocks
    capacity = 2 * tok_count * active_count // (local_blocks * lat_count)

    def columns(rows, which):
        return lax.dynamic_slice_in_dim(rows, which * half, half, axis=1)

    def places(names, offset, fine=1, sub=0):
        return [(offset + (lay_here ^ r)) * fine + sub for r in names]

    def weight_places(names):
        return jnp.stack(places(names, dp_here * lay_count))

    pre_rows = jnp.swapaxes(pre_codes[0], 0, 1).reshape(active_count * tok_count, block_size)
    id_rows = jnp.pad(block_ids[0].T, ((0, 16 - active_count), (0, 0))).astype(bf16)
    own = jnp.concatenate([pre_rows, id_rows], axis=0)
    at = places((1, 3), dp_here * lay_count, 2, 0) + places((2, 3), dp_here * lay_count, 2, 1)
    send_weights, token = gather_columns(decoder, jnp.stack(at), side)

    message = [own] + [flip(own, "latent", r) for r in range(1, lat_count)]

    own, inputs = lax.optimization_barrier((own, activations[0]))
    acts = jnp.concatenate([columns(inputs, dp_here), flip(columns(inputs, 1 - dp_here), "dp", 1)])
    message, acts = lax.optimization_barrier((join(message, token), acts))
    message = message.reshape((lat_count,) + own.shape)
    up, down = [acts], [acts]

    def next_hops():
        step = len(up)
        up.append(hop(up[-1], "latent", 1, step - 1))
        down.append(hop(down[-1], "latent", -1, step - 1))

    message = jnp.stack([message, flip(message, "dp", 1)], axis=1)
    message = message.reshape(lat_count * dp_count, own.shape[0], block_size)
    next_hops()

    codes = spread_codes(message, first, lat_rows)
    at = places((0, 2), dp_here * lay_count, 2, 0) + places((0, 1), dp_here * lay_count, 2, 1)
    at, codes, target = lax.optimization_barrier((jnp.stack(at), codes, target))
    keep_weights, _ = gather_columns(decoder, at, side)
    goals, _ = gather_columns(target, jnp.stack([which * lay_count + lay_here for which in (dp_here, 1 - dp_here)]), width)
    goals = jnp.concatenate([goals[:, :width], flip(goals[:, width:], "dp", 1)])

    codes = spread_codes(message, first, lat_rows)
    at = places((0, 2), dp_here * lay_count, 2, 0) + places((0, 1), dp_here * lay_count, 2, 1)
    at, codes, target = lax.optimization_barrier((jnp.stack(at), codes, target))
    keep_weights, _ = gather_columns(decoder, at, side)
    goals, _ = gather_columns(target, jnp.stack([which * lay_count + lay_here for which in (dp_here, 1 - dp_here)]), width)
    goals = jnp.concatenate([goals[:, :width], flip(goals[:, width:], "dp", 1)])

    def rows_for(spread, weights, n):
        return jnp.dot(spread, weights[:, n * width:(n + 1) * width], preferred_element_type=f32).astype(bf16)

    got = flip(rows_for(codes, send_weights, 0), "layer", 1), flip(rows_for(codes, send_weights, 1), "layer", 2)
    keep_codes, up[1], down[1] = lax.optimization_barrier((codes, up[1], down[1]))
    if lat_count > 2:
        next_hops()
    kept = rows_for(keep_codes, keep_weights, 0), rows_for(keep_codes, keep_weights, 1)

    def add(one, two):
        return (one[:, side:].astype(f32) + two[:, side:].astype(f32)).astype(bf16)

    far = [flip(add(got[n], kept[n]), "layer", 2 - n) for n in range(2)]
    far, goals, up[-1], down[-1] = lax.optimization_barrier((far, goals, up[-1], down[-1]))
    while len(up) < lat_count - 1:
        next_hops()
    early = group * 11 // 16
    ends = []
    if len(up) < lat_count:
        ends = [(up[-1][rows], down[-1][rows]) for rows in (slice(0, early), slice(early, group))]

    total, *sent = layer_sum((got[0], kept[0], far[0]), (got[1], kept[1], far[1]), lat_count)
    for r in range(1, lat_count):
        total = total + flip(sent[r - 1], "latent", r).astype(f32)
    errors = ((total - goals.astype(f32)) / tok_count).astype(bf16)
    others = [flip(errors, "latent", r) for r in range(1, lat_count)]
    one_near, two_near = flip(errors, "layer", 1), flip(errors, "layer", 2)
    made = make_slots(message, first, lat_rows, capacity)
    one_near, two_near, others, ends, made = lax.optimization_barrier((one_near, two_near, others, ends, made))
    hot, pre_slots, code_slots = made
    distant = join(others)
    one_far, two_far = flip(distant, "layer", 1), flip(distant, "layer", 2)
    ends = [(hop(one, "latent", 1, len(up) - 1), hop(two, "latent", -1, len(up) - 1)) for one, two in ends]

    def grads_of(here, names, grad, dec):
        slots, grad = piece_grad(here, hot, decoder, weight_places(names), block_size, grad)
        return grad, decoder_part(slots, code_slots, jnp.stack(places(names, 0)), half, dec)

    grad, dec = grads_of([[(errors,), (distant,)]], (0,), None, None)
    one_far, two_far, grad, dec, ends[:1] = lax.optimization_barrier((one_far, two_far, grad, dec, ends[:1]))
    three_a = flip(jnp.concatenate([two_near[:, :side], two_far[:, :side]]), "layer", 1)
    three_b = flip(jnp.concatenate([one_near[:, side:], one_far[:, side:]]), "layer", 2)
    grad, dec = grads_of([[(one_near,), (one_far,)], [(two_near,), (two_far,)]], (1, 2), grad, dec)

    ups, downs = [[part] for part in up], [[part] for part in down]
    if ends:
        ups.append([part[0] for part in ends])
        downs.append([part[1] for part in ends])
    terms_of = [[[acts]]] + [[downs[k], ups[lat_count - k]] for k in range(1, lat_count)]
    shards = [lax.rem(lat_here + k, lat_count) ^ lat_here for k in range(lat_count)]
    slotted = act_slots(terms_of, shards, hot, local_blocks)
    three_a, three_b, grad, dec, slotted = lax.optimization_barrier((three_a, three_b, grad, dec, slotted))
    grad, dec = grads_of([[(three_a, three_b)]], (3,), grad, dec)
    enc = encoder_part(pre_slots, grad, flip(grad, "dp", 1), slotted, capacity)
    return dec[None], enc[None]


def per_device(pre_codes, block_ids, activations, target, decoder):
    lat_count = lax.axis_size("latent")
    lay_count = lax.axis_size("layer")
    dp_count = lax.axis_size("dp")
    tok_count = activations.shape[1]
    model_width = activations.shape[2]
    active_count = block_ids.shape[2]
    block_size = pre_codes.shape[3]
    all_blocks = decoder.shape[1] // block_size * lat_count
    slots = 2 * tok_count * active_count // lat_count
    dense = (
        slots >= tok_count
        and dp_count == 2
        and active_count == 2
        and lay_count == 4
        and lat_count > 1
        and lat_count & (lat_count - 1) == 0
        and tok_count == block_size
        and lat_count * dp_count * 16 <= tok_count
        and model_width % (dp_count * 2 * lay_count * 128) == 0
        and all_blocks <= 256
        and 2 * tok_count * active_count == 8 * all_blocks
    )
    plan = dense_plan if dense else slot_plan
    return plan(pre_codes, block_ids, activations, target, decoder)


def solution(mesh):
    placed = (
        P("layer", ("latent", "dp"), None, None),
        P("layer", ("latent", "dp"), None),
        P("layer", ("latent", "dp"), None),
        P(("latent", "dp"), None),
        P("layer", "latent", None),
    )
    return jax.shard_map(
        per_device,
        mesh=mesh,
        in_specs=placed,
        out_specs=(P("layer", "latent", "dp"), P("layer", "latent", "dp")),
        check_vma=False,
    )
```

```python
import functools

import jax
import jax.numpy as jnp
from jax import lax
from jax.experimental import pallas as pl
from jax.experimental.pallas import tpu as pltpu
from jax.sharding import PartitionSpec as P

VMEM_BYTES = 40 * 1024 * 1024


def local_contrib(received_pre, weights, lat_count, local_blocks):
    code_vals = jnp.maximum(received_pre, jnp.zeros((), received_pre.dtype))
    slot_span = received_pre.shape[1]
    block_size = received_pre.shape[2]
    grouped = code_vals.reshape(lat_count, local_blocks, slot_span, block_size)
    contrib = jnp.einsum("sbcl,bld->sbcd", grouped, weights, preferred_element_type=jnp.float32)
    contrib = contrib.astype(jnp.bfloat16).reshape(
        lat_count * local_blocks, slot_span, weights.shape[2]
    )
    return lax.all_to_all(contrib, "latent", split_axis=0, concat_axis=0, tiled=True)


def slot_plan(pre_codes, block_ids, activations, target, decoder):
    lat_count = lax.axis_size("latent")
    tok_count = activations.shape[1]
    model_width = activations.shape[2]
    active_count = block_ids.shape[2]
    block_size = pre_codes.shape[3]
    lat_rows = decoder.shape[1]
    local_blocks = lat_rows // block_size
    all_blocks = local_blocks * lat_count
    capacity = 2 * tok_count * active_count // all_blocks
    slot_count = all_blocks * capacity
    pair_count = tok_count * active_count
    pair_block = block_ids[0].T.reshape(pair_count)
    member = (pair_block[:, None] == jnp.arange(all_blocks, dtype=jnp.int32)[None, :]).astype(
        jnp.int32
    )
    before = jnp.cumsum(member, axis=0) - member
    pair_rank = jnp.sum(before * member, axis=1)
    target_slot = pair_block * capacity + pair_rank
    slot_pair = (jnp.arange(slot_count, dtype=jnp.int32)[:, None] == target_slot[None, :]).astype(
        jnp.bfloat16
    )
    slot_token = jnp.sum(slot_pair.reshape(slot_count, active_count, tok_count), axis=1)
    pre_pairs = jnp.transpose(pre_codes[0], (1, 0, 2)).reshape(pair_count, block_size)
    pre_slots = jnp.dot(slot_pair, pre_pairs, preferred_element_type=jnp.float32).astype(
        jnp.bfloat16
    )
    pre_slots = pre_slots.reshape(all_blocks, capacity, block_size)
    inputs = activations[0]
    weights = decoder[0].reshape(local_blocks, block_size, model_width)
    input_slots = jnp.dot(slot_token, inputs, preferred_element_type=jnp.float32).astype(
        jnp.bfloat16
    )
    input_slots = input_slots.reshape(all_blocks, capacity, model_width)
    pieces = (
        lax.all_to_all(pre_slots, "latent", split_axis=0, concat_axis=0, tiled=True),
        lax.all_to_all(input_slots, "latent", split_axis=0, concat_axis=0, tiled=True),
    )
    returned = local_contrib(pieces[0], weights, lat_count, local_blocks)
    returned, received_pre, received_inputs = (returned, pieces[0], pieces[1])
    part_sum = jnp.einsum(
        "st,sd->td",
        slot_token,
        returned.reshape(slot_count, model_width),
        preferred_element_type=jnp.float32,
    )
    rebuilt = lax.psum(part_sum, "layer")
    errors = ((rebuilt - target.astype(jnp.float32)) / tok_count).astype(jnp.bfloat16)
    error_slots = jnp.dot(slot_token, errors, preferred_element_type=jnp.float32).astype(
        jnp.bfloat16
    )
    error_slots = error_slots.reshape(all_blocks, capacity, model_width)
    received_errors = lax.all_to_all(error_slots, "latent", split_axis=0, concat_axis=0, tiled=True)
    pre_blocks = received_pre.reshape(lat_count, local_blocks, capacity, block_size)
    code_blocks = jnp.maximum(pre_blocks, jnp.zeros((), pre_blocks.dtype))
    error_blocks = received_errors.reshape(lat_count, local_blocks, capacity, model_width)
    input_blocks = received_inputs.reshape(lat_count, local_blocks, capacity, model_width)
    code_grad = jnp.einsum(
        "sbcd,bld->sbcl", error_blocks, weights, preferred_element_type=jnp.float32
    )
    pre_grad = jnp.where(pre_blocks > 0, code_grad, jnp.zeros((), jnp.float32)).astype(jnp.bfloat16)
    dec_term = jnp.einsum(
        "sbcl,sbcd->bld", code_blocks, error_blocks, preferred_element_type=jnp.float32
    )
    enc_term = jnp.einsum(
        "sbcl,sbcd->bld", pre_grad, input_blocks, preferred_element_type=jnp.float32
    )
    dec_term = dec_term.reshape(lat_rows, model_width)
    enc_term = enc_term.reshape(lat_rows, model_width)
    dec_half, enc_half = (
        lax.psum_scatter(dec_term, "dp", scatter_dimension=1, tiled=True),
        lax.psum_scatter(enc_term, "dp", scatter_dimension=1, tiled=True),
    )
    return (dec_half.astype(jnp.bfloat16)[None], enc_half.astype(jnp.bfloat16)[None])


def flip(value, axis, bit):
    count = lax.axis_size(axis)
    return lax.ppermute(value, axis, [(i, i ^ bit) for i in range(count)])


def hop(value, axis, step, least):
    count = lax.axis_size(axis)
    if step > 0:
        pairs = [(i, i + 1) for i in range(least, count - 1)]
    else:
        pairs = [(i, i - 1) for i in range(1, count - least)]
    return lax.ppermute(value, axis, pairs)


def params():
    return pltpu.CompilerParams(vmem_limit_bytes=VMEM_BYTES)


def cost(microseconds):
    return pl.CostEstimate(flops=int(microseconds * 1.1e9), bytes_accessed=1, transcendentals=0)


def resident(shape):
    return pl.BlockSpec(shape, lambda i, s: (0,) * len(shape))


def gather_kernel(scalar_ref, source_ref, out_ref, token_ref):
    out_ref[...] = source_ref[...].reshape(out_ref.shape)
    token_ref[...] = jnp.zeros_like(token_ref)


def gather_columns(source, columns, width):
    rows = source.shape[-2]
    lead = (1,) * (source.ndim - 2)
    count = columns.shape[0]
    return pl.pallas_call(
        gather_kernel,
        out_shape=[
            pltpu.HBM((rows, count * width), source.dtype),
            jax.ShapeDtypeStruct((8, 128), jnp.float32),
        ],
        grid_spec=pltpu.PrefetchScalarGridSpec(
            num_scalar_prefetch=1,
            grid=(count,),
            in_specs=[pl.BlockSpec(lead + (rows, width), lambda i, s: (0,) * len(lead) + (0, s[i]))],
            out_specs=[pl.BlockSpec((rows, width), lambda i, s: (0, i)), resident((8, 128))],
        ),
        compiler_params=params(),
        cost_estimate=cost(0.9 * count),
        name="gather_columns",
    )(columns.astype(jnp.int32), source)


def codes_kernel(groups, blocks, scalar_ref, message_ref, codes, id_map, pre):
    tok = message_ref.shape[2]
    pad = message_ref.shape[1] - 2 * tok
    first = scalar_ref[0].astype(jnp.float32)
    rows = [message_ref[g, 2 * tok:2 * tok + pad, :].astype(jnp.float32) for g in range(groups)]
    fill = tok - groups * pad
    if fill:
        rows.append(jnp.zeros((fill, tok), jnp.float32))
    table = jnp.concatenate(rows, axis=0).T - first
    for g in range(groups):
        pre[g] = jnp.maximum(message_ref[g, 0:2 * tok, :], jnp.zeros((), jnp.bfloat16))
        for j in range(2):
            at = g * pad + j
            wide = jnp.broadcast_to(table[:, at:at + 1], (tok, tok))
            id_map[g, j * tok:(j + 1) * tok, :] = wide.astype(jnp.bfloat16)

    def block_step(b, carry):
        block = b.astype(jnp.float32).astype(jnp.bfloat16)
        at = pl.multiple_of(b * tok, tok)
        for g in range(groups):
            value = jnp.where(id_map[g, tok:2 * tok, :] == block, pre[g, tok:2 * tok, :], jnp.zeros((), jnp.bfloat16))
            value = jnp.where(id_map[g, 0:tok, :] == block, pre[g, 0:tok, :], value)
            codes[g * tok:(g + 1) * tok, pl.ds(at, tok)] = value
        return carry

    lax.fori_loop(0, blocks, block_step, 0)


def spread_codes(message, first, lat_rows):
    groups, _, tok = message.shape
    rows = groups * tok
    return pl.pallas_call(
        functools.partial(codes_kernel, groups, lat_rows // tok),
        out_shape=jax.ShapeDtypeStruct((rows, lat_rows), jnp.bfloat16),
        grid_spec=pltpu.PrefetchScalarGridSpec(
            num_scalar_prefetch=1,
            grid=(1,),
            in_specs=[resident(message.shape)],
            out_specs=resident((rows, lat_rows)),
            scratch_shapes=[
                pltpu.VMEM((groups, 2 * tok, tok), jnp.bfloat16),
                pltpu.VMEM((groups, 2 * tok, tok), jnp.bfloat16),
            ],
        ),
        compiler_params=params(),
        cost_estimate=cost(2.5),
        name="spread_codes",
    )(first[None].astype(jnp.int32), message)


def layer_sum_kernel(got_a, kept_a, far_a, got_b, kept_b, far_b, own_ref, *sent_refs):
    half = far_a.shape[1]
    rows = own_ref.shape[0]
    for side, (got, kept, far) in enumerate(((got_a, kept_a, far_a), (got_b, kept_b, far_b))):
        lanes = slice(side * half, (side + 1) * half)
        for n in range(1 + len(sent_refs)):
            at = slice(n * rows, (n + 1) * rows)
            total = got[at, :half].astype(jnp.float32) + kept[at, :half].astype(jnp.float32)
            total = total + far[at, :].astype(jnp.float32)
            if n:
                sent_refs[n - 1][:, lanes] = total.astype(jnp.bfloat16)
            else:
                own_ref[:, lanes] = total


def layer_sum(terms_a, terms_b, blocks):
    rows, half = terms_a[2].shape
    cut = (rows // blocks, 2 * half)
    return pl.pallas_call(
        layer_sum_kernel,
        out_shape=[jax.ShapeDtypeStruct(cut, jnp.float32)] + [jax.ShapeDtypeStruct(cut, jnp.bfloat16)] * (blocks - 1),
        grid=(1,),
        in_specs=[pl.BlockSpec((rows, half), lambda i: (0, 0)) for _ in range(6)],
        out_specs=[pl.BlockSpec(cut, lambda i: (0, 0))] * blocks,
        compiler_params=params(),
        cost_estimate=cost(0.5),
        name="layer_sum",
    )(*terms_a, *terms_b)


def join_kernel(count, *refs):
    out_ref = refs[-1]
    rows = out_ref.shape[0] // count
    for i in range(count):
        out_ref[i * rows:(i + 1) * rows] = refs[i][...]


def join(parts, *waited):
    shape = (len(parts) * parts[0].shape[0],) + parts[0].shape[1:]
    vmem = pl.BlockSpec(memory_space=pltpu.VMEM)
    return pl.pallas_call(
        functools.partial(join_kernel, len(parts)),
        out_shape=jax.ShapeDtypeStruct(shape, parts[0].dtype),
        in_specs=[vmem] * (len(parts) + len(waited)),
        out_specs=vmem,
        compiler_params=params(),
        cost_estimate=cost(0.4),
        name="join",
    )(*parts, *waited)


def slots_kernel(groups, blocks, cap, scalar_ref, message_ref, hot_ref, pre_ref, code_ref):
    tok = message_ref.shape[2]
    pad = message_ref.shape[1] - 2 * tok
    f32, bf16 = jnp.float32, jnp.bfloat16
    first = scalar_ref[0].astype(f32)
    rows = [message_ref[g, 2 * tok:2 * tok + pad, :].astype(f32) for g in range(groups)]
    fill = tok - groups * pad
    table = jnp.concatenate(rows + ([jnp.zeros((fill, tok), f32)] if fill else []), axis=0).T
    earlier = lax.broadcasted_iota(jnp.int32, (tok, tok), 0) < lax.broadcasted_iota(jnp.int32, (tok, tok), 1)
    per = 2 * cap
    for z in range(groups // 2):
        pre = 0.0
        hot = []
        for core in range(2):
            g = 2 * z + core
            lanes = [rows[g][j:j + 1] for j in range(2)]
            down = [table[:, g * pad + j:g * pad + j + 1] for j in range(2)]
            same = [jnp.where((down[j] == lanes[j]) & earlier, 1.0, 0.0) for j in range(2)]
            cross = jnp.where(down[0] == lanes[1], 1.0, 0.0)
            rank = [jnp.sum(same[0], axis=0, keepdims=True), jnp.sum(same[1] + cross, axis=0, keepdims=True)]
            here = []
            for j in range(2):
                block = lanes[j] - first
                slot = block * per + (core * cap + rank[j])
                slot = jnp.where((block >= 0) & (block < blocks), slot, -1.0)
                number = lax.broadcasted_iota(jnp.int32, (blocks * per, tok), 0).astype(f32)
                here.append(jnp.where(number == slot, 1.0, 0.0).astype(bf16))
                pre = pre + jnp.dot(
                    here[j], message_ref[g, j * tok:(j + 1) * tok, :], preferred_element_type=f32
                )
            hot.append(here[0] + here[1])
        hot_ref[z] = jnp.concatenate(hot, axis=1)
        for b in range(blocks):
            pre_ref[b, z * per:(z + 1) * per, :] = pre[b * per:(b + 1) * per].astype(bf16)
    for b in range(blocks):
        code_ref[b] = jnp.maximum(pre_ref[b].astype(f32), 0.0).T.astype(bf16)


def make_slots(message, first, lat_rows, cap):
    groups, _, tok = message.shape
    blocks = lat_rows // tok
    per = 2 * cap
    shards = groups // 2
    shapes = [(shards, blocks * per, 2 * tok), (blocks, shards * per, tok), (blocks, tok, shards * per)]
    return pl.pallas_call(
        functools.partial(slots_kernel, groups, blocks, cap),
        out_shape=[jax.ShapeDtypeStruct(shape, jnp.bfloat16) for shape in shapes],
        grid_spec=pltpu.PrefetchScalarGridSpec(
            num_scalar_prefetch=1,
            grid=(1,),
            in_specs=[resident(message.shape)],
            out_specs=[resident(shape) for shape in shapes],
        ),
        compiler_params=params(),
        cost_estimate=cost(1),
        name="make_slots",
    )(first[None].astype(jnp.int32), message)


def into_slots(hot, rows, out, z):
    per = out.shape[1] // hot.shape[0]
    value = jnp.dot(hot[z], rows, preferred_element_type=jnp.float32).astype(jnp.bfloat16)
    for b in range(out.shape[0]):
        out[b, z * per:(z + 1) * per, :] = value[b * per:(b + 1) * per]


def lanes_of(refs, rows):
    parts = [r[rows, :] for r in refs]
    return parts[0] if len(parts) == 1 else jnp.concatenate(parts, axis=1)


def piece_grad_kernel(layout, onto, scalar_ref, hot_ref, weight_ref, *refs):
    parts, (slots_ref, grad_ref) = refs[onto:-2], refs[-2:]
    blocks, _, size = grad_ref.shape
    group = hot_ref.shape[2]
    step = pl.program_id(0)

    @pl.when(step == 0)
    def _():
        grad_ref[...] = refs[0][...] if onto else jnp.zeros_like(grad_ref)

    at = 0
    for i, piece in enumerate(layout):
        z = 0
        for lanes in piece:
            here = parts[at:at + lanes]
            at += lanes
            for n in range(here[0].shape[0] // group):

                @pl.when(step == i)
                def _(z=z, n=n, here=here):
                    into_slots(hot_ref, lanes_of(here, slice(n * group, (n + 1) * group)), slots_ref.at[0], z)

                z += 1
    for b in range(blocks):
        grad_ref[b] += lax.dot_general(
            slots_ref[0, b],
            weight_ref[0, b * size:(b + 1) * size, :],
            (((1,), (1,)), ((), ())),
            preferred_element_type=jnp.float32,
        )


def piece_grad(pieces, hot, decoder, columns, size, held):
    lat_rows = decoder.shape[1]
    blocks = lat_rows // size
    slots = hot.shape[0] * hot.shape[1] // blocks
    width = sum(p.shape[1] for p in pieces[0][0])
    flat = [p for piece in pieces for row in piece for p in row]
    onto = [] if held is None else [held]
    return pl.pallas_call(
        functools.partial(piece_grad_kernel, [[len(row) for row in piece] for piece in pieces], len(onto)),
        out_shape=[
            jax.ShapeDtypeStruct((len(pieces), blocks, slots, width), jnp.bfloat16),
            jax.ShapeDtypeStruct((blocks, slots, size), jnp.float32),
        ],
        grid_spec=pltpu.PrefetchScalarGridSpec(
            num_scalar_prefetch=1,
            grid=(len(pieces),),
            in_specs=[resident(hot.shape), pl.BlockSpec((1, lat_rows, width), lambda i, s: (0, 0, s[i]))]
            + [resident(p.shape) for p in onto + flat],
            out_specs=[
                pl.BlockSpec((1, blocks, slots, width), lambda i, s: (i, 0, 0, 0)),
                resident((blocks, slots, size)),
            ],
        ),
        compiler_params=params(),
        cost_estimate=cost(0.8 + 2 * len(pieces)),
        name="piece_grad",
    )(columns.astype(jnp.int32), hot, decoder, *onto, *flat)


def decoder_kernel(skip, scalar_ref, code_ref, slots_ref, *refs):
    out_ref = refs[skip]
    size = code_ref.shape[1]
    for b in range(code_ref.shape[0]):
        out_ref[b * size:(b + 1) * size, :] = jnp.dot(
            code_ref[b], slots_ref[0, b], preferred_element_type=jnp.float32
        ).astype(jnp.bfloat16)


def decoder_part(slots, codes, columns, half, held):
    count, blocks, _, width = slots.shape
    lat_rows = blocks * codes.shape[1]
    onto = [] if held is None else [held]
    return pl.pallas_call(
        functools.partial(decoder_kernel, len(onto)),
        out_shape=jax.ShapeDtypeStruct((lat_rows, half), jnp.bfloat16),
        grid_spec=pltpu.PrefetchScalarGridSpec(
            num_scalar_prefetch=1,
            grid=(count,),
            in_specs=[resident(codes.shape), pl.BlockSpec((1,) + slots.shape[1:], lambda i, s: (i, 0, 0, 0))]
            + [pl.BlockSpec(memory_space=pl.ANY) for _ in onto],
            out_specs=pl.BlockSpec((lat_rows, width), lambda i, s: (0, s[i])),
        ),
        compiler_params=params(),
        input_output_aliases={3: 0} if onto else {},
        cost_estimate=cost(0.7 + 1.3 * count),
        name="decoder_part",
    )(columns.astype(jnp.int32), codes, slots, *onto)


def act_slots_kernel(layouts, scalar_ref, hot_ref, *refs):
    out_ref = refs[-1]
    per = out_ref.shape[1] // hot_ref.shape[0]
    at = 0
    for i, layout in enumerate(layouts):
        z = scalar_ref[i]
        total = None
        for count in layout:
            rows = [ref[...] for ref in refs[at:at + count]]
            rows = rows[0] if count == 1 else jnp.concatenate(rows, axis=0)
            total = rows if total is None else total + rows
            at += count
        value = jnp.dot(hot_ref[z], total, preferred_element_type=jnp.float32).astype(jnp.bfloat16)
        to = pl.ds(pl.multiple_of(z * per, per), per)
        for b in range(out_ref.shape[0]):
            out_ref[b, to, :] = value[b * per:(b + 1) * per]


def act_slots(terms_of, places, hot, count):
    half = terms_of[0][0][0].shape[1]
    slots = hot.shape[0] * hot.shape[1] // count
    tile = half // 4
    flat = [part for terms in terms_of for term in terms for part in term]
    return pl.pallas_call(
        functools.partial(act_slots_kernel, [[len(term) for term in terms] for terms in terms_of]),
        out_shape=jax.ShapeDtypeStruct((count, slots, half), jnp.bfloat16),
        grid_spec=pltpu.PrefetchScalarGridSpec(
            num_scalar_prefetch=1,
            grid=(4,),
            in_specs=[resident(hot.shape)] + [pl.BlockSpec((part.shape[0], tile), lambda i, s: (0, i)) for part in flat],
            out_specs=pl.BlockSpec((count, slots, tile), lambda i, s: (0, 0, i)),
        ),
        compiler_params=params(),
        cost_estimate=cost(3.3),
        name="act_slots",
    )(jnp.stack(places).astype(jnp.int32), hot, *flat)


def encoder_kernel(cap, shared, pre_ref, own_ref, theirs_ref, act_ref, out_ref):
    size = pre_ref.shape[2]
    for n in range(shared):
        parts = []
        for at in range(0, own_ref.shape[1], 2 * cap):
            for core in range(2):
                here = slice(at + core * cap, at + (core + 1) * cap)
                there = slice(at + (1 - core) * cap, at + (2 - core) * cap)
                parts.append(own_ref[n, here, :] + theirs_ref[n, there, :])
        total = jnp.concatenate(parts, axis=0)
        grad = jnp.where(pre_ref[n].astype(jnp.float32) > 0, total, 0.0).T.astype(jnp.bfloat16)
        out_ref[n * size:(n + 1) * size, :] = jnp.dot(
            grad, act_ref[n], preferred_element_type=jnp.float32
        ).astype(jnp.bfloat16)


def encoder_part(pre, own, theirs, acts, cap):
    blocks, slots, size = pre.shape
    half = acts.shape[2]
    shared = 2 if blocks % 2 == 0 else 1
    block = pl.BlockSpec((shared, slots, size), lambda i: (i, 0, 0))
    return pl.pallas_call(
        functools.partial(encoder_kernel, cap, shared),
        out_shape=jax.ShapeDtypeStruct((blocks * size, half), jnp.bfloat16),
        grid=(blocks // shared,),
        in_specs=[block, block, block, pl.BlockSpec((shared, slots, half), lambda i: (i, 0, 0))],
        out_specs=pl.BlockSpec((shared * size, half), lambda i: (i, 0)),
        compiler_params=params(),
        cost_estimate=cost(6.5),
        name="encoder_part",
    )(pre, own, theirs, acts)


def dense_plan(pre_codes, block_ids, activations, target, decoder):
    lay_count = lax.axis_size("layer")
    lat_count = lax.axis_size("latent")
    dp_count = lax.axis_size("dp")
    lay_here = lax.axis_index("layer")
    lat_here = lax.axis_index("latent")
    dp_here = lax.axis_index("dp")
    tok_count = activations.shape[1]
    model_width = activations.shape[2]
    active_count = block_ids.shape[2]
    block_size = pre_codes.shape[3]
    lat_rows = decoder.shape[1]
    local_blocks = lat_rows // block_size
    half = model_width // dp_count
    group = dp_count * tok_count
    tokens = lat_count * group
    width = half // lay_count
    side = width // 2
    f32, bf16 = jnp.float32, jnp.bfloat16
    first = lat_here * local_blocks
    capacity = 2 * tok_count * active_count // (local_blocks * lat_count)

    def columns(rows, which):
        return lax.dynamic_slice_in_dim(rows, which * half, half, axis=1)

    def places(names, offset, fine=1, sub=0):
        return [(offset + (lay_here ^ r)) * fine + sub for r in names]

    def weight_places(names):
        return jnp.stack(places(names, dp_here * lay_count))

    pre_rows = jnp.swapaxes(pre_codes[0], 0, 1).reshape(active_count * tok_count, block_size)
    id_rows = jnp.pad(block_ids[0].T, ((0, 16 - active_count), (0, 0))).astype(bf16)
    own = jnp.concatenate([pre_rows, id_rows], axis=0)
    at = places((1, 3), dp_here * lay_count, 2, 0) + places((2, 3), dp_here * lay_count, 2, 1)
    send_weights, token = gather_columns(decoder, jnp.stack(at), side)

    message = [own] + [flip(own, "latent", r) for r in range(1, lat_count)]

    own, inputs = lax.optimization_barrier((own, activations[0]))
    acts = jnp.concatenate([columns(inputs, dp_here), flip(columns(inputs, 1 - dp_here), "dp", 1)])
    message, acts = lax.optimization_barrier((join(message, token), acts))
    message = message.reshape((lat_count,) + own.shape)
    up, down = [acts], [acts]

    def next_hops():
        step = len(up)
        up.append(hop(up[-1], "latent", 1, step - 1))
        down.append(hop(down[-1], "latent", -1, step - 1))

    message = jnp.stack([message, flip(message, "dp", 1)], axis=1)
    message = message.reshape(lat_count * dp_count, own.shape[0], block_size)
    next_hops()

    codes = spread_codes(message, first, lat_rows)
    at = places((0, 2), dp_here * lay_count, 2, 0) + places((0, 1), dp_here * lay_count, 2, 1)
    at, codes, target = lax.optimization_barrier((jnp.stack(at), codes, target))
    keep_weights, _ = gather_columns(decoder, at, side)
    goals, _ = gather_columns(target, jnp.stack([which * lay_count + lay_here for which in (dp_here, 1 - dp_here)]), width)
    goals = jnp.concatenate([goals[:, :width], flip(goals[:, width:], "dp", 1)])

    codes = spread_codes(message, first, lat_rows)
    at = places((0, 2), dp_here * lay_count, 2, 0) + places((0, 1), dp_here * lay_count, 2, 1)
    at, codes, target = lax.optimization_barrier((jnp.stack(at), codes, target))
    keep_weights, _ = gather_columns(decoder, at, side)
    goals, _ = gather_columns(target, jnp.stack([which * lay_count + lay_here for which in (dp_here, 1 - dp_here)]), width)
    goals = jnp.concatenate([goals[:, :width], flip(goals[:, width:], "dp", 1)])

    def rows_for(spread, weights, n):
        return jnp.dot(spread, weights[:, n * width:(n + 1) * width], preferred_element_type=f32).astype(bf16)

    got = flip(rows_for(codes, send_weights, 0), "layer", 1), flip(rows_for(codes, send_weights, 1), "layer", 2)
    keep_codes, up[1], down[1] = lax.optimization_barrier((codes, up[1], down[1]))
    if lat_count > 2:
        next_hops()
    kept = rows_for(keep_codes, keep_weights, 0), rows_for(keep_codes, keep_weights, 1)

    def add(one, two):
        return (one[:, side:].astype(f32) + two[:, side:].astype(f32)).astype(bf16)

    far = [flip(add(got[n], kept[n]), "layer", 2 - n) for n in range(2)]
    made = make_slots(message, first, lat_rows, capacity)
    far, goals, up[-1], down[-1], made = lax.optimization_barrier((far, goals, up[-1], down[-1], made))
    while len(up) < lat_count - 1:
        next_hops()
    early = group * 3 // 8
    ends = []
    if len(up) < lat_count:
        ends = [(up[-1][rows], down[-1][rows]) for rows in (slice(0, early), slice(early, group))]

    total, *sent = layer_sum((got[0], kept[0], far[0]), (got[1], kept[1], far[1]), lat_count)
    for r in range(1, lat_count):
        total = total + flip(sent[r - 1], "latent", r).astype(f32)
    errors = ((total - goals.astype(f32)) / tok_count).astype(bf16)
    others = [flip(errors, "latent", r) for r in range(1, lat_count)]
    one_near, two_near = flip(errors, "layer", 1), flip(errors, "layer", 2)
    ends, others, two_near, one_near = lax.optimization_barrier((ends, others[::-1], two_near, one_near))
    others = others[::-1]
    hot, pre_slots, code_slots = made
    distant = join(others)
    one_far, two_far = flip(distant, "layer", 1), flip(distant, "layer", 2)
    ends = [(hop(one, "latent", 1, len(up) - 1), hop(two, "latent", -1, len(up) - 1)) for one, two in ends]

    def grads_of(here, names, grad, dec):
        slots, grad = piece_grad(here, hot, decoder, weight_places(names), block_size, grad)
        return grad, decoder_part(slots, code_slots, jnp.stack(places(names, 0)), half, dec)

    grad, dec = grads_of([[(errors,), (distant,)]], (0,), None, None)
    one_far, two_far, grad, dec, ends[:1] = lax.optimization_barrier((one_far, two_far, grad, dec, ends[:1]))
    three_a = flip(jnp.concatenate([two_near[:, :side], two_far[:, :side]]), "layer", 1)
    three_b = flip(jnp.concatenate([one_near[:, side:], one_far[:, side:]]), "layer", 2)
    grad, dec = grads_of([[(one_near,), (one_far,)], [(two_near,), (two_far,)]], (1, 2), grad, dec)

    ups, downs = [[part] for part in up], [[part] for part in down]
    if ends:
        ups.append([part[0] for part in ends])
        downs.append([part[1] for part in ends])
    terms_of = [[[acts]]] + [[downs[k], ups[lat_count - k]] for k in range(1, lat_count)]
    shards = [lax.rem(lat_here + k, lat_count) ^ lat_here for k in range(lat_count)]
    slotted = act_slots(terms_of, shards, hot, local_blocks)
    three_a, three_b, grad, dec, slotted = lax.optimization_barrier((three_a, three_b, grad, dec, slotted))
    grad, dec = grads_of([[(three_a, three_b)]], (3,), grad, dec)
    enc = encoder_part(pre_slots, grad, flip(grad, "dp", 1), slotted, capacity)
    return dec[None], enc[None]


def per_device(pre_codes, block_ids, activations, target, decoder):
    lat_count = lax.axis_size("latent")
    lay_count = lax.axis_size("layer")
    dp_count = lax.axis_size("dp")
    tok_count = activations.shape[1]
    model_width = activations.shape[2]
    active_count = block_ids.shape[2]
    block_size = pre_codes.shape[3]
    all_blocks = decoder.shape[1] // block_size * lat_count
    slots = 2 * tok_count * active_count // lat_count
    dense = (
        slots >= tok_count
        and dp_count == 2
        and active_count == 2
        and lay_count == 4
        and lat_count > 1
        and lat_count & (lat_count - 1) == 0
        and tok_count == block_size
        and lat_count * dp_count * 16 <= tok_count
        and model_width % (dp_count * 2 * lay_count * 128) == 0
        and all_blocks <= 256
        and 2 * tok_count * active_count == 8 * all_blocks
    )
    plan = dense_plan if dense else slot_plan
    return plan(pre_codes, block_ids, activations, target, decoder)


def solution(mesh):
    placed = (
        P("layer", ("latent", "dp"), None, None),
        P("layer", ("latent", "dp"), None),
        P("layer", ("latent", "dp"), None),
        P(("latent", "dp"), None),
        P("layer", "latent", None),
    )
    return jax.shard_map(
        per_device,
        mesh=mesh,
        in_specs=placed,
        out_specs=(P("layer", "latent", "dp"), P("layer", "latent", "dp")),
        check_vma=False,
    )
```

```python
import functools

import jax
import jax.numpy as jnp
from jax import lax
from jax.experimental import pallas as pl
from jax.experimental.pallas import tpu as pltpu
from jax.sharding import PartitionSpec as P

VMEM_BYTES = 40 * 1024 * 1024


def local_contrib(received_pre, weights, lat_count, local_blocks):
    code_vals = jnp.maximum(received_pre, jnp.zeros((), received_pre.dtype))
    slot_span = received_pre.shape[1]
    block_size = received_pre.shape[2]
    grouped = code_vals.reshape(lat_count, local_blocks, slot_span, block_size)
    contrib = jnp.einsum("sbcl,bld->sbcd", grouped, weights, preferred_element_type=jnp.float32)
    contrib = contrib.astype(jnp.bfloat16).reshape(
        lat_count * local_blocks, slot_span, weights.shape[2]
    )
    return lax.all_to_all(contrib, "latent", split_axis=0, concat_axis=0, tiled=True)


def slot_plan(pre_codes, block_ids, activations, target, decoder):
    lat_count = lax.axis_size("latent")
    tok_count = activations.shape[1]
    model_width = activations.shape[2]
    active_count = block_ids.shape[2]
    block_size = pre_codes.shape[3]
    lat_rows = decoder.shape[1]
    local_blocks = lat_rows // block_size
    all_blocks = local_blocks * lat_count
    capacity = 2 * tok_count * active_count // all_blocks
    slot_count = all_blocks * capacity
    pair_count = tok_count * active_count
    pair_block = block_ids[0].T.reshape(pair_count)
    member = (pair_block[:, None] == jnp.arange(all_blocks, dtype=jnp.int32)[None, :]).astype(
        jnp.int32
    )
    before = jnp.cumsum(member, axis=0) - member
    pair_rank = jnp.sum(before * member, axis=1)
    target_slot = pair_block * capacity + pair_rank
    slot_pair = (jnp.arange(slot_count, dtype=jnp.int32)[:, None] == target_slot[None, :]).astype(
        jnp.bfloat16
    )
    slot_token = jnp.sum(slot_pair.reshape(slot_count, active_count, tok_count), axis=1)
    pre_pairs = jnp.transpose(pre_codes[0], (1, 0, 2)).reshape(pair_count, block_size)
    pre_slots = jnp.dot(slot_pair, pre_pairs, preferred_element_type=jnp.float32).astype(
        jnp.bfloat16
    )
    pre_slots = pre_slots.reshape(all_blocks, capacity, block_size)
    inputs = activations[0]
    weights = decoder[0].reshape(local_blocks, block_size, model_width)
    input_slots = jnp.dot(slot_token, inputs, preferred_element_type=jnp.float32).astype(
        jnp.bfloat16
    )
    input_slots = input_slots.reshape(all_blocks, capacity, model_width)
    pieces = (
        lax.all_to_all(pre_slots, "latent", split_axis=0, concat_axis=0, tiled=True),
        lax.all_to_all(input_slots, "latent", split_axis=0, concat_axis=0, tiled=True),
    )
    returned = local_contrib(pieces[0], weights, lat_count, local_blocks)
    returned, received_pre, received_inputs = (returned, pieces[0], pieces[1])
    part_sum = jnp.einsum(
        "st,sd->td",
        slot_token,
        returned.reshape(slot_count, model_width),
        preferred_element_type=jnp.float32,
    )
    rebuilt = lax.psum(part_sum, "layer")
    errors = ((rebuilt - target.astype(jnp.float32)) / tok_count).astype(jnp.bfloat16)
    error_slots = jnp.dot(slot_token, errors, preferred_element_type=jnp.float32).astype(
        jnp.bfloat16
    )
    error_slots = error_slots.reshape(all_blocks, capacity, model_width)
    received_errors = lax.all_to_all(error_slots, "latent", split_axis=0, concat_axis=0, tiled=True)
    pre_blocks = received_pre.reshape(lat_count, local_blocks, capacity, block_size)
    code_blocks = jnp.maximum(pre_blocks, jnp.zeros((), pre_blocks.dtype))
    error_blocks = received_errors.reshape(lat_count, local_blocks, capacity, model_width)
    input_blocks = received_inputs.reshape(lat_count, local_blocks, capacity, model_width)
    code_grad = jnp.einsum(
        "sbcd,bld->sbcl", error_blocks, weights, preferred_element_type=jnp.float32
    )
    pre_grad = jnp.where(pre_blocks > 0, code_grad, jnp.zeros((), jnp.float32)).astype(jnp.bfloat16)
    dec_term = jnp.einsum(
        "sbcl,sbcd->bld", code_blocks, error_blocks, preferred_element_type=jnp.float32
    )
    enc_term = jnp.einsum(
        "sbcl,sbcd->bld", pre_grad, input_blocks, preferred_element_type=jnp.float32
    )
    dec_term = dec_term.reshape(lat_rows, model_width)
    enc_term = enc_term.reshape(lat_rows, model_width)
    dec_half, enc_half = (
        lax.psum_scatter(dec_term, "dp", scatter_dimension=1, tiled=True),
        lax.psum_scatter(enc_term, "dp", scatter_dimension=1, tiled=True),
    )
    return (dec_half.astype(jnp.bfloat16)[None], enc_half.astype(jnp.bfloat16)[None])


def flip(value, axis, bit):
    count = lax.axis_size(axis)
    return lax.ppermute(value, axis, [(i, i ^ bit) for i in range(count)])


def hop(value, axis, step, least):
    count = lax.axis_size(axis)
    if step > 0:
        pairs = [(i, i + 1) for i in range(least, count - 1)]
    else:
        pairs = [(i, i - 1) for i in range(1, count - least)]
    return lax.ppermute(value, axis, pairs)


def params():
    return pltpu.CompilerParams(vmem_limit_bytes=VMEM_BYTES)


def cost(microseconds):
    return pl.CostEstimate(flops=int(microseconds * 1.1e9), bytes_accessed=1, transcendentals=0)


def resident(shape):
    return pl.BlockSpec(shape, lambda i, s: (0,) * len(shape))


def gather_kernel(scalar_ref, source_ref, out_ref, token_ref):
    out_ref[...] = source_ref[...].reshape(out_ref.shape)
    token_ref[...] = jnp.zeros_like(token_ref)


def gather_columns(source, columns, width):
    rows = source.shape[-2]
    lead = (1,) * (source.ndim - 2)
    count = columns.shape[0]
    return pl.pallas_call(
        gather_kernel,
        out_shape=[
            pltpu.HBM((rows, count * width), source.dtype),
            jax.ShapeDtypeStruct((8, 128), jnp.float32),
        ],
        grid_spec=pltpu.PrefetchScalarGridSpec(
            num_scalar_prefetch=1,
            grid=(count,),
            in_specs=[pl.BlockSpec(lead + (rows, width), lambda i, s: (0,) * len(lead) + (0, s[i]))],
            out_specs=[pl.BlockSpec((rows, width), lambda i, s: (0, i)), resident((8, 128))],
        ),
        compiler_params=params(),
        cost_estimate=cost(0.9 * count),
        name="gather_columns",
    )(columns.astype(jnp.int32), source)


def codes_kernel(groups, blocks, scalar_ref, message_ref, codes, id_map, pre):
    tok = message_ref.shape[2]
    pad = message_ref.shape[1] - 2 * tok
    first = scalar_ref[0].astype(jnp.float32)
    rows = [message_ref[g, 2 * tok:2 * tok + pad, :].astype(jnp.float32) for g in range(groups)]
    fill = tok - groups * pad
    if fill:
        rows.append(jnp.zeros((fill, tok), jnp.float32))
    table = jnp.concatenate(rows, axis=0).T - first
    for g in range(groups):
        pre[g] = jnp.maximum(message_ref[g, 0:2 * tok, :], jnp.zeros((), jnp.bfloat16))
        for j in range(2):
            at = g * pad + j
            wide = jnp.broadcast_to(table[:, at:at + 1], (tok, tok))
            id_map[g, j * tok:(j + 1) * tok, :] = wide.astype(jnp.bfloat16)

    def block_step(b, carry):
        block = b.astype(jnp.float32).astype(jnp.bfloat16)
        at = pl.multiple_of(b * tok, tok)
        for g in range(groups):
            value = jnp.where(id_map[g, tok:2 * tok, :] == block, pre[g, tok:2 * tok, :], jnp.zeros((), jnp.bfloat16))
            value = jnp.where(id_map[g, 0:tok, :] == block, pre[g, 0:tok, :], value)
            codes[g * tok:(g + 1) * tok, pl.ds(at, tok)] = value
        return carry

    lax.fori_loop(0, blocks, block_step, 0)


def spread_codes(message, first, lat_rows):
    groups, _, tok = message.shape
    rows = groups * tok
    return pl.pallas_call(
        functools.partial(codes_kernel, groups, lat_rows // tok),
        out_shape=jax.ShapeDtypeStruct((rows, lat_rows), jnp.bfloat16),
        grid_spec=pltpu.PrefetchScalarGridSpec(
            num_scalar_prefetch=1,
            grid=(1,),
            in_specs=[resident(message.shape)],
            out_specs=resident((rows, lat_rows)),
            scratch_shapes=[
                pltpu.VMEM((groups, 2 * tok, tok), jnp.bfloat16),
                pltpu.VMEM((groups, 2 * tok, tok), jnp.bfloat16),
            ],
        ),
        compiler_params=params(),
        cost_estimate=cost(2.5),
        name="spread_codes",
    )(first[None].astype(jnp.int32), message)


def layer_sum_kernel(got_a, kept_a, far_a, got_b, kept_b, far_b, own_ref, *sent_refs):
    half = far_a.shape[1]
    rows = own_ref.shape[0]
    for side, (got, kept, far) in enumerate(((got_a, kept_a, far_a), (got_b, kept_b, far_b))):
        lanes = slice(side * half, (side + 1) * half)
        for n in range(1 + len(sent_refs)):
            at = slice(n * rows, (n + 1) * rows)
            total = got[at, :half].astype(jnp.float32) + kept[at, :half].astype(jnp.float32)
            total = total + far[at, :].astype(jnp.float32)
            if n:
                sent_refs[n - 1][:, lanes] = total.astype(jnp.bfloat16)
            else:
                own_ref[:, lanes] = total


def layer_sum(terms_a, terms_b, blocks):
    rows, half = terms_a[2].shape
    cut = (rows // blocks, 2 * half)
    return pl.pallas_call(
        layer_sum_kernel,
        out_shape=[jax.ShapeDtypeStruct(cut, jnp.float32)] + [jax.ShapeDtypeStruct(cut, jnp.bfloat16)] * (blocks - 1),
        grid=(1,),
        in_specs=[pl.BlockSpec((rows, half), lambda i: (0, 0)) for _ in range(6)],
        out_specs=[pl.BlockSpec(cut, lambda i: (0, 0))] * blocks,
        compiler_params=params(),
        cost_estimate=cost(0.5),
        name="layer_sum",
    )(*terms_a, *terms_b)


def join_kernel(count, *refs):
    out_ref = refs[-1]
    rows = out_ref.shape[0] // count
    for i in range(count):
        out_ref[i * rows:(i + 1) * rows] = refs[i][...]


def join(parts, *waited):
    shape = (len(parts) * parts[0].shape[0],) + parts[0].shape[1:]
    vmem = pl.BlockSpec(memory_space=pltpu.VMEM)
    return pl.pallas_call(
        functools.partial(join_kernel, len(parts)),
        out_shape=jax.ShapeDtypeStruct(shape, parts[0].dtype),
        in_specs=[vmem] * (len(parts) + len(waited)),
        out_specs=vmem,
        compiler_params=params(),
        cost_estimate=cost(0.4),
        name="join",
    )(*parts, *waited)


def slots_kernel(groups, blocks, cap, scalar_ref, message_ref, hot_ref, pre_ref, code_ref):
    tok = message_ref.shape[2]
    pad = message_ref.shape[1] - 2 * tok
    f32, bf16 = jnp.float32, jnp.bfloat16
    first = scalar_ref[0].astype(f32)
    rows = [message_ref[g, 2 * tok:2 * tok + pad, :].astype(f32) for g in range(groups)]
    fill = tok - groups * pad
    table = jnp.concatenate(rows + ([jnp.zeros((fill, tok), f32)] if fill else []), axis=0).T
    earlier = lax.broadcasted_iota(jnp.int32, (tok, tok), 0) < lax.broadcasted_iota(jnp.int32, (tok, tok), 1)
    per = 2 * cap
    for z in range(groups // 2):
        pre = 0.0
        hot = []
        for core in range(2):
            g = 2 * z + core
            lanes = [rows[g][j:j + 1] for j in range(2)]
            down = [table[:, g * pad + j:g * pad + j + 1] for j in range(2)]
            same = [jnp.where((down[j] == lanes[j]) & earlier, 1.0, 0.0) for j in range(2)]
            cross = jnp.where(down[0] == lanes[1], 1.0, 0.0)
            rank = [jnp.sum(same[0], axis=0, keepdims=True), jnp.sum(same[1] + cross, axis=0, keepdims=True)]
            here = []
            for j in range(2):
                block = lanes[j] - first
                slot = block * per + (core * cap + rank[j])
                slot = jnp.where((block >= 0) & (block < blocks), slot, -1.0)
                number = lax.broadcasted_iota(jnp.int32, (blocks * per, tok), 0).astype(f32)
                here.append(jnp.where(number == slot, 1.0, 0.0).astype(bf16))
                pre = pre + jnp.dot(
                    here[j], message_ref[g, j * tok:(j + 1) * tok, :], preferred_element_type=f32
                )
            hot.append(here[0] + here[1])
        hot_ref[z] = jnp.concatenate(hot, axis=1)
        for b in range(blocks):
            pre_ref[b, z * per:(z + 1) * per, :] = pre[b * per:(b + 1) * per].astype(bf16)
    for b in range(blocks):
        code_ref[b] = jnp.maximum(pre_ref[b].astype(f32), 0.0).T.astype(bf16)


def make_slots(message, first, lat_rows, cap):
    groups, _, tok = message.shape
    blocks = lat_rows // tok
    per = 2 * cap
    shards = groups // 2
    shapes = [(shards, blocks * per, 2 * tok), (blocks, shards * per, tok), (blocks, tok, shards * per)]
    return pl.pallas_call(
        functools.partial(slots_kernel, groups, blocks, cap),
        out_shape=[jax.ShapeDtypeStruct(shape, jnp.bfloat16) for shape in shapes],
        grid_spec=pltpu.PrefetchScalarGridSpec(
            num_scalar_prefetch=1,
            grid=(1,),
            in_specs=[resident(message.shape)],
            out_specs=[resident(shape) for shape in shapes],
        ),
        compiler_params=params(),
        cost_estimate=cost(1),
        name="make_slots",
    )(first[None].astype(jnp.int32), message)


def into_slots(hot, rows, out, z):
    per = out.shape[1] // hot.shape[0]
    value = jnp.dot(hot[z], rows, preferred_element_type=jnp.float32).astype(jnp.bfloat16)
    for b in range(out.shape[0]):
        out[b, z * per:(z + 1) * per, :] = value[b * per:(b + 1) * per]


def lanes_of(refs, rows):
    parts = [r[rows, :] for r in refs]
    return parts[0] if len(parts) == 1 else jnp.concatenate(parts, axis=1)


def piece_grad_kernel(layout, onto, scalar_ref, hot_ref, weight_ref, *refs):
    parts, (slots_ref, grad_ref) = refs[onto:-2], refs[-2:]
    blocks, _, size = grad_ref.shape
    group = hot_ref.shape[2]
    step = pl.program_id(0)

    @pl.when(step == 0)
    def _():
        grad_ref[...] = refs[0][...] if onto else jnp.zeros_like(grad_ref)

    at = 0
    for i, piece in enumerate(layout):
        z = 0
        for lanes in piece:
            here = parts[at:at + lanes]
            at += lanes
            for n in range(here[0].shape[0] // group):

                @pl.when(step == i)
                def _(z=z, n=n, here=here):
                    into_slots(hot_ref, lanes_of(here, slice(n * group, (n + 1) * group)), slots_ref.at[0], z)

                z += 1
    for b in range(blocks):
        grad_ref[b] += lax.dot_general(
            slots_ref[0, b],
            weight_ref[0, b * size:(b + 1) * size, :],
            (((1,), (1,)), ((), ())),
            preferred_element_type=jnp.float32,
        )


def piece_grad(pieces, hot, decoder, columns, size, held):
    lat_rows = decoder.shape[1]
    blocks = lat_rows // size
    slots = hot.shape[0] * hot.shape[1] // blocks
    width = sum(p.shape[1] for p in pieces[0][0])
    flat = [p for piece in pieces for row in piece for p in row]
    onto = [] if held is None else [held]
    return pl.pallas_call(
        functools.partial(piece_grad_kernel, [[len(row) for row in piece] for piece in pieces], len(onto)),
        out_shape=[
            jax.ShapeDtypeStruct((len(pieces), blocks, slots, width), jnp.bfloat16),
            jax.ShapeDtypeStruct((blocks, slots, size), jnp.float32),
        ],
        grid_spec=pltpu.PrefetchScalarGridSpec(
            num_scalar_prefetch=1,
            grid=(len(pieces),),
            in_specs=[resident(hot.shape), pl.BlockSpec((1, lat_rows, width), lambda i, s: (0, 0, s[i]))]
            + [resident(p.shape) for p in onto + flat],
            out_specs=[
                pl.BlockSpec((1, blocks, slots, width), lambda i, s: (i, 0, 0, 0)),
                resident((blocks, slots, size)),
            ],
        ),
        compiler_params=params(),
        cost_estimate=cost(0.8 + 2 * len(pieces)),
        name="piece_grad",
    )(columns.astype(jnp.int32), hot, decoder, *onto, *flat)


def decoder_kernel(skip, scalar_ref, code_ref, slots_ref, *refs):
    out_ref = refs[skip]
    size = code_ref.shape[1]
    for b in range(code_ref.shape[0]):
        out_ref[b * size:(b + 1) * size, :] = jnp.dot(
            code_ref[b], slots_ref[0, b], preferred_element_type=jnp.float32
        ).astype(jnp.bfloat16)


def decoder_part(slots, codes, columns, half, held):
    count, blocks, _, width = slots.shape
    lat_rows = blocks * codes.shape[1]
    onto = [] if held is None else [held]
    return pl.pallas_call(
        functools.partial(decoder_kernel, len(onto)),
        out_shape=jax.ShapeDtypeStruct((lat_rows, half), jnp.bfloat16),
        grid_spec=pltpu.PrefetchScalarGridSpec(
            num_scalar_prefetch=1,
            grid=(count,),
            in_specs=[resident(codes.shape), pl.BlockSpec((1,) + slots.shape[1:], lambda i, s: (i, 0, 0, 0))]
            + [pl.BlockSpec(memory_space=pl.ANY) for _ in onto],
            out_specs=pl.BlockSpec((lat_rows, width), lambda i, s: (0, s[i])),
        ),
        compiler_params=params(),
        input_output_aliases={3: 0} if onto else {},
        cost_estimate=cost(0.7 + 1.3 * count),
        name="decoder_part",
    )(columns.astype(jnp.int32), codes, slots, *onto)


def act_slots_kernel(scalar_ref, hot_ref, *refs):
    out_ref = refs[-1]
    shards = hot_ref.shape[0]
    per = out_ref.shape[1] // shards
    for i in range(shards):
        z = scalar_ref[i]
        rows, more = refs[2 * i][...], refs[2 * i + 1][...]
        rows = rows + jnp.where(scalar_ref[shards + i] > 0, more, jnp.zeros((), more.dtype))
        value = jnp.dot(hot_ref[z], rows, preferred_element_type=jnp.float32).astype(jnp.bfloat16)
        to = pl.ds(pl.multiple_of(z * per, per), per)
        for b in range(out_ref.shape[0]):
            out_ref[b, to, :] = value[b * per:(b + 1) * per]


def act_slots(terms_of, places, flags, hot, count):
    group, half = terms_of[0][0].shape
    slots = hot.shape[0] * hot.shape[1] // count
    tile = half // 4
    flat = [term for terms in terms_of for term in terms]
    scalars = jnp.stack([jnp.asarray(x, jnp.int32) for x in (*places, *flags)])
    return pl.pallas_call(
        act_slots_kernel,
        out_shape=jax.ShapeDtypeStruct((count, slots, half), jnp.bfloat16),
        grid_spec=pltpu.PrefetchScalarGridSpec(
            num_scalar_prefetch=1,
            grid=(4,),
            in_specs=[resident(hot.shape)] + [pl.BlockSpec((group, tile), lambda i, s: (0, i)) for _ in flat],
            out_specs=pl.BlockSpec((count, slots, tile), lambda i, s: (0, 0, i)),
        ),
        compiler_params=params(),
        cost_estimate=cost(3.3),
        name="act_slots",
    )(scalars, hot, *flat)


def encoder_kernel(cap, shared, pre_ref, own_ref, theirs_ref, act_ref, out_ref):
    size = pre_ref.shape[2]
    for n in range(shared):
        parts = []
        for at in range(0, own_ref.shape[1], 2 * cap):
            for core in range(2):
                here = slice(at + core * cap, at + (core + 1) * cap)
                there = slice(at + (1 - core) * cap, at + (2 - core) * cap)
                parts.append(own_ref[n, here, :] + theirs_ref[n, there, :])
        total = jnp.concatenate(parts, axis=0)
        grad = jnp.where(pre_ref[n].astype(jnp.float32) > 0, total, 0.0).T.astype(jnp.bfloat16)
        out_ref[n * size:(n + 1) * size, :] = jnp.dot(
            grad, act_ref[n], preferred_element_type=jnp.float32
        ).astype(jnp.bfloat16)


def encoder_part(pre, own, theirs, acts, cap):
    blocks, slots, size = pre.shape
    half = acts.shape[2]
    shared = 2 if blocks % 2 == 0 else 1
    block = pl.BlockSpec((shared, slots, size), lambda i: (i, 0, 0))
    return pl.pallas_call(
        functools.partial(encoder_kernel, cap, shared),
        out_shape=jax.ShapeDtypeStruct((blocks * size, half), jnp.bfloat16),
        grid=(blocks // shared,),
        in_specs=[block, block, block, pl.BlockSpec((shared, slots, half), lambda i: (i, 0, 0))],
        out_specs=pl.BlockSpec((shared * size, half), lambda i: (i, 0)),
        compiler_params=params(),
        cost_estimate=cost(6.5),
        name="encoder_part",
    )(pre, own, theirs, acts)


def dense_plan(pre_codes, block_ids, activations, target, decoder):
    lay_count = lax.axis_size("layer")
    lat_count = lax.axis_size("latent")
    dp_count = lax.axis_size("dp")
    lay_here = lax.axis_index("layer")
    lat_here = lax.axis_index("latent")
    dp_here = lax.axis_index("dp")
    tok_count = activations.shape[1]
    model_width = activations.shape[2]
    active_count = block_ids.shape[2]
    block_size = pre_codes.shape[3]
    lat_rows = decoder.shape[1]
    local_blocks = lat_rows // block_size
    half = model_width // dp_count
    group = dp_count * tok_count
    tokens = lat_count * group
    width = half // lay_count
    side = width // 2
    f32, bf16 = jnp.float32, jnp.bfloat16
    first = lat_here * local_blocks
    capacity = 2 * tok_count * active_count // (local_blocks * lat_count)

    def columns(rows, which):
        return lax.dynamic_slice_in_dim(rows, which * half, half, axis=1)

    def places(names, offset, fine=1, sub=0):
        return [(offset + (lay_here ^ r)) * fine + sub for r in names]

    def weight_places(names):
        return jnp.stack(places(names, dp_here * lay_count))

    pre_rows = jnp.swapaxes(pre_codes[0], 0, 1).reshape(active_count * tok_count, block_size)
    id_rows = jnp.pad(block_ids[0].T, ((0, 16 - active_count), (0, 0))).astype(bf16)
    own = jnp.concatenate([pre_rows, id_rows], axis=0)
    at = places((1, 3), dp_here * lay_count, 2, 0) + places((2, 3), dp_here * lay_count, 2, 1)
    send_weights, token = gather_columns(decoder, jnp.stack(at), side)

    message = [own] + [flip(own, "latent", r) for r in range(1, lat_count)]

    own, inputs = lax.optimization_barrier((own, activations[0]))
    acts = jnp.concatenate([columns(inputs, dp_here), flip(columns(inputs, 1 - dp_here), "dp", 1)])
    message, acts = lax.optimization_barrier((join(message, token), acts))
    message = message.reshape((lat_count,) + own.shape)
    up, down = [acts], [acts]

    def next_hops():
        step = len(up)
        up.append(hop(up[-1], "latent", 1, step - 1))
        down.append(hop(down[-1], "latent", -1, step - 1))

    message = jnp.stack([message, flip(message, "dp", 1)], axis=1)
    message = message.reshape(lat_count * dp_count, own.shape[0], block_size)
    next_hops()

    codes = spread_codes(message, first, lat_rows)
    at = places((0, 2), dp_here * lay_count, 2, 0) + places((0, 1), dp_here * lay_count, 2, 1)
    at, codes, target = lax.optimization_barrier((jnp.stack(at), codes, target))
    keep_weights, _ = gather_columns(decoder, at, side)
    goals, _ = gather_columns(target, jnp.stack([which * lay_count + lay_here for which in (dp_here, 1 - dp_here)]), width)
    goals = jnp.concatenate([goals[:, :width], flip(goals[:, width:], "dp", 1)])

    codes = spread_codes(message, first, lat_rows)
    at = places((0, 2), dp_here * lay_count, 2, 0) + places((0, 1), dp_here * lay_count, 2, 1)
    at, codes, target = lax.optimization_barrier((jnp.stack(at), codes, target))
    keep_weights, _ = gather_columns(decoder, at, side)
    goals, _ = gather_columns(target, jnp.stack([which * lay_count + lay_here for which in (dp_here, 1 - dp_here)]), width)
    goals = jnp.concatenate([goals[:, :width], flip(goals[:, width:], "dp", 1)])

    def rows_for(spread, weights, n):
        return jnp.dot(spread, weights[:, n * width:(n + 1) * width], preferred_element_type=f32).astype(bf16)

    got = flip(rows_for(codes, send_weights, 0), "layer", 1), flip(rows_for(codes, send_weights, 1), "layer", 2)
    keep_codes, up[1], down[1] = lax.optimization_barrier((codes, up[1], down[1]))
    if lat_count > 2:
        next_hops()
    kept = rows_for(keep_codes, keep_weights, 0), rows_for(keep_codes, keep_weights, 1)

    def add(one, two):
        return (one[:, side:].astype(f32) + two[:, side:].astype(f32)).astype(bf16)

    far = [flip(add(got[n], kept[n]), "layer", 2 - n) for n in range(2)]
    made = make_slots(message, first, lat_rows, capacity)
    far, goals, up[-1], down[-1], made = lax.optimization_barrier((far, goals, up[-1], down[-1], made))
    while len(up) < lat_count - 1:
        next_hops()
    relay = jnp.where(lat_here == 1, down[-1], up[-1])

    total, *sent = layer_sum((got[0], kept[0], far[0]), (got[1], kept[1], far[1]), lat_count)
    for r in range(1, lat_count):
        total = total + flip(sent[r - 1], "latent", r).astype(f32)
    errors = ((total - goals.astype(f32)) / tok_count).astype(bf16)
    others = [flip(errors, "latent", r) for r in range(1, lat_count)]
    one_near, two_near = flip(errors, "layer", 1), flip(errors, "layer", 2)
    relay, two_near, one_near, others = lax.optimization_barrier((relay, two_near, one_near, others[::-1]))
    distant = join(others[::-1])
    one_far, two_far = flip(distant, "layer", 1), flip(distant, "layer", 2)
    ends = lax.ppermute(relay, "latent", [(lat_count - 2, lat_count - 1), (1, 0)])

    hot, pre_slots, code_slots = made

    def grads_of(here, names, grad, dec):
        slots, grad = piece_grad(here, hot, decoder, weight_places(names), block_size, grad)
        return grad, decoder_part(slots, code_slots, jnp.stack(places(names, 0)), half, dec)

    grad, dec = grads_of([[(errors,), (distant,)]], (0,), None, None)
    grad, dec, two_far, one_far = lax.optimization_barrier((grad, dec, two_far, one_far))
    three_a = flip(jnp.concatenate([two_near[:, :side], two_far[:, :side]]), "layer", 1)
    three_b = flip(jnp.concatenate([one_near[:, side:], one_far[:, side:]]), "layer", 2)
    grad, dec = grads_of([[(one_near,), (one_far,)], [(two_near,), (two_far,)]], (1, 2), grad, dec)

    down_end, up_end = lat_here == 0, lat_here == lat_count - 1
    terms_of = [[acts, acts]]
    flags = [False]
    for k in range(1, lat_count):
        last = k == 1 or k == lat_count - 1
        terms_of.append([(down if k == 1 else up)[1] if last else down[k], ends if last else up[lat_count - k]])
        flags.append(True if not last else up_end if k == 1 else down_end)
    shards = [lax.rem(lat_here + k, lat_count) ^ lat_here for k in range(lat_count)]
    slotted = act_slots(terms_of, shards, flags, hot, local_blocks)
    three_a, three_b, grad, dec, slotted = lax.optimization_barrier((three_a, three_b, grad, dec, slotted))
    grad, dec = grads_of([[(three_a, three_b)]], (3,), grad, dec)
    enc = encoder_part(pre_slots, grad, flip(grad, "dp", 1), slotted, capacity)
    return dec[None], enc[None]


def per_device(pre_codes, block_ids, activations, target, decoder):
    lat_count = lax.axis_size("latent")
    lay_count = lax.axis_size("layer")
    dp_count = lax.axis_size("dp")
    tok_count = activations.shape[1]
    model_width = activations.shape[2]
    active_count = block_ids.shape[2]
    block_size = pre_codes.shape[3]
    all_blocks = decoder.shape[1] // block_size * lat_count
    slots = 2 * tok_count * active_count // lat_count
    dense = (
        slots >= tok_count
        and dp_count == 2
        and active_count == 2
        and lay_count == 4
        and lat_count > 3
        and lat_count & (lat_count - 1) == 0
        and tok_count == block_size
        and lat_count * dp_count * 16 <= tok_count
        and model_width % (dp_count * 2 * lay_count * 128) == 0
        and all_blocks <= 256
        and 2 * tok_count * active_count == 8 * all_blocks
    )
    plan = dense_plan if dense else slot_plan
    return plan(pre_codes, block_ids, activations, target, decoder)


def solution(mesh):
    placed = (
        P("layer", ("latent", "dp"), None, None),
        P("layer", ("latent", "dp"), None),
        P("layer", ("latent", "dp"), None),
        P(("latent", "dp"), None),
        P("layer", "latent", None),
    )
    return jax.shard_map(
        per_device,
        mesh=mesh,
        in_specs=placed,
        out_specs=(P("layer", "latent", "dp"), P("layer", "latent", "dp")),
        check_vma=False,
    )
```

```python
import functools

import jax
import jax.numpy as jnp
from jax import lax
from jax.experimental import pallas as pl
from jax.experimental.pallas import tpu as pltpu
from jax.sharding import PartitionSpec as P

VMEM_BYTES = 40 * 1024 * 1024


def local_contrib(received_pre, weights, lat_count, local_blocks):
    code_vals = jnp.maximum(received_pre, jnp.zeros((), received_pre.dtype))
    slot_span = received_pre.shape[1]
    block_size = received_pre.shape[2]
    grouped = code_vals.reshape(lat_count, local_blocks, slot_span, block_size)
    contrib = jnp.einsum("sbcl,bld->sbcd", grouped, weights, preferred_element_type=jnp.float32)
    contrib = contrib.astype(jnp.bfloat16).reshape(
        lat_count * local_blocks, slot_span, weights.shape[2]
    )
    return lax.all_to_all(contrib, "latent", split_axis=0, concat_axis=0, tiled=True)


def slot_plan(pre_codes, block_ids, activations, target, decoder):
    lat_count = lax.axis_size("latent")
    tok_count = activations.shape[1]
    model_width = activations.shape[2]
    active_count = block_ids.shape[2]
    block_size = pre_codes.shape[3]
    lat_rows = decoder.shape[1]
    local_blocks = lat_rows // block_size
    all_blocks = local_blocks * lat_count
    capacity = 2 * tok_count * active_count // all_blocks
    slot_count = all_blocks * capacity
    pair_count = tok_count * active_count
    pair_block = block_ids[0].T.reshape(pair_count)
    member = (pair_block[:, None] == jnp.arange(all_blocks, dtype=jnp.int32)[None, :]).astype(
        jnp.int32
    )
    before = jnp.cumsum(member, axis=0) - member
    pair_rank = jnp.sum(before * member, axis=1)
    target_slot = pair_block * capacity + pair_rank
    slot_pair = (jnp.arange(slot_count, dtype=jnp.int32)[:, None] == target_slot[None, :]).astype(
        jnp.bfloat16
    )
    slot_token = jnp.sum(slot_pair.reshape(slot_count, active_count, tok_count), axis=1)
    pre_pairs = jnp.transpose(pre_codes[0], (1, 0, 2)).reshape(pair_count, block_size)
    pre_slots = jnp.dot(slot_pair, pre_pairs, preferred_element_type=jnp.float32).astype(
        jnp.bfloat16
    )
    pre_slots = pre_slots.reshape(all_blocks, capacity, block_size)
    inputs = activations[0]
    weights = decoder[0].reshape(local_blocks, block_size, model_width)
    input_slots = jnp.dot(slot_token, inputs, preferred_element_type=jnp.float32).astype(
        jnp.bfloat16
    )
    input_slots = input_slots.reshape(all_blocks, capacity, model_width)
    pieces = (
        lax.all_to_all(pre_slots, "latent", split_axis=0, concat_axis=0, tiled=True),
        lax.all_to_all(input_slots, "latent", split_axis=0, concat_axis=0, tiled=True),
    )
    returned = local_contrib(pieces[0], weights, lat_count, local_blocks)
    returned, received_pre, received_inputs = (returned, pieces[0], pieces[1])
    part_sum = jnp.einsum(
        "st,sd->td",
        slot_token,
        returned.reshape(slot_count, model_width),
        preferred_element_type=jnp.float32,
    )
    rebuilt = lax.psum(part_sum, "layer")
    errors = ((rebuilt - target.astype(jnp.float32)) / tok_count).astype(jnp.bfloat16)
    error_slots = jnp.dot(slot_token, errors, preferred_element_type=jnp.float32).astype(
        jnp.bfloat16
    )
    error_slots = error_slots.reshape(all_blocks, capacity, model_width)
    received_errors = lax.all_to_all(error_slots, "latent", split_axis=0, concat_axis=0, tiled=True)
    pre_blocks = received_pre.reshape(lat_count, local_blocks, capacity, block_size)
    code_blocks = jnp.maximum(pre_blocks, jnp.zeros((), pre_blocks.dtype))
    error_blocks = received_errors.reshape(lat_count, local_blocks, capacity, model_width)
    input_blocks = received_inputs.reshape(lat_count, local_blocks, capacity, model_width)
    code_grad = jnp.einsum(
        "sbcd,bld->sbcl", error_blocks, weights, preferred_element_type=jnp.float32
    )
    pre_grad = jnp.where(pre_blocks > 0, code_grad, jnp.zeros((), jnp.float32)).astype(jnp.bfloat16)
    dec_term = jnp.einsum(
        "sbcl,sbcd->bld", code_blocks, error_blocks, preferred_element_type=jnp.float32
    )
    enc_term = jnp.einsum(
        "sbcl,sbcd->bld", pre_grad, input_blocks, preferred_element_type=jnp.float32
    )
    dec_term = dec_term.reshape(lat_rows, model_width)
    enc_term = enc_term.reshape(lat_rows, model_width)
    dec_half, enc_half = (
        lax.psum_scatter(dec_term, "dp", scatter_dimension=1, tiled=True),
        lax.psum_scatter(enc_term, "dp", scatter_dimension=1, tiled=True),
    )
    return (dec_half.astype(jnp.bfloat16)[None], enc_half.astype(jnp.bfloat16)[None])


def flip(value, axis, bit):
    count = lax.axis_size(axis)
    return lax.ppermute(value, axis, [(i, i ^ bit) for i in range(count)])


def hop(value, axis, step, least):
    count = lax.axis_size(axis)
    if step > 0:
        pairs = [(i, i + 1) for i in range(least, count - 1)]
    else:
        pairs = [(i, i - 1) for i in range(1, count - least)]
    return lax.ppermute(value, axis, pairs)


def params():
    return pltpu.CompilerParams(vmem_limit_bytes=VMEM_BYTES)


def cost(microseconds):
    return pl.CostEstimate(flops=int(microseconds * 1.1e9), bytes_accessed=1, transcendentals=0)


def resident(shape):
    return pl.BlockSpec(shape, lambda i, s: (0,) * len(shape))


def gather_kernel(scalar_ref, source_ref, out_ref, token_ref):
    out_ref[...] = source_ref[...].reshape(out_ref.shape)
    token_ref[...] = jnp.zeros_like(token_ref)


def gather_columns(source, columns, width):
    rows = source.shape[-2]
    lead = (1,) * (source.ndim - 2)
    count = columns.shape[0]
    return pl.pallas_call(
        gather_kernel,
        out_shape=[
            pltpu.HBM((rows, count * width), source.dtype),
            jax.ShapeDtypeStruct((8, 128), jnp.float32),
        ],
        grid_spec=pltpu.PrefetchScalarGridSpec(
            num_scalar_prefetch=1,
            grid=(count,),
            in_specs=[pl.BlockSpec(lead + (rows, width), lambda i, s: (0,) * len(lead) + (0, s[i]))],
            out_specs=[pl.BlockSpec((rows, width), lambda i, s: (0, i)), resident((8, 128))],
        ),
        compiler_params=params(),
        cost_estimate=cost(0.01 * count),
        name="gather_columns",
    )(columns.astype(jnp.int32), source)


def codes_kernel(groups, blocks, scalar_ref, message_ref, own_ref, rest_ref, id_map, pre):
    tok = message_ref.shape[2]
    pad = message_ref.shape[1] - 2 * tok
    first = scalar_ref[0].astype(jnp.float32)
    rows = [message_ref[g, 2 * tok:2 * tok + pad, :].astype(jnp.float32) for g in range(groups)]
    fill = tok - groups * pad
    if fill:
        rows.append(jnp.zeros((fill, tok), jnp.float32))
    table = jnp.concatenate(rows, axis=0).T - first
    for g in range(groups):
        pre[g] = jnp.maximum(message_ref[g, 0:2 * tok, :], jnp.zeros((), jnp.bfloat16))
        for j in range(2):
            at = g * pad + j
            wide = jnp.broadcast_to(table[:, at:at + 1], (tok, tok))
            id_map[g, j * tok:(j + 1) * tok, :] = wide.astype(jnp.bfloat16)

    def block_step(b, carry):
        block = b.astype(jnp.float32).astype(jnp.bfloat16)
        at = pl.multiple_of(b * tok, tok)
        for g in range(groups):
            value = jnp.where(id_map[g, tok:2 * tok, :] == block, pre[g, tok:2 * tok, :], jnp.zeros((), jnp.bfloat16))
            value = jnp.where(id_map[g, 0:tok, :] == block, pre[g, 0:tok, :], value)
            to, n = (own_ref, g) if g < 2 else (rest_ref, g - 2)
            to[n * tok:(n + 1) * tok, pl.ds(at, tok)] = value
        return carry

    lax.fori_loop(0, blocks, block_step, 0)


def spread_codes(message, first, lat_rows):
    groups, _, tok = message.shape
    shapes = [(2 * tok, lat_rows), ((groups - 2) * tok, lat_rows)]
    return pl.pallas_call(
        functools.partial(codes_kernel, groups, lat_rows // tok),
        out_shape=[jax.ShapeDtypeStruct(shape, jnp.bfloat16) for shape in shapes],
        grid_spec=pltpu.PrefetchScalarGridSpec(
            num_scalar_prefetch=1,
            grid=(1,),
            in_specs=[resident(message.shape)],
            out_specs=[resident(shape) for shape in shapes],
            scratch_shapes=[
                pltpu.VMEM((groups, 2 * tok, tok), jnp.bfloat16),
                pltpu.VMEM((groups, 2 * tok, tok), jnp.bfloat16),
            ],
        ),
        compiler_params=params(),
        cost_estimate=cost(2.5),
        name="spread_codes",
    )(first[None].astype(jnp.int32), message)


def layer_sum_kernel(got_a, kept_a, far_a, got_b, kept_b, far_b, *sent_refs):
    half = far_a.shape[1]
    rows = sent_refs[0].shape[0]
    for side, (got, kept, far) in enumerate(((got_a, kept_a, far_a), (got_b, kept_b, far_b))):
        lanes = slice(side * half, (side + 1) * half)
        for n, sent_ref in enumerate(sent_refs):
            at = slice(n * rows, (n + 1) * rows)
            total = got[at, :half].astype(jnp.float32) + kept[at, :half].astype(jnp.float32)
            total = total + far[at, :].astype(jnp.float32)
            sent_ref[:, lanes] = total.astype(jnp.bfloat16)


def layer_sum(terms_a, terms_b, blocks):
    rows, half = terms_a[2].shape
    cut = (rows // blocks, 2 * half)
    vmem = pl.BlockSpec(memory_space=pltpu.VMEM)
    return pl.pallas_call(
        layer_sum_kernel,
        out_shape=[jax.ShapeDtypeStruct(cut, jnp.bfloat16)] * blocks,
        in_specs=[vmem] * 6,
        out_specs=[vmem] * blocks,
        compiler_params=params(),
        cost_estimate=cost(0.5),
        name="layer_sum",
    )(*terms_a, *terms_b)


def join_kernel(count, *refs):
    out_ref = refs[-1]
    rows = out_ref.shape[0] // count
    for i in range(count):
        out_ref[i * rows:(i + 1) * rows] = refs[i][...]


def join(parts, *waited):
    shape = (len(parts) * parts[0].shape[0],) + parts[0].shape[1:]
    vmem = pl.BlockSpec(memory_space=pltpu.VMEM)
    return pl.pallas_call(
        functools.partial(join_kernel, len(parts)),
        out_shape=jax.ShapeDtypeStruct(shape, parts[0].dtype),
        in_specs=[vmem] * (len(parts) + len(waited)),
        out_specs=vmem,
        compiler_params=params(),
        cost_estimate=cost(0.4),
        name="join",
    )(*parts, *waited)


def slots_kernel(groups, blocks, cap, scalar_ref, message_ref, hot_ref, pre_ref, code_ref):
    tok = message_ref.shape[2]
    pad = message_ref.shape[1] - 2 * tok
    f32, bf16 = jnp.float32, jnp.bfloat16
    first = scalar_ref[0].astype(f32)
    rows = [message_ref[g, 2 * tok:2 * tok + pad, :].astype(f32) for g in range(groups)]
    fill = tok - groups * pad
    table = jnp.concatenate(rows + ([jnp.zeros((fill, tok), f32)] if fill else []), axis=0).T
    earlier = lax.broadcasted_iota(jnp.int32, (tok, tok), 0) < lax.broadcasted_iota(jnp.int32, (tok, tok), 1)
    per = 2 * cap
    for z in range(groups // 2):
        pre = 0.0
        hot = []
        for core in range(2):
            g = 2 * z + core
            lanes = [rows[g][j:j + 1] for j in range(2)]
            down = [table[:, g * pad + j:g * pad + j + 1] for j in range(2)]
            same = [jnp.where((down[j] == lanes[j]) & earlier, 1.0, 0.0) for j in range(2)]
            cross = jnp.where(down[0] == lanes[1], 1.0, 0.0)
            rank = [jnp.sum(same[0], axis=0, keepdims=True), jnp.sum(same[1] + cross, axis=0, keepdims=True)]
            here = []
            for j in range(2):
                block = lanes[j] - first
                slot = block * per + (core * cap + rank[j])
                slot = jnp.where((block >= 0) & (block < blocks), slot, -1.0)
                number = lax.broadcasted_iota(jnp.int32, (blocks * per, tok), 0).astype(f32)
                here.append(jnp.where(number == slot, 1.0, 0.0).astype(bf16))
                pre = pre + jnp.dot(
                    here[j], message_ref[g, j * tok:(j + 1) * tok, :], preferred_element_type=f32
                )
            hot.append(here[0] + here[1])
        hot_ref[z] = jnp.concatenate(hot, axis=1)
        for b in range(blocks):
            pre_ref[b, z * per:(z + 1) * per, :] = pre[b * per:(b + 1) * per].astype(bf16)
    for b in range(blocks):
        code_ref[b] = jnp.maximum(pre_ref[b].astype(f32), 0.0).T.astype(bf16)


def make_slots(message, first, lat_rows, cap):
    groups, _, tok = message.shape
    blocks = lat_rows // tok
    per = 2 * cap
    shards = groups // 2
    shapes = [(shards, blocks * per, 2 * tok), (blocks, shards * per, tok), (blocks, tok, shards * per)]
    return pl.pallas_call(
        functools.partial(slots_kernel, groups, blocks, cap),
        out_shape=[jax.ShapeDtypeStruct(shape, jnp.bfloat16) for shape in shapes],
        grid_spec=pltpu.PrefetchScalarGridSpec(
            num_scalar_prefetch=1,
            grid=(1,),
            in_specs=[resident(message.shape)],
            out_specs=[resident(shape) for shape in shapes],
        ),
        compiler_params=params(),
        cost_estimate=cost(0.01),
        name="make_slots",
    )(first[None].astype(jnp.int32), message)


def into_slots(hot, rows, out, z):
    per = out.shape[1] // hot.shape[0]
    value = jnp.dot(hot[z], rows, preferred_element_type=jnp.float32).astype(jnp.bfloat16)
    for b in range(out.shape[0]):
        out[b, z * per:(z + 1) * per, :] = value[b * per:(b + 1) * per]


def lanes_of(refs, rows):
    parts = [r[rows, :] for r in refs]
    return parts[0] if len(parts) == 1 else jnp.concatenate(parts, axis=1)


def piece_grad_kernel(layout, onto, scalar_ref, hot_ref, weight_ref, *refs):
    parts, (slots_ref, grad_ref) = refs[onto:-2], refs[-2:]
    blocks, _, size = grad_ref.shape
    group = hot_ref.shape[2]
    step = pl.program_id(0)

    @pl.when(step == 0)
    def _():
        grad_ref[...] = refs[0][...] if onto else jnp.zeros_like(grad_ref)

    at = 0
    for i, piece in enumerate(layout):
        z = 0
        for lanes in piece:
            here = parts[at:at + lanes]
            at += lanes
            for n in range(here[0].shape[0] // group):

                @pl.when(step == i)
                def _(z=z, n=n, here=here):
                    into_slots(hot_ref, lanes_of(here, slice(n * group, (n + 1) * group)), slots_ref.at[0], z)

                z += 1
    for b in range(blocks):
        grad_ref[b] += lax.dot_general(
            slots_ref[0, b],
            weight_ref[0, b * size:(b + 1) * size, :],
            (((1,), (1,)), ((), ())),
            preferred_element_type=jnp.float32,
        )


def piece_grad(pieces, hot, decoder, columns, size, held):
    lat_rows = decoder.shape[1]
    blocks = lat_rows // size
    slots = hot.shape[0] * hot.shape[1] // blocks
    width = sum(p.shape[1] for p in pieces[0][0])
    flat = [p for piece in pieces for row in piece for p in row]
    onto = [] if held is None else [held]
    return pl.pallas_call(
        functools.partial(piece_grad_kernel, [[len(row) for row in piece] for piece in pieces], len(onto)),
        out_shape=[
            jax.ShapeDtypeStruct((len(pieces), blocks, slots, width), jnp.bfloat16),
            jax.ShapeDtypeStruct((blocks, slots, size), jnp.float32),
        ],
        grid_spec=pltpu.PrefetchScalarGridSpec(
            num_scalar_prefetch=1,
            grid=(len(pieces),),
            in_specs=[resident(hot.shape), pl.BlockSpec((1, lat_rows, width), lambda i, s: (0, 0, s[i]))]
            + [resident(p.shape) for p in onto + flat],
            out_specs=[
                pl.BlockSpec((1, blocks, slots, width), lambda i, s: (i, 0, 0, 0)),
                resident((blocks, slots, size)),
            ],
        ),
        compiler_params=params(),
        cost_estimate=cost(0.8 + 2 * len(pieces)),
        name="piece_grad",
    )(columns.astype(jnp.int32), hot, decoder, *onto, *flat)


def decoder_kernel(skip, scalar_ref, code_ref, slots_ref, *refs):
    out_ref = refs[skip]
    size = code_ref.shape[1]
    for b in range(code_ref.shape[0]):
        out_ref[b * size:(b + 1) * size, :] = jnp.dot(
            code_ref[b], slots_ref[0, b], preferred_element_type=jnp.float32
        ).astype(jnp.bfloat16)


def decoder_part(slots, codes, columns, half, held):
    count, blocks, _, width = slots.shape
    lat_rows = blocks * codes.shape[1]
    onto = [] if held is None else [held]
    return pl.pallas_call(
        functools.partial(decoder_kernel, len(onto)),
        out_shape=jax.ShapeDtypeStruct((lat_rows, half), jnp.bfloat16),
        grid_spec=pltpu.PrefetchScalarGridSpec(
            num_scalar_prefetch=1,
            grid=(count,),
            in_specs=[resident(codes.shape), pl.BlockSpec((1,) + slots.shape[1:], lambda i, s: (i, 0, 0, 0))]
            + [pl.BlockSpec(memory_space=pl.ANY) for _ in onto],
            out_specs=pl.BlockSpec((lat_rows, width), lambda i, s: (0, s[i])),
        ),
        compiler_params=params(),
        input_output_aliases={3: 0} if onto else {},
        cost_estimate=cost(0.7 + 1.3 * count),
        name="decoder_part",
    )(columns.astype(jnp.int32), codes, slots, *onto)


def act_slots_kernel(scalar_ref, hot_ref, own_ref, down_ref, up_ref, *refs):
    middle, ends, out_ref = refs[:2], refs[2:4], refs[4]
    per = out_ref.shape[1] // hot_ref.shape[0]
    last = jnp.concatenate([ref[...] for ref in ends], axis=0)
    zero = jnp.zeros((), last.dtype)
    rows = [
        own_ref[...],
        down_ref[...] + jnp.where(scalar_ref[4] > 0, last, zero),
        jnp.concatenate([ref[...] for ref in middle], axis=0),
        up_ref[...] + jnp.where(scalar_ref[5] > 0, last, zero),
    ]
    for i in range(4):
        z = scalar_ref[i]
        value = jnp.dot(hot_ref[z], rows[i], preferred_element_type=jnp.float32).astype(jnp.bfloat16)
        to = pl.ds(pl.multiple_of(z * per, per), per)
        for b in range(out_ref.shape[0]):
            out_ref[b, to, :] = value[b * per:(b + 1) * per]


def act_slots(own, down, up, middle, ends, scalars, hot, count):
    half = own.shape[1]
    slots = hot.shape[0] * hot.shape[1] // count
    tile = half // 4
    flat = [own, down, up, *middle, *ends]
    return pl.pallas_call(
        act_slots_kernel,
        out_shape=jax.ShapeDtypeStruct((count, slots, half), jnp.bfloat16),
        grid_spec=pltpu.PrefetchScalarGridSpec(
            num_scalar_prefetch=1,
            grid=(4,),
            in_specs=[resident(hot.shape)] + [pl.BlockSpec((part.shape[0], tile), lambda i, s: (0, i)) for part in flat],
            out_specs=pl.BlockSpec((count, slots, tile), lambda i, s: (0, 0, i)),
        ),
        compiler_params=params(),
        cost_estimate=cost(3.3),
        name="act_slots",
    )(scalars, hot, *flat)


def encoder_kernel(cap, shared, pre_ref, own_ref, theirs_ref, act_ref, out_ref):
    size = pre_ref.shape[2]
    for n in range(shared):
        parts = []
        for at in range(0, own_ref.shape[1], 2 * cap):
            for core in range(2):
                here = slice(at + core * cap, at + (core + 1) * cap)
                there = slice(at + (1 - core) * cap, at + (2 - core) * cap)
                parts.append(own_ref[n, here, :] + theirs_ref[n, there, :])
        total = jnp.concatenate(parts, axis=0)
        grad = jnp.where(pre_ref[n].astype(jnp.float32) > 0, total, 0.0).T.astype(jnp.bfloat16)
        out_ref[n * size:(n + 1) * size, :] = jnp.dot(
            grad, act_ref[n], preferred_element_type=jnp.float32
        ).astype(jnp.bfloat16)


def encoder_part(pre, own, theirs, acts, cap):
    blocks, slots, size = pre.shape
    half = acts.shape[2]
    shared = 2 if blocks % 2 == 0 else 1
    block = pl.BlockSpec((shared, slots, size), lambda i: (i, 0, 0))
    return pl.pallas_call(
        functools.partial(encoder_kernel, cap, shared),
        out_shape=jax.ShapeDtypeStruct((blocks * size, half), jnp.bfloat16),
        grid=(blocks // shared,),
        in_specs=[block, block, block, pl.BlockSpec((shared, slots, half), lambda i: (i, 0, 0))],
        out_specs=pl.BlockSpec((shared * size, half), lambda i: (i, 0)),
        compiler_params=params(),
        cost_estimate=cost(6.5),
        name="encoder_part",
    )(pre, own, theirs, acts)


def dense_plan(pre_codes, block_ids, activations, target, decoder):
    lay_count = lax.axis_size("layer")
    lat_count = lax.axis_size("latent")
    dp_count = lax.axis_size("dp")
    lay_here = lax.axis_index("layer")
    lat_here = lax.axis_index("latent")
    dp_here = lax.axis_index("dp")
    tok_count = activations.shape[1]
    model_width = activations.shape[2]
    active_count = block_ids.shape[2]
    block_size = pre_codes.shape[3]
    lat_rows = decoder.shape[1]
    local_blocks = lat_rows // block_size
    half = model_width // dp_count
    group = dp_count * tok_count
    tokens = lat_count * group
    width = half // lay_count
    side = width // 2
    f32, bf16 = jnp.float32, jnp.bfloat16
    first = lat_here * local_blocks
    capacity = 2 * tok_count * active_count // (local_blocks * lat_count)

    def columns(rows, which):
        return lax.dynamic_slice_in_dim(rows, which * half, half, axis=1)

    def places(names, offset, fine=1, sub=0):
        return [(offset + (lay_here ^ r)) * fine + sub for r in names]

    def weight_places(names):
        return jnp.stack(places(names, dp_here * lay_count))

    pre_rows = jnp.swapaxes(pre_codes[0], 0, 1).reshape(active_count * tok_count, block_size)
    id_rows = jnp.pad(block_ids[0].T, ((0, 16 - active_count), (0, 0))).astype(bf16)
    own = jnp.concatenate([pre_rows, id_rows], axis=0)
    at = places((1, 3), dp_here * lay_count, 2, 0) + places((2, 3), dp_here * lay_count, 2, 1)
    send_weights, token = gather_columns(decoder, jnp.stack(at), side)

    message = [own] + [flip(own, "latent", r) for r in range(1, lat_count)]

    own, inputs = lax.optimization_barrier((own, activations[0]))
    acts = jnp.concatenate([columns(inputs, dp_here), flip(columns(inputs, 1 - dp_here), "dp", 1)])
    message, acts = lax.optimization_barrier((join(message, token), acts))
    message = message.reshape((lat_count,) + own.shape)
    message = jnp.stack([message, flip(message, "dp", 1)], axis=1)
    message = message.reshape(lat_count * dp_count, own.shape[0], block_size)
    up, down = hop(acts, "latent", 1, 0), hop(acts, "latent", -1, 0)

    here, rest = spread_codes(message, first, lat_rows)
    at = places((0, 2), dp_here * lay_count, 2, 0) + places((0, 1), dp_here * lay_count, 2, 1)
    at, rest, target = lax.optimization_barrier((jnp.stack(at), rest, target))
    keep_weights, _ = gather_columns(decoder, at, side)
    goals, _ = gather_columns(target, jnp.stack([which * lay_count + lay_here for which in (dp_here, 1 - dp_here)]), width)
    goals = jnp.concatenate([goals[:, :width], flip(goals[:, width:], "dp", 1)])

    here, rest = spread_codes(message, first, lat_rows)
    at = places((0, 2), dp_here * lay_count, 2, 0) + places((0, 1), dp_here * lay_count, 2, 1)
    at, rest, target = lax.optimization_barrier((jnp.stack(at), rest, target))
    keep_weights, _ = gather_columns(decoder, at, side)
    goals, _ = gather_columns(target, jnp.stack([which * lay_count + lay_here for which in (dp_here, 1 - dp_here)]), width)
    goals = jnp.concatenate([goals[:, :width], flip(goals[:, width:], "dp", 1)])

    def rows_for(spread, weights, n):
        return jnp.dot(spread, weights[:, n * width:(n + 1) * width], preferred_element_type=f32).astype(bf16)

    def add(one, two):
        return (one[:, side:].astype(f32) + two[:, side:].astype(f32)).astype(bf16)

    got = flip(rows_for(rest, send_weights, 0), "layer", 1), flip(rows_for(rest, send_weights, 1), "layer", 2)
    keep_rest, up, down = lax.optimization_barrier((rest, up, down))
    cuts = slice(0, tok_count), slice(tok_count, group)
    ups, downs = [up[cut] for cut in cuts], [down[cut] for cut in cuts]
    up_two, down_two = [hop(ups[0], "latent", 1, 1)], [hop(downs[0], "latent", -1, 1)]
    kept = rows_for(keep_rest, keep_weights, 0), rows_for(keep_rest, keep_weights, 1)
    far = [flip(add(got[n], kept[n]), "layer", 2 - n) for n in range(2)]
    sent_here = rows_for(here, send_weights, 0), rows_for(here, send_weights, 1)
    kept_here = rows_for(here, keep_weights, 0), rows_for(here, keep_weights, 1)
    made = make_slots(message, first, lat_rows, capacity)
    made, goals, sent_here, kept_here, up_two, down_two, ups[1], downs[1], far = lax.optimization_barrier(
        (made, goals, sent_here, kept_here, up_two, down_two, ups[1], downs[1], far)
    )

    sent = layer_sum((got[0], kept[0], far[0]), (got[1], kept[1], far[1]), lat_count - 1)
    came = [flip(sent[r - 1], "latent", r) for r in range(1, lat_count)]
    got_here = flip(sent_here[0], "layer", 1), flip(sent_here[1], "layer", 2)
    far = [flip(add(got_here[n], kept_here[n]), "layer", 2 - n) for n in range(2)]
    relay = jnp.where(lat_here == 1, down_two[0], up_two[0])
    far, relay, came = lax.optimization_barrier((far, relay, came[::-1]))
    total = [got_here[n][:, :side].astype(f32) + kept_here[n][:, :side].astype(f32) + far[n].astype(f32) for n in range(2)]
    total = jnp.concatenate(total, axis=1)
    for block in came:
        total = total + block.astype(f32)
    errors = ((total - goals.astype(f32)) / tok_count).astype(bf16)
    others = [flip(errors, "latent", r) for r in range(1, lat_count)]
    one_near, two_near = flip(errors, "layer", 1), flip(errors, "layer", 2)
    others, one_near, two_near, relay, ups[1], downs[1] = lax.optimization_barrier(
        (others, one_near, two_near, relay, ups[1], downs[1])
    )
    distant = join(others)
    one_far, two_far = flip(distant, "layer", 1), flip(distant, "layer", 2)
    up_two.append(hop(ups[1], "latent", 1, 1))
    down_two.append(hop(downs[1], "latent", -1, 1))

    def last_hop(value):
        return lax.ppermute(value, "latent", [(lat_count - 2, lat_count - 1), (1, 0)])

    ends = [last_hop(relay)]
    hot, pre_slots, code_slots = made

    def grads_of(here, names, grad, dec):
        slots, grad = piece_grad(here, hot, decoder, weight_places(names), block_size, grad)
        return grad, decoder_part(slots, code_slots, jnp.stack(places(names, 0)), half, dec)

    grad, dec = grads_of([[(errors,), (distant,)]], (0,), None, None)
    grad, dec, up_two[1], down_two[1], two_far, one_far = lax.optimization_barrier(
        (grad, dec, up_two[1], down_two[1], two_far, one_far)
    )
    ends.append(last_hop(jnp.where(lat_here == 1, down_two[1], up_two[1])))
    three_a = flip(jnp.concatenate([two_near[:, :side], two_far[:, :side]]), "layer", 1)
    three_b = flip(jnp.concatenate([one_near[:, side:], one_far[:, side:]]), "layer", 2)
    grad, dec = grads_of([[(one_near,), (one_far,)], [(two_near,), (two_far,)]], (1, 2), grad, dec)

    middle = [down_two[part] + up_two[part] for part in range(2)]
    scalars = [lax.rem(lat_here + k, lat_count) ^ lat_here for k in range(lat_count)]
    scalars = jnp.stack(scalars + [(lat_here == lat_count - 1).astype(jnp.int32), (lat_here == 0).astype(jnp.int32)])
    slotted = act_slots(acts, down, up, middle, ends, scalars, hot, local_blocks)
    grad, dec, three_b, three_a = lax.optimization_barrier((grad, dec, three_b, three_a))
    grad, dec = grads_of([[(three_a, three_b)]], (3,), grad, dec)
    enc = encoder_part(pre_slots, grad, flip(grad, "dp", 1), slotted, capacity)
    return dec[None], enc[None]


def per_device(pre_codes, block_ids, activations, target, decoder):
    lat_count = lax.axis_size("latent")
    lay_count = lax.axis_size("layer")
    dp_count = lax.axis_size("dp")
    tok_count = activations.shape[1]
    model_width = activations.shape[2]
    active_count = block_ids.shape[2]
    block_size = pre_codes.shape[3]
    all_blocks = decoder.shape[1] // block_size * lat_count
    slots = 2 * tok_count * active_count // lat_count
    dense = (
        slots >= tok_count
        and dp_count == 2
        and active_count == 2
        and lay_count == 4
        and lat_count == 4
        and tok_count == block_size
        and lat_count * dp_count * 16 <= tok_count
        and model_width % (dp_count * 2 * lay_count * 128) == 0
        and all_blocks <= 256
        and 2 * tok_count * active_count == 8 * all_blocks
    )
    plan = dense_plan if dense else slot_plan
    return plan(pre_codes, block_ids, activations, target, decoder)


def solution(mesh):
    placed = (
        P("layer", ("latent", "dp"), None, None),
        P("layer", ("latent", "dp"), None),
        P("layer", ("latent", "dp"), None),
        P(("latent", "dp"), None),
        P("layer", "latent", None),
    )
    return jax.shard_map(
        per_device,
        mesh=mesh,
        in_specs=placed,
        out_specs=(P("layer", "latent", "dp"), P("layer", "latent", "dp")),
        check_vma=False,
    )
```

```python
import functools

import jax
import jax.numpy as jnp
from jax import lax
from jax.experimental import pallas as pl
from jax.experimental.pallas import tpu as pltpu
from jax.sharding import PartitionSpec as P

VMEM_BYTES = 40 * 1024 * 1024


def local_contrib(received_pre, weights, lat_count, local_blocks):
    code_vals = jnp.maximum(received_pre, jnp.zeros((), received_pre.dtype))
    slot_span = received_pre.shape[1]
    block_size = received_pre.shape[2]
    grouped = code_vals.reshape(lat_count, local_blocks, slot_span, block_size)
    contrib = jnp.einsum("sbcl,bld->sbcd", grouped, weights, preferred_element_type=jnp.float32)
    contrib = contrib.astype(jnp.bfloat16).reshape(
        lat_count * local_blocks, slot_span, weights.shape[2]
    )
    return lax.all_to_all(contrib, "latent", split_axis=0, concat_axis=0, tiled=True)


def slot_plan(pre_codes, block_ids, activations, target, decoder):
    lat_count = lax.axis_size("latent")
    tok_count = activations.shape[1]
    model_width = activations.shape[2]
    active_count = block_ids.shape[2]
    block_size = pre_codes.shape[3]
    lat_rows = decoder.shape[1]
    local_blocks = lat_rows // block_size
    all_blocks = local_blocks * lat_count
    capacity = 2 * tok_count * active_count // all_blocks
    slot_count = all_blocks * capacity
    pair_count = tok_count * active_count
    pair_block = block_ids[0].T.reshape(pair_count)
    member = (pair_block[:, None] == jnp.arange(all_blocks, dtype=jnp.int32)[None, :]).astype(
        jnp.int32
    )
    before = jnp.cumsum(member, axis=0) - member
    pair_rank = jnp.sum(before * member, axis=1)
    target_slot = pair_block * capacity + pair_rank
    slot_pair = (jnp.arange(slot_count, dtype=jnp.int32)[:, None] == target_slot[None, :]).astype(
        jnp.bfloat16
    )
    slot_token = jnp.sum(slot_pair.reshape(slot_count, active_count, tok_count), axis=1)
    pre_pairs = jnp.transpose(pre_codes[0], (1, 0, 2)).reshape(pair_count, block_size)
    pre_slots = jnp.dot(slot_pair, pre_pairs, preferred_element_type=jnp.float32).astype(
        jnp.bfloat16
    )
    pre_slots = pre_slots.reshape(all_blocks, capacity, block_size)
    inputs = activations[0]
    weights = decoder[0].reshape(local_blocks, block_size, model_width)
    input_slots = jnp.dot(slot_token, inputs, preferred_element_type=jnp.float32).astype(
        jnp.bfloat16
    )
    input_slots = input_slots.reshape(all_blocks, capacity, model_width)
    pieces = (
        lax.all_to_all(pre_slots, "latent", split_axis=0, concat_axis=0, tiled=True),
        lax.all_to_all(input_slots, "latent", split_axis=0, concat_axis=0, tiled=True),
    )
    returned = local_contrib(pieces[0], weights, lat_count, local_blocks)
    returned, received_pre, received_inputs = (returned, pieces[0], pieces[1])
    part_sum = jnp.einsum(
        "st,sd->td",
        slot_token,
        returned.reshape(slot_count, model_width),
        preferred_element_type=jnp.float32,
    )
    rebuilt = lax.psum(part_sum, "layer")
    errors = ((rebuilt - target.astype(jnp.float32)) / tok_count).astype(jnp.bfloat16)
    error_slots = jnp.dot(slot_token, errors, preferred_element_type=jnp.float32).astype(
        jnp.bfloat16
    )
    error_slots = error_slots.reshape(all_blocks, capacity, model_width)
    received_errors = lax.all_to_all(error_slots, "latent", split_axis=0, concat_axis=0, tiled=True)
    pre_blocks = received_pre.reshape(lat_count, local_blocks, capacity, block_size)
    code_blocks = jnp.maximum(pre_blocks, jnp.zeros((), pre_blocks.dtype))
    error_blocks = received_errors.reshape(lat_count, local_blocks, capacity, model_width)
    input_blocks = received_inputs.reshape(lat_count, local_blocks, capacity, model_width)
    code_grad = jnp.einsum(
        "sbcd,bld->sbcl", error_blocks, weights, preferred_element_type=jnp.float32
    )
    pre_grad = jnp.where(pre_blocks > 0, code_grad, jnp.zeros((), jnp.float32)).astype(jnp.bfloat16)
    dec_term = jnp.einsum(
        "sbcl,sbcd->bld", code_blocks, error_blocks, preferred_element_type=jnp.float32
    )
    enc_term = jnp.einsum(
        "sbcl,sbcd->bld", pre_grad, input_blocks, preferred_element_type=jnp.float32
    )
    dec_term = dec_term.reshape(lat_rows, model_width)
    enc_term = enc_term.reshape(lat_rows, model_width)
    dec_half, enc_half = (
        lax.psum_scatter(dec_term, "dp", scatter_dimension=1, tiled=True),
        lax.psum_scatter(enc_term, "dp", scatter_dimension=1, tiled=True),
    )
    return (dec_half.astype(jnp.bfloat16)[None], enc_half.astype(jnp.bfloat16)[None])


def flip(value, axis, bit):
    count = lax.axis_size(axis)
    return lax.ppermute(value, axis, [(i, i ^ bit) for i in range(count)])


def hop(value, axis, step, least):
    count = lax.axis_size(axis)
    if step > 0:
        pairs = [(i, i + 1) for i in range(least, count - 1)]
    else:
        pairs = [(i, i - 1) for i in range(1, count - least)]
    return lax.ppermute(value, axis, pairs)


def params():
    return pltpu.CompilerParams(vmem_limit_bytes=VMEM_BYTES)


def cost(microseconds):
    return pl.CostEstimate(flops=int(microseconds * 1.1e9), bytes_accessed=1, transcendentals=0)


def resident(shape):
    return pl.BlockSpec(shape, lambda i, s: (0,) * len(shape))


def gather_kernel(scalar_ref, source_ref, out_ref, token_ref):
    out_ref[...] = source_ref[...].reshape(out_ref.shape)
    token_ref[...] = jnp.zeros_like(token_ref)


def gather_columns(source, columns, width):
    rows = source.shape[-2]
    lead = (1,) * (source.ndim - 2)
    count = columns.shape[0]
    return pl.pallas_call(
        gather_kernel,
        out_shape=[
            pltpu.HBM((rows, count * width), source.dtype),
            jax.ShapeDtypeStruct((8, 128), jnp.float32),
        ],
        grid_spec=pltpu.PrefetchScalarGridSpec(
            num_scalar_prefetch=1,
            grid=(count,),
            in_specs=[pl.BlockSpec(lead + (rows, width), lambda i, s: (0,) * len(lead) + (0, s[i]))],
            out_specs=[pl.BlockSpec((rows, width), lambda i, s: (0, i)), resident((8, 128))],
        ),
        compiler_params=params(),
        cost_estimate=cost(0.9 * count),
        name="gather_columns",
    )(columns.astype(jnp.int32), source)


def codes_kernel(groups, blocks, scalar_ref, message_ref, codes, id_map, pre):
    tok = message_ref.shape[2]
    pad = message_ref.shape[1] - 2 * tok
    first = scalar_ref[0].astype(jnp.float32)
    rows = [message_ref[g, 2 * tok:2 * tok + pad, :].astype(jnp.float32) for g in range(groups)]
    fill = tok - groups * pad
    if fill:
        rows.append(jnp.zeros((fill, tok), jnp.float32))
    table = jnp.concatenate(rows, axis=0).T - first
    for g in range(groups):
        pre[g] = jnp.maximum(message_ref[g, 0:2 * tok, :], jnp.zeros((), jnp.bfloat16))
        for j in range(2):
            at = g * pad + j
            wide = jnp.broadcast_to(table[:, at:at + 1], (tok, tok))
            id_map[g, j * tok:(j + 1) * tok, :] = wide.astype(jnp.bfloat16)

    def block_step(b, carry):
        block = b.astype(jnp.float32).astype(jnp.bfloat16)
        at = pl.multiple_of(b * tok, tok)
        for g in range(groups):
            value = jnp.where(id_map[g, tok:2 * tok, :] == block, pre[g, tok:2 * tok, :], jnp.zeros((), jnp.bfloat16))
            value = jnp.where(id_map[g, 0:tok, :] == block, pre[g, 0:tok, :], value)
            codes[g * tok:(g + 1) * tok, pl.ds(at, tok)] = value
        return carry

    lax.fori_loop(0, blocks, block_step, 0)


def spread_codes(message, first, lat_rows):
    groups, _, tok = message.shape
    rows = groups * tok
    return pl.pallas_call(
        functools.partial(codes_kernel, groups, lat_rows // tok),
        out_shape=jax.ShapeDtypeStruct((rows, lat_rows), jnp.bfloat16),
        grid_spec=pltpu.PrefetchScalarGridSpec(
            num_scalar_prefetch=1,
            grid=(1,),
            in_specs=[resident(message.shape)],
            out_specs=resident((rows, lat_rows)),
            scratch_shapes=[
                pltpu.VMEM((groups, 2 * tok, tok), jnp.bfloat16),
                pltpu.VMEM((groups, 2 * tok, tok), jnp.bfloat16),
            ],
        ),
        compiler_params=params(),
        cost_estimate=cost(2.5),
        name="spread_codes",
    )(first[None].astype(jnp.int32), message)


def layer_sum_kernel(got_a, kept_a, far_a, got_b, kept_b, far_b, own_ref, *sent_refs):
    half = far_a.shape[1]
    rows = own_ref.shape[0]
    for side, (got, kept, far) in enumerate(((got_a, kept_a, far_a), (got_b, kept_b, far_b))):
        lanes = slice(side * half, (side + 1) * half)
        for n in range(1 + len(sent_refs)):
            at = slice(n * rows, (n + 1) * rows)
            total = got[at, :half].astype(jnp.float32) + kept[at, :half].astype(jnp.float32)
            total = total + far[at, :].astype(jnp.float32)
            if n:
                sent_refs[n - 1][:, lanes] = total.astype(jnp.bfloat16)
            else:
                own_ref[:, lanes] = total


def layer_sum(terms_a, terms_b, blocks):
    rows, half = terms_a[2].shape
    cut = (rows // blocks, 2 * half)
    return pl.pallas_call(
        layer_sum_kernel,
        out_shape=[jax.ShapeDtypeStruct(cut, jnp.float32)] + [jax.ShapeDtypeStruct(cut, jnp.bfloat16)] * (blocks - 1),
        grid=(1,),
        in_specs=[pl.BlockSpec((rows, half), lambda i: (0, 0)) for _ in range(6)],
        out_specs=[pl.BlockSpec(cut, lambda i: (0, 0))] * blocks,
        compiler_params=params(),
        cost_estimate=cost(0.5),
        name="layer_sum",
    )(*terms_a, *terms_b)


def join_kernel(count, *refs):
    out_ref = refs[-1]
    rows = out_ref.shape[0] // count
    for i in range(count):
        out_ref[i * rows:(i + 1) * rows] = refs[i][...]


def join(parts, *waited):
    shape = (len(parts) * parts[0].shape[0],) + parts[0].shape[1:]
    vmem = pl.BlockSpec(memory_space=pltpu.VMEM)
    return pl.pallas_call(
        functools.partial(join_kernel, len(parts)),
        out_shape=jax.ShapeDtypeStruct(shape, parts[0].dtype),
        in_specs=[vmem] * (len(parts) + len(waited)),
        out_specs=vmem,
        compiler_params=params(),
        cost_estimate=cost(0.4),
        name="join",
    )(*parts, *waited)


def slots_kernel(groups, blocks, cap, scalar_ref, message_ref, hot_ref, pre_ref, code_ref):
    tok = message_ref.shape[2]
    pad = message_ref.shape[1] - 2 * tok
    f32, bf16 = jnp.float32, jnp.bfloat16
    first = scalar_ref[0].astype(f32)
    rows = [message_ref[g, 2 * tok:2 * tok + pad, :].astype(f32) for g in range(groups)]
    fill = tok - groups * pad
    table = jnp.concatenate(rows + ([jnp.zeros((fill, tok), f32)] if fill else []), axis=0).T
    earlier = lax.broadcasted_iota(jnp.int32, (tok, tok), 0) < lax.broadcasted_iota(jnp.int32, (tok, tok), 1)
    per = 2 * cap
    for z in range(groups // 2):
        pre = 0.0
        hot = []
        for core in range(2):
            g = 2 * z + core
            lanes = [rows[g][j:j + 1] for j in range(2)]
            down = [table[:, g * pad + j:g * pad + j + 1] for j in range(2)]
            same = [jnp.where((down[j] == lanes[j]) & earlier, 1.0, 0.0) for j in range(2)]
            cross = jnp.where(down[0] == lanes[1], 1.0, 0.0)
            rank = [jnp.sum(same[0], axis=0, keepdims=True), jnp.sum(same[1] + cross, axis=0, keepdims=True)]
            here = []
            for j in range(2):
                block = lanes[j] - first
                slot = block * per + (core * cap + rank[j])
                slot = jnp.where((block >= 0) & (block < blocks), slot, -1.0)
                number = lax.broadcasted_iota(jnp.int32, (blocks * per, tok), 0).astype(f32)
                here.append(jnp.where(number == slot, 1.0, 0.0).astype(bf16))
                pre = pre + jnp.dot(
                    here[j], message_ref[g, j * tok:(j + 1) * tok, :], preferred_element_type=f32
                )
            hot.append(here[0] + here[1])
        hot_ref[z] = jnp.concatenate(hot, axis=1)
        for b in range(blocks):
            pre_ref[b, z * per:(z + 1) * per, :] = pre[b * per:(b + 1) * per].astype(bf16)
    for b in range(blocks):
        code_ref[b] = jnp.maximum(pre_ref[b].astype(f32), 0.0).T.astype(bf16)


def make_slots(message, first, lat_rows, cap):
    groups, _, tok = message.shape
    blocks = lat_rows // tok
    per = 2 * cap
    shards = groups // 2
    shapes = [(shards, blocks * per, 2 * tok), (blocks, shards * per, tok), (blocks, tok, shards * per)]
    return pl.pallas_call(
        functools.partial(slots_kernel, groups, blocks, cap),
        out_shape=[jax.ShapeDtypeStruct(shape, jnp.bfloat16) for shape in shapes],
        grid_spec=pltpu.PrefetchScalarGridSpec(
            num_scalar_prefetch=1,
            grid=(1,),
            in_specs=[resident(message.shape)],
            out_specs=[resident(shape) for shape in shapes],
        ),
        compiler_params=params(),
        cost_estimate=cost(1),
        name="make_slots",
    )(first[None].astype(jnp.int32), message)


def into_slots(hot, rows, out, z):
    per = out.shape[1] // hot.shape[0]
    value = jnp.dot(hot[z], rows, preferred_element_type=jnp.float32).astype(jnp.bfloat16)
    for b in range(out.shape[0]):
        out[b, z * per:(z + 1) * per, :] = value[b * per:(b + 1) * per]


def lanes_of(refs, rows):
    parts = [r[rows, :] for r in refs]
    return parts[0] if len(parts) == 1 else jnp.concatenate(parts, axis=1)


def piece_grad_kernel(layout, onto, scalar_ref, hot_ref, weight_ref, *refs):
    parts, (slots_ref, grad_ref) = refs[onto:-2], refs[-2:]
    blocks, _, size = grad_ref.shape
    group = hot_ref.shape[2]
    step = pl.program_id(0)

    @pl.when(step == 0)
    def _():
        grad_ref[...] = refs[0][...] if onto else jnp.zeros_like(grad_ref)

    at = 0
    for i, piece in enumerate(layout):
        z = 0
        for lanes in piece:
            here = parts[at:at + lanes]
            at += lanes
            for n in range(here[0].shape[0] // group):

                @pl.when(step == i)
                def _(z=z, n=n, here=here):
                    into_slots(hot_ref, lanes_of(here, slice(n * group, (n + 1) * group)), slots_ref.at[0], z)

                z += 1
    for b in range(blocks):
        grad_ref[b] += lax.dot_general(
            slots_ref[0, b],
            weight_ref[0, b * size:(b + 1) * size, :],
            (((1,), (1,)), ((), ())),
            preferred_element_type=jnp.float32,
        )


def piece_grad(pieces, hot, decoder, columns, size, held):
    lat_rows = decoder.shape[1]
    blocks = lat_rows // size
    slots = hot.shape[0] * hot.shape[1] // blocks
    width = sum(p.shape[1] for p in pieces[0][0])
    flat = [p for piece in pieces for row in piece for p in row]
    onto = [] if held is None else [held]
    return pl.pallas_call(
        functools.partial(piece_grad_kernel, [[len(row) for row in piece] for piece in pieces], len(onto)),
        out_shape=[
            jax.ShapeDtypeStruct((len(pieces), blocks, slots, width), jnp.bfloat16),
            jax.ShapeDtypeStruct((blocks, slots, size), jnp.float32),
        ],
        grid_spec=pltpu.PrefetchScalarGridSpec(
            num_scalar_prefetch=1,
            grid=(len(pieces),),
            in_specs=[resident(hot.shape), pl.BlockSpec((1, lat_rows, width), lambda i, s: (0, 0, s[i]))]
            + [resident(p.shape) for p in onto + flat],
            out_specs=[
                pl.BlockSpec((1, blocks, slots, width), lambda i, s: (i, 0, 0, 0)),
                resident((blocks, slots, size)),
            ],
        ),
        compiler_params=params(),
        cost_estimate=cost(0.8 + 2 * len(pieces)),
        name="piece_grad",
    )(columns.astype(jnp.int32), hot, decoder, *onto, *flat)


def decoder_kernel(skip, scalar_ref, code_ref, slots_ref, *refs):
    out_ref = refs[skip]
    size = code_ref.shape[1]
    for b in range(code_ref.shape[0]):
        out_ref[b * size:(b + 1) * size, :] = jnp.dot(
            code_ref[b], slots_ref[0, b], preferred_element_type=jnp.float32
        ).astype(jnp.bfloat16)


def decoder_part(slots, codes, columns, half, held):
    count, blocks, _, width = slots.shape
    lat_rows = blocks * codes.shape[1]
    onto = [] if held is None else [held]
    return pl.pallas_call(
        functools.partial(decoder_kernel, len(onto)),
        out_shape=jax.ShapeDtypeStruct((lat_rows, half), jnp.bfloat16),
        grid_spec=pltpu.PrefetchScalarGridSpec(
            num_scalar_prefetch=1,
            grid=(count,),
            in_specs=[resident(codes.shape), pl.BlockSpec((1,) + slots.shape[1:], lambda i, s: (i, 0, 0, 0))]
            + [pl.BlockSpec(memory_space=pl.ANY) for _ in onto],
            out_specs=pl.BlockSpec((lat_rows, width), lambda i, s: (0, s[i])),
        ),
        compiler_params=params(),
        input_output_aliases={3: 0} if onto else {},
        cost_estimate=cost(0.7 + 1.3 * count),
        name="decoder_part",
    )(columns.astype(jnp.int32), codes, slots, *onto)


def act_slots_kernel(scalar_ref, hot_ref, own_ref, down_ref, up_ref, down_two_ref, up_two_ref, end_ref, out_ref):
    per = out_ref.shape[1] // hot_ref.shape[0]
    last = end_ref[...]
    zero = jnp.zeros((), last.dtype)
    rows = [
        own_ref[...],
        down_ref[...] + jnp.where(scalar_ref[4] > 0, last, zero),
        down_two_ref[...] + up_two_ref[...],
        up_ref[...] + jnp.where(scalar_ref[5] > 0, last, zero),
    ]
    for i in range(4):
        z = scalar_ref[i]
        value = jnp.dot(hot_ref[z], rows[i], preferred_element_type=jnp.float32).astype(jnp.bfloat16)
        to = pl.ds(pl.multiple_of(z * per, per), per)
        for b in range(out_ref.shape[0]):
            out_ref[b, to, :] = value[b * per:(b + 1) * per]


def act_slots(parts, scalars, hot, count):
    half = parts[0].shape[1]
    slots = hot.shape[0] * hot.shape[1] // count
    tile = half // 4
    return pl.pallas_call(
        act_slots_kernel,
        out_shape=jax.ShapeDtypeStruct((count, slots, half), jnp.bfloat16),
        grid_spec=pltpu.PrefetchScalarGridSpec(
            num_scalar_prefetch=1,
            grid=(4,),
            in_specs=[resident(hot.shape)] + [pl.BlockSpec((part.shape[0], tile), lambda i, s: (0, i)) for part in parts],
            out_specs=pl.BlockSpec((count, slots, tile), lambda i, s: (0, 0, i)),
        ),
        compiler_params=params(),
        cost_estimate=cost(3.3),
        name="act_slots",
    )(scalars, hot, *parts)


def encoder_kernel(cap, shared, pre_ref, own_ref, theirs_ref, act_ref, out_ref):
    size = pre_ref.shape[2]
    for n in range(shared):
        parts = []
        for at in range(0, own_ref.shape[1], 2 * cap):
            for core in range(2):
                here = slice(at + core * cap, at + (core + 1) * cap)
                there = slice(at + (1 - core) * cap, at + (2 - core) * cap)
                parts.append(own_ref[n, here, :] + theirs_ref[n, there, :])
        total = jnp.concatenate(parts, axis=0)
        grad = jnp.where(pre_ref[n].astype(jnp.float32) > 0, total, 0.0).T.astype(jnp.bfloat16)
        out_ref[n * size:(n + 1) * size, :] = jnp.dot(
            grad, act_ref[n], preferred_element_type=jnp.float32
        ).astype(jnp.bfloat16)


def encoder_part(pre, own, theirs, acts, cap):
    blocks, slots, size = pre.shape
    half = acts.shape[2]
    shared = 2 if blocks % 2 == 0 else 1
    block = pl.BlockSpec((shared, slots, size), lambda i: (i, 0, 0))
    return pl.pallas_call(
        functools.partial(encoder_kernel, cap, shared),
        out_shape=jax.ShapeDtypeStruct((blocks * size, half), jnp.bfloat16),
        grid=(blocks // shared,),
        in_specs=[block, block, block, pl.BlockSpec((shared, slots, half), lambda i: (i, 0, 0))],
        out_specs=pl.BlockSpec((shared * size, half), lambda i: (i, 0)),
        compiler_params=params(),
        cost_estimate=cost(6.5),
        name="encoder_part",
    )(pre, own, theirs, acts)


def dense_plan(pre_codes, block_ids, activations, target, decoder):
    lay_count = lax.axis_size("layer")
    lat_count = lax.axis_size("latent")
    dp_count = lax.axis_size("dp")
    lay_here = lax.axis_index("layer")
    lat_here = lax.axis_index("latent")
    dp_here = lax.axis_index("dp")
    tok_count = activations.shape[1]
    model_width = activations.shape[2]
    active_count = block_ids.shape[2]
    block_size = pre_codes.shape[3]
    lat_rows = decoder.shape[1]
    local_blocks = lat_rows // block_size
    half = model_width // dp_count
    group = dp_count * tok_count
    tokens = lat_count * group
    width = half // lay_count
    side = width // 2
    f32, bf16 = jnp.float32, jnp.bfloat16
    first = lat_here * local_blocks
    capacity = 2 * tok_count * active_count // (local_blocks * lat_count)

    def columns(rows, which):
        return lax.dynamic_slice_in_dim(rows, which * half, half, axis=1)

    def places(names, offset, fine=1, sub=0):
        return [(offset + (lay_here ^ r)) * fine + sub for r in names]

    def weight_places(names):
        return jnp.stack(places(names, dp_here * lay_count))

    pre_rows = jnp.swapaxes(pre_codes[0], 0, 1).reshape(active_count * tok_count, block_size)
    id_rows = jnp.pad(block_ids[0].T, ((0, 16 - active_count), (0, 0))).astype(bf16)
    own = jnp.concatenate([pre_rows, id_rows], axis=0)
    at = places((1, 3), dp_here * lay_count, 2, 0) + places((2, 3), dp_here * lay_count, 2, 1)
    send_weights, token = gather_columns(decoder, jnp.stack(at), side)

    message = [own] + [flip(own, "latent", r) for r in range(1, lat_count)]

    own, inputs = lax.optimization_barrier((own, activations[0]))
    acts = jnp.concatenate([columns(inputs, dp_here), flip(columns(inputs, 1 - dp_here), "dp", 1)])
    message, acts = lax.optimization_barrier((join(message, token), acts))
    message = message.reshape((lat_count,) + own.shape)
    up, down = [acts], [acts]

    def next_hops():
        step = len(up)
        up.append(hop(up[-1], "latent", 1, step - 1))
        down.append(hop(down[-1], "latent", -1, step - 1))

    message = jnp.stack([message, flip(message, "dp", 1)], axis=1)
    message = message.reshape(lat_count * dp_count, own.shape[0], block_size)
    next_hops()

    codes = spread_codes(message, first, lat_rows)
    at = places((0, 2), dp_here * lay_count, 2, 0) + places((0, 1), dp_here * lay_count, 2, 1)
    at, codes, target = lax.optimization_barrier((jnp.stack(at), codes, target))
    keep_weights, _ = gather_columns(decoder, at, side)
    goals, _ = gather_columns(target, jnp.stack([which * lay_count + lay_here for which in (dp_here, 1 - dp_here)]), width)
    goals = jnp.concatenate([goals[:, :width], flip(goals[:, width:], "dp", 1)])

    codes = spread_codes(message, first, lat_rows)
    at = places((0, 2), dp_here * lay_count, 2, 0) + places((0, 1), dp_here * lay_count, 2, 1)
    at, codes, target = lax.optimization_barrier((jnp.stack(at), codes, target))
    keep_weights, _ = gather_columns(decoder, at, side)
    goals, _ = gather_columns(target, jnp.stack([which * lay_count + lay_here for which in (dp_here, 1 - dp_here)]), width)
    goals = jnp.concatenate([goals[:, :width], flip(goals[:, width:], "dp", 1)])

    def rows_for(spread, weights, n):
        return jnp.dot(spread, weights[:, n * width:(n + 1) * width], preferred_element_type=f32).astype(bf16)

    got = flip(rows_for(codes, send_weights, 0), "layer", 1), flip(rows_for(codes, send_weights, 1), "layer", 2)
    keep_codes, up[1], down[1] = lax.optimization_barrier((codes, up[1], down[1]))
    if lat_count > 2:
        next_hops()
    kept = rows_for(keep_codes, keep_weights, 0), rows_for(keep_codes, keep_weights, 1)

    def add(one, two):
        return (one[:, side:].astype(f32) + two[:, side:].astype(f32)).astype(bf16)

    far = [flip(add(got[n], kept[n]), "layer", 2 - n) for n in range(2)]
    made = make_slots(message, first, lat_rows, capacity)
    far, goals, up[-1], down[-1], made = lax.optimization_barrier((far, goals, up[-1], down[-1], made))
    while len(up) < lat_count - 1:
        next_hops()
    relay = jnp.where(lat_here == 1, down[-1], up[-1])

    total, *sent = layer_sum((got[0], kept[0], far[0]), (got[1], kept[1], far[1]), lat_count)
    for r in range(1, lat_count):
        total = total + flip(sent[r - 1], "latent", r).astype(f32)
    errors = ((total - goals.astype(f32)) / tok_count).astype(bf16)
    others = [flip(errors, "latent", r) for r in range(1, lat_count)]
    one_near, two_near = flip(errors, "layer", 1), flip(errors, "layer", 2)
    next_block, *others = others
    one_next, two_next = flip(next_block, "layer", 1), flip(next_block, "layer", 2)
    others, two_next, one_next, two_near, one_near, next_block, relay = lax.optimization_barrier(
        (others, two_next, one_next, two_near, one_near, next_block, relay)
    )
    distant = join(others)
    one_far, two_far = flip(distant, "layer", 1), flip(distant, "layer", 2)
    ends = lax.ppermute(relay, "latent", [(lat_count - 2, lat_count - 1), (1, 0)])

    hot, pre_slots, code_slots = made

    def grads_of(here, names, grad, dec):
        slots, grad = piece_grad(here, hot, decoder, weight_places(names), block_size, grad)
        return grad, decoder_part(slots, code_slots, jnp.stack(places(names, 0)), half, dec)

    grad, dec = grads_of([[(errors,), (next_block,), (distant,)]], (0,), None, None)
    grad, dec, two_far, one_far = lax.optimization_barrier((grad, dec, two_far, one_far))
    one, two = (one_near, one_next, one_far), (two_near, two_next, two_far)
    three_a = flip(jnp.concatenate([rows[:, :side] for rows in two]), "layer", 1)
    three_b = flip(jnp.concatenate([rows[:, side:] for rows in one]), "layer", 2)
    grad, dec = grads_of([[(rows,) for rows in one], [(rows,) for rows in two]], (1, 2), grad, dec)

    scalars = [lax.rem(lat_here + k, lat_count) ^ lat_here for k in range(lat_count)]
    scalars = jnp.stack(scalars + [(lat_here == lat_count - 1).astype(jnp.int32), (lat_here == 0).astype(jnp.int32)])
    slotted = act_slots((acts, down[1], up[1], down[2], up[2], ends), scalars, hot, local_blocks)
    three_a, three_b, grad, dec, slotted = lax.optimization_barrier((three_a, three_b, grad, dec, slotted))
    grad, dec = grads_of([[(three_a, three_b)]], (3,), grad, dec)
    enc = encoder_part(pre_slots, grad, flip(grad, "dp", 1), slotted, capacity)
    return dec[None], enc[None]


def per_device(pre_codes, block_ids, activations, target, decoder):
    lat_count = lax.axis_size("latent")
    lay_count = lax.axis_size("layer")
    dp_count = lax.axis_size("dp")
    tok_count = activations.shape[1]
    model_width = activations.shape[2]
    active_count = block_ids.shape[2]
    block_size = pre_codes.shape[3]
    all_blocks = decoder.shape[1] // block_size * lat_count
    slots = 2 * tok_count * active_count // lat_count
    dense = (
        slots >= tok_count
        and dp_count == 2
        and active_count == 2
        and lay_count == 4
        and lat_count == 4
        and tok_count == block_size
        and lat_count * dp_count * 16 <= tok_count
        and model_width % (dp_count * 2 * lay_count * 128) == 0
        and all_blocks <= 256
        and 2 * tok_count * active_count == 8 * all_blocks
    )
    plan = dense_plan if dense else slot_plan
    return plan(pre_codes, block_ids, activations, target, decoder)


def solution(mesh):
    placed = (
        P("layer", ("latent", "dp"), None, None),
        P("layer", ("latent", "dp"), None),
        P("layer", ("latent", "dp"), None),
        P(("latent", "dp"), None),
        P("layer", "latent", None),
    )
    return jax.shard_map(
        per_device,
        mesh=mesh,
        in_specs=placed,
        out_specs=(P("layer", "latent", "dp"), P("layer", "latent", "dp")),
        check_vma=False,
    )
```

```python
import functools

import jax
import jax.numpy as jnp
from jax import lax
from jax.experimental import pallas as pl
from jax.experimental.pallas import tpu as pltpu
from jax.sharding import PartitionSpec as P

VMEM_BYTES = 40 * 1024 * 1024


def local_contrib(received_pre, weights, lat_count, local_blocks):
    code_vals = jnp.maximum(received_pre, jnp.zeros((), received_pre.dtype))
    slot_span = received_pre.shape[1]
    block_size = received_pre.shape[2]
    grouped = code_vals.reshape(lat_count, local_blocks, slot_span, block_size)
    contrib = jnp.einsum("sbcl,bld->sbcd", grouped, weights, preferred_element_type=jnp.float32)
    contrib = contrib.astype(jnp.bfloat16).reshape(
        lat_count * local_blocks, slot_span, weights.shape[2]
    )
    return lax.all_to_all(contrib, "latent", split_axis=0, concat_axis=0, tiled=True)


def slot_plan(pre_codes, block_ids, activations, target, decoder):
    lat_count = lax.axis_size("latent")
    tok_count = activations.shape[1]
    model_width = activations.shape[2]
    active_count = block_ids.shape[2]
    block_size = pre_codes.shape[3]
    lat_rows = decoder.shape[1]
    local_blocks = lat_rows // block_size
    all_blocks = local_blocks * lat_count
    capacity = 2 * tok_count * active_count // all_blocks
    slot_count = all_blocks * capacity
    pair_count = tok_count * active_count
    pair_block = block_ids[0].T.reshape(pair_count)
    member = (pair_block[:, None] == jnp.arange(all_blocks, dtype=jnp.int32)[None, :]).astype(
        jnp.int32
    )
    before = jnp.cumsum(member, axis=0) - member
    pair_rank = jnp.sum(before * member, axis=1)
    target_slot = pair_block * capacity + pair_rank
    slot_pair = (jnp.arange(slot_count, dtype=jnp.int32)[:, None] == target_slot[None, :]).astype(
        jnp.bfloat16
    )
    slot_token = jnp.sum(slot_pair.reshape(slot_count, active_count, tok_count), axis=1)
    pre_pairs = jnp.transpose(pre_codes[0], (1, 0, 2)).reshape(pair_count, block_size)
    pre_slots = jnp.dot(slot_pair, pre_pairs, preferred_element_type=jnp.float32).astype(
        jnp.bfloat16
    )
    pre_slots = pre_slots.reshape(all_blocks, capacity, block_size)
    inputs = activations[0]
    weights = decoder[0].reshape(local_blocks, block_size, model_width)
    input_slots = jnp.dot(slot_token, inputs, preferred_element_type=jnp.float32).astype(
        jnp.bfloat16
    )
    input_slots = input_slots.reshape(all_blocks, capacity, model_width)
    pieces = (
        lax.all_to_all(pre_slots, "latent", split_axis=0, concat_axis=0, tiled=True),
        lax.all_to_all(input_slots, "latent", split_axis=0, concat_axis=0, tiled=True),
    )
    returned = local_contrib(pieces[0], weights, lat_count, local_blocks)
    returned, received_pre, received_inputs = (returned, pieces[0], pieces[1])
    part_sum = jnp.einsum(
        "st,sd->td",
        slot_token,
        returned.reshape(slot_count, model_width),
        preferred_element_type=jnp.float32,
    )
    rebuilt = lax.psum(part_sum, "layer")
    errors = ((rebuilt - target.astype(jnp.float32)) / tok_count).astype(jnp.bfloat16)
    error_slots = jnp.dot(slot_token, errors, preferred_element_type=jnp.float32).astype(
        jnp.bfloat16
    )
    error_slots = error_slots.reshape(all_blocks, capacity, model_width)
    received_errors = lax.all_to_all(error_slots, "latent", split_axis=0, concat_axis=0, tiled=True)
    pre_blocks = received_pre.reshape(lat_count, local_blocks, capacity, block_size)
    code_blocks = jnp.maximum(pre_blocks, jnp.zeros((), pre_blocks.dtype))
    error_blocks = received_errors.reshape(lat_count, local_blocks, capacity, model_width)
    input_blocks = received_inputs.reshape(lat_count, local_blocks, capacity, model_width)
    code_grad = jnp.einsum(
        "sbcd,bld->sbcl", error_blocks, weights, preferred_element_type=jnp.float32
    )
    pre_grad = jnp.where(pre_blocks > 0, code_grad, jnp.zeros((), jnp.float32)).astype(jnp.bfloat16)
    dec_term = jnp.einsum(
        "sbcl,sbcd->bld", code_blocks, error_blocks, preferred_element_type=jnp.float32
    )
    enc_term = jnp.einsum(
        "sbcl,sbcd->bld", pre_grad, input_blocks, preferred_element_type=jnp.float32
    )
    dec_term = dec_term.reshape(lat_rows, model_width)
    enc_term = enc_term.reshape(lat_rows, model_width)
    dec_half, enc_half = (
        lax.psum_scatter(dec_term, "dp", scatter_dimension=1, tiled=True),
        lax.psum_scatter(enc_term, "dp", scatter_dimension=1, tiled=True),
    )
    return (dec_half.astype(jnp.bfloat16)[None], enc_half.astype(jnp.bfloat16)[None])


def flip(value, axis, bit):
    count = lax.axis_size(axis)
    return lax.ppermute(value, axis, [(i, i ^ bit) for i in range(count)])


def hop(value, axis, step, least):
    count = lax.axis_size(axis)
    if step > 0:
        pairs = [(i, i + 1) for i in range(least, count - 1)]
    else:
        pairs = [(i, i - 1) for i in range(1, count - least)]
    return lax.ppermute(value, axis, pairs)


def params():
    return pltpu.CompilerParams(vmem_limit_bytes=VMEM_BYTES)


def cost(microseconds):
    return pl.CostEstimate(flops=int(microseconds * 1.1e9), bytes_accessed=1, transcendentals=0)


def resident(shape):
    return pl.BlockSpec(shape, lambda i, s: (0,) * len(shape))


def gather_kernel(scalar_ref, source_ref, out_ref, token_ref):
    out_ref[...] = source_ref[...].reshape(out_ref.shape)
    token_ref[...] = jnp.zeros_like(token_ref)


def gather_columns(source, columns, width):
    rows = source.shape[-2]
    lead = (1,) * (source.ndim - 2)
    count = columns.shape[0]
    return pl.pallas_call(
        gather_kernel,
        out_shape=[
            pltpu.HBM((rows, count * width), source.dtype),
            jax.ShapeDtypeStruct((8, 128), jnp.float32),
        ],
        grid_spec=pltpu.PrefetchScalarGridSpec(
            num_scalar_prefetch=1,
            grid=(count,),
            in_specs=[pl.BlockSpec(lead + (rows, width), lambda i, s: (0,) * len(lead) + (0, s[i]))],
            out_specs=[pl.BlockSpec((rows, width), lambda i, s: (0, i)), resident((8, 128))],
        ),
        compiler_params=params(),
        cost_estimate=cost(0.9 * count),
        name="gather_columns",
    )(columns.astype(jnp.int32), source)


def codes_kernel(groups, blocks, scalar_ref, message_ref, codes, id_map, pre):
    tok = message_ref.shape[2]
    pad = message_ref.shape[1] - 2 * tok
    first = scalar_ref[0].astype(jnp.float32)
    rows = [message_ref[g, 2 * tok:2 * tok + pad, :].astype(jnp.float32) for g in range(groups)]
    fill = tok - groups * pad
    if fill:
        rows.append(jnp.zeros((fill, tok), jnp.float32))
    table = jnp.concatenate(rows, axis=0).T - first
    for g in range(groups):
        pre[g] = jnp.maximum(message_ref[g, 0:2 * tok, :], jnp.zeros((), jnp.bfloat16))
        for j in range(2):
            at = g * pad + j
            wide = jnp.broadcast_to(table[:, at:at + 1], (tok, tok))
            id_map[g, j * tok:(j + 1) * tok, :] = wide.astype(jnp.bfloat16)

    def block_step(b, carry):
        block = b.astype(jnp.float32).astype(jnp.bfloat16)
        at = pl.multiple_of(b * tok, tok)
        for g in range(groups):
            value = jnp.where(id_map[g, tok:2 * tok, :] == block, pre[g, tok:2 * tok, :], jnp.zeros((), jnp.bfloat16))
            value = jnp.where(id_map[g, 0:tok, :] == block, pre[g, 0:tok, :], value)
            codes[g * tok:(g + 1) * tok, pl.ds(at, tok)] = value
        return carry

    lax.fori_loop(0, blocks, block_step, 0)


def spread_codes(message, first, lat_rows):
    groups, _, tok = message.shape
    rows = groups * tok
    return pl.pallas_call(
        functools.partial(codes_kernel, groups, lat_rows // tok),
        out_shape=jax.ShapeDtypeStruct((rows, lat_rows), jnp.bfloat16),
        grid_spec=pltpu.PrefetchScalarGridSpec(
            num_scalar_prefetch=1,
            grid=(1,),
            in_specs=[resident(message.shape)],
            out_specs=resident((rows, lat_rows)),
            scratch_shapes=[
                pltpu.VMEM((groups, 2 * tok, tok), jnp.bfloat16),
                pltpu.VMEM((groups, 2 * tok, tok), jnp.bfloat16),
            ],
        ),
        compiler_params=params(),
        cost_estimate=cost(2.5),
        name="spread_codes",
    )(first[None].astype(jnp.int32), message)


def layer_sum_kernel(got_a, kept_a, far_a, got_b, kept_b, far_b, own_ref, *sent_refs):
    half = far_a.shape[1]
    rows = own_ref.shape[0]
    for side, (got, kept, far) in enumerate(((got_a, kept_a, far_a), (got_b, kept_b, far_b))):
        lanes = slice(side * half, (side + 1) * half)
        for n in range(1 + len(sent_refs)):
            at = slice(n * rows, (n + 1) * rows)
            total = got[at, :half].astype(jnp.float32) + kept[at, :half].astype(jnp.float32)
            total = total + far[at, :].astype(jnp.float32)
            if n:
                sent_refs[n - 1][:, lanes] = total.astype(jnp.bfloat16)
            else:
                own_ref[:, lanes] = total


def layer_sum(terms_a, terms_b, blocks):
    rows, half = terms_a[2].shape
    cut = (rows // blocks, 2 * half)
    return pl.pallas_call(
        layer_sum_kernel,
        out_shape=[jax.ShapeDtypeStruct(cut, jnp.float32)] + [jax.ShapeDtypeStruct(cut, jnp.bfloat16)] * (blocks - 1),
        grid=(1,),
        in_specs=[pl.BlockSpec((rows, half), lambda i: (0, 0)) for _ in range(6)],
        out_specs=[pl.BlockSpec(cut, lambda i: (0, 0))] * blocks,
        compiler_params=params(),
        cost_estimate=cost(0.5),
        name="layer_sum",
    )(*terms_a, *terms_b)


def join_kernel(count, *refs):
    out_ref = refs[-1]
    rows = out_ref.shape[0] // count
    for i in range(count):
        out_ref[i * rows:(i + 1) * rows] = refs[i][...]


def join(parts, *waited):
    shape = (len(parts) * parts[0].shape[0],) + parts[0].shape[1:]
    vmem = pl.BlockSpec(memory_space=pltpu.VMEM)
    return pl.pallas_call(
        functools.partial(join_kernel, len(parts)),
        out_shape=jax.ShapeDtypeStruct(shape, parts[0].dtype),
        in_specs=[vmem] * (len(parts) + len(waited)),
        out_specs=vmem,
        compiler_params=params(),
        cost_estimate=cost(0.4),
        name="join",
    )(*parts, *waited)


def slots_kernel(groups, blocks, cap, scalar_ref, message_ref, hot_ref, pre_ref, code_ref):
    tok = message_ref.shape[2]
    pad = message_ref.shape[1] - 2 * tok
    f32, bf16 = jnp.float32, jnp.bfloat16
    first = scalar_ref[0].astype(f32)
    rows = [message_ref[g, 2 * tok:2 * tok + pad, :].astype(f32) for g in range(groups)]
    fill = tok - groups * pad
    table = jnp.concatenate(rows + ([jnp.zeros((fill, tok), f32)] if fill else []), axis=0).T
    earlier = lax.broadcasted_iota(jnp.int32, (tok, tok), 0) < lax.broadcasted_iota(jnp.int32, (tok, tok), 1)
    per = 2 * cap
    for z in range(groups // 2):
        pre = 0.0
        hot = []
        for core in range(2):
            g = 2 * z + core
            lanes = [rows[g][j:j + 1] for j in range(2)]
            down = [table[:, g * pad + j:g * pad + j + 1] for j in range(2)]
            same = [jnp.where((down[j] == lanes[j]) & earlier, 1.0, 0.0) for j in range(2)]
            cross = jnp.where(down[0] == lanes[1], 1.0, 0.0)
            rank = [jnp.sum(same[0], axis=0, keepdims=True), jnp.sum(same[1] + cross, axis=0, keepdims=True)]
            here = []
            for j in range(2):
                block = lanes[j] - first
                slot = block * per + (core * cap + rank[j])
                slot = jnp.where((block >= 0) & (block < blocks), slot, -1.0)
                number = lax.broadcasted_iota(jnp.int32, (blocks * per, tok), 0).astype(f32)
                here.append(jnp.where(number == slot, 1.0, 0.0).astype(bf16))
                pre = pre + jnp.dot(
                    here[j], message_ref[g, j * tok:(j + 1) * tok, :], preferred_element_type=f32
                )
            hot.append(here[0] + here[1])
        hot_ref[z] = jnp.concatenate(hot, axis=1)
        for b in range(blocks):
            pre_ref[b, z * per:(z + 1) * per, :] = pre[b * per:(b + 1) * per].astype(bf16)
    for b in range(blocks):
        code_ref[b] = jnp.maximum(pre_ref[b].astype(f32), 0.0).T.astype(bf16)


def make_slots(message, first, lat_rows, cap):
    groups, _, tok = message.shape
    blocks = lat_rows // tok
    per = 2 * cap
    shards = groups // 2
    shapes = [(shards, blocks * per, 2 * tok), (blocks, shards * per, tok), (blocks, tok, shards * per)]
    return pl.pallas_call(
        functools.partial(slots_kernel, groups, blocks, cap),
        out_shape=[jax.ShapeDtypeStruct(shape, jnp.bfloat16) for shape in shapes],
        grid_spec=pltpu.PrefetchScalarGridSpec(
            num_scalar_prefetch=1,
            grid=(1,),
            in_specs=[resident(message.shape)],
            out_specs=[resident(shape) for shape in shapes],
        ),
        compiler_params=params(),
        cost_estimate=cost(1),
        name="make_slots",
    )(first[None].astype(jnp.int32), message)


def into_slots(hot, rows, out, z):
    per = out.shape[1] // hot.shape[0]
    value = jnp.dot(hot[z], rows, preferred_element_type=jnp.float32).astype(jnp.bfloat16)
    for b in range(out.shape[0]):
        out[b, z * per:(z + 1) * per, :] = value[b * per:(b + 1) * per]


def lanes_of(refs, rows):
    parts = [r[rows, :] for r in refs]
    return parts[0] if len(parts) == 1 else jnp.concatenate(parts, axis=1)


def piece_grad_kernel(layout, onto, scalar_ref, hot_ref, weight_ref, *refs):
    parts, (slots_ref, grad_ref) = refs[onto:-2], refs[-2:]
    blocks, _, size = grad_ref.shape
    group = hot_ref.shape[2]
    step = pl.program_id(0)

    @pl.when(step == 0)
    def _():
        grad_ref[...] = refs[0][...] if onto else jnp.zeros_like(grad_ref)

    at = 0
    for i, piece in enumerate(layout):
        z = 0
        for lanes in piece:
            here = parts[at:at + lanes]
            at += lanes
            for n in range(here[0].shape[0] // group):

                @pl.when(step == i)
                def _(z=z, n=n, here=here):
                    into_slots(hot_ref, lanes_of(here, slice(n * group, (n + 1) * group)), slots_ref.at[0], z)

                z += 1
    for b in range(blocks):
        grad_ref[b] += lax.dot_general(
            slots_ref[0, b],
            weight_ref[0, b * size:(b + 1) * size, :],
            (((1,), (1,)), ((), ())),
            preferred_element_type=jnp.float32,
        )


def piece_grad(pieces, hot, decoder, columns, size, held):
    lat_rows = decoder.shape[1]
    blocks = lat_rows // size
    slots = hot.shape[0] * hot.shape[1] // blocks
    width = sum(p.shape[1] for p in pieces[0][0])
    flat = [p for piece in pieces for row in piece for p in row]
    onto = [] if held is None else [held]
    return pl.pallas_call(
        functools.partial(piece_grad_kernel, [[len(row) for row in piece] for piece in pieces], len(onto)),
        out_shape=[
            jax.ShapeDtypeStruct((len(pieces), blocks, slots, width), jnp.bfloat16),
            jax.ShapeDtypeStruct((blocks, slots, size), jnp.float32),
        ],
        grid_spec=pltpu.PrefetchScalarGridSpec(
            num_scalar_prefetch=1,
            grid=(len(pieces),),
            in_specs=[resident(hot.shape), pl.BlockSpec((1, lat_rows, width), lambda i, s: (0, 0, s[i]))]
            + [resident(p.shape) for p in onto + flat],
            out_specs=[
                pl.BlockSpec((1, blocks, slots, width), lambda i, s: (i, 0, 0, 0)),
                resident((blocks, slots, size)),
            ],
        ),
        compiler_params=params(),
        cost_estimate=cost(0.8 + 2 * len(pieces)),
        name="piece_grad",
    )(columns.astype(jnp.int32), hot, decoder, *onto, *flat)


def decoder_kernel(skip, scalar_ref, code_ref, slots_ref, *refs):
    out_ref = refs[skip]
    size = code_ref.shape[1]
    for b in range(code_ref.shape[0]):
        out_ref[b * size:(b + 1) * size, :] = jnp.dot(
            code_ref[b], slots_ref[0, b], preferred_element_type=jnp.float32
        ).astype(jnp.bfloat16)


def decoder_part(slots, codes, columns, half, held):
    count, blocks, _, width = slots.shape
    lat_rows = blocks * codes.shape[1]
    onto = [] if held is None else [held]
    return pl.pallas_call(
        functools.partial(decoder_kernel, len(onto)),
        out_shape=jax.ShapeDtypeStruct((lat_rows, half), jnp.bfloat16),
        grid_spec=pltpu.PrefetchScalarGridSpec(
            num_scalar_prefetch=1,
            grid=(count,),
            in_specs=[resident(codes.shape), pl.BlockSpec((1,) + slots.shape[1:], lambda i, s: (i, 0, 0, 0))]
            + [pl.BlockSpec(memory_space=pl.ANY) for _ in onto],
            out_specs=pl.BlockSpec((lat_rows, width), lambda i, s: (0, s[i])),
        ),
        compiler_params=params(),
        input_output_aliases={3: 0} if onto else {},
        cost_estimate=cost(0.7 + 1.3 * count),
        name="decoder_part",
    )(columns.astype(jnp.int32), codes, slots, *onto)


def act_slots_kernel(scalar_ref, hot_ref, own_ref, down_ref, up_ref, down_two_ref, up_two_ref, end_ref, out_ref):
    per = out_ref.shape[1] // hot_ref.shape[0]
    last = end_ref[...]
    zero = jnp.zeros((), last.dtype)
    rows = [
        own_ref[...],
        down_ref[...] + jnp.where(scalar_ref[4] > 0, last, zero),
        down_two_ref[...] + up_two_ref[...],
        up_ref[...] + jnp.where(scalar_ref[5] > 0, last, zero),
    ]
    for i in range(4):
        z = scalar_ref[i]
        value = jnp.dot(hot_ref[z], rows[i], preferred_element_type=jnp.float32).astype(jnp.bfloat16)
        to = pl.ds(pl.multiple_of(z * per, per), per)
        for b in range(out_ref.shape[0]):
            out_ref[b, to, :] = value[b * per:(b + 1) * per]


def act_slots(parts, scalars, hot, count):
    half = parts[0].shape[1]
    slots = hot.shape[0] * hot.shape[1] // count
    tile = half // 4
    return pl.pallas_call(
        act_slots_kernel,
        out_shape=jax.ShapeDtypeStruct((count, slots, half), jnp.bfloat16),
        grid_spec=pltpu.PrefetchScalarGridSpec(
            num_scalar_prefetch=1,
            grid=(4,),
            in_specs=[resident(hot.shape)] + [pl.BlockSpec((part.shape[0], tile), lambda i, s: (0, i)) for part in parts],
            out_specs=pl.BlockSpec((count, slots, tile), lambda i, s: (0, 0, i)),
        ),
        compiler_params=params(),
        cost_estimate=cost(3.3),
        name="act_slots",
    )(scalars, hot, *parts)


def encoder_kernel(cap, shared, pre_ref, own_ref, theirs_ref, act_ref, out_ref):
    size = pre_ref.shape[2]
    for n in range(shared):
        parts = []
        for at in range(0, own_ref.shape[1], 2 * cap):
            for core in range(2):
                here = slice(at + core * cap, at + (core + 1) * cap)
                there = slice(at + (1 - core) * cap, at + (2 - core) * cap)
                parts.append(own_ref[n, here, :] + theirs_ref[n, there, :])
        total = jnp.concatenate(parts, axis=0)
        grad = jnp.where(pre_ref[n].astype(jnp.float32) > 0, total, 0.0).T.astype(jnp.bfloat16)
        out_ref[n * size:(n + 1) * size, :] = jnp.dot(
            grad, act_ref[n], preferred_element_type=jnp.float32
        ).astype(jnp.bfloat16)


def encoder_part(pre, own, theirs, acts, cap):
    blocks, slots, size = pre.shape
    half = acts.shape[2]
    shared = 2 if blocks % 2 == 0 else 1
    block = pl.BlockSpec((shared, slots, size), lambda i: (i, 0, 0))
    return pl.pallas_call(
        functools.partial(encoder_kernel, cap, shared),
        out_shape=jax.ShapeDtypeStruct((blocks * size, half), jnp.bfloat16),
        grid=(blocks // shared,),
        in_specs=[block, block, block, pl.BlockSpec((shared, slots, half), lambda i: (i, 0, 0))],
        out_specs=pl.BlockSpec((shared * size, half), lambda i: (i, 0)),
        compiler_params=params(),
        cost_estimate=cost(6.5),
        name="encoder_part",
    )(pre, own, theirs, acts)


def dense_plan(pre_codes, block_ids, activations, target, decoder):
    lay_count = lax.axis_size("layer")
    lat_count = lax.axis_size("latent")
    dp_count = lax.axis_size("dp")
    lay_here = lax.axis_index("layer")
    lat_here = lax.axis_index("latent")
    dp_here = lax.axis_index("dp")
    tok_count = activations.shape[1]
    model_width = activations.shape[2]
    active_count = block_ids.shape[2]
    block_size = pre_codes.shape[3]
    lat_rows = decoder.shape[1]
    local_blocks = lat_rows // block_size
    half = model_width // dp_count
    group = dp_count * tok_count
    tokens = lat_count * group
    width = half // lay_count
    side = width // 2
    f32, bf16 = jnp.float32, jnp.bfloat16
    first = lat_here * local_blocks
    capacity = 2 * tok_count * active_count // (local_blocks * lat_count)

    def columns(rows, which):
        return lax.dynamic_slice_in_dim(rows, which * half, half, axis=1)

    def places(names, offset, fine=1, sub=0):
        return [(offset + (lay_here ^ r)) * fine + sub for r in names]

    def weight_places(names):
        return jnp.stack(places(names, dp_here * lay_count))

    pre_rows = jnp.swapaxes(pre_codes[0], 0, 1).reshape(active_count * tok_count, block_size)
    id_rows = jnp.pad(block_ids[0].T, ((0, 16 - active_count), (0, 0))).astype(bf16)
    own = jnp.concatenate([pre_rows, id_rows], axis=0)
    at = places((1, 3), dp_here * lay_count, 2, 0) + places((2, 3), dp_here * lay_count, 2, 1)
    send_weights, token = gather_columns(decoder, jnp.stack(at), side)

    message = [own] + [flip(own, "latent", r) for r in range(1, lat_count)]

    own, inputs = lax.optimization_barrier((own, activations[0]))
    acts = jnp.concatenate([columns(inputs, dp_here), flip(columns(inputs, 1 - dp_here), "dp", 1)])
    message, acts = lax.optimization_barrier((join(message, token), acts))
    message = message.reshape((lat_count,) + own.shape)
    up, down = [acts], [acts]

    def next_hops():
        step = len(up)
        up.append(hop(up[-1], "latent", 1, step - 1))
        down.append(hop(down[-1], "latent", -1, step - 1))

    message = jnp.stack([message, flip(message, "dp", 1)], axis=1)
    message = message.reshape(lat_count * dp_count, own.shape[0], block_size)
    next_hops()

    codes = spread_codes(message, first, lat_rows)
    at = places((0, 2), dp_here * lay_count, 2, 0) + places((0, 1), dp_here * lay_count, 2, 1)
    at, codes, target = lax.optimization_barrier((jnp.stack(at), codes, target))
    keep_weights, _ = gather_columns(decoder, at, side)
    goals, _ = gather_columns(target, jnp.stack([which * lay_count + lay_here for which in (dp_here, 1 - dp_here)]), width)
    goals = jnp.concatenate([goals[:, :width], flip(goals[:, width:], "dp", 1)])

    codes = spread_codes(message, first, lat_rows)
    at = places((0, 2), dp_here * lay_count, 2, 0) + places((0, 1), dp_here * lay_count, 2, 1)
    at, codes, target = lax.optimization_barrier((jnp.stack(at), codes, target))
    keep_weights, _ = gather_columns(decoder, at, side)
    goals, _ = gather_columns(target, jnp.stack([which * lay_count + lay_here for which in (dp_here, 1 - dp_here)]), width)
    goals = jnp.concatenate([goals[:, :width], flip(goals[:, width:], "dp", 1)])

    def rows_for(spread, weights, n):
        return jnp.dot(spread, weights[:, n * width:(n + 1) * width], preferred_element_type=f32).astype(bf16)

    got = flip(rows_for(codes, send_weights, 0), "layer", 1), flip(rows_for(codes, send_weights, 1), "layer", 2)
    keep_codes, up[1], down[1] = lax.optimization_barrier((codes, up[1], down[1]))
    if lat_count > 2:
        next_hops()
    kept = rows_for(keep_codes, keep_weights, 0), rows_for(keep_codes, keep_weights, 1)

    def add(one, two):
        return (one[:, side:].astype(f32) + two[:, side:].astype(f32)).astype(bf16)

    far = [flip(add(got[n], kept[n]), "layer", 2 - n) for n in range(2)]
    made = make_slots(message, first, lat_rows, capacity)
    far, goals, up[-1], down[-1], made = lax.optimization_barrier((far, goals, up[-1], down[-1], made))
    while len(up) < lat_count - 1:
        next_hops()
    relay = jnp.where(lat_here == 1, down[-1], up[-1])

    total, *sent = layer_sum((got[0], kept[0], far[0]), (got[1], kept[1], far[1]), lat_count)
    for r in range(1, lat_count):
        total = total + flip(sent[r - 1], "latent", r).astype(f32)
    errors = ((total - goals.astype(f32)) / tok_count).astype(bf16)
    others = [flip(errors, "latent", r) for r in range(1, lat_count)]
    one_near, two_near = flip(errors, "layer", 1), flip(errors, "layer", 2)
    next_block, *others = others
    one_next, two_next = flip(next_block, "layer", 1), flip(next_block, "layer", 2)
    others, two_next, one_next, two_near, one_near, next_block, relay = lax.optimization_barrier(
        (others, two_next, one_next, two_near, one_near, next_block, relay)
    )
    distant = join(others)
    one_far, two_far = flip(distant, "layer", 1), flip(distant, "layer", 2)
    ends = lax.ppermute(relay, "latent", [(lat_count - 2, lat_count - 1), (1, 0)])

    hot, pre_slots, code_slots = made

    def grads_of(here, names, grad, dec):
        slots, grad = piece_grad(here, hot, decoder, weight_places(names), block_size, grad)
        return grad, decoder_part(slots, code_slots, jnp.stack(places(names, 0)), half, dec)

    grad, dec = grads_of([[(errors,), (next_block,), (distant,)]], (0,), None, None)
    grad, dec, two_far, one_far = lax.optimization_barrier((grad, dec, two_far, one_far))
    one, two = (one_near, one_next, one_far), (two_near, two_next, two_far)
    three_a = flip(jnp.concatenate([rows[:, :side] for rows in two]), "layer", 1)
    three_b = flip(jnp.concatenate([rows[:, side:] for rows in one]), "layer", 2)
    grad, dec = grads_of([[(rows,) for rows in one], [(rows,) for rows in two]], (1, 2), grad, dec)

    scalars = [lax.rem(lat_here + k, lat_count) ^ lat_here for k in range(lat_count)]
    scalars = jnp.stack(scalars + [(lat_here == lat_count - 1).astype(jnp.int32), (lat_here == 0).astype(jnp.int32)])
    slotted = act_slots((acts, down[1], up[1], down[2], up[2], ends), scalars, hot, local_blocks)
    three_a, three_b, grad, dec = lax.optimization_barrier((three_a, three_b, grad, dec))
    grad, dec = grads_of([[(three_a, three_b)]], (3,), grad, dec)
    enc = encoder_part(pre_slots, grad, flip(grad, "dp", 1), slotted, capacity)
    return dec[None], enc[None]


def per_device(pre_codes, block_ids, activations, target, decoder):
    lat_count = lax.axis_size("latent")
    lay_count = lax.axis_size("layer")
    dp_count = lax.axis_size("dp")
    tok_count = activations.shape[1]
    model_width = activations.shape[2]
    active_count = block_ids.shape[2]
    block_size = pre_codes.shape[3]
    all_blocks = decoder.shape[1] // block_size * lat_count
    slots = 2 * tok_count * active_count // lat_count
    dense = (
        slots >= tok_count
        and dp_count == 2
        and active_count == 2
        and lay_count == 4
        and lat_count == 4
        and tok_count == block_size
        and lat_count * dp_count * 16 <= tok_count
        and model_width % (dp_count * 2 * lay_count * 128) == 0
        and all_blocks <= 256
        and 2 * tok_count * active_count == 8 * all_blocks
    )
    plan = dense_plan if dense else slot_plan
    return plan(pre_codes, block_ids, activations, target, decoder)


def solution(mesh):
    placed = (
        P("layer", ("latent", "dp"), None, None),
        P("layer", ("latent", "dp"), None),
        P("layer", ("latent", "dp"), None),
        P(("latent", "dp"), None),
        P("layer", "latent", None),
    )
    return jax.shard_map(
        per_device,
        mesh=mesh,
        in_specs=placed,
        out_specs=(P("layer", "latent", "dp"), P("layer", "latent", "dp")),
        check_vma=False,
    )
```
